32 devices in a mesh: dp: 4 (over y, core), ctx: 8 (over z, x).
Axes of the slice: x: 2, y: 2, z: 4, core: 2. Of those that a mesh axis runs over, the one named last changes fastest.
Arguments:
- layer_input: bfloat16 [2, 4, 1024, 768], P(None, 'dp', 'ctx'), may hold values from -6 to 6
- doc_lengths: int32 [2, 4, 5], P(None, 'dp'), may hold values from 1 to 1020, as said below
- ln1_gain: float32 [768], replicated, may hold values from 0.5 to 1.5
- ln1_bias: float32 [768], replicated, may hold values from -3 to 3
- w_qkv: bfloat16 [768, 2304], P('dp'), may hold values from -0.21875 to 0.21875
- w_out: bfloat16 [768, 768], P('dp'), may hold values from -1.25 to 1.25
- ln2_gain: float32 [768], replicated, may hold values from 0.5 to 1.5
- ln2_bias: float32 [768], replicated, may hold values from -3 to 3
- w_up: bfloat16 [768, 3072], P('dp'), may hold values from -0.21875 to 0.21875
- b_up: float32 [3072], replicated, may hold values from -3 to 3
- w_down: bfloat16 [3072, 768], P('dp'), may hold values from -0.109375 to 0.109375
- cotangent: bfloat16 [2, 4, 1024, 768], P(None, 'dp', 'ctx'), may hold values from -6 to 6
Outputs:
- layer_output: bfloat16 [2, 4, 1024, 768], P(None, 'dp', 'ctx')
- d_x: bfloat16 [2, 4, 1024, 768], P(None, 'dp', 'ctx')
- d_ln1_gain: float32 [768], replicated
- d_ln1_bias: float32 [768], replicated
- d_w_qkv: float32 [768, 2304], P('dp', 'ctx')
- d_w_out: float32 [768, 768], P('dp', 'ctx')
- d_ln2_gain: float32 [768], replicated
- d_ln2_bias: float32 [768], replicated
- d_w_up: float32 [768, 3072], P('dp', 'ctx')
- d_b_up: float32 [3072], replicated
- d_w_down: float32 [3072, 768], P('dp', 'ctx')
The draws below stay inside these ranges and needn't reach their ends.
Inputs may be any that keep to these rules, and one draw needn't show every extreme that they name: `doc_lengths`: each row packs 5 documents in order: a first one shorter than 128 tokens, a second one that ends within the last 128 positions of the row, then 5 - 2 documents of at most 32 tokens each; positions after their sum are padding. Some row of each draw has padding of zero length.
All inputs are finite; a program needn't handle non-finite values.
Results may differ from the reference program's by a relative error of at most 0.014.
Values may be sent and summed in bfloat16 or wider, within the bound.
A program may use at most 256 MiB of HBM per device.

```python
import jax
import jax.numpy as jnp
from jax import lax

D = 768
HD = 64
FF = 3072
MB = 2
NDOC = 5
Q_DEV = 128
BATCH = 4
ROW = 1024
KEY_BLOCK = 512


def draw_doc_lengths(key, part):
    key = jax.random.fold_in(key, 11)
    key_parts = jax.random.split(key, 4)
    row_count = MB * BATCH
    quarter = Q_DEV // 4
    first_len = jax.random.randint(key_parts[0], (row_count,), 1, Q_DEV)
    tail_lens = jax.random.randint(key_parts[1], (row_count, NDOC - 2), 1, quarter + 1)
    padding = jax.random.randint(key_parts[2], (row_count,), 0, quarter)
    forced_row = jax.random.randint(key_parts[3], (), 0, row_count)
    is_forced = jnp.arange(row_count) == forced_row
    first_len = jnp.where(is_forced, 1, first_len)
    tail_lens = jnp.where(is_forced[:, None], 1, tail_lens)
    padding = jnp.where(is_forced, 0, padding)
    long_len = ROW - first_len - jnp.sum(tail_lens, axis=1).astype(jnp.int32) - padding
    lengths = jnp.concatenate([first_len[:, None], long_len[:, None], tail_lens], axis=1)
    return lengths.reshape(MB, BATCH, NDOC).astype(jnp.int32)


def block_scale(own_key, extent, cuts, least, high):
    loudness = 1.0
    for axis_at, parts in cuts:
        heights = jax.random.uniform(jax.random.fold_in(jax.random.fold_in(own_key, 6), axis_at), (parts,), jnp.float32, least / len(cuts), high / len(cuts))
        loudness = loudness * jnp.repeat(jnp.exp(heights), extent[axis_at] // parts).reshape((-1,) + (1,) * (len(extent) - 1 - axis_at))
    return loudness


def bell_draw(rng, extent, deviation, limit, cuts=(), held_as=jnp.bfloat16):
    entries = deviation * jax.random.normal(rng, extent, jnp.float32)
    if cuts:
        entries = entries * block_scale(rng, extent, cuts, -0.22, 0.18)
    return jnp.clip(entries, -limit, limit).astype(held_as)


def setup_inputs(seed: int = 0) -> dict:
    seeds = jax.random.split(jax.random.key(seed), 13)
    return {
        "layer_input": bell_draw(seeds[0], (MB, BATCH, ROW, D), 1.0, 6.0, ((1, 4), (2, 8))),
        "doc_lengths": draw_doc_lengths(jax.random.fold_in(seeds[12], 71), 0),
        "ln1_gain": jnp.clip(1.0 + 0.1 * jax.random.normal(seeds[2], (D,), jnp.float32), 0.5, 1.5),
        "ln1_bias": bell_draw(seeds[3], (D,), 0.5, 3.0, (), jnp.float32),
        "w_qkv": bell_draw(seeds[4], (D, 3 * D), D ** -0.5, 0.21875, ((0, 4),)),
        "w_out": bell_draw(seeds[5], (D, D), (max(1, D * 32 // ROW)) ** -0.5, 1.25, ((0, 4),)),
        "ln2_gain": jnp.clip(1.0 + 0.1 * jax.random.normal(seeds[6], (D,), jnp.float32), 0.5, 1.5),
        "ln2_bias": bell_draw(seeds[7], (D,), 0.5, 3.0, (), jnp.float32),
        "w_up": bell_draw(seeds[8], (D, FF), D ** -0.5, 0.21875, ((0, 4),)),
        "b_up": bell_draw(seeds[9], (FF,), 0.5, 3.0, (), jnp.float32),
        "w_down": bell_draw(seeds[10], (FF, D), FF ** -0.5, 0.109375, ((0, 4),)),
        "cotangent": bell_draw(seeds[11], (MB, BATCH, ROW, D), 1.0, 6.0, ((1, 4), (2, 8))),
    }


NORM_EPSILON = 1e-05
MASKED = -1e+30
HIGHEST_PRECISION = lax.Precision.HIGHEST

@jax.custom_vjp
def low(v):
    return lax.optimization_barrier(v.astype(jnp.bfloat16)).astype(jnp.float32)

@jax.custom_vjp
def low_back(v):
    return v

def low_keep(v):
    return (low(v), None)

def low_pass(kept, grad):
    return (grad,)

def back_keep(v):
    return (v, None)

def back_low(kept, grad):
    return (low(grad),)
low.defvjp(low_keep, low_pass)
low_back.defvjp(back_keep, back_low)

def layer_norm(value, gain, bias):
    row_mean = lax.optimization_barrier(jnp.mean(value, axis=-1, keepdims=True))
    centered = value - row_mean
    spread = lax.optimization_barrier(jnp.mean(centered * centered, axis=-1, keepdims=True))
    return centered * lax.rsqrt(spread + NORM_EPSILON) * gain + bias

def matmul(left, right):
    return jnp.dot(left, right, precision=HIGHEST_PRECISION)

def segment_table(lengths, row_length):
    doc_ends = jnp.cumsum(lengths).astype(jnp.int32)
    places = jnp.arange(row_length, dtype=jnp.int32)
    segment = lax.optimization_barrier(jnp.sum((places[:, None] >= doc_ends[None, :]).astype(jnp.int32), axis=1)).astype(jnp.int32)
    opening = jnp.concatenate([jnp.ones((1,), jnp.bool_), segment[1:] != segment[:-1]])
    return (segment, opening)

def row_forward(params, row_data, segment, opening):
    ln1_gain, ln1_bias, w_qkv, w_out, ln2_gain, ln2_bias, w_up, b_up, w_down = params
    row_length = row_data.shape[0]
    head_count = D // HD
    score_scale = HD ** (-0.5)
    strength = 8.0 / ROW
    normed_one = low(layer_norm(row_data, ln1_gain, ln1_bias))
    projected = low(low_back(matmul(normed_one, w_qkv)))
    queries = projected[:, :D].reshape(row_length, head_count, HD)
    keys_all = projected[:, D:2 * D].reshape(row_length, head_count, HD)
    values_all = projected[:, 2 * D:].reshape(row_length, head_count, HD)
    places = jnp.arange(row_length, dtype=jnp.int32)
    block_count = row_length // KEY_BLOCK

    def block(prefix, row_item):
        query_block, query_seg, query_pos = row_item
        scores = low_back(jnp.einsum('qhd,khd->hqk', query_block, keys_all, precision=HIGHEST_PRECISION) * score_scale)
        same_doc = query_seg[:, None] == segment[None, :]
        allowed = same_doc & (places[None, :] <= query_pos[:, None])
        chosen = same_doc & (places[None, :] < query_pos[:, None]) & jnp.logical_not(opening)[None, :]
        picked = jnp.where(chosen, strength * jax.nn.softplus(scores[0]), 0.0)
        penalty = prefix[None, :] + jnp.cumsum(picked, axis=0) - picked
        logits = jnp.where(allowed[None], scores - penalty[None], MASKED)
        row_top = lax.optimization_barrier(jnp.max(logits, axis=-1, keepdims=True))
        weights = jnp.exp(logits - row_top)
        normalized = weights / lax.optimization_barrier(jnp.sum(weights, axis=-1, keepdims=True))
        block_out = jnp.einsum('hqk,khd->qhd', low(normalized), values_all, precision=HIGHEST_PRECISION)
        return (prefix + lax.optimization_barrier(jnp.sum(picked, axis=0)), block_out)
    _, block_outs = lax.scan(jax.checkpoint(block), jnp.zeros((row_length,), jnp.float32), (queries.reshape(block_count, KEY_BLOCK, head_count, HD), segment.reshape(block_count, KEY_BLOCK), places.reshape(block_count, KEY_BLOCK)))
    attended = low(low_back(block_outs.reshape(row_length, D)))
    mid_stream = row_data + low_back(matmul(attended, w_out))
    normed_two = low(layer_norm(mid_stream, ln2_gain, ln2_bias))
    hidden = low_back(matmul(normed_two, w_up) + b_up)
    activated = low(jax.nn.gelu(hidden, approximate=False))
    return mid_stream + low_back(matmul(activated, w_down))

def reference(layer_input, doc_lengths, ln1_gain, ln1_bias, w_qkv, w_out, ln2_gain, ln2_bias, w_up, b_up, w_down, cotangent):
    row_count = MB * BATCH
    row_data = layer_input.astype(jnp.float32).reshape(row_count, ROW, D)
    cot_rows = cotangent.astype(jnp.float32).reshape(row_count, ROW, D)

    def table_of(lengths):
        return segment_table(lengths, ROW)
    segment, opening = jax.vmap(table_of)(doc_lengths.reshape(row_count, NDOC))
    params = tuple((value.astype(jnp.float32) for value in (ln1_gain, ln1_bias, w_qkv, w_out, ln2_gain, ln2_bias, w_up, b_up, w_down)))

    def forward(all_rows, weights):
        row_fn = jax.checkpoint(row_forward)

        def row_step(running, row_item):
            return (running, row_fn(weights, row_item[0], row_item[1], row_item[2]))
        _, outputs = lax.scan(row_step, jnp.zeros((), jnp.float32), (all_rows, segment, opening))
        return outputs
    outputs, pull = jax.vjp(forward, row_data, params)
    grad_rows, grad_params = pull(cot_rows)
    return (outputs.astype(jnp.bfloat16).reshape(layer_input.shape), grad_rows.astype(jnp.bfloat16).reshape(layer_input.shape), grad_params[0], grad_params[1], grad_params[2], grad_params[3], grad_params[4], grad_params[5], grad_params[6], grad_params[7], grad_params[8])
```

```python
import math
from functools import partial

import jax
import jax.numpy as jnp
from jax import lax
from jax.experimental import pallas as pl
from jax.experimental.pallas import tpu as pltpu
from jax.sharding import PartitionSpec as P

HD = 64


NORM_EPSILON = 1e-05
MASKED = -1e30
START_TOP = -1e20


def prefix_2(array, axis, combine, identity, reverse):
    peers, index = (lax.axis_size(axis), lax.axis_index(axis))
    everything = lax.all_gather(array, axis)
    start = jnp.broadcast_to(jnp.asarray(identity, array.dtype), array.shape)

    def turn(k, before):
        at = peers - 1 - k if reverse else k
        reached = at > index if reverse else at < index
        new = combine(before, everything[at])
        return jnp.where(reached, new, before)

    return lax.fori_loop(0, peers, turn, start)


def layer_norm(value, gain, bias):
    row_mean = jnp.mean(value, axis=-1, keepdims=True)
    centered = value - row_mean
    spread = jnp.mean(centered * centered, axis=-1, keepdims=True)
    return centered * lax.rsqrt(spread + NORM_EPSILON) * gain + bias


def matmul(left, right):
    return jnp.dot(left, right, preferred_element_type=jnp.float32)


def contract_rows(left, right):
    return lax.dot_general(
        left, right, (((0,), (0,)), ((), ())), preferred_element_type=jnp.float32
    )


def contract_cols(left, right):
    return lax.dot_general(
        left, right, (((1,), (1,)), ((), ())), preferred_element_type=jnp.float32
    )


def segment_table(lengths, row_length):
    doc_ends = jnp.cumsum(lengths)
    places = jnp.arange(row_length, dtype=jnp.int32)
    segment = jnp.sum((places[:, None] >= doc_ends[None, :]).astype(jnp.int32), axis=1)
    opening = jnp.concatenate([jnp.ones((1,), jnp.bool_), segment[1:] != segment[:-1]])
    return (segment, opening)


def add_up(earlier, later):
    return earlier + later


def per_token_device(
    layer_input,
    doc_lengths,
    ln1_gain,
    ln1_bias,
    w_qkv,
    w_out,
    ln2_gain,
    ln2_bias,
    w_up,
    b_up,
    w_down,
    cotangent,
):
    micro_count = layer_input.shape[0]
    query_rows = layer_input.shape[2]
    model_width = layer_input.shape[3]
    head_count = model_width // HD
    row_length = query_rows * lax.axis_size("ctx")
    key_block = min(512, row_length)
    score_scale = HD ** (-0.5)
    strength = 8.0 / row_length
    ctx_place = lax.axis_index("ctx")
    query_pos = ctx_place * query_rows + jnp.arange(query_rows, dtype=jnp.int32)
    block_total = ((ctx_place + 1) * query_rows + key_block - 1) // key_block
    later_heads = (jnp.arange(head_count) > 0).astype(jnp.float32)[:, None, None]
    zeros_row = jnp.zeros((row_length,), jnp.float32)
    gelu_exact = partial(jax.nn.gelu, approximate=False)
    output_list = []
    input_grads = []
    matrix_total = None
    vector_total = None
    for micro_step in range(micro_count):
        w_qkv_all, w_out_all, w_up_all, w_down_all = (
            lax.all_gather(w_qkv, "dp", axis=0, tiled=True),
            lax.all_gather(w_out, "dp", axis=0, tiled=True),
            lax.all_gather(w_up, "dp", axis=0, tiled=True),
            lax.all_gather(w_down, "dp", axis=0, tiled=True),
        )
        inputs = layer_input[micro_step, 0].astype(jnp.float32)
        segment, opening = segment_table(doc_lengths[micro_step, 0], row_length)
        query_seg = lax.dynamic_slice_in_dim(segment, ctx_place * query_rows, query_rows, 0)
        normed_one = layer_norm(inputs, ln1_gain, ln1_bias).astype(jnp.bfloat16)
        projected = matmul(normed_one, w_qkv_all).astype(jnp.bfloat16)
        queries = projected[:, :model_width]
        queries3 = queries.reshape(query_rows, head_count, HD)
        query_zero = queries[:, :HD]
        keys_all, values_all = (
            lax.all_gather(projected[:, model_width : 2 * model_width], "ctx", axis=0, tiled=True),
            lax.all_gather(projected[:, 2 * model_width :], "ctx", axis=0, tiled=True),
        )

        def masks(key_start):
            key_seg = lax.dynamic_slice_in_dim(segment, key_start, key_block, 0)
            key_open = lax.dynamic_slice_in_dim(opening, key_start, key_block, 0)
            key_pos = key_start + jnp.arange(key_block, dtype=jnp.int32)
            same_doc = query_seg[:, None] == key_seg[None, :]
            allowed = same_doc & (key_pos[None, :] <= query_pos[:, None])
            chosen = (
                same_doc
                & (key_pos[None, :] < query_pos[:, None])
                & jnp.logical_not(key_open)[None, :]
            )
            return (allowed, chosen.astype(jnp.float32))

        def head_scores(key_start):
            key_zero = lax.dynamic_slice_in_dim(keys_all, key_start, key_block, 0)[:, :HD]
            return (key_zero, contract_cols(query_zero, key_zero) * score_scale)

        def block_keys(key_start):
            keys3 = lax.dynamic_slice_in_dim(keys_all, key_start, key_block, 0).reshape(
                key_block, head_count, HD
            )
            values3 = lax.dynamic_slice_in_dim(values_all, key_start, key_block, 0).reshape(
                key_block, head_count, HD
            )
            return (keys3, values3)

        def logits_of(key_start, keys3):
            allowed, chosen = masks(key_start)
            raw_scores = (
                jnp.einsum("qhd,khd->hqk", queries3, keys3, preferred_element_type=jnp.float32)
                * score_scale
            )
            picked = strength * jax.nn.softplus(raw_scores[0]) * chosen
            before = lax.dynamic_slice_in_dim(prefix, key_start, key_block, 0)
            penalty = before[None, :] + jnp.cumsum(picked, axis=0) - picked
            return jnp.where(allowed[None], raw_scores - penalty[None], MASKED)

        def total_block(block_index, totals):
            key_start = block_index * key_block
            _, chosen = masks(key_start)
            _, first_scores = head_scores(key_start)
            picked = strength * jax.nn.softplus(first_scores) * chosen
            return lax.dynamic_update_slice_in_dim(totals, jnp.sum(picked, axis=0), key_start, 0)

        totals = lax.fori_loop(0, block_total, total_block, zeros_row)
        prefix = prefix_2(totals, "ctx", add_up, zeros_row, False)

        def stat_block(block_index, running):
            row_top, row_total = running
            key_start = block_index * key_block
            keys3, _ = block_keys(key_start)
            logits = logits_of(key_start, keys3)
            new_top = jnp.maximum(row_top, jnp.max(logits, axis=-1))
            row_total = row_total * jnp.exp(row_top - new_top) + jnp.sum(
                jnp.exp(logits - new_top[..., None]), axis=-1
            )
            return (new_top, row_total)

        row_top, row_total = lax.fori_loop(
            0,
            block_total,
            stat_block,
            (
                jnp.full((head_count, query_rows), START_TOP, jnp.float32),
                jnp.zeros((head_count, query_rows), jnp.float32),
            ),
        )
        log_total = row_top + jnp.log(row_total)

        def out_block(block_index, gathered_out):
            key_start = block_index * key_block
            keys3, values3 = block_keys(key_start)
            attn_probs = jnp.exp(logits_of(key_start, keys3) - log_total[..., None]).astype(
                jnp.bfloat16
            )
            return gathered_out + jnp.einsum(
                "hqk,khd->qhd", attn_probs, values3, preferred_element_type=jnp.float32
            )

        gathered_out = lax.fori_loop(
            0, block_total, out_block, jnp.zeros((query_rows, head_count, HD), jnp.float32)
        )
        attended = gathered_out.reshape(query_rows, model_width).astype(jnp.bfloat16)
        mid_stream = inputs + matmul(attended, w_out_all)
        normed_two = layer_norm(mid_stream, ln2_gain, ln2_bias).astype(jnp.bfloat16)
        hidden = matmul(normed_two, w_up_all) + b_up
        activated = gelu_exact(hidden).astype(jnp.bfloat16)
        output_list.append((mid_stream + matmul(activated, w_down_all)).astype(jnp.bfloat16))
        cot_rows = cotangent[micro_step, 0]
        grad_down = contract_rows(activated, cot_rows)
        grad_act = contract_cols(cot_rows, w_down_all)
        _, gelu_back = jax.vjp(gelu_exact, hidden)
        grad_hidden = gelu_back(grad_act)[0].astype(jnp.bfloat16)
        grad_up = contract_rows(normed_two, grad_hidden)
        grad_bias_up = jnp.sum(grad_hidden.astype(jnp.float32), axis=0)
        grad_normed_two = contract_cols(grad_hidden, w_up_all)
        _, norm_two_back = jax.vjp(layer_norm, mid_stream, ln2_gain, ln2_bias)
        grad_mid_part, grad_gain_two, grad_bias_two = norm_two_back(grad_normed_two)
        grad_mid = cot_rows.astype(jnp.float32) + grad_mid_part
        grad_branch = grad_mid.astype(jnp.bfloat16)
        grad_outproj = contract_rows(attended, grad_branch)
        grad_attended = contract_cols(grad_branch, w_out_all).astype(jnp.bfloat16)
        grad_att3 = grad_attended.reshape(query_rows, head_count, HD)
        row_delta = jnp.einsum("qhd,qhd->hq", grad_att3.astype(jnp.float32), gathered_out)

        def grad_block(block_index, running):
            grad_query, grad_key_all, grad_value_all, penalty_grad, first_grad = running
            key_start = block_index * key_block
            keys3, values3 = block_keys(key_start)
            probs_f32 = jnp.exp(logits_of(key_start, keys3) - log_total[..., None])
            grad_probs = jnp.einsum(
                "qhd,khd->hqk", grad_att3, values3, preferred_element_type=jnp.float32
            )
            grad_logits = probs_f32 * (grad_probs - row_delta[..., None])
            penalty_grad = lax.dynamic_update_slice_in_dim(
                penalty_grad, -jnp.sum(grad_logits, axis=0), key_start, 1
            )
            first_grad = lax.dynamic_update_slice_in_dim(first_grad, grad_logits[0], key_start, 1)
            grad_scores = (grad_logits * later_heads).astype(jnp.bfloat16)
            grad_query = (
                grad_query
                + jnp.einsum("hqk,khd->qhd", grad_scores, keys3, preferred_element_type=jnp.float32)
                * score_scale
            )
            key_part = (
                jnp.einsum(
                    "hqk,qhd->khd", grad_scores, queries3, preferred_element_type=jnp.float32
                )
                * score_scale
            )
            value_part = jnp.einsum(
                "hqk,qhd->khd",
                probs_f32.astype(jnp.bfloat16),
                grad_att3,
                preferred_element_type=jnp.float32,
            )
            grad_key_all = lax.dynamic_update_slice_in_dim(
                grad_key_all, key_part.reshape(key_block, model_width), key_start, 0
            )
            grad_value_all = lax.dynamic_update_slice_in_dim(
                grad_value_all, value_part.reshape(key_block, model_width), key_start, 0
            )
            return (grad_query, grad_key_all, grad_value_all, penalty_grad, first_grad)

        grad_query, grad_key_all, grad_value_all, penalty_grad, first_grad = lax.fori_loop(
            0,
            block_total,
            grad_block,
            (
                jnp.zeros((query_rows, head_count, HD), jnp.float32),
                jnp.zeros((row_length, model_width), jnp.float32),
                jnp.zeros((row_length, model_width), jnp.float32),
                jnp.zeros((query_rows, row_length), jnp.float32),
                jnp.zeros((query_rows, row_length), jnp.float32),
            ),
        )
        column_sums = jnp.sum(penalty_grad, axis=0)
        after = prefix_2(column_sums, "ctx", add_up, zeros_row, True)
        reach_sums = after + column_sums

        def head_block(block_index, running):
            grad_query_zero, grad_key_all = running
            key_start = block_index * key_block
            _, chosen = masks(key_start)
            key_zero, first_scores = head_scores(key_start)
            flow_block = lax.dynamic_slice_in_dim(penalty_grad, key_start, key_block, 1)
            reach_block = lax.dynamic_slice_in_dim(reach_sums, key_start, key_block, 0)
            grad_picked = reach_block[None, :] - jnp.cumsum(flow_block, axis=0)
            grad_select = grad_picked * strength * jax.nn.sigmoid(first_scores) * chosen
            grad_head = (
                lax.dynamic_slice_in_dim(first_grad, key_start, key_block, 1) + grad_select
            ).astype(jnp.bfloat16)
            grad_query_zero = grad_query_zero + matmul(grad_head, key_zero) * score_scale
            key_zero_grad = contract_rows(grad_head, query_zero) * score_scale
            grad_key_all = lax.dynamic_update_slice(
                grad_key_all, key_zero_grad, (key_start, jnp.zeros((), jnp.int32))
            )
            return (grad_query_zero, grad_key_all)

        grad_query_zero, grad_key_all = lax.fori_loop(
            0, block_total, head_block, (jnp.zeros((query_rows, HD), jnp.float32), grad_key_all)
        )
        grad_query = grad_query.at[:, 0, :].add(grad_query_zero).reshape(query_rows, model_width)
        grad_key_own, grad_value_own = (
            lax.psum_scatter(grad_key_all, "ctx", scatter_dimension=0, tiled=True),
            lax.psum_scatter(grad_value_all, "ctx", scatter_dimension=0, tiled=True),
        )
        grad_project = jnp.concatenate([grad_query, grad_key_own, grad_value_own], axis=1).astype(
            jnp.bfloat16
        )
        grad_qkv = contract_rows(normed_one, grad_project)
        grad_normed_one = contract_cols(grad_project, w_qkv_all)
        _, norm_one_back = jax.vjp(layer_norm, inputs, ln1_gain, ln1_bias)
        grad_in_part, grad_gain_one, grad_bias_one = norm_one_back(grad_normed_one)
        input_grads.append((grad_mid + grad_in_part).astype(jnp.bfloat16))
        matrix_grads = (grad_qkv, grad_outproj, grad_up, grad_down)
        vector_grads = (grad_gain_one, grad_bias_one, grad_gain_two, grad_bias_two, grad_bias_up)
        matrix_grads = (
            lax.psum_scatter(matrix_grads[0], "ctx", scatter_dimension=1, tiled=True),
            lax.psum_scatter(matrix_grads[1], "ctx", scatter_dimension=1, tiled=True),
            lax.psum_scatter(matrix_grads[2], "ctx", scatter_dimension=1, tiled=True),
            lax.psum_scatter(matrix_grads[3], "ctx", scatter_dimension=1, tiled=True),
        )
        matrix_grads = (
            lax.psum_scatter(
                matrix_grads[0].astype(jnp.bfloat16), "dp", scatter_dimension=0, tiled=True
            ).astype(jnp.float32),
            lax.psum_scatter(
                matrix_grads[1].astype(jnp.bfloat16), "dp", scatter_dimension=0, tiled=True
            ).astype(jnp.float32),
            lax.psum_scatter(
                matrix_grads[2].astype(jnp.bfloat16), "dp", scatter_dimension=0, tiled=True
            ).astype(jnp.float32),
            lax.psum_scatter(
                matrix_grads[3].astype(jnp.bfloat16), "dp", scatter_dimension=0, tiled=True
            ).astype(jnp.float32),
        )
        vector_grads = lax.psum(
            (vector_grads[0], vector_grads[1], vector_grads[2], vector_grads[3], vector_grads[4]),
            ("dp", "ctx"),
        )
        if matrix_total is None:
            matrix_total = matrix_grads
            vector_total = vector_grads
        else:
            matrix_total = tuple((old + new for old, new in zip(matrix_total, matrix_grads)))
            vector_total = tuple((old + new for old, new in zip(vector_total, vector_grads)))
    layer_out = jnp.stack(output_list)[:, None]
    input_out = jnp.stack(input_grads)[:, None]
    return (
        layer_out,
        input_out,
        vector_total[0],
        vector_total[1],
        matrix_total[0],
        matrix_total[1],
        vector_total[2],
        vector_total[3],
        matrix_total[2],
        vector_total[4],
        matrix_total[3],
    )


MESH = pl.DeviceIdType.MESH
EXCLUDED = 1e30
QUERY_BLOCK = 256


def whole(ref, peer):
    return ref


def piece(ref, peer):
    return ref.at[peer]


def exchange_body(jobs, sizes, *refs):
    count = len(jobs)
    sources, targets = refs[:count], refs[count : 2 * count]
    send_sems, recv_sems = refs[2 * count : 3 * count], refs[3 * count : 4 * count]
    local_sem = refs[4 * count]
    barrier = pltpu.get_barrier_semaphore()
    greeted = 0
    for axis, size in sizes.items():
        me = lax.axis_index(axis)
        for step in range(1, size):
            pl.semaphore_signal(
                barrier, inc=1, device_id={axis: lax.rem(me + step, size)}, device_id_type=MESH
            )
            greeted += 1
    own = []
    for at, (axis, select) in enumerate(jobs):
        me = lax.axis_index(axis)
        copy = pltpu.make_async_copy(
            select(sources[at], me), targets[at].at[me], local_sem.at[at]
        )
        copy.start()
        own.append(copy)
    pl.semaphore_wait(barrier, greeted)
    sent = []
    for at, (axis, select) in enumerate(jobs):
        me, size = lax.axis_index(axis), sizes[axis]
        for step in range(1, size):
            peer = lax.rem(me + step, size)
            copy = pltpu.make_async_remote_copy(
                src_ref=select(sources[at], peer),
                dst_ref=targets[at].at[me],
                send_sem=send_sems[at].at[step - 1],
                recv_sem=recv_sems[at].at[step - 1],
                device_id={axis: peer},
                device_id_type=MESH,
            )
            copy.start()
            sent.append(copy)
    for copy in own + sent:
        copy.wait()


def exchange(collective_id, name, *jobs):
    arrays = [job[0] for job in jobs]
    axes = [job[1] for job in jobs]
    sizes = {axis: lax.axis_size(axis) for axis in axes}
    count = len(jobs)
    return pl.pallas_call(
        partial(exchange_body, [(job[1], job[2]) for job in jobs], sizes),
        out_shape=[
            jax.ShapeDtypeStruct((sizes[axis],) + tuple(job[3]), job[0].dtype)
            for axis, job in zip(axes, jobs)
        ],
        in_specs=[pl.BlockSpec(memory_space=pl.ANY)] * count,
        out_specs=[pl.BlockSpec(memory_space=pl.ANY)] * count,
        scratch_shapes=[pltpu.SemaphoreType.DMA((sizes[axis] - 1,)) for axis in axes] * 2
        + [pltpu.SemaphoreType.DMA((count,))],
        compiler_params=pltpu.CompilerParams(
            collective_id=collective_id, has_side_effects=True
        ),
        name=name,
    )(*arrays)


def segment_of(places, ends_ref, doc_count):
    total = jnp.zeros(places.shape, jnp.int32)
    for at in range(doc_count):
        total += jnp.where(places >= ends_ref[at], 1, 0)
    return total


def attend_body(hpg, strength, doc_count, ends_ref, proj_ref, probs_ref, slope_ref, out_ref, inv_ref, prefix):
    rows_all = proj_ref.shape[0]
    width = hpg * HD
    block = QUERY_BLOCK
    prefix[...] = jnp.zeros_like(prefix)
    row_at = lax.broadcasted_iota(jnp.int32, (block, block), 0)
    col_at = lax.broadcasted_iota(jnp.int32, (block, block), 1)
    earlier = (col_at < row_at).astype(jnp.bfloat16)
    scale = HD ** (-0.5)
    for start in range(0, rows_all, block):
        reach = start + block
        rows = pl.ds(start, block)
        row_pos = start + lax.broadcasted_iota(jnp.int32, (block, 1), 0)
        col_pos = lax.broadcasted_iota(jnp.int32, (1, reach), 1)
        row_seg = segment_of(row_pos, ends_ref, doc_count)
        col_seg = segment_of(col_pos, ends_ref, doc_count)
        before_seg = segment_of(col_pos - 1, ends_ref, doc_count)
        opening = (col_seg != before_seg) | (col_pos == 0)
        pick_seg = jnp.where(opening, -1, col_seg)
        query = proj_ref[rows, 3 * width : 3 * width + HD] * scale
        key = proj_ref[:reach, 3 * width + HD : 3 * width + 2 * HD]
        scores = contract_cols(query.astype(jnp.bfloat16), key)
        small = jnp.exp(-jnp.abs(scores))
        soft = jnp.maximum(scores, 0.0) + jnp.log(1.0 + small)
        recip = 1.0 / (1.0 + small)
        sigmoid = jnp.where(scores >= 0.0, recip, small * recip)
        chosen = (row_seg == pick_seg) & (col_pos < row_pos)
        picked = jnp.where(chosen, strength * soft, 0.0)
        slope_ref[rows, :reach] = jnp.where(chosen, strength * sigmoid, 0.0).astype(jnp.bfloat16)
        high = picked.astype(jnp.bfloat16)
        low = (picked - high.astype(jnp.float32)).astype(jnp.bfloat16)
        penalty = prefix[:, :reach] + (matmul(earlier, high) + matmul(earlier, low))
        allowed = (row_seg == col_seg) & (col_pos <= row_pos)
        penalty = jnp.where(allowed, penalty, EXCLUDED)
        prefix[:, :reach] += jnp.sum(picked, axis=0, keepdims=True)
        for head in range(hpg):
            at = head * HD
            query = (proj_ref[rows, at : at + HD] * scale).astype(jnp.bfloat16)
            key = proj_ref[:reach, width + at : width + at + HD]
            value = proj_ref[:reach, 2 * width + at : 2 * width + at + HD]
            logits = contract_cols(query, key) - penalty
            top = jnp.max(logits, axis=1, keepdims=True)
            probs = jnp.exp(logits - top)
            inverse = 1.0 / jnp.sum(probs, axis=1, keepdims=True)
            probs = probs.astype(jnp.bfloat16)
            probs_ref[head, rows, :reach] = probs
            out_ref[rows, at : at + HD] = matmul(probs, value) * inverse
            inv_ref[rows, head : head + 1] = inverse


def attend(ends, proj, hpg, strength):
    rows = proj.shape[0]
    vmem = pl.BlockSpec(memory_space=pltpu.VMEM)
    return pl.pallas_call(
        partial(attend_body, hpg, strength, ends.shape[0]),
        out_shape=[
            jax.ShapeDtypeStruct((hpg, rows, rows), jnp.bfloat16),
            jax.ShapeDtypeStruct((rows, rows), jnp.bfloat16),
            jax.ShapeDtypeStruct((rows, hpg * HD), jnp.float32),
            jax.ShapeDtypeStruct((rows, hpg), jnp.float32),
        ],
        in_specs=[pl.BlockSpec(memory_space=pltpu.SMEM), vmem],
        out_specs=[vmem] * 4,
        scratch_shapes=[pltpu.VMEM((1, rows), jnp.float32)],
        compiler_params=pltpu.CompilerParams(vmem_limit_bytes=48 * 1024 * 1024),
        name="attend",
    )(ends, proj)


def attend_back_body(
    hpg, proj_ref, probs_ref, slope_ref, out_ref, inv_ref, grad_ref, dq_ref, dkv_ref,
    suffix, acc,
):
    rows_all = proj_ref.shape[0]
    width = hpg * HD
    block = QUERY_BLOCK
    scale = HD ** (-0.5)
    suffix[...] = jnp.zeros_like(suffix)
    acc[...] = jnp.zeros_like(acc)
    row_at = lax.broadcasted_iota(jnp.int32, (block, block), 0)
    col_at = lax.broadcasted_iota(jnp.int32, (block, block), 1)
    later = (col_at > row_at).astype(jnp.bfloat16)
    for start in reversed(range(0, rows_all, block)):
        reach = start + block
        rows = pl.ds(start, block)
        total = None
        for head in range(hpg):
            at = head * HD
            query_t = (proj_ref[rows, at : at + HD].astype(jnp.float32) * scale).T.astype(jnp.bfloat16)
            key = proj_ref[:reach, width + at : width + at + HD]
            value = proj_ref[:reach, 2 * width + at : 2 * width + at + HD]
            inverse = inv_ref[rows, head : head + 1]
            grad = grad_ref[rows, at : at + HD].astype(jnp.float32) * inverse
            delta = jnp.sum(grad * out_ref[rows, at : at + HD], axis=1, keepdims=True)
            probs = probs_ref[head, rows, :reach]
            grad_probs = contract_cols(grad.astype(jnp.bfloat16), value)
            grad_logits = probs.astype(jnp.float32) * (grad_probs - delta)
            total = grad_logits if total is None else total + grad_logits
            grad_scores = grad_logits.astype(jnp.bfloat16)
            dq_ref[rows, at : at + HD] = (matmul(grad_scores, key) * scale).astype(jnp.bfloat16)
            acc[at : at + HD, :reach] += matmul(query_t, grad_scores)
            acc[width + at : width + at + HD, :reach] += matmul(grad.T.astype(jnp.bfloat16), probs)
        query_t = (
            proj_ref[rows, 3 * width : 3 * width + HD].astype(jnp.float32) * scale
        ).T.astype(jnp.bfloat16)
        key = proj_ref[:reach, 3 * width + HD : 3 * width + 2 * HD]
        flow = suffix[:, :reach] + matmul(later, total.astype(jnp.bfloat16))
        grad_scores = (-flow * slope_ref[rows, :reach].astype(jnp.float32)).astype(jnp.bfloat16)
        dq_ref[rows, width : width + HD] = (matmul(grad_scores, key) * scale).astype(jnp.bfloat16)
        acc[2 * width : 2 * width + HD, :reach] += matmul(query_t, grad_scores)
        suffix[:, :reach] += jnp.sum(total, axis=0, keepdims=True)
    dkv_ref[...] = acc[...].astype(jnp.bfloat16)


def attend_back(proj, probs, slope, out, inverse, grad, hpg):
    rows = proj.shape[0]
    width = hpg * HD
    vmem = pl.BlockSpec(memory_space=pltpu.VMEM)
    return pl.pallas_call(
        partial(attend_back_body, hpg),
        out_shape=[
            jax.ShapeDtypeStruct((rows, width + HD), jnp.bfloat16),
            jax.ShapeDtypeStruct((2 * width + HD, rows), jnp.bfloat16),
        ],
        in_specs=[vmem] * 6,
        out_specs=[vmem] * 2,
        scratch_shapes=[
            pltpu.VMEM((1, rows), jnp.float32),
            pltpu.VMEM((2 * width + HD, rows), jnp.float32),
        ],
        compiler_params=pltpu.CompilerParams(vmem_limit_bytes=48 * 1024 * 1024),
        name="attend_back",
    )(proj, probs, slope, out, inverse, grad)


def deal_body(plan, grad_ref, vec_ref, got_ref, extra_ref, vecs_ref, send_sem, recv_sem, extra_send, extra_recv, vec_send, vec_recv, local_sem):
    width, part, shard, groups, ctx_size, dp_size = plan
    me = lax.axis_index("ctx")
    dp = lax.axis_index("dp")
    mb, grp = me // groups, lax.rem(me, groups)
    per = width // part
    slots = shard // part
    barrier = pltpu.get_barrier_semaphore()
    for axis, size in (("ctx", ctx_size), ("dp", dp_size)):
        place = lax.axis_index(axis)
        for step in range(1, size):
            pl.semaphore_signal(
                barrier, inc=1, device_id={axis: lax.rem(place + step, size)}, device_id_type=MESH
            )
    own_vec = pltpu.make_async_copy(vec_ref, vecs_ref.at[dp], local_sem.at[0])
    own_vec.start()
    pl.semaphore_wait(barrier, ctx_size + dp_size - 2)
    vec_copies = []
    for step in range(1, dp_size):
        peer = lax.rem(dp + step, dp_size)
        copy = pltpu.make_async_remote_copy(
            src_ref=vec_ref,
            dst_ref=vecs_ref.at[dp],
            send_sem=vec_send.at[step - 1],
            recv_sem=vec_recv.at[step - 1],
            device_id={"dp": peer},
            device_id_type=MESH,
        )
        copy.start()
        vec_copies.append(copy)

    def outgoing(kind, half):
        section = (kind * groups + grp) * per + half
        target, slot = section // slots, lax.rem(section, slots)
        return target, pltpu.make_async_remote_copy(
            src_ref=grad_ref.at[pl.ds((kind * per + half) * part, part)],
            dst_ref=got_ref.at[slot, mb],
            send_sem=send_sem.at[kind * per + half],
            recv_sem=recv_sem.at[slot, mb],
            device_id={"ctx": target},
            device_id_type=MESH,
        ), pltpu.make_async_copy(
            grad_ref.at[pl.ds((kind * per + half) * part, part)],
            got_ref.at[slot, mb],
            recv_sem.at[slot, mb],
        )

    for kind in range(3):
        for half in range(per):
            target, remote, local = outgoing(kind, half)

            @pl.when(target != me)
            def _():
                remote.start()

            @pl.when(target == me)
            def _():
                local.start()

    def extra_copy(kind):
        target = kind * groups * per // slots
        return target, pltpu.make_async_remote_copy(
            src_ref=grad_ref.at[pl.ds(3 * width + kind * HD, HD)],
            dst_ref=extra_ref.at[me],
            send_sem=extra_send.at[kind],
            recv_sem=extra_recv.at[me],
            device_id={"ctx": target},
            device_id_type=MESH,
        ), pltpu.make_async_copy(
            grad_ref.at[pl.ds(3 * width + kind * HD, HD)],
            extra_ref.at[me],
            extra_recv.at[me],
        )

    for kind in range(2):
        target, remote, local = extra_copy(kind)

        @pl.when(target != me)
        def _():
            remote.start()

        @pl.when(target == me)
        def _():
            local.start()

    for copy in [own_vec] + vec_copies:
        copy.wait()
    for kind in range(3):
        for half in range(per):
            target, remote, local = outgoing(kind, half)

            @pl.when(target != me)
            def _():
                remote.wait_send()

    for slot in range(slots):
        for place in range(ctx_size // groups):
            pltpu.make_async_copy(
                grad_ref.at[pl.ds(0, part)], got_ref.at[slot, place], recv_sem.at[slot, place]
            ).wait()
    for kind in range(2):
        target, remote, local = extra_copy(kind)

        @pl.when(target != me)
        def _():
            remote.wait_send()

        @pl.when(target == me)
        def _():
            for place in range(ctx_size):
                pltpu.make_async_copy(
                    grad_ref.at[pl.ds(0, HD)], extra_ref.at[place], extra_recv.at[place]
                ).wait()


def deal(collective_id, grad, vec, width, shard, groups):
    ctx_size, dp_size = lax.axis_size("ctx"), lax.axis_size("dp")
    part = math.gcd(width, shard)
    slots = shard // part
    mbs = ctx_size // groups
    columns = grad.shape[1]
    plan = (width, part, shard, groups, ctx_size, dp_size)
    anywhere = pl.BlockSpec(memory_space=pl.ANY)
    return pl.pallas_call(
        partial(deal_body, plan),
        out_shape=[
            jax.ShapeDtypeStruct((slots, mbs, part, columns), grad.dtype),
            jax.ShapeDtypeStruct((ctx_size, HD, columns), grad.dtype),
            jax.ShapeDtypeStruct((dp_size,) + vec.shape, vec.dtype),
        ],
        in_specs=[anywhere] * 2,
        out_specs=[anywhere] * 3,
        scratch_shapes=[
            pltpu.SemaphoreType.DMA((3 * (width // part),)),
            pltpu.SemaphoreType.DMA((slots, mbs)),
            pltpu.SemaphoreType.DMA((2,)),
            pltpu.SemaphoreType.DMA((ctx_size,)),
            pltpu.SemaphoreType.DMA((dp_size - 1,)),
            pltpu.SemaphoreType.DMA((dp_size - 1,)),
            pltpu.SemaphoreType.DMA((1,)),
        ],
        compiler_params=pltpu.CompilerParams(
            collective_id=collective_id, has_side_effects=True
        ),
        name="deal",
    )(grad, vec)


def norm_parts(value):
    row_mean = jnp.mean(value, axis=-1, keepdims=True)
    centered = value - row_mean
    spread = jnp.mean(centered * centered, axis=-1, keepdims=True)
    inverse = lax.rsqrt(spread + NORM_EPSILON)
    return centered * inverse, inverse


def norm_back(xhat, inverse, grad, gain):
    scaled = grad * gain
    return (
        scaled
        - jnp.mean(scaled, axis=-1, keepdims=True)
        - xhat * jnp.mean(scaled * xhat, axis=-1, keepdims=True)
    ) * inverse


def per_head_device(
    layer_input,
    doc_lengths,
    ln1_gain,
    ln1_bias,
    w_qkv,
    w_out,
    ln2_gain,
    ln2_bias,
    w_up,
    b_up,
    w_down,
    cotangent,
):
    bf16, f32 = jnp.bfloat16, jnp.float32
    mbs, _, tokens, model = layer_input.shape
    ctx_size, dp_size = lax.axis_size("ctx"), lax.axis_size("dp")
    ctx, dp = lax.axis_index("ctx"), lax.axis_index("dp")
    row_length = tokens * ctx_size
    groups = ctx_size // mbs
    hpg = model // HD // groups
    width = hpg * HD
    strength = 8.0 / row_length
    my_mb, grp = ctx // groups, lax.rem(ctx, groups)
    ff_own = b_up.shape[0] // dp_size
    x_own = layer_input[:, 0]
    cot_own = cotangent[:, 0].reshape(mbs * tokens, model)
    w_pick = jnp.concatenate(
        [lax.dynamic_slice_in_dim(w_qkv, kind * model + grp * width, width, 1) for kind in range(3)]
        + [w_qkv[:, :HD], w_qkv[:, model : model + HD]],
        axis=1,
    )

    def peer_mb(ref, peer):
        return ref.at[peer // groups]

    def peer_columns(ref, peer):
        return ref.at[:, pl.ds(pl.multiple_of(peer * ff_own, 128), ff_own)]

    x_row, w_pick, w_up_own, w_out_all = exchange(
        0,
        "gather_start",
        (x_own, "ctx", peer_mb, (tokens, model)),
        (w_pick, "dp", whole, w_pick.shape),
        (w_up, "dp", peer_columns, (w_up.shape[0], ff_own)),
        (w_out, "dp", whole, w_out.shape),
    )
    x_row = x_row.reshape(row_length, model).astype(f32)
    w_pick = w_pick.reshape(model, -1)
    w_up_own = w_up_own.reshape(model, ff_own)
    w_out_all = w_out_all.reshape(model, model)
    xhat_row, _ = norm_parts(x_row)
    normed_one = (xhat_row * ln1_gain + ln1_bias).astype(bf16)
    proj = matmul(normed_one, w_pick).astype(bf16)
    lengths = lax.dynamic_index_in_dim(doc_lengths[:, 0], my_mb, 0, keepdims=False)
    ends = jnp.cumsum(lengths).astype(jnp.int32)
    probs, slope, out, inverse = attend(ends, proj, hpg, strength)
    att_got, cot_all = exchange(
        1,
        "deal_attended",
        (out.astype(bf16).reshape(ctx_size, tokens, width), "ctx", piece, (tokens, width)),
        (cot_own, "dp", whole, cot_own.shape),
    )

    def to_tokens(got):
        got = got.reshape(mbs, groups, tokens, width)
        return jnp.transpose(got, (0, 2, 1, 3)).reshape(mbs * tokens, model)

    def to_heads(array):
        array = array.reshape(mbs, tokens, groups, width)
        return jnp.transpose(array, (0, 2, 1, 3)).reshape(ctx_size, tokens, width)

    attended = to_tokens(att_got)
    mid_stream = x_own.reshape(mbs * tokens, model).astype(f32) + matmul(attended, w_out_all)
    mid_hat, mid_inv = norm_parts(mid_stream)
    normed_two_own = (mid_hat * ln2_gain + ln2_bias).astype(bf16)
    (normed_two,) = exchange(
        2, "gather_normed", (normed_two_own, "dp", whole, normed_two_own.shape)
    )
    normed_two = normed_two.reshape(-1, model)
    cot_all = cot_all.reshape(-1, model)
    b_own = lax.dynamic_slice_in_dim(b_up, dp * ff_own, ff_own, 0)
    hidden = matmul(normed_two, w_up_own) + b_own
    cdf = 0.5 * (1.0 + lax.erf(hidden * (2.0**-0.5)))
    density = jnp.exp(-0.5 * hidden * hidden) * ((2.0 * math.pi) ** -0.5)
    activated = (hidden * cdf).astype(bf16)
    grad_hidden = (contract_cols(cot_all, w_down) * (cdf + hidden * density)).astype(bf16)
    grad_normed_part = contract_cols(grad_hidden, w_up_own).astype(bf16)
    out_part = matmul(activated, w_down).astype(bf16)
    (grad_normed_got,) = exchange(
        3,
        "deal_grad_normed",
        (grad_normed_part.reshape(dp_size, -1, model), "dp", piece, normed_two_own.shape),
    )
    grad_down_t = contract_rows(cot_all, activated).astype(bf16)
    shards = ctx_size // dp_size
    grad_up = jnp.concatenate(
        [
            contract_rows(normed_two, grad_hidden[:, at * ff_own // shards : (at + 1) * ff_own // shards])
            for at in range(shards)
        ],
        axis=0,
    ).astype(bf16)
    grad_bias_up = jnp.sum(grad_hidden.astype(f32), axis=0)
    d_down = lax.psum_scatter(grad_down_t, "ctx", scatter_dimension=0, tiled=True)
    d_up = lax.psum_scatter(grad_up, "ctx", scatter_dimension=0, tiled=True)
    pairs = []
    for i in range(dp_size):
        for j in range(ctx_size):
            pairs.append((i * ctx_size + j, (j % dp_size) * ctx_size + shards * i + j // dp_size))
    d_up = lax.ppermute(d_up, ("dp", "ctx"), pairs)

    grad_normed_two = jnp.sum(grad_normed_got.astype(f32), axis=0)
    grad_mid = cot_own.astype(f32) + norm_back(mid_hat, mid_inv, grad_normed_two, ln2_gain)
    d_gain_two = jnp.sum(grad_normed_two * mid_hat, axis=0)
    d_bias_two = jnp.sum(grad_normed_two, axis=0)
    grad_branch = grad_mid.astype(bf16)
    grad_attended = contract_cols(grad_branch, w_out_all).astype(bf16)
    (grad_att_got,) = exchange(
        4, "deal_grad_attended", (to_heads(grad_attended), "ctx", piece, (tokens, width))
    )
    d_out_t = lax.psum_scatter(
        contract_rows(grad_branch, attended).astype(bf16), "ctx", scatter_dimension=0, tiled=True
    )
    d_out_t = jnp.transpose(d_out_t.reshape(-1, dp_size, model // dp_size), (1, 0, 2))
    dq, dkv = attend_back(
        proj, probs, slope, out, inverse, grad_att_got.reshape(row_length, width), hpg
    )
    w_q = jnp.concatenate([w_pick[:, :width], w_pick[:, 3 * width : 3 * width + HD]], axis=1)
    w_kv = jnp.concatenate([w_pick[:, width : 3 * width], w_pick[:, 3 * width + HD :]], axis=1)
    grad_normed_one = contract_cols(dq, w_q) + lax.dot_general(
        dkv, w_kv, (((0,), (1,)), ((), ())), preferred_element_type=f32
    )
    d_q = contract_rows(dq, normed_one)
    d_kv = matmul(dkv, normed_one)
    d_qkv_t = jnp.concatenate([d_q[:width], d_kv[: 2 * width], d_q[width:], d_kv[2 * width :]], axis=0)
    d_qkv_t = jnp.transpose(d_qkv_t.reshape(-1, dp_size, model // dp_size), (1, 0, 2)).astype(bf16)
    vec = jnp.stack(
        [
            jnp.sum(grad_normed_one * xhat_row, axis=0),
            jnp.sum(grad_normed_one, axis=0),
            d_gain_two,
            d_bias_two,
        ]
        + [grad_bias_up[at * model : (at + 1) * model] for at in range(ff_own // model)]
    )
    grad_one_got, d_qkv_got, out_got, d_out_got, vec_got = exchange(
        5,
        "deal_grad_one",
        (grad_normed_one.astype(bf16).reshape(ctx_size, tokens, model), "ctx", piece, (tokens, model)),
        (d_qkv_t, "dp", piece, d_qkv_t.shape[1:]),
        (out_part.reshape(dp_size, -1, model), "dp", piece, normed_two_own.shape),
        (d_out_t, "dp", piece, d_out_t.shape[1:]),
        (vec, "ctx", whole, vec.shape),
    )
    vec = jnp.sum(vec_got, axis=0)
    d_qkv_sum = jnp.sum(d_qkv_got.astype(f32), axis=0).astype(bf16)
    shard = 3 * model // ctx_size
    qkv_got, extra, vecs = deal(6, d_qkv_sum, vec, width, shard, groups)
    part = math.gcd(width, shard)
    slots = shard // part
    d_qkv = jnp.sum(qkv_got.astype(f32), axis=1)
    extra = jnp.sum(extra.astype(f32), axis=0)
    for kind in range(2):
        section = kind * groups * (width // part)
        target, slot = section // slots, section % slots
        d_qkv = d_qkv.at[slot, :HD].add(jnp.where(ctx == target, extra, 0.0))
    d_qkv = d_qkv.reshape(shard, -1).T

    layer_out = (mid_stream + jnp.sum(out_got.astype(f32), axis=0)).astype(bf16)
    x_own = x_own.reshape(mbs * tokens, model).astype(f32)
    own_hat, own_inv = norm_parts(x_own)
    grad_one = jnp.sum(grad_one_got.reshape(mbs, groups, tokens, model).astype(f32), axis=1)
    grad_one = grad_one.reshape(mbs * tokens, model)
    d_x = (grad_mid + norm_back(own_hat, own_inv, grad_one, ln1_gain)).astype(bf16)
    vec = jnp.sum(vecs[:, :4], axis=0)
    d_bias_up = vecs[:, 4:].reshape(-1)
    return (
        layer_out.reshape(mbs, 1, tokens, model),
        d_x.reshape(mbs, 1, tokens, model),
        vec[0],
        vec[1],
        d_qkv,
        jnp.sum(d_out_got.astype(f32), axis=0).T,
        vec[2],
        vec[3],
        d_up.astype(f32),
        d_bias_up,
        d_down.astype(f32).T,
    )


def on_device(*arguments):
    layer_input = arguments[0]
    mbs, model = layer_input.shape[0], layer_input.shape[3]
    heads, ctx_size, dp_size = model // HD, lax.axis_size("ctx"), lax.axis_size("dp")
    groups = ctx_size // mbs
    fits = (
        ctx_size % mbs == 0
        and heads % groups == 0
        and ctx_size % dp_size == 0
        and (layer_input.shape[2] * ctx_size) % QUERY_BLOCK == 0
    )
    return (per_head_device if fits else per_token_device)(*arguments)


def solution(mesh):
    return jax.shard_map(
        on_device,
        mesh=mesh,
        in_specs=(
            P(None, "dp", "ctx", None),
            P(None, "dp", None),
            P(),
            P(),
            P("dp", None),
            P("dp", None),
            P(),
            P(),
            P("dp", None),
            P(),
            P("dp", None),
            P(None, "dp", "ctx", None),
        ),
        out_specs=(
            P(None, "dp", "ctx", None),
            P(None, "dp", "ctx", None),
            P(),
            P(),
            P("dp", "ctx"),
            P("dp", "ctx"),
            P(),
            P(),
            P("dp", "ctx"),
            P(),
            P("dp", "ctx"),
        ),
        check_vma=False,
    )
```

```python
import math
from functools import partial

import jax
import jax.numpy as jnp
from jax import lax
from jax.experimental import pallas as pl
from jax.experimental.pallas import tpu as pltpu
from jax.sharding import PartitionSpec as P

HD = 64


NORM_EPSILON = 1e-05
MASKED = -1e30
START_TOP = -1e20


def prefix_2(array, axis, combine, identity, reverse):
    peers, index = (lax.axis_size(axis), lax.axis_index(axis))
    everything = lax.all_gather(array, axis)
    start = jnp.broadcast_to(jnp.asarray(identity, array.dtype), array.shape)

    def turn(k, before):
        at = peers - 1 - k if reverse else k
        reached = at > index if reverse else at < index
        new = combine(before, everything[at])
        return jnp.where(reached, new, before)

    return lax.fori_loop(0, peers, turn, start)


def layer_norm(value, gain, bias):
    row_mean = jnp.mean(value, axis=-1, keepdims=True)
    centered = value - row_mean
    spread = jnp.mean(centered * centered, axis=-1, keepdims=True)
    return centered * lax.rsqrt(spread + NORM_EPSILON) * gain + bias


def matmul(left, right):
    return jnp.dot(left, right, preferred_element_type=jnp.float32)


def contract_rows(left, right):
    return lax.dot_general(
        left, right, (((0,), (0,)), ((), ())), preferred_element_type=jnp.float32
    )


def contract_cols(left, right):
    return lax.dot_general(
        left, right, (((1,), (1,)), ((), ())), preferred_element_type=jnp.float32
    )


def segment_table(lengths, row_length):
    doc_ends = jnp.cumsum(lengths)
    places = jnp.arange(row_length, dtype=jnp.int32)
    segment = jnp.sum((places[:, None] >= doc_ends[None, :]).astype(jnp.int32), axis=1)
    opening = jnp.concatenate([jnp.ones((1,), jnp.bool_), segment[1:] != segment[:-1]])
    return (segment, opening)


def add_up(earlier, later):
    return earlier + later


def per_token_device(
    layer_input,
    doc_lengths,
    ln1_gain,
    ln1_bias,
    w_qkv,
    w_out,
    ln2_gain,
    ln2_bias,
    w_up,
    b_up,
    w_down,
    cotangent,
):
    micro_count = layer_input.shape[0]
    query_rows = layer_input.shape[2]
    model_width = layer_input.shape[3]
    head_count = model_width // HD
    row_length = query_rows * lax.axis_size("ctx")
    key_block = min(512, row_length)
    score_scale = HD ** (-0.5)
    strength = 8.0 / row_length
    ctx_place = lax.axis_index("ctx")
    query_pos = ctx_place * query_rows + jnp.arange(query_rows, dtype=jnp.int32)
    block_total = ((ctx_place + 1) * query_rows + key_block - 1) // key_block
    later_heads = (jnp.arange(head_count) > 0).astype(jnp.float32)[:, None, None]
    zeros_row = jnp.zeros((row_length,), jnp.float32)
    gelu_exact = partial(jax.nn.gelu, approximate=False)
    output_list = []
    input_grads = []
    matrix_total = None
    vector_total = None
    for micro_step in range(micro_count):
        w_qkv_all, w_out_all, w_up_all, w_down_all = (
            lax.all_gather(w_qkv, "dp", axis=0, tiled=True),
            lax.all_gather(w_out, "dp", axis=0, tiled=True),
            lax.all_gather(w_up, "dp", axis=0, tiled=True),
            lax.all_gather(w_down, "dp", axis=0, tiled=True),
        )
        inputs = layer_input[micro_step, 0].astype(jnp.float32)
        segment, opening = segment_table(doc_lengths[micro_step, 0], row_length)
        query_seg = lax.dynamic_slice_in_dim(segment, ctx_place * query_rows, query_rows, 0)
        normed_one = layer_norm(inputs, ln1_gain, ln1_bias).astype(jnp.bfloat16)
        projected = matmul(normed_one, w_qkv_all).astype(jnp.bfloat16)
        queries = projected[:, :model_width]
        queries3 = queries.reshape(query_rows, head_count, HD)
        query_zero = queries[:, :HD]
        keys_all, values_all = (
            lax.all_gather(projected[:, model_width : 2 * model_width], "ctx", axis=0, tiled=True),
            lax.all_gather(projected[:, 2 * model_width :], "ctx", axis=0, tiled=True),
        )

        def masks(key_start):
            key_seg = lax.dynamic_slice_in_dim(segment, key_start, key_block, 0)
            key_open = lax.dynamic_slice_in_dim(opening, key_start, key_block, 0)
            key_pos = key_start + jnp.arange(key_block, dtype=jnp.int32)
            same_doc = query_seg[:, None] == key_seg[None, :]
            allowed = same_doc & (key_pos[None, :] <= query_pos[:, None])
            chosen = (
                same_doc
                & (key_pos[None, :] < query_pos[:, None])
                & jnp.logical_not(key_open)[None, :]
            )
            return (allowed, chosen.astype(jnp.float32))

        def head_scores(key_start):
            key_zero = lax.dynamic_slice_in_dim(keys_all, key_start, key_block, 0)[:, :HD]
            return (key_zero, contract_cols(query_zero, key_zero) * score_scale)

        def block_keys(key_start):
            keys3 = lax.dynamic_slice_in_dim(keys_all, key_start, key_block, 0).reshape(
                key_block, head_count, HD
            )
            values3 = lax.dynamic_slice_in_dim(values_all, key_start, key_block, 0).reshape(
                key_block, head_count, HD
            )
            return (keys3, values3)

        def logits_of(key_start, keys3):
            allowed, chosen = masks(key_start)
            raw_scores = (
                jnp.einsum("qhd,khd->hqk", queries3, keys3, preferred_element_type=jnp.float32)
                * score_scale
            )
            picked = strength * jax.nn.softplus(raw_scores[0]) * chosen
            before = lax.dynamic_slice_in_dim(prefix, key_start, key_block, 0)
            penalty = before[None, :] + jnp.cumsum(picked, axis=0) - picked
            return jnp.where(allowed[None], raw_scores - penalty[None], MASKED)

        def total_block(block_index, totals):
            key_start = block_index * key_block
            _, chosen = masks(key_start)
            _, first_scores = head_scores(key_start)
            picked = strength * jax.nn.softplus(first_scores) * chosen
            return lax.dynamic_update_slice_in_dim(totals, jnp.sum(picked, axis=0), key_start, 0)

        totals = lax.fori_loop(0, block_total, total_block, zeros_row)
        prefix = prefix_2(totals, "ctx", add_up, zeros_row, False)

        def stat_block(block_index, running):
            row_top, row_total = running
            key_start = block_index * key_block
            keys3, _ = block_keys(key_start)
            logits = logits_of(key_start, keys3)
            new_top = jnp.maximum(row_top, jnp.max(logits, axis=-1))
            row_total = row_total * jnp.exp(row_top - new_top) + jnp.sum(
                jnp.exp(logits - new_top[..., None]), axis=-1
            )
            return (new_top, row_total)

        row_top, row_total = lax.fori_loop(
            0,
            block_total,
            stat_block,
            (
                jnp.full((head_count, query_rows), START_TOP, jnp.float32),
                jnp.zeros((head_count, query_rows), jnp.float32),
            ),
        )
        log_total = row_top + jnp.log(row_total)

        def out_block(block_index, gathered_out):
            key_start = block_index * key_block
            keys3, values3 = block_keys(key_start)
            attn_probs = jnp.exp(logits_of(key_start, keys3) - log_total[..., None]).astype(
                jnp.bfloat16
            )
            return gathered_out + jnp.einsum(
                "hqk,khd->qhd", attn_probs, values3, preferred_element_type=jnp.float32
            )

        gathered_out = lax.fori_loop(
            0, block_total, out_block, jnp.zeros((query_rows, head_count, HD), jnp.float32)
        )
        attended = gathered_out.reshape(query_rows, model_width).astype(jnp.bfloat16)
        mid_stream = inputs + matmul(attended, w_out_all)
        normed_two = layer_norm(mid_stream, ln2_gain, ln2_bias).astype(jnp.bfloat16)
        hidden = matmul(normed_two, w_up_all) + b_up
        activated = gelu_exact(hidden).astype(jnp.bfloat16)
        output_list.append((mid_stream + matmul(activated, w_down_all)).astype(jnp.bfloat16))
        cot_rows = cotangent[micro_step, 0]
        grad_down = contract_rows(activated, cot_rows)
        grad_act = contract_cols(cot_rows, w_down_all)
        _, gelu_back = jax.vjp(gelu_exact, hidden)
        grad_hidden = gelu_back(grad_act)[0].astype(jnp.bfloat16)
        grad_up = contract_rows(normed_two, grad_hidden)
        grad_bias_up = jnp.sum(grad_hidden.astype(jnp.float32), axis=0)
        grad_normed_two = contract_cols(grad_hidden, w_up_all)
        _, norm_two_back = jax.vjp(layer_norm, mid_stream, ln2_gain, ln2_bias)
        grad_mid_part, grad_gain_two, grad_bias_two = norm_two_back(grad_normed_two)
        grad_mid = cot_rows.astype(jnp.float32) + grad_mid_part
        grad_branch = grad_mid.astype(jnp.bfloat16)
        grad_outproj = contract_rows(attended, grad_branch)
        grad_attended = contract_cols(grad_branch, w_out_all).astype(jnp.bfloat16)
        grad_att3 = grad_attended.reshape(query_rows, head_count, HD)
        row_delta = jnp.einsum("qhd,qhd->hq", grad_att3.astype(jnp.float32), gathered_out)

        def grad_block(block_index, running):
            grad_query, grad_key_all, grad_value_all, penalty_grad, first_grad = running
            key_start = block_index * key_block
            keys3, values3 = block_keys(key_start)
            probs_f32 = jnp.exp(logits_of(key_start, keys3) - log_total[..., None])
            grad_probs = jnp.einsum(
                "qhd,khd->hqk", grad_att3, values3, preferred_element_type=jnp.float32
            )
            grad_logits = probs_f32 * (grad_probs - row_delta[..., None])
            penalty_grad = lax.dynamic_update_slice_in_dim(
                penalty_grad, -jnp.sum(grad_logits, axis=0), key_start, 1
            )
            first_grad = lax.dynamic_update_slice_in_dim(first_grad, grad_logits[0], key_start, 1)
            grad_scores = (grad_logits * later_heads).astype(jnp.bfloat16)
            grad_query = (
                grad_query
                + jnp.einsum("hqk,khd->qhd", grad_scores, keys3, preferred_element_type=jnp.float32)
                * score_scale
            )
            key_part = (
                jnp.einsum(
                    "hqk,qhd->khd", grad_scores, queries3, preferred_element_type=jnp.float32
                )
                * score_scale
            )
            value_part = jnp.einsum(
                "hqk,qhd->khd",
                probs_f32.astype(jnp.bfloat16),
                grad_att3,
                preferred_element_type=jnp.float32,
            )
            grad_key_all = lax.dynamic_update_slice_in_dim(
                grad_key_all, key_part.reshape(key_block, model_width), key_start, 0
            )
            grad_value_all = lax.dynamic_update_slice_in_dim(
                grad_value_all, value_part.reshape(key_block, model_width), key_start, 0
            )
            return (grad_query, grad_key_all, grad_value_all, penalty_grad, first_grad)

        grad_query, grad_key_all, grad_value_all, penalty_grad, first_grad = lax.fori_loop(
            0,
            block_total,
            grad_block,
            (
                jnp.zeros((query_rows, head_count, HD), jnp.float32),
                jnp.zeros((row_length, model_width), jnp.float32),
                jnp.zeros((row_length, model_width), jnp.float32),
                jnp.zeros((query_rows, row_length), jnp.float32),
                jnp.zeros((query_rows, row_length), jnp.float32),
            ),
        )
        column_sums = jnp.sum(penalty_grad, axis=0)
        after = prefix_2(column_sums, "ctx", add_up, zeros_row, True)
        reach_sums = after + column_sums

        def head_block(block_index, running):
            grad_query_zero, grad_key_all = running
            key_start = block_index * key_block
            _, chosen = masks(key_start)
            key_zero, first_scores = head_scores(key_start)
            flow_block = lax.dynamic_slice_in_dim(penalty_grad, key_start, key_block, 1)
            reach_block = lax.dynamic_slice_in_dim(reach_sums, key_start, key_block, 0)
            grad_picked = reach_block[None, :] - jnp.cumsum(flow_block, axis=0)
            grad_select = grad_picked * strength * jax.nn.sigmoid(first_scores) * chosen
            grad_head = (
                lax.dynamic_slice_in_dim(first_grad, key_start, key_block, 1) + grad_select
            ).astype(jnp.bfloat16)
            grad_query_zero = grad_query_zero + matmul(grad_head, key_zero) * score_scale
            key_zero_grad = contract_rows(grad_head, query_zero) * score_scale
            grad_key_all = lax.dynamic_update_slice(
                grad_key_all, key_zero_grad, (key_start, jnp.zeros((), jnp.int32))
            )
            return (grad_query_zero, grad_key_all)

        grad_query_zero, grad_key_all = lax.fori_loop(
            0, block_total, head_block, (jnp.zeros((query_rows, HD), jnp.float32), grad_key_all)
        )
        grad_query = grad_query.at[:, 0, :].add(grad_query_zero).reshape(query_rows, model_width)
        grad_key_own, grad_value_own = (
            lax.psum_scatter(grad_key_all, "ctx", scatter_dimension=0, tiled=True),
            lax.psum_scatter(grad_value_all, "ctx", scatter_dimension=0, tiled=True),
        )
        grad_project = jnp.concatenate([grad_query, grad_key_own, grad_value_own], axis=1).astype(
            jnp.bfloat16
        )
        grad_qkv = contract_rows(normed_one, grad_project)
        grad_normed_one = contract_cols(grad_project, w_qkv_all)
        _, norm_one_back = jax.vjp(layer_norm, inputs, ln1_gain, ln1_bias)
        grad_in_part, grad_gain_one, grad_bias_one = norm_one_back(grad_normed_one)
        input_grads.append((grad_mid + grad_in_part).astype(jnp.bfloat16))
        matrix_grads = (grad_qkv, grad_outproj, grad_up, grad_down)
        vector_grads = (grad_gain_one, grad_bias_one, grad_gain_two, grad_bias_two, grad_bias_up)
        matrix_grads = (
            lax.psum_scatter(matrix_grads[0], "ctx", scatter_dimension=1, tiled=True),
            lax.psum_scatter(matrix_grads[1], "ctx", scatter_dimension=1, tiled=True),
            lax.psum_scatter(matrix_grads[2], "ctx", scatter_dimension=1, tiled=True),
            lax.psum_scatter(matrix_grads[3], "ctx", scatter_dimension=1, tiled=True),
        )
        matrix_grads = (
            lax.psum_scatter(
                matrix_grads[0].astype(jnp.bfloat16), "dp", scatter_dimension=0, tiled=True
            ).astype(jnp.float32),
            lax.psum_scatter(
                matrix_grads[1].astype(jnp.bfloat16), "dp", scatter_dimension=0, tiled=True
            ).astype(jnp.float32),
            lax.psum_scatter(
                matrix_grads[2].astype(jnp.bfloat16), "dp", scatter_dimension=0, tiled=True
            ).astype(jnp.float32),
            lax.psum_scatter(
                matrix_grads[3].astype(jnp.bfloat16), "dp", scatter_dimension=0, tiled=True
            ).astype(jnp.float32),
        )
        vector_grads = lax.psum(
            (vector_grads[0], vector_grads[1], vector_grads[2], vector_grads[3], vector_grads[4]),
            ("dp", "ctx"),
        )
        if matrix_total is None:
            matrix_total = matrix_grads
            vector_total = vector_grads
        else:
            matrix_total = tuple((old + new for old, new in zip(matrix_total, matrix_grads)))
            vector_total = tuple((old + new for old, new in zip(vector_total, vector_grads)))
    layer_out = jnp.stack(output_list)[:, None]
    input_out = jnp.stack(input_grads)[:, None]
    return (
        layer_out,
        input_out,
        vector_total[0],
        vector_total[1],
        matrix_total[0],
        matrix_total[1],
        vector_total[2],
        vector_total[3],
        matrix_total[2],
        vector_total[4],
        matrix_total[3],
    )


MESH = pl.DeviceIdType.MESH
EXCLUDED = 1e30
QUERY_BLOCK = 256


def whole(ref, peer):
    return ref


def piece(ref, peer):
    return ref.at[peer]


def exchange_body(jobs, sizes, *refs):
    count = len(jobs)
    sources, targets = refs[:count], refs[count : 2 * count]
    send_sems, recv_sems = refs[2 * count : 3 * count], refs[3 * count : 4 * count]
    local_sem = refs[4 * count]
    barrier = pltpu.get_barrier_semaphore()
    greeted = 0
    for axis, size in sizes.items():
        me = lax.axis_index(axis)
        for step in range(1, size):
            pl.semaphore_signal(
                barrier, inc=1, device_id={axis: lax.rem(me + step, size)}, device_id_type=MESH
            )
            greeted += 1
    own = []
    for at, (axis, select) in enumerate(jobs):
        me = lax.axis_index(axis)
        copy = pltpu.make_async_copy(
            select(sources[at], me), targets[at].at[me], local_sem.at[at]
        )
        copy.start()
        own.append(copy)
    pl.semaphore_wait(barrier, greeted)
    sent = []
    for at, (axis, select) in enumerate(jobs):
        me, size = lax.axis_index(axis), sizes[axis]
        for step in range(1, size):
            peer = lax.rem(me + step, size)
            copy = pltpu.make_async_remote_copy(
                src_ref=select(sources[at], peer),
                dst_ref=targets[at].at[me],
                send_sem=send_sems[at].at[step - 1],
                recv_sem=recv_sems[at].at[step - 1],
                device_id={axis: peer},
                device_id_type=MESH,
            )
            copy.start()
            sent.append(copy)
    for copy in own + sent:
        copy.wait()


def exchange(collective_id, name, *jobs):
    arrays = [job[0] for job in jobs]
    axes = [job[1] for job in jobs]
    sizes = {axis: lax.axis_size(axis) for axis in axes}
    count = len(jobs)
    return pl.pallas_call(
        partial(exchange_body, [(job[1], job[2]) for job in jobs], sizes),
        out_shape=[
            jax.ShapeDtypeStruct((sizes[axis],) + tuple(job[3]), job[0].dtype)
            for axis, job in zip(axes, jobs)
        ],
        in_specs=[pl.BlockSpec(memory_space=pl.ANY)] * count,
        out_specs=[pl.BlockSpec(memory_space=pl.ANY)] * count,
        scratch_shapes=[pltpu.SemaphoreType.DMA((sizes[axis] - 1,)) for axis in axes] * 2
        + [pltpu.SemaphoreType.DMA((count,))],
        compiler_params=pltpu.CompilerParams(
            collective_id=collective_id, has_side_effects=True
        ),
        name=name,
    )(*arrays)


def segment_of(places, ends_ref, doc_count):
    total = jnp.zeros(places.shape, jnp.int32)
    for at in range(doc_count):
        total += jnp.where(places >= ends_ref[at], 1, 0)
    return total


def attend_body(hpg, strength, doc_count, ends_ref, proj_ref, probs_ref, slope_ref, out_ref, inv_ref, prefix):
    rows_all = proj_ref.shape[0]
    width = hpg * HD
    block = QUERY_BLOCK
    prefix[...] = jnp.zeros_like(prefix)
    row_at = lax.broadcasted_iota(jnp.int32, (block, block), 0)
    col_at = lax.broadcasted_iota(jnp.int32, (block, block), 1)
    earlier = (col_at < row_at).astype(jnp.bfloat16)
    scale = HD ** (-0.5)
    for start in range(0, rows_all, block):
        reach = start + block
        rows = pl.ds(start, block)
        row_pos = start + lax.broadcasted_iota(jnp.int32, (block, 1), 0)
        col_pos = lax.broadcasted_iota(jnp.int32, (1, reach), 1)
        row_seg = segment_of(row_pos, ends_ref, doc_count)
        col_seg = segment_of(col_pos, ends_ref, doc_count)
        before_seg = segment_of(col_pos - 1, ends_ref, doc_count)
        opening = (col_seg != before_seg) | (col_pos == 0)
        pick_seg = jnp.where(opening, -1, col_seg)
        query = proj_ref[rows, 3 * width : 3 * width + HD] * scale
        key = proj_ref[:reach, 3 * width + HD : 3 * width + 2 * HD]
        scores = contract_cols(query.astype(jnp.bfloat16), key)
        small = jnp.exp(-jnp.abs(scores))
        soft = jnp.maximum(scores, 0.0) + jnp.log(1.0 + small)
        recip = 1.0 / (1.0 + small)
        sigmoid = jnp.where(scores >= 0.0, recip, small * recip)
        chosen = (row_seg == pick_seg) & (col_pos < row_pos)
        picked = jnp.where(chosen, strength * soft, 0.0)
        slope_ref[rows, :reach] = jnp.where(chosen, strength * sigmoid, 0.0).astype(jnp.bfloat16)
        high = picked.astype(jnp.bfloat16)
        low = (picked - high.astype(jnp.float32)).astype(jnp.bfloat16)
        penalty = prefix[:, :reach] + (matmul(earlier, high) + matmul(earlier, low))
        allowed = (row_seg == col_seg) & (col_pos <= row_pos)
        penalty = jnp.where(allowed, penalty, EXCLUDED)
        prefix[:, :reach] += jnp.sum(picked, axis=0, keepdims=True)
        for head in range(hpg):
            at = head * HD
            query = (proj_ref[rows, at : at + HD] * scale).astype(jnp.bfloat16)
            key = proj_ref[:reach, width + at : width + at + HD]
            value = proj_ref[:reach, 2 * width + at : 2 * width + at + HD]
            logits = contract_cols(query, key) - penalty
            top = jnp.max(logits, axis=1, keepdims=True)
            probs = jnp.exp(logits - top)
            inverse = 1.0 / jnp.sum(probs, axis=1, keepdims=True)
            probs = probs.astype(jnp.bfloat16)
            probs_ref[head, rows, :reach] = probs
            out_ref[rows, at : at + HD] = matmul(probs, value) * inverse
            inv_ref[rows, head : head + 1] = inverse


def attend(ends, proj, hpg, strength):
    rows = proj.shape[0]
    vmem = pl.BlockSpec(memory_space=pltpu.VMEM)
    return pl.pallas_call(
        partial(attend_body, hpg, strength, ends.shape[0]),
        out_shape=[
            jax.ShapeDtypeStruct((hpg, rows, rows), jnp.bfloat16),
            jax.ShapeDtypeStruct((rows, rows), jnp.bfloat16),
            jax.ShapeDtypeStruct((rows, hpg * HD), jnp.float32),
            jax.ShapeDtypeStruct((rows, hpg), jnp.float32),
        ],
        in_specs=[pl.BlockSpec(memory_space=pltpu.SMEM), vmem],
        out_specs=[vmem] * 4,
        scratch_shapes=[pltpu.VMEM((1, rows), jnp.float32)],
        compiler_params=pltpu.CompilerParams(vmem_limit_bytes=48 * 1024 * 1024),
        name="attend",
    )(ends, proj)


def attend_back_body(
    hpg, proj_ref, probs_ref, slope_ref, out_ref, inv_ref, grad_ref, dq_ref, dkv_ref,
    suffix, acc,
):
    rows_all = proj_ref.shape[0]
    width = hpg * HD
    block = QUERY_BLOCK
    scale = HD ** (-0.5)
    suffix[...] = jnp.zeros_like(suffix)
    acc[...] = jnp.zeros_like(acc)
    row_at = lax.broadcasted_iota(jnp.int32, (block, block), 0)
    col_at = lax.broadcasted_iota(jnp.int32, (block, block), 1)
    later = (col_at > row_at).astype(jnp.bfloat16)
    for start in reversed(range(0, rows_all, block)):
        reach = start + block
        rows = pl.ds(start, block)
        total = None
        for head in range(hpg):
            at = head * HD
            query_t = (proj_ref[rows, at : at + HD].astype(jnp.float32) * scale).T.astype(jnp.bfloat16)
            key = proj_ref[:reach, width + at : width + at + HD]
            value = proj_ref[:reach, 2 * width + at : 2 * width + at + HD]
            inverse = inv_ref[rows, head : head + 1]
            grad = grad_ref[rows, at : at + HD].astype(jnp.float32) * inverse
            delta = jnp.sum(grad * out_ref[rows, at : at + HD], axis=1, keepdims=True)
            probs = probs_ref[head, rows, :reach]
            grad_probs = contract_cols(grad.astype(jnp.bfloat16), value)
            grad_logits = probs.astype(jnp.float32) * (grad_probs - delta)
            total = grad_logits if total is None else total + grad_logits
            grad_scores = grad_logits.astype(jnp.bfloat16)
            dq_ref[rows, at : at + HD] = (matmul(grad_scores, key) * scale).astype(jnp.bfloat16)
            acc[at : at + HD, :reach] += matmul(query_t, grad_scores)
            acc[width + at : width + at + HD, :reach] += matmul(grad.T.astype(jnp.bfloat16), probs)
        query_t = (
            proj_ref[rows, 3 * width : 3 * width + HD].astype(jnp.float32) * scale
        ).T.astype(jnp.bfloat16)
        key = proj_ref[:reach, 3 * width + HD : 3 * width + 2 * HD]
        flow = suffix[:, :reach] + matmul(later, total.astype(jnp.bfloat16))
        grad_scores = (-flow * slope_ref[rows, :reach].astype(jnp.float32)).astype(jnp.bfloat16)
        dq_ref[rows, width : width + HD] = (matmul(grad_scores, key) * scale).astype(jnp.bfloat16)
        acc[2 * width : 2 * width + HD, :reach] += matmul(query_t, grad_scores)
        suffix[:, :reach] += jnp.sum(total, axis=0, keepdims=True)
    dkv_ref[...] = acc[...].astype(jnp.bfloat16)


def attend_back(proj, probs, slope, out, inverse, grad, hpg):
    rows = proj.shape[0]
    width = hpg * HD
    vmem = pl.BlockSpec(memory_space=pltpu.VMEM)
    return pl.pallas_call(
        partial(attend_back_body, hpg),
        out_shape=[
            jax.ShapeDtypeStruct((rows, width + HD), jnp.bfloat16),
            jax.ShapeDtypeStruct((2 * width + HD, rows), jnp.bfloat16),
        ],
        in_specs=[vmem] * 6,
        out_specs=[vmem] * 2,
        scratch_shapes=[
            pltpu.VMEM((1, rows), jnp.float32),
            pltpu.VMEM((2 * width + HD, rows), jnp.float32),
        ],
        compiler_params=pltpu.CompilerParams(vmem_limit_bytes=48 * 1024 * 1024),
        name="attend_back",
    )(proj, probs, slope, out, inverse, grad)


def deal_body(plan, grad_ref, vec_ref, got_ref, extra_ref, vecs_ref, send_sem, recv_sem, extra_send, extra_recv, vec_send, vec_recv, local_sem):
    width, part, shard, groups, ctx_size, dp_size = plan
    me = lax.axis_index("ctx")
    dp = lax.axis_index("dp")
    mb, grp = me // groups, lax.rem(me, groups)
    per = width // part
    slots = shard // part
    barrier = pltpu.get_barrier_semaphore()
    for axis, size in (("ctx", ctx_size), ("dp", dp_size)):
        place = lax.axis_index(axis)
        for step in range(1, size):
            pl.semaphore_signal(
                barrier, inc=1, device_id={axis: lax.rem(place + step, size)}, device_id_type=MESH
            )
    own_vec = pltpu.make_async_copy(vec_ref, vecs_ref.at[dp], local_sem.at[0])
    own_vec.start()
    pl.semaphore_wait(barrier, ctx_size + dp_size - 2)
    vec_copies = []
    for step in range(1, dp_size):
        peer = lax.rem(dp + step, dp_size)
        copy = pltpu.make_async_remote_copy(
            src_ref=vec_ref,
            dst_ref=vecs_ref.at[dp],
            send_sem=vec_send.at[step - 1],
            recv_sem=vec_recv.at[step - 1],
            device_id={"dp": peer},
            device_id_type=MESH,
        )
        copy.start()
        vec_copies.append(copy)

    def outgoing(kind, half):
        section = (kind * groups + grp) * per + half
        target, slot = section // slots, lax.rem(section, slots)
        return target, pltpu.make_async_remote_copy(
            src_ref=grad_ref.at[pl.ds((kind * per + half) * part, part)],
            dst_ref=got_ref.at[slot, mb],
            send_sem=send_sem.at[kind * per + half],
            recv_sem=recv_sem.at[slot, mb],
            device_id={"ctx": target},
            device_id_type=MESH,
        ), pltpu.make_async_copy(
            grad_ref.at[pl.ds((kind * per + half) * part, part)],
            got_ref.at[slot, mb],
            recv_sem.at[slot, mb],
        )

    for kind in range(3):
        for half in range(per):
            target, remote, local = outgoing(kind, half)

            @pl.when(target != me)
            def _():
                remote.start()

            @pl.when(target == me)
            def _():
                local.start()

    def extra_copy(kind):
        target = kind * groups * per // slots
        return target, pltpu.make_async_remote_copy(
            src_ref=grad_ref.at[pl.ds(3 * width + kind * HD, HD)],
            dst_ref=extra_ref.at[me],
            send_sem=extra_send.at[kind],
            recv_sem=extra_recv.at[me],
            device_id={"ctx": target},
            device_id_type=MESH,
        ), pltpu.make_async_copy(
            grad_ref.at[pl.ds(3 * width + kind * HD, HD)],
            extra_ref.at[me],
            extra_recv.at[me],
        )

    for kind in range(2):
        target, remote, local = extra_copy(kind)

        @pl.when(target != me)
        def _():
            remote.start()

        @pl.when(target == me)
        def _():
            local.start()

    for copy in [own_vec] + vec_copies:
        copy.wait()
    for kind in range(3):
        for half in range(per):
            target, remote, local = outgoing(kind, half)

            @pl.when(target != me)
            def _():
                remote.wait_send()

    for slot in range(slots):
        for place in range(ctx_size // groups):
            pltpu.make_async_copy(
                grad_ref.at[pl.ds(0, part)], got_ref.at[slot, place], recv_sem.at[slot, place]
            ).wait()
    for kind in range(2):
        target, remote, local = extra_copy(kind)

        @pl.when(target != me)
        def _():
            remote.wait_send()

        @pl.when(target == me)
        def _():
            for place in range(ctx_size):
                pltpu.make_async_copy(
                    grad_ref.at[pl.ds(0, HD)], extra_ref.at[place], extra_recv.at[place]
                ).wait()


def deal(collective_id, grad, vec, width, shard, groups):
    ctx_size, dp_size = lax.axis_size("ctx"), lax.axis_size("dp")
    part = math.gcd(width, shard)
    slots = shard // part
    mbs = ctx_size // groups
    columns = grad.shape[1]
    plan = (width, part, shard, groups, ctx_size, dp_size)
    anywhere = pl.BlockSpec(memory_space=pl.ANY)
    return pl.pallas_call(
        partial(deal_body, plan),
        out_shape=[
            jax.ShapeDtypeStruct((slots, mbs, part, columns), grad.dtype),
            jax.ShapeDtypeStruct((ctx_size, HD, columns), grad.dtype),
            jax.ShapeDtypeStruct((dp_size,) + vec.shape, vec.dtype),
        ],
        in_specs=[anywhere] * 2,
        out_specs=[anywhere] * 3,
        scratch_shapes=[
            pltpu.SemaphoreType.DMA((3 * (width // part),)),
            pltpu.SemaphoreType.DMA((slots, mbs)),
            pltpu.SemaphoreType.DMA((2,)),
            pltpu.SemaphoreType.DMA((ctx_size,)),
            pltpu.SemaphoreType.DMA((dp_size - 1,)),
            pltpu.SemaphoreType.DMA((dp_size - 1,)),
            pltpu.SemaphoreType.DMA((1,)),
        ],
        compiler_params=pltpu.CompilerParams(
            collective_id=collective_id, has_side_effects=True
        ),
        name="deal",
    )(grad, vec)


def norm_parts(value):
    row_mean = jnp.mean(value, axis=-1, keepdims=True)
    centered = value - row_mean
    spread = jnp.mean(centered * centered, axis=-1, keepdims=True)
    inverse = lax.rsqrt(spread + NORM_EPSILON)
    return centered * inverse, inverse


def norm_back(xhat, inverse, grad, gain):
    scaled = grad * gain
    return (
        scaled
        - jnp.mean(scaled, axis=-1, keepdims=True)
        - xhat * jnp.mean(scaled * xhat, axis=-1, keepdims=True)
    ) * inverse


class Wires:
    def __init__(self, send_sem, recv_sem):
        self.send_sem, self.recv_sem, self.used, self.made = send_sem, recv_sem, 0, []

    def send(self, source, target, where):
        copy = pltpu.make_async_remote_copy(
            src_ref=source,
            dst_ref=target,
            send_sem=self.send_sem.at[self.used],
            recv_sem=self.recv_sem.at[self.used],
            device_id=where,
            device_id_type=MESH,
        )
        copy.start()
        self.used += 1
        self.made.append(copy)
        return copy

    def drain(self):
        for copy in self.made:
            copy.wait_send()


def greet(peers):
    barrier = pltpu.get_barrier_semaphore()
    for where in peers:
        pl.semaphore_signal(barrier, inc=1, device_id=where, device_id_type=MESH)
    pl.semaphore_wait(barrier, len(peers))


def other_core(dp):
    return {"dp": dp + 1 - 2 * lax.rem(dp, 2)}


def other_y(dp):
    return {"dp": lax.rem(dp + 2, 4)}


def rounded(value):
    return value.astype(jnp.bfloat16)


def middle_body(
    groups,
    att_ref,
    x_ref,
    cot_ref,
    w_out_ref,
    w_up_ref,
    w_down_ref,
    b_up_ref,
    gain_ref,
    bias_ref,
    layer_ref,
    mid_grad_ref,
    grad_att_ref,
    vec_ref,
    d_bias_ref,
    d_down_ref,
    d_up_ref,
    d_out_ref,
    att_got,
    mid,
    hat,
    normed,
    cots,
    act,
    grad_hid,
    part,
    out_part,
    part_got,
    out_got,
    att_out,
    send_sem,
    recv_sem,
):
    f32 = jnp.float32
    ctx, dp = lax.axis_index("ctx"), lax.axis_index("dp")
    ctx_size, tokens, width = att_ref.shape
    mbs = ctx_size // groups
    model = x_ref.shape[1]
    own = mbs * tokens
    ff = w_down_ref.shape[0]
    wires = Wires(send_sem, recv_sem)
    core, far = other_core(dp), other_y(dp)
    around = [{"ctx": lax.rem(ctx + step, ctx_size)} for step in range(1, ctx_size)]
    greet(around + [core, far])

    att_in = []
    for step in range(1, ctx_size):
        peer = lax.rem(ctx + step, ctx_size)
        att_in.append(wires.send(att_ref.at[peer], att_got.at[ctx], {"ctx": peer}))
    cot_core = wires.send(cot_ref, cots.at[1], core)
    cot_far = wires.send(cot_ref, cots.at[2], far)
    att_got[ctx] = att_ref[ctx]
    cots[0] = cot_ref[...]
    cot_far.wait_recv()
    cot_fwd = wires.send(cots.at[2], cots.at[3], core)
    for copy in att_in:
        copy.wait_recv()

    gain, bias = gain_ref[...], bias_ref[...]
    for micro in range(mbs):
        rows = pl.ds(micro * tokens, tokens)
        stream = x_ref[rows, :].astype(f32)
        for group in range(groups):
            stream += matmul(
                att_got[micro * groups + group], w_out_ref[pl.ds(group * width, width), :]
            )
        mid[rows, :] = stream
    xhat, inverse = norm_parts(mid[...])
    hat[...] = xhat
    normed[0] = rounded(xhat * gain + bias)
    to_core = wires.send(normed.at[0], normed.at[1], core)
    to_far = wires.send(normed.at[0], normed.at[2], far)

    def feed(slot):
        hidden = matmul(normed[slot], w_up_ref[...]) + b_up_ref[...]
        cdf = 0.5 * (1.0 + lax.erf(hidden * (2.0**-0.5)))
        density = jnp.exp(-0.5 * hidden * hidden) * ((2.0 * math.pi) ** -0.5)
        act[slot] = rounded(hidden * cdf)
        grad = contract_cols(cots[slot], w_down_ref[...])
        grad_hid[slot] = rounded(grad * (cdf + hidden * density))
        part[slot] = rounded(contract_cols(grad_hid[slot], w_up_ref[...]))

    def feed_out(slot):
        out_part[slot] = rounded(matmul(act[slot], w_down_ref[...]))

    feed(0)
    cot_core.wait_recv()
    to_core.wait_recv()
    feed(1)
    part_core = wires.send(part.at[1], part_got.at[0], core)
    to_far.wait_recv()
    forward = wires.send(normed.at[2], normed.at[3], core)
    feed(2)
    forward.wait_recv()
    cot_fwd.wait_recv()
    feed(3)
    part_far_core = wires.send(part.at[3], part_got.at[1], core)
    feed_out(3)
    out_far_core = wires.send(out_part.at[3], out_got.at[1], core)
    part_far_core.wait_recv()
    part[2] = rounded(part[2].astype(f32) + part_got[1].astype(f32))
    part_far = wires.send(part.at[2], part_got.at[2], far)
    feed_out(1)
    out_core = wires.send(out_part.at[1], out_got.at[0], core)
    feed_out(2)
    out_far_core.wait_recv()
    out_part[2] = rounded(out_part[2].astype(f32) + out_got[1].astype(f32))
    out_far = wires.send(out_part.at[2], out_got.at[2], far)

    flat_cot = cots[...].reshape(4 * own, model)
    flat_act = act[...].reshape(4 * own, ff)
    flat_normed = normed[...].reshape(4 * own, model)
    flat_grad = grad_hid[...].reshape(4 * own, ff)
    d_down_ref[...] = rounded(contract_rows(flat_cot, flat_act))
    shards = d_up_ref.shape[0] // model
    for at in range(shards):
        d_up_ref[pl.ds(at * model, model), :] = rounded(
            contract_rows(flat_normed, flat_grad[:, at * ff // shards : (at + 1) * ff // shards])
        )
    d_bias_ref[...] = jnp.sum(flat_grad.astype(f32), axis=0, keepdims=True)
    feed_out(0)

    part_core.wait_recv()
    part_far.wait_recv()
    grad_normed = part[0].astype(f32) + part_got[0].astype(f32) + part_got[2].astype(f32)
    xhat = hat[...]
    vec_ref[0:1, :] = jnp.sum(grad_normed * xhat, axis=0, keepdims=True)
    vec_ref[1:2, :] = jnp.sum(grad_normed, axis=0, keepdims=True)
    grad_mid = cot_ref[...].astype(f32) + norm_back(xhat, inverse, grad_normed, gain)
    mid_grad_ref[...] = grad_mid
    branch = rounded(grad_mid)
    for group in range(groups):
        grad = rounded(contract_cols(branch, w_out_ref[pl.ds(group * width, width), :]))
        for micro in range(mbs):
            att_out[micro * groups + group] = grad[micro * tokens : (micro + 1) * tokens]
    att_in = []
    for step in range(1, ctx_size):
        peer = lax.rem(ctx + step, ctx_size)
        att_in.append(wires.send(att_out.at[peer], grad_att_ref.at[ctx], {"ctx": peer}))
    grad_att_ref[ctx] = att_out[ctx]
    for group in range(groups):
        total = None
        for micro in range(mbs):
            some = contract_rows(
                branch[micro * tokens : (micro + 1) * tokens], att_got[micro * groups + group]
            )
            total = some if total is None else total + some
        d_out_ref[group] = rounded(total)
    out_core.wait_recv()
    out_far.wait_recv()
    layer_ref[...] = rounded(
        mid[...]
        + (out_part[0].astype(f32) + out_got[0].astype(f32) + out_got[2].astype(f32))
    )
    for copy in att_in:
        copy.wait_recv()
    wires.drain()


MIDDLE_COPIES = 32


def middle(collective_id, attended, x_own, cot_own, w_out, w_up, w_down, b_up, gain, bias, groups, shards):
    bf16, f32 = jnp.bfloat16, jnp.float32
    own, model = x_own.shape
    ff = w_down.shape[0]
    width = attended.shape[2]
    vmem = pl.BlockSpec(memory_space=pltpu.VMEM)
    shape = jax.ShapeDtypeStruct
    return pl.pallas_call(
        partial(middle_body, groups),
        out_shape=[
            shape((own, model), bf16),
            shape((own, model), f32),
            shape(attended.shape, bf16),
            shape((2, model), f32),
            shape((1, ff), f32),
            shape((model, ff), bf16),
            shape((shards * model, ff // shards), bf16),
            shape((groups, model, width), bf16),
        ],
        in_specs=[vmem] * 9,
        out_specs=[vmem] * 8,
        scratch_shapes=[
            pltpu.VMEM(attended.shape, bf16),
            pltpu.VMEM((own, model), f32),
            pltpu.VMEM((own, model), f32),
            pltpu.VMEM((4, own, model), bf16),
            pltpu.VMEM((4, own, model), bf16),
            pltpu.VMEM((4, own, ff), bf16),
            pltpu.VMEM((4, own, ff), bf16),
            pltpu.VMEM((4, own, model), bf16),
            pltpu.VMEM((4, own, model), bf16),
            pltpu.VMEM((3, own, model), bf16),
            pltpu.VMEM((3, own, model), bf16),
            pltpu.VMEM(attended.shape, bf16),
            pltpu.SemaphoreType.DMA((MIDDLE_COPIES,)),
            pltpu.SemaphoreType.DMA((MIDDLE_COPIES,)),
        ],
        compiler_params=pltpu.CompilerParams(
            collective_id=collective_id, has_side_effects=True, vmem_limit_bytes=56 * 1024 * 1024
        ),
        name="middle",
    )(attended, x_own, cot_own, w_out, w_up, w_down, b_up, gain, bias)


def per_head_device(
    layer_input,
    doc_lengths,
    ln1_gain,
    ln1_bias,
    w_qkv,
    w_out,
    ln2_gain,
    ln2_bias,
    w_up,
    b_up,
    w_down,
    cotangent,
):
    bf16, f32 = jnp.bfloat16, jnp.float32
    mbs, _, tokens, model = layer_input.shape
    ctx_size, dp_size = lax.axis_size("ctx"), lax.axis_size("dp")
    ctx, dp = lax.axis_index("ctx"), lax.axis_index("dp")
    row_length = tokens * ctx_size
    groups = ctx_size // mbs
    hpg = model // HD // groups
    width = hpg * HD
    strength = 8.0 / row_length
    my_mb, grp = ctx // groups, lax.rem(ctx, groups)
    ff_own = b_up.shape[0] // dp_size
    x_own = layer_input[:, 0]
    cot_own = cotangent[:, 0].reshape(mbs * tokens, model)
    w_pick = jnp.concatenate(
        [lax.dynamic_slice_in_dim(w_qkv, kind * model + grp * width, width, 1) for kind in range(3)]
        + [w_qkv[:, :HD], w_qkv[:, model : model + HD]],
        axis=1,
    )

    def peer_mb(ref, peer):
        return ref.at[peer // groups]

    def peer_columns(ref, peer):
        return ref.at[:, pl.ds(pl.multiple_of(peer * ff_own, 128), ff_own)]

    x_row, w_pick, w_up_own, w_out_all = exchange(
        0,
        "gather_start",
        (x_own, "ctx", peer_mb, (tokens, model)),
        (w_pick, "dp", whole, w_pick.shape),
        (w_up, "dp", peer_columns, (w_up.shape[0], ff_own)),
        (w_out, "dp", whole, w_out.shape),
    )
    x_row = x_row.reshape(row_length, model).astype(f32)
    w_pick = w_pick.reshape(model, -1)
    w_up_own = w_up_own.reshape(model, ff_own)
    w_out_all = w_out_all.reshape(model, model)
    xhat_row, _ = norm_parts(x_row)
    normed_one = (xhat_row * ln1_gain + ln1_bias).astype(bf16)
    proj = matmul(normed_one, w_pick).astype(bf16)
    lengths = lax.dynamic_index_in_dim(doc_lengths[:, 0], my_mb, 0, keepdims=False)
    ends = jnp.cumsum(lengths).astype(jnp.int32)
    probs, slope, out, inverse = attend(ends, proj, hpg, strength)
    x_flat = x_own.reshape(mbs * tokens, model)
    shards = ctx_size // dp_size
    b_own = lax.dynamic_slice_in_dim(b_up, dp * ff_own, ff_own, 0)
    layer_out, grad_mid, grad_att_got, vec_two, d_bias_own, grad_down_t, grad_up, d_out_t = middle(
        1,
        out.astype(bf16).reshape(ctx_size, tokens, width),
        x_flat,
        cot_own,
        w_out_all,
        w_up_own,
        w_down,
        b_own[None],
        ln2_gain[None],
        ln2_bias[None],
        groups,
        shards,
    )
    d_down = lax.psum_scatter(grad_down_t, "ctx", scatter_dimension=0, tiled=True)
    d_up = lax.psum_scatter(grad_up, "ctx", scatter_dimension=0, tiled=True)
    pairs = []
    for i in range(dp_size):
        for j in range(ctx_size):
            pairs.append((i * ctx_size + j, (j % dp_size) * ctx_size + shards * i + j // dp_size))
    d_up = lax.ppermute(d_up, ("dp", "ctx"), pairs)
    d_out_t = lax.psum_scatter(
        jnp.transpose(d_out_t, (1, 0, 2)).reshape(model, model), "ctx", scatter_dimension=0, tiled=True
    )
    d_out_t = jnp.transpose(d_out_t.reshape(-1, dp_size, model // dp_size), (1, 0, 2))
    dq, dkv = attend_back(
        proj, probs, slope, out, inverse, grad_att_got.reshape(row_length, width), hpg
    )
    w_q = jnp.concatenate([w_pick[:, :width], w_pick[:, 3 * width : 3 * width + HD]], axis=1)
    w_kv = jnp.concatenate([w_pick[:, width : 3 * width], w_pick[:, 3 * width + HD :]], axis=1)
    grad_normed_one = contract_cols(dq, w_q) + lax.dot_general(
        dkv, w_kv, (((0,), (1,)), ((), ())), preferred_element_type=f32
    )
    d_q = contract_rows(dq, normed_one)
    d_kv = matmul(dkv, normed_one)
    d_qkv_t = jnp.concatenate([d_q[:width], d_kv[: 2 * width], d_q[width:], d_kv[2 * width :]], axis=0)
    d_qkv_t = jnp.transpose(d_qkv_t.reshape(-1, dp_size, model // dp_size), (1, 0, 2)).astype(bf16)
    vec = jnp.stack(
        [
            jnp.sum(grad_normed_one * xhat_row, axis=0),
            jnp.sum(grad_normed_one, axis=0),
            vec_two[0],
            vec_two[1],
        ]
        + [d_bias_own[0, at * model : (at + 1) * model] for at in range(ff_own // model)]
    )
    grad_one_got, d_qkv_got, d_out_got, vec_got = exchange(
        5,
        "deal_grad_one",
        (grad_normed_one.astype(bf16).reshape(ctx_size, tokens, model), "ctx", piece, (tokens, model)),
        (d_qkv_t, "dp", piece, d_qkv_t.shape[1:]),
        (d_out_t, "dp", piece, d_out_t.shape[1:]),
        (vec, "ctx", whole, vec.shape),
    )
    vec = jnp.sum(vec_got, axis=0)
    d_qkv_sum = jnp.sum(d_qkv_got.astype(f32), axis=0).astype(bf16)
    shard = 3 * model // ctx_size
    qkv_got, extra, vecs = deal(6, d_qkv_sum, vec, width, shard, groups)
    part = math.gcd(width, shard)
    slots = shard // part
    d_qkv = jnp.sum(qkv_got.astype(f32), axis=1)
    extra = jnp.sum(extra.astype(f32), axis=0)
    for kind in range(2):
        section = kind * groups * (width // part)
        target, slot = section // slots, section % slots
        d_qkv = d_qkv.at[slot, :HD].add(jnp.where(ctx == target, extra, 0.0))
    d_qkv = d_qkv.reshape(shard, -1).T

    x_own = x_own.reshape(mbs * tokens, model).astype(f32)
    own_hat, own_inv = norm_parts(x_own)
    grad_one = jnp.sum(grad_one_got.reshape(mbs, groups, tokens, model).astype(f32), axis=1)
    grad_one = grad_one.reshape(mbs * tokens, model)
    d_x = (grad_mid + norm_back(own_hat, own_inv, grad_one, ln1_gain)).astype(bf16)
    vec = jnp.sum(vecs[:, :4], axis=0)
    d_bias_up = vecs[:, 4:].reshape(-1)
    return (
        layer_out.reshape(mbs, 1, tokens, model),
        d_x.reshape(mbs, 1, tokens, model),
        vec[0],
        vec[1],
        d_qkv,
        jnp.sum(d_out_got.astype(f32), axis=0).T,
        vec[2],
        vec[3],
        d_up.astype(f32),
        d_bias_up,
        d_down.astype(f32).T,
    )


def on_device(*arguments):
    layer_input = arguments[0]
    mbs, model = layer_input.shape[0], layer_input.shape[3]
    heads, ctx_size, dp_size = model // HD, lax.axis_size("ctx"), lax.axis_size("dp")
    groups = ctx_size // mbs
    fits = (
        ctx_size % mbs == 0
        and heads % groups == 0
        and dp_size == 4
        and ctx_size % dp_size == 0
        and model % HD == 0
        and (layer_input.shape[2] * ctx_size) % QUERY_BLOCK == 0
    )
    return (per_head_device if fits else per_token_device)(*arguments)


def solution(mesh):
    return jax.shard_map(
        on_device,
        mesh=mesh,
        in_specs=(
            P(None, "dp", "ctx", None),
            P(None, "dp", None),
            P(),
            P(),
            P("dp", None),
            P("dp", None),
            P(),
            P(),
            P("dp", None),
            P(),
            P("dp", None),
            P(None, "dp", "ctx", None),
        ),
        out_specs=(
            P(None, "dp", "ctx", None),
            P(None, "dp", "ctx", None),
            P(),
            P(),
            P("dp", "ctx"),
            P("dp", "ctx"),
            P(),
            P(),
            P("dp", "ctx"),
            P(),
            P("dp", "ctx"),
        ),
        check_vma=False,
    )
```

```python
import math
from functools import partial
from types import SimpleNamespace

import jax
import jax.numpy as jnp
from jax import lax
from jax.experimental import pallas as pl
from jax.experimental.pallas import tpu as pltpu
from jax.sharding import PartitionSpec as P

HD = 64


NORM_EPSILON = 1e-05
MASKED = -1e30
START_TOP = -1e20


def prefix_2(array, axis, combine, identity, reverse):
    peers, index = (lax.axis_size(axis), lax.axis_index(axis))
    everything = lax.all_gather(array, axis)
    start = jnp.broadcast_to(jnp.asarray(identity, array.dtype), array.shape)

    def turn(k, before):
        at = peers - 1 - k if reverse else k
        reached = at > index if reverse else at < index
        new = combine(before, everything[at])
        return jnp.where(reached, new, before)

    return lax.fori_loop(0, peers, turn, start)


def layer_norm(value, gain, bias):
    row_mean = jnp.mean(value, axis=-1, keepdims=True)
    centered = value - row_mean
    spread = jnp.mean(centered * centered, axis=-1, keepdims=True)
    return centered * lax.rsqrt(spread + NORM_EPSILON) * gain + bias


def matmul(left, right):
    return jnp.dot(left, right, preferred_element_type=jnp.float32)


def contract_rows(left, right):
    return lax.dot_general(
        left, right, (((0,), (0,)), ((), ())), preferred_element_type=jnp.float32
    )


def contract_cols(left, right):
    return lax.dot_general(
        left, right, (((1,), (1,)), ((), ())), preferred_element_type=jnp.float32
    )


def segment_table(lengths, row_length):
    doc_ends = jnp.cumsum(lengths)
    places = jnp.arange(row_length, dtype=jnp.int32)
    segment = jnp.sum((places[:, None] >= doc_ends[None, :]).astype(jnp.int32), axis=1)
    opening = jnp.concatenate([jnp.ones((1,), jnp.bool_), segment[1:] != segment[:-1]])
    return (segment, opening)


def add_up(earlier, later):
    return earlier + later


def per_token_device(
    layer_input,
    doc_lengths,
    ln1_gain,
    ln1_bias,
    w_qkv,
    w_out,
    ln2_gain,
    ln2_bias,
    w_up,
    b_up,
    w_down,
    cotangent,
):
    micro_count = layer_input.shape[0]
    query_rows = layer_input.shape[2]
    model_width = layer_input.shape[3]
    head_count = model_width // HD
    row_length = query_rows * lax.axis_size("ctx")
    key_block = min(512, row_length)
    score_scale = HD ** (-0.5)
    strength = 8.0 / row_length
    ctx_place = lax.axis_index("ctx")
    query_pos = ctx_place * query_rows + jnp.arange(query_rows, dtype=jnp.int32)
    block_total = ((ctx_place + 1) * query_rows + key_block - 1) // key_block
    later_heads = (jnp.arange(head_count) > 0).astype(jnp.float32)[:, None, None]
    zeros_row = jnp.zeros((row_length,), jnp.float32)
    gelu_exact = partial(jax.nn.gelu, approximate=False)
    output_list = []
    input_grads = []
    matrix_total = None
    vector_total = None
    for micro_step in range(micro_count):
        w_qkv_all, w_out_all, w_up_all, w_down_all = (
            lax.all_gather(w_qkv, "dp", axis=0, tiled=True),
            lax.all_gather(w_out, "dp", axis=0, tiled=True),
            lax.all_gather(w_up, "dp", axis=0, tiled=True),
            lax.all_gather(w_down, "dp", axis=0, tiled=True),
        )
        inputs = layer_input[micro_step, 0].astype(jnp.float32)
        segment, opening = segment_table(doc_lengths[micro_step, 0], row_length)
        query_seg = lax.dynamic_slice_in_dim(segment, ctx_place * query_rows, query_rows, 0)
        normed_one = layer_norm(inputs, ln1_gain, ln1_bias).astype(jnp.bfloat16)
        projected = matmul(normed_one, w_qkv_all).astype(jnp.bfloat16)
        queries = projected[:, :model_width]
        queries3 = queries.reshape(query_rows, head_count, HD)
        query_zero = queries[:, :HD]
        keys_all, values_all = (
            lax.all_gather(projected[:, model_width : 2 * model_width], "ctx", axis=0, tiled=True),
            lax.all_gather(projected[:, 2 * model_width :], "ctx", axis=0, tiled=True),
        )

        def masks(key_start):
            key_seg = lax.dynamic_slice_in_dim(segment, key_start, key_block, 0)
            key_open = lax.dynamic_slice_in_dim(opening, key_start, key_block, 0)
            key_pos = key_start + jnp.arange(key_block, dtype=jnp.int32)
            same_doc = query_seg[:, None] == key_seg[None, :]
            allowed = same_doc & (key_pos[None, :] <= query_pos[:, None])
            chosen = (
                same_doc
                & (key_pos[None, :] < query_pos[:, None])
                & jnp.logical_not(key_open)[None, :]
            )
            return (allowed, chosen.astype(jnp.float32))

        def head_scores(key_start):
            key_zero = lax.dynamic_slice_in_dim(keys_all, key_start, key_block, 0)[:, :HD]
            return (key_zero, contract_cols(query_zero, key_zero) * score_scale)

        def block_keys(key_start):
            keys3 = lax.dynamic_slice_in_dim(keys_all, key_start, key_block, 0).reshape(
                key_block, head_count, HD
            )
            values3 = lax.dynamic_slice_in_dim(values_all, key_start, key_block, 0).reshape(
                key_block, head_count, HD
            )
            return (keys3, values3)

        def logits_of(key_start, keys3):
            allowed, chosen = masks(key_start)
            raw_scores = (
                jnp.einsum("qhd,khd->hqk", queries3, keys3, preferred_element_type=jnp.float32)
                * score_scale
            )
            picked = strength * jax.nn.softplus(raw_scores[0]) * chosen
            before = lax.dynamic_slice_in_dim(prefix, key_start, key_block, 0)
            penalty = before[None, :] + jnp.cumsum(picked, axis=0) - picked
            return jnp.where(allowed[None], raw_scores - penalty[None], MASKED)

        def total_block(block_index, totals):
            key_start = block_index * key_block
            _, chosen = masks(key_start)
            _, first_scores = head_scores(key_start)
            picked = strength * jax.nn.softplus(first_scores) * chosen
            return lax.dynamic_update_slice_in_dim(totals, jnp.sum(picked, axis=0), key_start, 0)

        totals = lax.fori_loop(0, block_total, total_block, zeros_row)
        prefix = prefix_2(totals, "ctx", add_up, zeros_row, False)

        def stat_block(block_index, running):
            row_top, row_total = running
            key_start = block_index * key_block
            keys3, _ = block_keys(key_start)
            logits = logits_of(key_start, keys3)
            new_top = jnp.maximum(row_top, jnp.max(logits, axis=-1))
            row_total = row_total * jnp.exp(row_top - new_top) + jnp.sum(
                jnp.exp(logits - new_top[..., None]), axis=-1
            )
            return (new_top, row_total)

        row_top, row_total = lax.fori_loop(
            0,
            block_total,
            stat_block,
            (
                jnp.full((head_count, query_rows), START_TOP, jnp.float32),
                jnp.zeros((head_count, query_rows), jnp.float32),
            ),
        )
        log_total = row_top + jnp.log(row_total)

        def out_block(block_index, gathered_out):
            key_start = block_index * key_block
            keys3, values3 = block_keys(key_start)
            attn_probs = jnp.exp(logits_of(key_start, keys3) - log_total[..., None]).astype(
                jnp.bfloat16
            )
            return gathered_out + jnp.einsum(
                "hqk,khd->qhd", attn_probs, values3, preferred_element_type=jnp.float32
            )

        gathered_out = lax.fori_loop(
            0, block_total, out_block, jnp.zeros((query_rows, head_count, HD), jnp.float32)
        )
        attended = gathered_out.reshape(query_rows, model_width).astype(jnp.bfloat16)
        mid_stream = inputs + matmul(attended, w_out_all)
        normed_two = layer_norm(mid_stream, ln2_gain, ln2_bias).astype(jnp.bfloat16)
        hidden = matmul(normed_two, w_up_all) + b_up
        activated = gelu_exact(hidden).astype(jnp.bfloat16)
        output_list.append((mid_stream + matmul(activated, w_down_all)).astype(jnp.bfloat16))
        cot_rows = cotangent[micro_step, 0]
        grad_down = contract_rows(activated, cot_rows)
        grad_act = contract_cols(cot_rows, w_down_all)
        _, gelu_back = jax.vjp(gelu_exact, hidden)
        grad_hidden = gelu_back(grad_act)[0].astype(jnp.bfloat16)
        grad_up = contract_rows(normed_two, grad_hidden)
        grad_bias_up = jnp.sum(grad_hidden.astype(jnp.float32), axis=0)
        grad_normed_two = contract_cols(grad_hidden, w_up_all)
        _, norm_two_back = jax.vjp(layer_norm, mid_stream, ln2_gain, ln2_bias)
        grad_mid_part, grad_gain_two, grad_bias_two = norm_two_back(grad_normed_two)
        grad_mid = cot_rows.astype(jnp.float32) + grad_mid_part
        grad_branch = grad_mid.astype(jnp.bfloat16)
        grad_outproj = contract_rows(attended, grad_branch)
        grad_attended = contract_cols(grad_branch, w_out_all).astype(jnp.bfloat16)
        grad_att3 = grad_attended.reshape(query_rows, head_count, HD)
        row_delta = jnp.einsum("qhd,qhd->hq", grad_att3.astype(jnp.float32), gathered_out)

        def grad_block(block_index, running):
            grad_query, grad_key_all, grad_value_all, penalty_grad, first_grad = running
            key_start = block_index * key_block
            keys3, values3 = block_keys(key_start)
            probs_f32 = jnp.exp(logits_of(key_start, keys3) - log_total[..., None])
            grad_probs = jnp.einsum(
                "qhd,khd->hqk", grad_att3, values3, preferred_element_type=jnp.float32
            )
            grad_logits = probs_f32 * (grad_probs - row_delta[..., None])
            penalty_grad = lax.dynamic_update_slice_in_dim(
                penalty_grad, -jnp.sum(grad_logits, axis=0), key_start, 1
            )
            first_grad = lax.dynamic_update_slice_in_dim(first_grad, grad_logits[0], key_start, 1)
            grad_scores = (grad_logits * later_heads).astype(jnp.bfloat16)
            grad_query = (
                grad_query
                + jnp.einsum("hqk,khd->qhd", grad_scores, keys3, preferred_element_type=jnp.float32)
                * score_scale
            )
            key_part = (
                jnp.einsum(
                    "hqk,qhd->khd", grad_scores, queries3, preferred_element_type=jnp.float32
                )
                * score_scale
            )
            value_part = jnp.einsum(
                "hqk,qhd->khd",
                probs_f32.astype(jnp.bfloat16),
                grad_att3,
                preferred_element_type=jnp.float32,
            )
            grad_key_all = lax.dynamic_update_slice_in_dim(
                grad_key_all, key_part.reshape(key_block, model_width), key_start, 0
            )
            grad_value_all = lax.dynamic_update_slice_in_dim(
                grad_value_all, value_part.reshape(key_block, model_width), key_start, 0
            )
            return (grad_query, grad_key_all, grad_value_all, penalty_grad, first_grad)

        grad_query, grad_key_all, grad_value_all, penalty_grad, first_grad = lax.fori_loop(
            0,
            block_total,
            grad_block,
            (
                jnp.zeros((query_rows, head_count, HD), jnp.float32),
                jnp.zeros((row_length, model_width), jnp.float32),
                jnp.zeros((row_length, model_width), jnp.float32),
                jnp.zeros((query_rows, row_length), jnp.float32),
                jnp.zeros((query_rows, row_length), jnp.float32),
            ),
        )
        column_sums = jnp.sum(penalty_grad, axis=0)
        after = prefix_2(column_sums, "ctx", add_up, zeros_row, True)
        reach_sums = after + column_sums

        def head_block(block_index, running):
            grad_query_zero, grad_key_all = running
            key_start = block_index * key_block
            _, chosen = masks(key_start)
            key_zero, first_scores = head_scores(key_start)
            flow_block = lax.dynamic_slice_in_dim(penalty_grad, key_start, key_block, 1)
            reach_block = lax.dynamic_slice_in_dim(reach_sums, key_start, key_block, 0)
            grad_picked = reach_block[None, :] - jnp.cumsum(flow_block, axis=0)
            grad_select = grad_picked * strength * jax.nn.sigmoid(first_scores) * chosen
            grad_head = (
                lax.dynamic_slice_in_dim(first_grad, key_start, key_block, 1) + grad_select
            ).astype(jnp.bfloat16)
            grad_query_zero = grad_query_zero + matmul(grad_head, key_zero) * score_scale
            key_zero_grad = contract_rows(grad_head, query_zero) * score_scale
            grad_key_all = lax.dynamic_update_slice(
                grad_key_all, key_zero_grad, (key_start, jnp.zeros((), jnp.int32))
            )
            return (grad_query_zero, grad_key_all)

        grad_query_zero, grad_key_all = lax.fori_loop(
            0, block_total, head_block, (jnp.zeros((query_rows, HD), jnp.float32), grad_key_all)
        )
        grad_query = grad_query.at[:, 0, :].add(grad_query_zero).reshape(query_rows, model_width)
        grad_key_own, grad_value_own = (
            lax.psum_scatter(grad_key_all, "ctx", scatter_dimension=0, tiled=True),
            lax.psum_scatter(grad_value_all, "ctx", scatter_dimension=0, tiled=True),
        )
        grad_project = jnp.concatenate([grad_query, grad_key_own, grad_value_own], axis=1).astype(
            jnp.bfloat16
        )
        grad_qkv = contract_rows(normed_one, grad_project)
        grad_normed_one = contract_cols(grad_project, w_qkv_all)
        _, norm_one_back = jax.vjp(layer_norm, inputs, ln1_gain, ln1_bias)
        grad_in_part, grad_gain_one, grad_bias_one = norm_one_back(grad_normed_one)
        input_grads.append((grad_mid + grad_in_part).astype(jnp.bfloat16))
        matrix_grads = (grad_qkv, grad_outproj, grad_up, grad_down)
        vector_grads = (grad_gain_one, grad_bias_one, grad_gain_two, grad_bias_two, grad_bias_up)
        matrix_grads = (
            lax.psum_scatter(matrix_grads[0], "ctx", scatter_dimension=1, tiled=True),
            lax.psum_scatter(matrix_grads[1], "ctx", scatter_dimension=1, tiled=True),
            lax.psum_scatter(matrix_grads[2], "ctx", scatter_dimension=1, tiled=True),
            lax.psum_scatter(matrix_grads[3], "ctx", scatter_dimension=1, tiled=True),
        )
        matrix_grads = (
            lax.psum_scatter(
                matrix_grads[0].astype(jnp.bfloat16), "dp", scatter_dimension=0, tiled=True
            ).astype(jnp.float32),
            lax.psum_scatter(
                matrix_grads[1].astype(jnp.bfloat16), "dp", scatter_dimension=0, tiled=True
            ).astype(jnp.float32),
            lax.psum_scatter(
                matrix_grads[2].astype(jnp.bfloat16), "dp", scatter_dimension=0, tiled=True
            ).astype(jnp.float32),
            lax.psum_scatter(
                matrix_grads[3].astype(jnp.bfloat16), "dp", scatter_dimension=0, tiled=True
            ).astype(jnp.float32),
        )
        vector_grads = lax.psum(
            (vector_grads[0], vector_grads[1], vector_grads[2], vector_grads[3], vector_grads[4]),
            ("dp", "ctx"),
        )
        if matrix_total is None:
            matrix_total = matrix_grads
            vector_total = vector_grads
        else:
            matrix_total = tuple((old + new for old, new in zip(matrix_total, matrix_grads)))
            vector_total = tuple((old + new for old, new in zip(vector_total, vector_grads)))
    layer_out = jnp.stack(output_list)[:, None]
    input_out = jnp.stack(input_grads)[:, None]
    return (
        layer_out,
        input_out,
        vector_total[0],
        vector_total[1],
        matrix_total[0],
        matrix_total[1],
        vector_total[2],
        vector_total[3],
        matrix_total[2],
        vector_total[4],
        matrix_total[3],
    )


MESH = pl.DeviceIdType.MESH
EXCLUDED = 1e30
QUERY_BLOCK = 256


def whole(ref, peer):
    return ref


def piece(ref, peer):
    return ref.at[peer]


def exchange_body(jobs, sizes, *refs):
    count = len(jobs)
    sources, targets = refs[:count], refs[count : 2 * count]
    send_sems, recv_sems = refs[2 * count : 3 * count], refs[3 * count : 4 * count]
    local_sem = refs[4 * count]
    barrier = pltpu.get_barrier_semaphore()
    greeted = 0
    for axis, size in sizes.items():
        me = lax.axis_index(axis)
        for step in range(1, size):
            pl.semaphore_signal(
                barrier, inc=1, device_id={axis: lax.rem(me + step, size)}, device_id_type=MESH
            )
            greeted += 1
    own = []
    for at, (axis, select) in enumerate(jobs):
        me = lax.axis_index(axis)
        copy = pltpu.make_async_copy(
            select(sources[at], me), targets[at].at[me], local_sem.at[at]
        )
        copy.start()
        own.append(copy)
    pl.semaphore_wait(barrier, greeted)
    sent = []
    for at, (axis, select) in enumerate(jobs):
        me, size = lax.axis_index(axis), sizes[axis]
        for step in range(1, size):
            peer = lax.rem(me + step, size)
            copy = pltpu.make_async_remote_copy(
                src_ref=select(sources[at], peer),
                dst_ref=targets[at].at[me],
                send_sem=send_sems[at].at[step - 1],
                recv_sem=recv_sems[at].at[step - 1],
                device_id={axis: peer},
                device_id_type=MESH,
            )
            copy.start()
            sent.append(copy)
    for copy in own + sent:
        copy.wait()


def exchange(collective_id, name, *jobs):
    arrays = [job[0] for job in jobs]
    axes = [job[1] for job in jobs]
    sizes = {axis: lax.axis_size(axis) for axis in axes}
    count = len(jobs)
    return pl.pallas_call(
        partial(exchange_body, [(job[1], job[2]) for job in jobs], sizes),
        out_shape=[
            jax.ShapeDtypeStruct((sizes[axis],) + tuple(job[3]), job[0].dtype)
            for axis, job in zip(axes, jobs)
        ],
        in_specs=[pl.BlockSpec(memory_space=pl.ANY)] * count,
        out_specs=[pl.BlockSpec(memory_space=pl.ANY)] * count,
        scratch_shapes=[pltpu.SemaphoreType.DMA((sizes[axis] - 1,)) for axis in axes] * 2
        + [pltpu.SemaphoreType.DMA((count,))],
        compiler_params=pltpu.CompilerParams(
            collective_id=collective_id, has_side_effects=True
        ),
        name=name,
    )(*arrays)


def segment_of(places, ends_ref, doc_count):
    total = jnp.zeros(places.shape, jnp.int32)
    for at in range(doc_count):
        total += jnp.where(places >= ends_ref[at], 1, 0)
    return total


def attend_body(hpg, strength, doc_count, ends_ref, proj_ref, probs_ref, slope_ref, out_ref, inv_ref, prefix):
    rows_all = proj_ref.shape[0]
    width = hpg * HD
    block = QUERY_BLOCK
    prefix[...] = jnp.zeros_like(prefix)
    row_at = lax.broadcasted_iota(jnp.int32, (block, block), 0)
    col_at = lax.broadcasted_iota(jnp.int32, (block, block), 1)
    earlier = (col_at < row_at).astype(jnp.bfloat16)
    scale = HD ** (-0.5)
    for start in range(0, rows_all, block):
        reach = start + block
        rows = pl.ds(start, block)
        row_pos = start + lax.broadcasted_iota(jnp.int32, (block, 1), 0)
        col_pos = lax.broadcasted_iota(jnp.int32, (1, reach), 1)
        row_seg = segment_of(row_pos, ends_ref, doc_count)
        col_seg = segment_of(col_pos, ends_ref, doc_count)
        before_seg = segment_of(col_pos - 1, ends_ref, doc_count)
        opening = (col_seg != before_seg) | (col_pos == 0)
        pick_seg = jnp.where(opening, -1, col_seg)
        query = proj_ref[rows, 3 * width : 3 * width + HD] * scale
        key = proj_ref[:reach, 3 * width + HD : 3 * width + 2 * HD]
        scores = contract_cols(query.astype(jnp.bfloat16), key)
        small = jnp.exp(-jnp.abs(scores))
        soft = jnp.maximum(scores, 0.0) + jnp.log(1.0 + small)
        recip = 1.0 / (1.0 + small)
        sigmoid = jnp.where(scores >= 0.0, recip, small * recip)
        chosen = (row_seg == pick_seg) & (col_pos < row_pos)
        picked = jnp.where(chosen, strength * soft, 0.0)
        slope_ref[rows, :reach] = jnp.where(chosen, strength * sigmoid, 0.0).astype(jnp.bfloat16)
        high = picked.astype(jnp.bfloat16)
        low = (picked - high.astype(jnp.float32)).astype(jnp.bfloat16)
        penalty = prefix[:, :reach] + (matmul(earlier, high) + matmul(earlier, low))
        allowed = (row_seg == col_seg) & (col_pos <= row_pos)
        penalty = jnp.where(allowed, penalty, EXCLUDED)
        prefix[:, :reach] += jnp.sum(picked, axis=0, keepdims=True)
        for head in range(hpg):
            at = head * HD
            query = (proj_ref[rows, at : at + HD] * scale).astype(jnp.bfloat16)
            key = proj_ref[:reach, width + at : width + at + HD]
            value = proj_ref[:reach, 2 * width + at : 2 * width + at + HD]
            logits = contract_cols(query, key) - penalty
            top = jnp.max(logits, axis=1, keepdims=True)
            probs = jnp.exp(logits - top)
            inverse = 1.0 / jnp.sum(probs, axis=1, keepdims=True)
            probs = probs.astype(jnp.bfloat16)
            probs_ref[head, rows, :reach] = probs
            out_ref[rows, at : at + HD] = matmul(probs, value) * inverse
            inv_ref[rows, head : head + 1] = inverse


def attend(ends, proj, hpg, strength):
    rows = proj.shape[0]
    vmem = pl.BlockSpec(memory_space=pltpu.VMEM)
    return pl.pallas_call(
        partial(attend_body, hpg, strength, ends.shape[0]),
        out_shape=[
            jax.ShapeDtypeStruct((hpg, rows, rows), jnp.bfloat16),
            jax.ShapeDtypeStruct((rows, rows), jnp.bfloat16),
            jax.ShapeDtypeStruct((rows, hpg * HD), jnp.float32),
            jax.ShapeDtypeStruct((rows, hpg), jnp.float32),
        ],
        in_specs=[pl.BlockSpec(memory_space=pltpu.SMEM), vmem],
        out_specs=[vmem] * 4,
        scratch_shapes=[pltpu.VMEM((1, rows), jnp.float32)],
        compiler_params=pltpu.CompilerParams(vmem_limit_bytes=48 * 1024 * 1024),
        name="attend",
    )(ends, proj)


def norm_parts(value):
    row_mean = jnp.mean(value, axis=-1, keepdims=True)
    centered = value - row_mean
    spread = jnp.mean(centered * centered, axis=-1, keepdims=True)
    inverse = lax.rsqrt(spread + NORM_EPSILON)
    return centered * inverse, inverse


def norm_back(xhat, inverse, grad, gain):
    scaled = grad * gain
    return (
        scaled
        - jnp.mean(scaled, axis=-1, keepdims=True)
        - xhat * jnp.mean(scaled * xhat, axis=-1, keepdims=True)
    ) * inverse


class Wires:
    def __init__(self, send_sem, recv_sem):
        self.send_sem, self.recv_sem, self.used, self.made = send_sem, recv_sem, 0, []

    def send(self, source, target, where):
        copy = pltpu.make_async_remote_copy(
            src_ref=source,
            dst_ref=target,
            send_sem=self.send_sem.at[self.used],
            recv_sem=self.recv_sem.at[self.used],
            device_id=where,
            device_id_type=MESH,
        )
        copy.start()
        self.used += 1
        self.made.append(copy)
        return copy

    def drain(self):
        for copy in self.made:
            copy.wait_send()


def rounded(value):
    return value.astype(jnp.bfloat16)


def swap(index):
    return index + 1 - 2 * lax.rem(index, 2)


def rest_body(plan, names, *refs):
    r = SimpleNamespace(**dict(zip(names, refs)))
    groups, shards = plan
    f32 = jnp.float32
    ctx, dp = lax.axis_index("ctx"), lax.axis_index("dp")
    ctx_size, tokens, width = r.att.shape
    lines = ctx_size // 2
    mbs = ctx_size // groups
    hpg = width // HD
    own, model = r.x.shape
    ff = r.w_down_hbm.shape[0]
    row_length = tokens * ctx_size
    side, line = lax.rem(ctx, 2), ctx // 2
    my_mb, my_group = ctx // groups, lax.rem(ctx, groups)
    wires = Wires(r.send_sem, r.recv_sem)
    core, far, far_core = {"dp": swap(dp)}, {"dp": lax.rem(dp + 2, 4)}, {"dp": lax.rem(swap(dp) + 2, 4)}
    beside = {"ctx": swap(ctx)}
    up_to = {"dp": lax.rem(ctx, 4), "ctx": shards * dp + ctx // 4}
    up_from = {"dp": ctx // shards, "ctx": lax.rem(ctx, shards) * 4 + dp}
    around = [{"ctx": lax.rem(ctx + step, ctx_size)} for step in range(1, ctx_size)]

    loads = {}
    for at, name in enumerate(("cot", "w_out", "w_up", "w_down", "probs", "slope", "proj", "out", "w_pick", "normed_one", "hat_one")):
        loads[name] = pltpu.make_async_copy(
            getattr(r, name + "_hbm"), getattr(r, name), r.load_sem.at[at]
        )
        loads[name].start()
    barrier = pltpu.get_barrier_semaphore()
    for where in around + [core, far, far_core, up_from]:
        pl.semaphore_signal(barrier, inc=1, device_id=where, device_id_type=MESH)
    pl.semaphore_wait(barrier, ctx_size + 3)

    att_in = []
    for step in range(1, ctx_size):
        peer = lax.rem(ctx + step, ctx_size)
        att_in.append(wires.send(r.att.at[peer], r.att_got.at[ctx], {"ctx": peer}))
    loads["cot"].wait()
    cot_core = wires.send(r.cot, r.cots.at[1], core)
    cot_far = wires.send(r.cot, r.cots.at[2], far)
    r.att_got[ctx] = r.att[ctx]
    r.cots[0] = r.cot[...]
    for name in ("w_out", "w_up", "w_down"):
        loads[name].wait()
    cot_far.wait_recv()
    cot_fwd = wires.send(r.cots.at[2], r.cots.at[3], core)
    for copy in att_in:
        copy.wait_recv()

    gain, bias = r.gain_two[...], r.bias_two[...]
    for micro in range(mbs):
        rows = pl.ds(micro * tokens, tokens)
        stream = r.x[rows, :].astype(f32)
        for group in range(groups):
            stream += matmul(
                r.att_got[micro * groups + group], r.w_out[pl.ds(group * width, width), :]
            )
        r.mid[rows, :] = stream
    xhat, inverse_two = norm_parts(r.mid[...])
    r.hat_two[...] = xhat
    r.normed[0] = rounded(xhat * gain + bias)
    to_core = wires.send(r.normed.at[0], r.normed.at[1], core)
    to_far = wires.send(r.normed.at[0], r.normed.at[2], far)

    def feed(slot):
        hidden = matmul(r.normed[slot], r.w_up[...]) + r.b_up[...]
        cdf = 0.5 * (1.0 + lax.erf(hidden * (2.0**-0.5)))
        density = jnp.exp(-0.5 * hidden * hidden) * ((2.0 * math.pi) ** -0.5)
        r.act[slot] = rounded(hidden * cdf)
        grad = contract_cols(r.cots[slot], r.w_down[...])
        r.grad_hid[slot] = rounded(grad * (cdf + hidden * density))
        r.part[slot] = rounded(contract_cols(r.grad_hid[slot], r.w_up[...]))

    def feed_out(slot):
        r.out_part[slot] = rounded(matmul(r.act[slot], r.w_down[...]))

    feed(0)
    cot_core.wait_recv()
    to_core.wait_recv()
    feed(1)
    part_core = wires.send(r.part.at[1], r.part_got.at[0], core)
    to_far.wait_recv()
    forward = wires.send(r.normed.at[2], r.normed.at[3], core)
    feed(2)
    forward.wait_recv()
    cot_fwd.wait_recv()
    feed(3)
    part_far_core = wires.send(r.part.at[3], r.part_got.at[1], core)
    feed_out(3)
    out_far_core = wires.send(r.out_part.at[3], r.out_got.at[1], core)
    part_far_core.wait_recv()
    r.part[2] = rounded(r.part[2].astype(f32) + r.part_got[1].astype(f32))
    part_far = wires.send(r.part.at[2], r.part_got.at[2], far)
    feed_out(1)
    out_core = wires.send(r.out_part.at[1], r.out_got.at[0], core)
    feed_out(2)
    out_far_core.wait_recv()
    r.out_part[2] = rounded(r.out_part[2].astype(f32) + r.out_got[1].astype(f32))
    out_far = wires.send(r.out_part.at[2], r.out_got.at[2], far)

    flat_cot = r.cots[...].reshape(4 * own, model)
    flat_act = r.act[...].reshape(4 * own, ff)
    grads = rounded(contract_rows(flat_cot, flat_act))
    size = model // ctx_size
    for at in range(ctx_size):
        r.down_grad[at % 2, at // 2] = grads[at * size : (at + 1) * size]
    down_side = wires.send(r.down_grad.at[1 - side], r.down_side, beside)
    flat_normed = r.normed[...].reshape(4 * own, model)
    flat_grad = r.grad_hid[...].reshape(4 * own, ff)
    size = model // 4
    for at in range(shards):
        grads = rounded(
            contract_rows(flat_normed, flat_grad[:, at * ff // shards : (at + 1) * ff // shards])
        )
        for row in range(4):
            index = at * 4 + row
            r.up_grad[index % 2, index // 2] = grads[row * size : (row + 1) * size]
    up_side = wires.send(r.up_grad.at[1 - side], r.up_side, beside)
    feed_out(0)
    vec_rows = 4 + ff // model
    d_bias_up = jnp.sum(flat_grad.astype(f32), axis=0, keepdims=True)
    for at in range(ff // model):
        r.vec[4 + at : 5 + at, :] = d_bias_up[:, at * model : (at + 1) * model]

    part_core.wait_recv()
    part_far.wait_recv()
    grad_normed = r.part[0].astype(f32) + r.part_got[0].astype(f32) + r.part_got[2].astype(f32)
    xhat = r.hat_two[...]
    r.vec[2:3, :] = jnp.sum(grad_normed * xhat, axis=0, keepdims=True)
    r.vec[3:4, :] = jnp.sum(grad_normed, axis=0, keepdims=True)
    r.grad_mid[...] = r.cot[...].astype(f32) + norm_back(xhat, inverse_two, grad_normed, gain)
    branch = rounded(r.grad_mid[...])
    for group in range(groups):
        grad = rounded(contract_cols(branch, r.w_out[pl.ds(group * width, width), :]))
        for micro in range(mbs):
            r.att_out[micro * groups + group] = grad[micro * tokens : (micro + 1) * tokens]
    att_in = []
    for step in range(1, ctx_size):
        peer = lax.rem(ctx + step, ctx_size)
        att_in.append(wires.send(r.att_out.at[peer], r.grad_att.at[ctx], {"ctx": peer}))
    r.grad_att[ctx] = r.att_out[ctx]
    for group in range(groups):
        total = None
        for micro in range(mbs):
            some = contract_rows(
                branch[micro * tokens : (micro + 1) * tokens], r.att_got[micro * groups + group]
            )
            total = some if total is None else total + some
        r.out_grad[group] = rounded(total)
    out_grad_core = wires.send(r.out_grad.at[swap(dp)], r.out_grad_got.at[0], core)
    out_grad_far_core = wires.send(
        r.out_grad.at[lax.rem(swap(dp) + 2, 4)], r.out_grad_got.at[1], core
    )
    out_core.wait_recv()
    out_far.wait_recv()
    r.layer[...] = rounded(
        r.mid[...]
        + (r.out_part[0].astype(f32) + r.out_got[0].astype(f32) + r.out_got[2].astype(f32))
    )
    out_grad_far_core.wait_recv()
    mine = lax.rem(dp + 2, 4)
    r.out_grad[mine] = rounded(r.out_grad[mine].astype(f32) + r.out_grad_got[1].astype(f32))
    out_grad_far = wires.send(r.out_grad.at[mine], r.out_grad_got.at[2], far)
    for name in ("probs", "slope", "proj", "out", "w_pick", "normed_one", "hat_one"):
        loads[name].wait()
    for copy in att_in:
        copy.wait_recv()

    def spread(side_copy, grad, side_got, ready, line_got):
        side_copy.wait_recv()
        for step in range(lines):
            place = lax.rem(line + step, lines)
            ready[place] = rounded(grad[side, place].astype(f32) + side_got[place].astype(f32))
        return [
            wires.send(
                ready.at[lax.rem(line + step, lines)],
                line_got.at[line],
                {"ctx": lax.rem(line + step, lines) * 2 + side},
            )
            for step in range(1, lines)
        ]

    def gather_up(copies, ready, line_got):
        line_got[line] = ready[line]
        for copy in copies:
            copy.wait_recv()
        total = line_got[0].astype(f32)
        for place in range(1, lines):
            total += line_got[place].astype(f32)
        return total

    block = QUERY_BLOCK
    per_block = block // tokens
    scale = HD ** (-0.5)
    r.suffix[...] = jnp.zeros_like(r.suffix)
    r.acc[...] = jnp.zeros_like(r.acc)
    row_at = lax.broadcasted_iota(jnp.int32, (block, block), 0)
    col_at = lax.broadcasted_iota(jnp.int32, (block, block), 1)
    later = (col_at > row_at).astype(jnp.bfloat16)

    def back_block(start):
        reach = start + block
        rows = pl.ds(start, block)
        total = None
        first = start // tokens
        grad_block = r.grad_att[first : first + per_block].reshape(block, width)
        for head in range(hpg):
            at = head * HD
            query_t = rounded((r.proj[rows, at : at + HD].astype(f32) * scale).T)
            key = r.proj[:reach, width + at : width + at + HD]
            value = r.proj[:reach, 2 * width + at : 2 * width + at + HD]
            grad = grad_block[:, at : at + HD].astype(f32) * r.inverse[rows, head : head + 1]
            delta = jnp.sum(grad * r.out[rows, at : at + HD], axis=1, keepdims=True)
            probs = r.probs[head, rows, :reach]
            grad_probs = contract_cols(rounded(grad), value)
            grad_logits = probs.astype(f32) * (grad_probs - delta)
            total = grad_logits if total is None else total + grad_logits
            grad_scores = rounded(grad_logits)
            r.grad_proj[rows, at : at + HD] = rounded(matmul(grad_scores, key) * scale)
            r.acc[at : at + HD, :reach] += matmul(query_t, grad_scores)
            r.acc[width + at : width + at + HD, :reach] += matmul(rounded(grad.T), probs)
        query_t = rounded((r.proj[rows, 3 * width : 3 * width + HD].astype(f32) * scale).T)
        key = r.proj[:reach, 3 * width + HD : 3 * width + 2 * HD]
        flow = r.suffix[:, :reach] + matmul(later, rounded(total))
        grad_scores = rounded(-flow * r.slope[rows, :reach].astype(f32))
        r.grad_proj[rows, 3 * width : 3 * width + HD] = rounded(matmul(grad_scores, key) * scale)
        r.acc[2 * width : 2 * width + HD, :reach] += matmul(query_t, grad_scores)
        r.suffix[:, :reach] += jnp.sum(total, axis=0, keepdims=True)

    starts = list(reversed(range(0, row_length, block)))
    back_block(starts[0])
    down_line = spread(down_side, r.down_grad, r.down_side, r.down_ready, r.down_line)
    for start in starts[1:-1]:
        back_block(start)
    up_line = spread(up_side, r.up_grad, r.up_side, r.up_ready, r.up_line)
    out_grad_core.wait_recv()
    out_grad_far.wait_recv()
    grads = rounded(
        r.out_grad[dp].astype(f32) + r.out_grad_got[0].astype(f32) + r.out_grad_got[2].astype(f32)
    )
    size = model // ctx_size
    for at in range(ctx_size):
        r.out_piece[at % 2, at // 2] = grads[at * size : (at + 1) * size]
    out_side = wires.send(r.out_piece.at[1 - side], r.out_side, beside)
    back_block(starts[-1])
    r.grad_kv[...] = rounded(r.acc[...])
    r.grad_proj[:, width : 3 * width] = rounded(r.acc[: 2 * width, :].T)
    r.grad_proj[:, 3 * width + HD :] = rounded(r.acc[2 * width :, :].T)

    def one_piece(place, add):
        rows = pl.ds(pl.multiple_of(place * tokens, tokens), tokens)
        grad = contract_cols(r.grad_proj[rows, :], r.w_pick[...])
        gain_sum = jnp.sum(grad * r.hat_one[rows, :].astype(f32), axis=0, keepdims=True)
        bias_sum = jnp.sum(grad, axis=0, keepdims=True)
        r.vec[0:1, :] = r.vec[0:1, :] + gain_sum if add else gain_sum
        r.vec[1:2, :] = r.vec[1:2, :] + bias_sum if add else bias_sum
        return grad

    one_side = []
    for step in range(lines):
        place = lax.rem(line + lines - 1 - step, lines)
        r.one_piece[step] = rounded(one_piece(place * 2 + 1 - side, step > 0))
        one_side.append(wires.send(r.one_piece.at[step], r.one_side.at[step], beside))
    for step in range(lines):
        place = lax.rem(line + lines - 1 - step, lines)
        r.one_own[step] = one_piece(place * 2 + side, True)
    one_line = []
    for step in range(lines):
        place = lax.rem(line + lines - 1 - step, lines)
        one_side[step].wait_recv()
        r.one_ready[step] = rounded(r.one_own[step] + r.one_side[step].astype(f32))
        if step < lines - 1:
            one_line.append(
                wires.send(r.one_ready.at[step], r.one_line.at[line], {"ctx": place * 2 + side})
            )
    r.one_line[line] = r.one_ready[lines - 1]
    vec_in = []
    for step in range(1, ctx_size):
        peer = lax.rem(ctx + step, ctx_size)
        vec_in.append(wires.send(r.vec, r.vec_got.at[ctx], {"ctx": peer}))
    r.vec_got[ctx] = r.vec[...]

    size = model // 4
    grads_q = rounded(
        contract_rows(
            jnp.concatenate(
                [r.grad_proj[:, :width], r.grad_proj[:, 3 * width : 3 * width + HD]], axis=1
            ),
            r.normed_one[...],
        )
    )
    for at in range(4):
        cols = slice(at * size, (at + 1) * size)
        r.qkv_grad[at, :width, :] = grads_q[:width, cols]
        r.qkv_grad[at, 3 * width : 3 * width + HD, :] = grads_q[width:, cols]
    grads_kv = rounded(matmul(r.grad_kv[...], r.normed_one[...]))
    for at in range(4):
        cols = slice(at * size, (at + 1) * size)
        r.qkv_grad[at, width : 3 * width, :] = grads_kv[: 2 * width, cols]
        r.qkv_grad[at, 3 * width + HD :, :] = grads_kv[2 * width :, cols]
    qkv_far_core = wires.send(r.qkv_grad.at[lax.rem(swap(dp) + 2, 4)], r.qkv_got.at[1], core)
    qkv_core = wires.send(r.qkv_grad.at[swap(dp)], r.qkv_got.at[0], core)

    r.d_down[...] = gather_up(down_line, r.down_ready, r.down_line).T
    r.up_sum[...] = rounded(gather_up(up_line, r.up_ready, r.up_line))
    stays = (lax.rem(ctx, 4) == dp) & (shards * dp + ctx // 4 == ctx)
    up_copy = pltpu.make_async_remote_copy(
        src_ref=r.up_sum,
        dst_ref=r.up_final,
        send_sem=r.up_send.at[0],
        recv_sem=r.up_recv.at[0],
        device_id=up_to,
        device_id_type=MESH,
    )

    @pl.when(jnp.logical_not(stays))
    def _():
        up_copy.start()

    @pl.when(stays)
    def _():
        r.up_final[...] = r.up_sum[...]

    qkv_far_core.wait_recv()
    r.qkv_grad[mine] = rounded(r.qkv_grad[mine].astype(f32) + r.qkv_got[1].astype(f32))
    qkv_far = wires.send(r.qkv_grad.at[mine], r.qkv_got.at[2], far)
    out_line = spread(out_side, r.out_piece, r.out_side, r.out_ready, r.out_line)
    for copy in vec_in:
        copy.wait_recv()
    total = r.vec_got[0]
    for at in range(1, ctx_size):
        total += r.vec_got[at]
    r.vec_sum[...] = total
    vec_out = [
        wires.send(r.vec_sum, r.vecs.at[dp], where) for where in (core, far, far_core)
    ]
    r.vecs[dp] = total
    qkv_core.wait_recv()
    qkv_far.wait_recv()
    r.qkv_sum[...] = rounded(
        r.qkv_grad[dp].astype(f32) + r.qkv_got[0].astype(f32) + r.qkv_got[2].astype(f32)
    )
    part = r.deal_got.shape[2]
    per = width // part
    slots = r.deal_got.shape[0]

    def outgoing(kind, half):
        section = (kind * groups + my_group) * per + half
        target, slot = section // slots, lax.rem(section, slots)
        index = kind * per + half
        return target, slot, index, pltpu.make_async_remote_copy(
            src_ref=r.qkv_sum.at[pl.ds(index * part, part)],
            dst_ref=r.deal_got.at[slot, my_mb],
            send_sem=r.deal_send.at[index],
            recv_sem=r.deal_recv.at[slot, my_mb],
            device_id={"ctx": target},
            device_id_type=MESH,
        )

    def extra_copy(kind):
        return pltpu.make_async_remote_copy(
            src_ref=r.qkv_sum.at[pl.ds(3 * width + kind * HD, HD)],
            dst_ref=r.extra_got.at[ctx],
            send_sem=r.extra_send.at[kind],
            recv_sem=r.extra_recv.at[ctx],
            device_id={"ctx": kind * groups * per // slots},
            device_id_type=MESH,
        )

    for kind in range(3):
        for half in range(per):
            target, slot, index, copy = outgoing(kind, half)

            @pl.when(target != ctx)
            def _():
                copy.start()

            @pl.when(target == ctx)
            def _():
                r.deal_got[slot, my_mb] = r.qkv_sum[index * part : (index + 1) * part, :]

    for kind in range(2):
        target = kind * groups * per // slots
        copy = extra_copy(kind)

        @pl.when(ctx != target)
        def _():
            copy.start()

        @pl.when(ctx == target)
        def _():
            r.extra_got[ctx] = r.qkv_sum[3 * width + kind * HD : 3 * width + (kind + 1) * HD, :]

    xhat, inverse_one = norm_parts(r.x[...].astype(f32))
    gain_one = r.gain_one[...]
    for copy in one_line:
        copy.wait_recv()
    half_lines = lines // mbs
    for micro in range(mbs):
        grad = r.one_line[micro * half_lines].astype(f32)
        for at in range(1, half_lines):
            grad += r.one_line[micro * half_lines + at].astype(f32)
        rows = slice(micro * tokens, (micro + 1) * tokens)
        r.d_x[rows, :] = rounded(
            r.grad_mid[rows, :] + norm_back(xhat[rows], inverse_one[rows], grad, gain_one)
        )
    r.d_out[...] = gather_up(out_line, r.out_ready, r.out_line).T

    @pl.when(jnp.logical_not(stays))
    def _():
        up_copy.wait_send()
        up_copy.wait_recv()

    r.d_up[...] = r.up_final[...].astype(f32)

    for kind in range(3):
        for half in range(per):
            target, slot, index, copy = outgoing(kind, half)

            @pl.when(target != ctx)
            def _():
                copy.wait_send()

    for slot in range(slots):
        section = ctx * slots + slot
        source_group = lax.rem(section // per, groups)
        for place in range(mbs):

            @pl.when(place * groups + source_group != ctx)
            def _():
                pltpu.make_async_copy(
                    r.qkv_sum.at[pl.ds(0, part)],
                    r.deal_got.at[slot, place],
                    r.deal_recv.at[slot, place],
                ).wait()

        total = r.deal_got[slot, 0].astype(f32)
        for place in range(1, mbs):
            total += r.deal_got[slot, place].astype(f32)
        r.deal_sum[slot * part : (slot + 1) * part, :] = total
    for kind in range(2):
        section = kind * groups * per
        target, slot = section // slots, section % slots
        copy = extra_copy(kind)

        @pl.when(ctx != target)
        def _():
            copy.wait_send()

        @pl.when(ctx == target)
        def _():
            total = jnp.zeros((HD, size), f32)
            for place in range(ctx_size):
                if place != target:
                    pltpu.make_async_copy(
                        r.qkv_sum.at[pl.ds(0, HD)], r.extra_got.at[place], r.extra_recv.at[place]
                    ).wait()
                total += r.extra_got[place].astype(f32)
            r.deal_sum[slot * part : slot * part + HD, :] += total

    r.d_qkv[...] = r.deal_sum[...].T
    for copy in vec_out:
        copy.wait_recv()
    for row in range(4):
        r.d_vec[row : row + 1, :] = (
            r.vecs[0, row : row + 1, :] + r.vecs[1, row : row + 1, :]
        ) + (r.vecs[2, row : row + 1, :] + r.vecs[3, row : row + 1, :])
    for at in range(4):
        r.d_bias[at] = r.vecs[at, 4:vec_rows, :]
    wires.drain()


REST_COPIES = 72


def rest(collective_id, groups, shards, small, large):
    bf16, f32 = jnp.bfloat16, jnp.float32
    att, x_own = small["att"], small["x"]
    ctx_size, tokens, width = att.shape
    own, model = x_own.shape
    row_length = ctx_size * tokens
    lines = ctx_size // 2
    ff = large["w_down"].shape[0]
    size, shard = model // 4, 3 * model // ctx_size
    part = math.gcd(width, shard)
    slots, mbs = shard // part, ctx_size // groups
    picked = large["w_pick"].shape[1]
    vec_rows = 4 + ff // model
    narrow = model // ctx_size
    vmem = pl.BlockSpec(memory_space=pltpu.VMEM)
    anywhere = pl.BlockSpec(memory_space=pl.ANY)
    outs = {
        "layer": ((own, model), bf16),
        "d_x": ((own, model), bf16),
        "d_vec": ((4, model), f32),
        "d_bias": ((4, ff // model, model), f32),
        "d_qkv": ((size, shard), f32),
        "d_out": ((size, narrow), f32),
        "d_up": ((size, ff // shards), f32),
        "d_down": ((ff, narrow), f32),
    }
    scratch = {name: (array.shape, array.dtype) for name, array in large.items()}
    scratch |= {
        "att_got": (att.shape, bf16),
        "cots": ((4, own, model), bf16),
        "mid": ((own, model), f32),
        "hat_two": ((own, model), f32),
        "grad_mid": ((own, model), f32),
        "normed": ((4, own, model), bf16),
        "act": ((4, own, ff), bf16),
        "grad_hid": ((4, own, ff), bf16),
        "part": ((4, own, model), bf16),
        "out_part": ((4, own, model), bf16),
        "part_got": ((3, own, model), bf16),
        "out_got": ((3, own, model), bf16),
        "att_out": (att.shape, bf16),
        "grad_att": (att.shape, bf16),
        "down_grad": ((2, lines, narrow, ff), bf16),
        "down_side": ((lines, narrow, ff), bf16),
        "down_ready": ((lines, narrow, ff), bf16),
        "down_line": ((lines, narrow, ff), bf16),
        "up_grad": ((2, lines, size, ff // shards), bf16),
        "up_side": ((lines, size, ff // shards), bf16),
        "up_ready": ((lines, size, ff // shards), bf16),
        "up_line": ((lines, size, ff // shards), bf16),
        "up_sum": ((size, ff // shards), bf16),
        "up_final": ((size, ff // shards), bf16),
        "out_grad": ((4, model, size), bf16),
        "out_grad_got": ((3, model, size), bf16),
        "out_piece": ((2, lines, narrow, size), bf16),
        "out_side": ((lines, narrow, size), bf16),
        "out_ready": ((lines, narrow, size), bf16),
        "out_line": ((lines, narrow, size), bf16),
        "suffix": ((1, row_length), f32),
        "acc": ((2 * width + HD, row_length), f32),
        "grad_kv": ((2 * width + HD, row_length), bf16),
        "grad_proj": ((row_length, picked), bf16),
        "one_piece": ((lines, tokens, model), bf16),
        "one_own": ((lines, tokens, model), f32),
        "one_side": ((lines, tokens, model), bf16),
        "one_ready": ((lines, tokens, model), bf16),
        "one_line": ((lines, tokens, model), bf16),
        "qkv_grad": ((4, picked, size), bf16),
        "qkv_got": ((3, picked, size), bf16),
        "qkv_sum": ((picked, size), bf16),
        "deal_got": ((slots, mbs, part, size), bf16),
        "deal_sum": ((shard, size), f32),
        "extra_got": ((ctx_size, HD, size), bf16),
        "vec": ((vec_rows, model), f32),
        "vec_got": ((ctx_size, vec_rows, model), f32),
        "vec_sum": ((vec_rows, model), f32),
        "vecs": ((4, vec_rows, model), f32),
    }
    dma = pltpu.SemaphoreType.DMA
    sems = {
        "send_sem": dma((REST_COPIES,)),
        "recv_sem": dma((REST_COPIES,)),
        "load_sem": dma((len(large),)),
        "up_send": dma((1,)),
        "up_recv": dma((1,)),
        "deal_send": dma((3 * (width // part),)),
        "deal_recv": dma((slots, mbs)),
        "extra_send": dma((2,)),
        "extra_recv": dma((ctx_size,)),
    }
    names = list(small) + [name + "_hbm" for name in large] + list(outs) + list(scratch) + list(sems)
    return pl.pallas_call(
        partial(rest_body, (groups, shards), names),
        out_shape=[jax.ShapeDtypeStruct(*spec) for spec in outs.values()],
        in_specs=[vmem] * len(small) + [anywhere] * len(large),
        out_specs=[vmem] * len(outs),
        scratch_shapes=[pltpu.VMEM(*spec) for spec in scratch.values()] + list(sems.values()),
        compiler_params=pltpu.CompilerParams(
            collective_id=collective_id, has_side_effects=True, vmem_limit_bytes=60 * 1024 * 1024
        ),
        name="rest",
    )(*small.values(), *large.values())


def per_head_device(
    layer_input,
    doc_lengths,
    ln1_gain,
    ln1_bias,
    w_qkv,
    w_out,
    ln2_gain,
    ln2_bias,
    w_up,
    b_up,
    w_down,
    cotangent,
):
    bf16, f32 = jnp.bfloat16, jnp.float32
    mbs, _, tokens, model = layer_input.shape
    ctx_size, dp_size = lax.axis_size("ctx"), lax.axis_size("dp")
    ctx, dp = lax.axis_index("ctx"), lax.axis_index("dp")
    row_length = tokens * ctx_size
    groups = ctx_size // mbs
    hpg = model // HD // groups
    width = hpg * HD
    strength = 8.0 / row_length
    my_mb, grp = ctx // groups, lax.rem(ctx, groups)
    ff_own = b_up.shape[0] // dp_size
    x_own = layer_input[:, 0]
    cot_own = cotangent[:, 0].reshape(mbs * tokens, model)
    w_pick = jnp.concatenate(
        [lax.dynamic_slice_in_dim(w_qkv, kind * model + grp * width, width, 1) for kind in range(3)]
        + [w_qkv[:, :HD], w_qkv[:, model : model + HD]],
        axis=1,
    )

    def peer_mb(ref, peer):
        return ref.at[peer // groups]

    def peer_columns(ref, peer):
        return ref.at[:, pl.ds(pl.multiple_of(peer * ff_own, 128), ff_own)]

    x_row, w_pick, w_up_own, w_out_all = exchange(
        0,
        "gather_start",
        (x_own, "ctx", peer_mb, (tokens, model)),
        (w_pick, "dp", whole, w_pick.shape),
        (w_up, "dp", peer_columns, (w_up.shape[0], ff_own)),
        (w_out, "dp", whole, w_out.shape),
    )
    x_row = x_row.reshape(row_length, model).astype(f32)
    w_pick = w_pick.reshape(model, -1)
    w_up_own = w_up_own.reshape(model, ff_own)
    w_out_all = w_out_all.reshape(model, model)
    xhat_row, _ = norm_parts(x_row)
    normed_one = (xhat_row * ln1_gain + ln1_bias).astype(bf16)
    proj = matmul(normed_one, w_pick).astype(bf16)
    lengths = lax.dynamic_index_in_dim(doc_lengths[:, 0], my_mb, 0, keepdims=False)
    ends = jnp.cumsum(lengths).astype(jnp.int32)
    probs, slope, out, inverse = attend(ends, proj, hpg, strength)
    shards = ctx_size // dp_size
    small = {
        "att": out.astype(bf16).reshape(ctx_size, tokens, width),
        "x": x_own.reshape(mbs * tokens, model),
        "inverse": inverse,
        "b_up": lax.dynamic_slice_in_dim(b_up, dp * ff_own, ff_own, 0)[None],
        "gain_one": ln1_gain[None],
        "gain_two": ln2_gain[None],
        "bias_two": ln2_bias[None],
    }
    large = {
        "cot": cot_own,
        "w_out": w_out_all,
        "w_up": w_up_own,
        "w_down": w_down,
        "probs": probs,
        "slope": slope,
        "proj": proj,
        "out": out,
        "w_pick": w_pick,
        "normed_one": normed_one,
        "hat_one": xhat_row.astype(bf16),
    }
    layer_out, d_x, d_vec, d_bias, d_qkv, d_out, d_up, d_down = rest(1, groups, shards, small, large)
    return (
        layer_out.reshape(mbs, 1, tokens, model),
        d_x.reshape(mbs, 1, tokens, model),
        d_vec[0],
        d_vec[1],
        d_qkv,
        d_out,
        d_vec[2],
        d_vec[3],
        d_up,
        d_bias.reshape(-1),
        d_down,
    )


def on_device(*arguments):
    layer_input = arguments[0]
    mbs, model = layer_input.shape[0], layer_input.shape[3]
    heads, ctx_size, dp_size = model // HD, lax.axis_size("ctx"), lax.axis_size("dp")
    groups = ctx_size // mbs
    fits = (
        ctx_size % mbs == 0
        and heads % groups == 0
        and dp_size == 4
        and ctx_size % dp_size == 0
        and ctx_size == 8
        and mbs == 2
        and (layer_input.shape[2] * ctx_size) % QUERY_BLOCK == 0
    )
    return (per_head_device if fits else per_token_device)(*arguments)


def solution(mesh):
    return jax.shard_map(
        on_device,
        mesh=mesh,
        in_specs=(
            P(None, "dp", "ctx", None),
            P(None, "dp", None),
            P(),
            P(),
            P("dp", None),
            P("dp", None),
            P(),
            P(),
            P("dp", None),
            P(),
            P("dp", None),
            P(None, "dp", "ctx", None),
        ),
        out_specs=(
            P(None, "dp", "ctx", None),
            P(None, "dp", "ctx", None),
            P(),
            P(),
            P("dp", "ctx"),
            P("dp", "ctx"),
            P(),
            P(),
            P("dp", "ctx"),
            P(),
            P("dp", "ctx"),
        ),
        check_vma=False,
    )
```

```python
import math
from functools import partial
from types import SimpleNamespace

import jax
import jax.numpy as jnp
from jax import lax
from jax.experimental import pallas as pl
from jax.experimental.pallas import tpu as pltpu
from jax.sharding import PartitionSpec as P

HD = 64


NORM_EPSILON = 1e-05
MASKED = -1e30
START_TOP = -1e20


def prefix_2(array, axis, combine, identity, reverse):
    peers, index = (lax.axis_size(axis), lax.axis_index(axis))
    everything = lax.all_gather(array, axis)
    start = jnp.broadcast_to(jnp.asarray(identity, array.dtype), array.shape)

    def turn(k, before):
        at = peers - 1 - k if reverse else k
        reached = at > index if reverse else at < index
        new = combine(before, everything[at])
        return jnp.where(reached, new, before)

    return lax.fori_loop(0, peers, turn, start)


def layer_norm(value, gain, bias):
    row_mean = jnp.mean(value, axis=-1, keepdims=True)
    centered = value - row_mean
    spread = jnp.mean(centered * centered, axis=-1, keepdims=True)
    return centered * lax.rsqrt(spread + NORM_EPSILON) * gain + bias


def matmul(left, right):
    return jnp.dot(left, right, preferred_element_type=jnp.float32)


def contract_rows(left, right):
    return lax.dot_general(
        left, right, (((0,), (0,)), ((), ())), preferred_element_type=jnp.float32
    )


def contract_cols(left, right):
    return lax.dot_general(
        left, right, (((1,), (1,)), ((), ())), preferred_element_type=jnp.float32
    )


def segment_table(lengths, row_length):
    doc_ends = jnp.cumsum(lengths)
    places = jnp.arange(row_length, dtype=jnp.int32)
    segment = jnp.sum((places[:, None] >= doc_ends[None, :]).astype(jnp.int32), axis=1)
    opening = jnp.concatenate([jnp.ones((1,), jnp.bool_), segment[1:] != segment[:-1]])
    return (segment, opening)


def add_up(earlier, later):
    return earlier + later


def per_token_device(
    layer_input,
    doc_lengths,
    ln1_gain,
    ln1_bias,
    w_qkv,
    w_out,
    ln2_gain,
    ln2_bias,
    w_up,
    b_up,
    w_down,
    cotangent,
):
    micro_count = layer_input.shape[0]
    query_rows = layer_input.shape[2]
    model_width = layer_input.shape[3]
    head_count = model_width // HD
    row_length = query_rows * lax.axis_size("ctx")
    key_block = min(512, row_length)
    score_scale = HD ** (-0.5)
    strength = 8.0 / row_length
    ctx_place = lax.axis_index("ctx")
    query_pos = ctx_place * query_rows + jnp.arange(query_rows, dtype=jnp.int32)
    block_total = ((ctx_place + 1) * query_rows + key_block - 1) // key_block
    later_heads = (jnp.arange(head_count) > 0).astype(jnp.float32)[:, None, None]
    zeros_row = jnp.zeros((row_length,), jnp.float32)
    gelu_exact = partial(jax.nn.gelu, approximate=False)
    output_list = []
    input_grads = []
    matrix_total = None
    vector_total = None
    for micro_step in range(micro_count):
        w_qkv_all, w_out_all, w_up_all, w_down_all = (
            lax.all_gather(w_qkv, "dp", axis=0, tiled=True),
            lax.all_gather(w_out, "dp", axis=0, tiled=True),
            lax.all_gather(w_up, "dp", axis=0, tiled=True),
            lax.all_gather(w_down, "dp", axis=0, tiled=True),
        )
        inputs = layer_input[micro_step, 0].astype(jnp.float32)
        segment, opening = segment_table(doc_lengths[micro_step, 0], row_length)
        query_seg = lax.dynamic_slice_in_dim(segment, ctx_place * query_rows, query_rows, 0)
        normed_one = layer_norm(inputs, ln1_gain, ln1_bias).astype(jnp.bfloat16)
        projected = matmul(normed_one, w_qkv_all).astype(jnp.bfloat16)
        queries = projected[:, :model_width]
        queries3 = queries.reshape(query_rows, head_count, HD)
        query_zero = queries[:, :HD]
        keys_all, values_all = (
            lax.all_gather(projected[:, model_width : 2 * model_width], "ctx", axis=0, tiled=True),
            lax.all_gather(projected[:, 2 * model_width :], "ctx", axis=0, tiled=True),
        )

        def masks(key_start):
            key_seg = lax.dynamic_slice_in_dim(segment, key_start, key_block, 0)
            key_open = lax.dynamic_slice_in_dim(opening, key_start, key_block, 0)
            key_pos = key_start + jnp.arange(key_block, dtype=jnp.int32)
            same_doc = query_seg[:, None] == key_seg[None, :]
            allowed = same_doc & (key_pos[None, :] <= query_pos[:, None])
            chosen = (
                same_doc
                & (key_pos[None, :] < query_pos[:, None])
                & jnp.logical_not(key_open)[None, :]
            )
            return (allowed, chosen.astype(jnp.float32))

        def head_scores(key_start):
            key_zero = lax.dynamic_slice_in_dim(keys_all, key_start, key_block, 0)[:, :HD]
            return (key_zero, contract_cols(query_zero, key_zero) * score_scale)

        def block_keys(key_start):
            keys3 = lax.dynamic_slice_in_dim(keys_all, key_start, key_block, 0).reshape(
                key_block, head_count, HD
            )
            values3 = lax.dynamic_slice_in_dim(values_all, key_start, key_block, 0).reshape(
                key_block, head_count, HD
            )
            return (keys3, values3)

        def logits_of(key_start, keys3):
            allowed, chosen = masks(key_start)
            raw_scores = (
                jnp.einsum("qhd,khd->hqk", queries3, keys3, preferred_element_type=jnp.float32)
                * score_scale
            )
            picked = strength * jax.nn.softplus(raw_scores[0]) * chosen
            before = lax.dynamic_slice_in_dim(prefix, key_start, key_block, 0)
            penalty = before[None, :] + jnp.cumsum(picked, axis=0) - picked
            return jnp.where(allowed[None], raw_scores - penalty[None], MASKED)

        def total_block(block_index, totals):
            key_start = block_index * key_block
            _, chosen = masks(key_start)
            _, first_scores = head_scores(key_start)
            picked = strength * jax.nn.softplus(first_scores) * chosen
            return lax.dynamic_update_slice_in_dim(totals, jnp.sum(picked, axis=0), key_start, 0)

        totals = lax.fori_loop(0, block_total, total_block, zeros_row)
        prefix = prefix_2(totals, "ctx", add_up, zeros_row, False)

        def stat_block(block_index, running):
            row_top, row_total = running
            key_start = block_index * key_block
            keys3, _ = block_keys(key_start)
            logits = logits_of(key_start, keys3)
            new_top = jnp.maximum(row_top, jnp.max(logits, axis=-1))
            row_total = row_total * jnp.exp(row_top - new_top) + jnp.sum(
                jnp.exp(logits - new_top[..., None]), axis=-1
            )
            return (new_top, row_total)

        row_top, row_total = lax.fori_loop(
            0,
            block_total,
            stat_block,
            (
                jnp.full((head_count, query_rows), START_TOP, jnp.float32),
                jnp.zeros((head_count, query_rows), jnp.float32),
            ),
        )
        log_total = row_top + jnp.log(row_total)

        def out_block(block_index, gathered_out):
            key_start = block_index * key_block
            keys3, values3 = block_keys(key_start)
            attn_probs = jnp.exp(logits_of(key_start, keys3) - log_total[..., None]).astype(
                jnp.bfloat16
            )
            return gathered_out + jnp.einsum(
                "hqk,khd->qhd", attn_probs, values3, preferred_element_type=jnp.float32
            )

        gathered_out = lax.fori_loop(
            0, block_total, out_block, jnp.zeros((query_rows, head_count, HD), jnp.float32)
        )
        attended = gathered_out.reshape(query_rows, model_width).astype(jnp.bfloat16)
        mid_stream = inputs + matmul(attended, w_out_all)
        normed_two = layer_norm(mid_stream, ln2_gain, ln2_bias).astype(jnp.bfloat16)
        hidden = matmul(normed_two, w_up_all) + b_up
        activated = gelu_exact(hidden).astype(jnp.bfloat16)
        output_list.append((mid_stream + matmul(activated, w_down_all)).astype(jnp.bfloat16))
        cot_rows = cotangent[micro_step, 0]
        grad_down = contract_rows(activated, cot_rows)
        grad_act = contract_cols(cot_rows, w_down_all)
        _, gelu_back = jax.vjp(gelu_exact, hidden)
        grad_hidden = gelu_back(grad_act)[0].astype(jnp.bfloat16)
        grad_up = contract_rows(normed_two, grad_hidden)
        grad_bias_up = jnp.sum(grad_hidden.astype(jnp.float32), axis=0)
        grad_normed_two = contract_cols(grad_hidden, w_up_all)
        _, norm_two_back = jax.vjp(layer_norm, mid_stream, ln2_gain, ln2_bias)
        grad_mid_part, grad_gain_two, grad_bias_two = norm_two_back(grad_normed_two)
        grad_mid = cot_rows.astype(jnp.float32) + grad_mid_part
        grad_branch = grad_mid.astype(jnp.bfloat16)
        grad_outproj = contract_rows(attended, grad_branch)
        grad_attended = contract_cols(grad_branch, w_out_all).astype(jnp.bfloat16)
        grad_att3 = grad_attended.reshape(query_rows, head_count, HD)
        row_delta = jnp.einsum("qhd,qhd->hq", grad_att3.astype(jnp.float32), gathered_out)

        def grad_block(block_index, running):
            grad_query, grad_key_all, grad_value_all, penalty_grad, first_grad = running
            key_start = block_index * key_block
            keys3, values3 = block_keys(key_start)
            probs_f32 = jnp.exp(logits_of(key_start, keys3) - log_total[..., None])
            grad_probs = jnp.einsum(
                "qhd,khd->hqk", grad_att3, values3, preferred_element_type=jnp.float32
            )
            grad_logits = probs_f32 * (grad_probs - row_delta[..., None])
            penalty_grad = lax.dynamic_update_slice_in_dim(
                penalty_grad, -jnp.sum(grad_logits, axis=0), key_start, 1
            )
            first_grad = lax.dynamic_update_slice_in_dim(first_grad, grad_logits[0], key_start, 1)
            grad_scores = (grad_logits * later_heads).astype(jnp.bfloat16)
            grad_query = (
                grad_query
                + jnp.einsum("hqk,khd->qhd", grad_scores, keys3, preferred_element_type=jnp.float32)
                * score_scale
            )
            key_part = (
                jnp.einsum(
                    "hqk,qhd->khd", grad_scores, queries3, preferred_element_type=jnp.float32
                )
                * score_scale
            )
            value_part = jnp.einsum(
                "hqk,qhd->khd",
                probs_f32.astype(jnp.bfloat16),
                grad_att3,
                preferred_element_type=jnp.float32,
            )
            grad_key_all = lax.dynamic_update_slice_in_dim(
                grad_key_all, key_part.reshape(key_block, model_width), key_start, 0
            )
            grad_value_all = lax.dynamic_update_slice_in_dim(
                grad_value_all, value_part.reshape(key_block, model_width), key_start, 0
            )
            return (grad_query, grad_key_all, grad_value_all, penalty_grad, first_grad)

        grad_query, grad_key_all, grad_value_all, penalty_grad, first_grad = lax.fori_loop(
            0,
            block_total,
            grad_block,
            (
                jnp.zeros((query_rows, head_count, HD), jnp.float32),
                jnp.zeros((row_length, model_width), jnp.float32),
                jnp.zeros((row_length, model_width), jnp.float32),
                jnp.zeros((query_rows, row_length), jnp.float32),
                jnp.zeros((query_rows, row_length), jnp.float32),
            ),
        )
        column_sums = jnp.sum(penalty_grad, axis=0)
        after = prefix_2(column_sums, "ctx", add_up, zeros_row, True)
        reach_sums = after + column_sums

        def head_block(block_index, running):
            grad_query_zero, grad_key_all = running
            key_start = block_index * key_block
            _, chosen = masks(key_start)
            key_zero, first_scores = head_scores(key_start)
            flow_block = lax.dynamic_slice_in_dim(penalty_grad, key_start, key_block, 1)
            reach_block = lax.dynamic_slice_in_dim(reach_sums, key_start, key_block, 0)
            grad_picked = reach_block[None, :] - jnp.cumsum(flow_block, axis=0)
            grad_select = grad_picked * strength * jax.nn.sigmoid(first_scores) * chosen
            grad_head = (
                lax.dynamic_slice_in_dim(first_grad, key_start, key_block, 1) + grad_select
            ).astype(jnp.bfloat16)
            grad_query_zero = grad_query_zero + matmul(grad_head, key_zero) * score_scale
            key_zero_grad = contract_rows(grad_head, query_zero) * score_scale
            grad_key_all = lax.dynamic_update_slice(
                grad_key_all, key_zero_grad, (key_start, jnp.zeros((), jnp.int32))
            )
            return (grad_query_zero, grad_key_all)

        grad_query_zero, grad_key_all = lax.fori_loop(
            0, block_total, head_block, (jnp.zeros((query_rows, HD), jnp.float32), grad_key_all)
        )
        grad_query = grad_query.at[:, 0, :].add(grad_query_zero).reshape(query_rows, model_width)
        grad_key_own, grad_value_own = (
            lax.psum_scatter(grad_key_all, "ctx", scatter_dimension=0, tiled=True),
            lax.psum_scatter(grad_value_all, "ctx", scatter_dimension=0, tiled=True),
        )
        grad_project = jnp.concatenate([grad_query, grad_key_own, grad_value_own], axis=1).astype(
            jnp.bfloat16
        )
        grad_qkv = contract_rows(normed_one, grad_project)
        grad_normed_one = contract_cols(grad_project, w_qkv_all)
        _, norm_one_back = jax.vjp(layer_norm, inputs, ln1_gain, ln1_bias)
        grad_in_part, grad_gain_one, grad_bias_one = norm_one_back(grad_normed_one)
        input_grads.append((grad_mid + grad_in_part).astype(jnp.bfloat16))
        matrix_grads = (grad_qkv, grad_outproj, grad_up, grad_down)
        vector_grads = (grad_gain_one, grad_bias_one, grad_gain_two, grad_bias_two, grad_bias_up)
        matrix_grads = (
            lax.psum_scatter(matrix_grads[0], "ctx", scatter_dimension=1, tiled=True),
            lax.psum_scatter(matrix_grads[1], "ctx", scatter_dimension=1, tiled=True),
            lax.psum_scatter(matrix_grads[2], "ctx", scatter_dimension=1, tiled=True),
            lax.psum_scatter(matrix_grads[3], "ctx", scatter_dimension=1, tiled=True),
        )
        matrix_grads = (
            lax.psum_scatter(
                matrix_grads[0].astype(jnp.bfloat16), "dp", scatter_dimension=0, tiled=True
            ).astype(jnp.float32),
            lax.psum_scatter(
                matrix_grads[1].astype(jnp.bfloat16), "dp", scatter_dimension=0, tiled=True
            ).astype(jnp.float32),
            lax.psum_scatter(
                matrix_grads[2].astype(jnp.bfloat16), "dp", scatter_dimension=0, tiled=True
            ).astype(jnp.float32),
            lax.psum_scatter(
                matrix_grads[3].astype(jnp.bfloat16), "dp", scatter_dimension=0, tiled=True
            ).astype(jnp.float32),
        )
        vector_grads = lax.psum(
            (vector_grads[0], vector_grads[1], vector_grads[2], vector_grads[3], vector_grads[4]),
            ("dp", "ctx"),
        )
        if matrix_total is None:
            matrix_total = matrix_grads
            vector_total = vector_grads
        else:
            matrix_total = tuple((old + new for old, new in zip(matrix_total, matrix_grads)))
            vector_total = tuple((old + new for old, new in zip(vector_total, vector_grads)))
    layer_out = jnp.stack(output_list)[:, None]
    input_out = jnp.stack(input_grads)[:, None]
    return (
        layer_out,
        input_out,
        vector_total[0],
        vector_total[1],
        matrix_total[0],
        matrix_total[1],
        vector_total[2],
        vector_total[3],
        matrix_total[2],
        vector_total[4],
        matrix_total[3],
    )


MESH = pl.DeviceIdType.MESH
EXCLUDED = 1e30
QUERY_BLOCK = 256


def norm_parts(value):
    row_mean = jnp.mean(value, axis=-1, keepdims=True)
    centered = value - row_mean
    spread = jnp.mean(centered * centered, axis=-1, keepdims=True)
    inverse = lax.rsqrt(spread + NORM_EPSILON)
    return centered * inverse, inverse


def norm_back(xhat, inverse, grad, gain):
    scaled = grad * gain
    return (
        scaled
        - jnp.mean(scaled, axis=-1, keepdims=True)
        - xhat * jnp.mean(scaled * xhat, axis=-1, keepdims=True)
    ) * inverse


class Wires:
    def __init__(self, send_sem, recv_sem):
        self.send_sem, self.recv_sem, self.used, self.made = send_sem, recv_sem, 0, []

    def send(self, source, target, where):
        copy = pltpu.make_async_remote_copy(
            src_ref=source,
            dst_ref=target,
            send_sem=self.send_sem.at[self.used],
            recv_sem=self.recv_sem.at[self.used],
            device_id=where,
            device_id_type=MESH,
        )
        copy.start()
        self.used += 1
        self.made.append(copy)
        return copy

    def drain(self):
        for copy in self.made:
            copy.wait_send()


def rounded(value):
    return value.astype(jnp.bfloat16)


def swap(index):
    return index + 1 - 2 * lax.rem(index, 2)


LOADED = (
    "x", "w_qkv", "gain_one", "bias_one", "cot", "w_out_own", "w_up_own", "gain_two", "bias_two", "w_down", "b_up",
)


def layer_body(plan, names, *refs):
    r = SimpleNamespace(**dict(zip(names, refs)))
    groups, shards = plan
    f32 = jnp.float32
    ctx, dp = lax.axis_index("ctx"), lax.axis_index("dp")
    ctx_size, tokens, model = r.x_row.shape
    width = r.out.shape[1]
    lines = ctx_size // 2
    mbs = ctx_size // groups
    hpg = width // HD
    own = r.x.shape[0]
    ff = r.w_down.shape[0]
    row_length = tokens * ctx_size
    side, line = lax.rem(ctx, 2), ctx // 2
    my_mb, my_group = ctx // groups, lax.rem(ctx, groups)
    wires = Wires(r.send_sem, r.recv_sem)
    core, far, far_core = {"dp": swap(dp)}, {"dp": lax.rem(dp + 2, 4)}, {"dp": lax.rem(swap(dp) + 2, 4)}
    beside = {"ctx": swap(ctx)}
    up_to = {"dp": lax.rem(ctx, 4), "ctx": shards * dp + ctx // 4}
    up_from = {"dp": ctx // shards, "ctx": lax.rem(ctx, shards) * 4 + dp}
    around = [{"ctx": lax.rem(ctx + step, ctx_size)} for step in range(1, ctx_size)]

    mirror = {"ctx": lax.rem(line + lines // 2, lines) * 2 + side}
    ahead = {"ctx": swap(line) * 2 + side}
    beside_at, mirror_at, ahead_at = beside["ctx"], mirror["ctx"], ahead["ctx"]
    half = tokens // 2

    loads = {}
    for at, name in enumerate(LOADED):
        loads[name] = pltpu.make_async_copy(
            getattr(r, name + "_hbm"), getattr(r, name), r.load_sem.at[at]
        )
        loads[name].start()
    barrier = pltpu.get_barrier_semaphore()
    for where in around + [core, far, far_core, up_from]:
        pl.semaphore_signal(barrier, inc=1, device_id=where, device_id_type=MESH)
    loads["x"].wait()
    loads["w_qkv"].wait()
    pl.semaphore_wait(barrier, ctx_size + 3)

    def x_of(micro):
        return r.x.at[pl.ds(pl.multiple_of(micro * tokens, tokens), tokens)]

    x_mirror = wires.send(x_of(1 - my_mb), r.x_row.at[ctx], mirror)
    x_beside = wires.send(x_of(my_mb), r.x_row.at[ctx], beside)
    x_ahead = wires.send(x_of(my_mb), r.x_row.at[ctx], ahead)
    for group in range(groups):

        @pl.when(my_group == group)
        def _():
            for kind in range(3):
                first = kind * model + group * width
                r.w_pick[dp, :, kind * width : (kind + 1) * width] = r.w_qkv[:, first : first + width]

    for kind in range(2):
        r.w_pick[dp, :, 3 * width + kind * HD : 3 * width + (kind + 1) * HD] = r.w_qkv[
            :, kind * model : kind * model + HD
        ]
    pick_far = wires.send(r.w_pick.at[dp], r.w_pick.at[dp], far)
    pick_core = wires.send(r.w_pick.at[dp], r.w_pick.at[dp], core)
    r.x_row[ctx] = x_of(my_mb)[...]

    loads["gain_one"].wait()
    loads["bias_one"].wait()
    gain_one = r.gain_one[...].reshape(1, model)
    bias_one = r.bias_one[...].reshape(1, model)

    def normalise(place):
        xhat, _ = norm_parts(r.x_row[place].astype(f32))
        rows = pl.ds(pl.multiple_of(place * tokens, tokens), tokens)
        r.hat_one[rows, :] = rounded(xhat)
        r.normed_one[rows, :] = rounded(xhat * gain_one + bias_one)

    x_beside.wait_recv()
    top, bottom = pl.ds(0, half), pl.ds(half, half)
    x_fwd_a = wires.send(r.x_row.at[beside_at, top], r.x_row.at[beside_at, top], ahead)
    x_ahead.wait_recv()
    x_fwd_b = wires.send(r.x_row.at[ahead_at, bottom], r.x_row.at[ahead_at, bottom], beside)
    normalise(ctx)
    x_mirror.wait_recv()
    x_mirror_beside = wires.send(r.x_row.at[mirror_at], r.x_row.at[mirror_at], beside)
    x_mirror_ahead = wires.send(r.x_row.at[mirror_at], r.x_row.at[mirror_at], ahead)
    pick_far.wait_recv()
    pick_at = far["dp"]
    pick_fwd = wires.send(r.w_pick.at[pick_at], r.w_pick.at[pick_at], core)

    for name in ("cot", "w_out_own", "w_up_own"):
        loads[name].wait()

    def rows_of(place):
        return pl.ds(pl.multiple_of(place * size_dp, size_dp), size_dp)

    size_dp = model // 4
    out_far = wires.send(r.w_out_own, r.w_out.at[rows_of(dp)], far)
    out_core = wires.send(r.w_out_own, r.w_out.at[rows_of(dp)], core)

    def up_part(peer):
        return r.w_up_own.at[:, pl.ds(pl.multiple_of(peer * ff, 128), ff)]

    up_in = [
        wires.send(up_part(where["dp"]), r.w_up.at[rows_of(dp)], where)
        for where in (far, far_core, core)
    ]
    cot_far = wires.send(r.cot, r.cots.at[2], far)
    cot_core = wires.send(r.cot, r.cots.at[1], core)
    r.w_out[rows_of(dp), :] = r.w_out_own[...]
    r.w_up[rows_of(dp), :] = up_part(dp)[...]
    r.cots[0] = r.cot[...]

    normalise(beside_at)
    normalise(ahead_at)
    normalise(mirror_at)
    x_mirror_beside.wait_recv()
    place = swap(mirror_at)
    x_fwd_c = wires.send(r.x_row.at[place, top], r.x_row.at[place, top], ahead)
    x_mirror_ahead.wait_recv()
    place = lax.rem(ahead_at + ctx_size // 2, ctx_size)
    x_fwd_d = wires.send(r.x_row.at[place, bottom], r.x_row.at[place, bottom], beside)
    normalise(swap(mirror_at))
    normalise(place)
    x_fwd_a.wait_recv()
    x_fwd_b.wait_recv()
    normalise(swap(ahead_at))
    pick_core.wait_recv()
    pick_fwd.wait_recv()
    x_fwd_c.wait_recv()
    x_fwd_d.wait_recv()
    normalise(swap(place))
    w_pick = r.w_pick[...].reshape(model, 3 * width + 2 * HD)
    r.proj[...] = rounded(matmul(r.normed_one[...], w_pick))

    def att_copy(place):
        return pltpu.make_async_remote_copy(
            src_ref=r.att.at[place],
            dst_ref=r.att_got.at[ctx],
            send_sem=r.att_send.at[place],
            recv_sem=r.att_recv.at[ctx],
            device_id={"ctx": place},
            device_id_type=MESH,
        )

    block = QUERY_BLOCK
    per_block = block // tokens
    scale = HD ** (-0.5)
    strength = 8.0 / row_length
    row_at = lax.broadcasted_iota(jnp.int32, (block, block), 0)
    col_at = lax.broadcasted_iota(jnp.int32, (block, block), 1)
    earlier = (col_at < row_at).astype(jnp.bfloat16)
    later = (col_at > row_at).astype(jnp.bfloat16)
    doc_ends, doc_end = [], 0
    for at in range(r.lengths.shape[2]):
        doc_end = doc_end + r.lengths[my_mb, 0, at]
        doc_ends.append(doc_end)

    def segment_of(places):
        total = jnp.zeros(places.shape, jnp.int32)
        for end in doc_ends:
            total += jnp.where(places >= end, 1, 0)
        return total

    r.suffix[...] = jnp.zeros_like(r.suffix)
    for start in range(0, row_length, block):
        reach = start + block
        rows = pl.ds(start, block)
        probs_ref, slope_ref = getattr(r, f"probs_{start}"), getattr(r, f"slope_{start}")
        row_pos = start + lax.broadcasted_iota(jnp.int32, (block, 1), 0)
        col_pos = lax.broadcasted_iota(jnp.int32, (1, reach), 1)
        row_seg, col_seg = segment_of(row_pos), segment_of(col_pos)
        opening = (col_seg != segment_of(col_pos - 1)) | (col_pos == 0)
        pick_seg = jnp.where(opening, -1, col_seg)
        query = rounded(r.proj[rows, 3 * width : 3 * width + HD] * scale)
        key = r.proj[:reach, 3 * width + HD : 3 * width + 2 * HD]
        scores = contract_cols(query, key)
        small = jnp.exp(-jnp.abs(scores))
        soft = jnp.maximum(scores, 0.0) + jnp.log(1.0 + small)
        recip = 1.0 / (1.0 + small)
        sigmoid = jnp.where(scores >= 0.0, recip, small * recip)
        chosen = (row_seg == pick_seg) & (col_pos < row_pos)
        picked = jnp.where(chosen, strength * soft, 0.0)
        slope_ref[...] = rounded(jnp.where(chosen, strength * sigmoid, 0.0))
        high = rounded(picked)
        low = rounded(picked - high.astype(f32))
        penalty = r.suffix[:, :reach] + (matmul(earlier, high) + matmul(earlier, low))
        allowed = (row_seg == col_seg) & (col_pos <= row_pos)
        penalty = jnp.where(allowed, penalty, EXCLUDED)
        r.suffix[:, :reach] += jnp.sum(picked, axis=0, keepdims=True)
        for head in range(hpg):
            at = head * HD
            query = rounded(r.proj[rows, at : at + HD] * scale)
            key = r.proj[:reach, width + at : width + at + HD]
            value = r.proj[:reach, 2 * width + at : 2 * width + at + HD]
            logits = contract_cols(query, key) - penalty
            top_logit = jnp.max(logits, axis=1, keepdims=True)
            probs = jnp.exp(logits - top_logit)
            inverse = 1.0 / jnp.sum(probs, axis=1, keepdims=True)
            probs = rounded(probs)
            probs_ref[head] = probs
            result = matmul(probs, value) * inverse
            r.out[rows, at : at + HD] = result
            r.inverse[rows, head : head + 1] = inverse
            result = rounded(result)
            for step in range(per_block):
                r.att[start // tokens + step, :, at : at + HD] = result[
                    step * tokens : (step + 1) * tokens
                ]
        for step in range(per_block):
            place = start // tokens + step
            copy = att_copy(place)

            @pl.when(ctx != place)
            def _():
                copy.start()

    r.att_got[ctx] = r.att[ctx]
    cot_far.wait_recv()
    cot_fwd = wires.send(r.cots.at[2], r.cots.at[3], core)
    out_far.wait_recv()
    out_at = rows_of(far["dp"])
    out_fwd = wires.send(r.w_out.at[out_at], r.w_out.at[out_at], core)
    for copy in up_in:
        copy.wait_recv()
    out_core.wait_recv()
    out_fwd.wait_recv()
    for name in ("gain_two", "bias_two", "w_down", "b_up"):
        loads[name].wait()
    for step in range(1, ctx_size):
        place = lax.rem(ctx + step, ctx_size)
        pltpu.make_async_copy(r.att.at[0], r.att_got.at[place], r.att_recv.at[place]).wait()

    gain = r.gain_two[...].reshape(1, model)
    bias = r.bias_two[...].reshape(1, model)
    b_own = r.b_up[...].reshape(1, ff)
    for micro in range(mbs):
        rows = pl.ds(micro * tokens, tokens)
        stream = r.x[rows, :].astype(f32)
        for group in range(groups):
            stream += matmul(
                r.att_got[micro * groups + group], r.w_out[pl.ds(group * width, width), :]
            )
        r.mid[rows, :] = stream
    xhat, inverse_two = norm_parts(r.mid[...])
    r.hat_two[...] = xhat
    r.normed[0] = rounded(xhat * gain + bias)
    to_core = wires.send(r.normed.at[0], r.normed.at[1], core)
    to_far = wires.send(r.normed.at[0], r.normed.at[2], far)

    def feed(slot):
        hidden = matmul(r.normed[slot], r.w_up[...]) + b_own
        cdf = 0.5 * (1.0 + lax.erf(hidden * (2.0**-0.5)))
        density = jnp.exp(-0.5 * hidden * hidden) * ((2.0 * math.pi) ** -0.5)
        r.act[slot] = rounded(hidden * cdf)
        grad = contract_cols(r.cots[slot], r.w_down[...])
        r.grad_hid[slot] = rounded(grad * (cdf + hidden * density))
        r.part[slot] = rounded(contract_cols(r.grad_hid[slot], r.w_up[...]))

    def feed_out(slot):
        r.out_part[slot] = rounded(matmul(r.act[slot], r.w_down[...]))

    feed(0)
    cot_core.wait_recv()
    to_core.wait_recv()
    feed(1)
    part_core = wires.send(r.part.at[1], r.part_got.at[0], core)
    to_far.wait_recv()
    forward = wires.send(r.normed.at[2], r.normed.at[3], core)
    feed(2)
    forward.wait_recv()
    cot_fwd.wait_recv()
    feed(3)
    part_far_core = wires.send(r.part.at[3], r.part_got.at[1], core)
    feed_out(3)
    out_far_core = wires.send(r.out_part.at[3], r.out_got.at[1], core)
    part_far_core.wait_recv()
    r.part[2] = rounded(r.part[2].astype(f32) + r.part_got[1].astype(f32))
    part_far = wires.send(r.part.at[2], r.part_got.at[2], far)
    feed_out(1)
    out_core = wires.send(r.out_part.at[1], r.out_got.at[0], core)
    feed_out(2)
    out_far_core.wait_recv()
    r.out_part[2] = rounded(r.out_part[2].astype(f32) + r.out_got[1].astype(f32))
    out_far = wires.send(r.out_part.at[2], r.out_got.at[2], far)

    flat_cot = r.cots[...].reshape(4 * own, model)
    flat_act = r.act[...].reshape(4 * own, ff)
    grads = rounded(contract_rows(flat_cot, flat_act))
    size = model // ctx_size
    for at in range(ctx_size):
        r.down_grad[at % 2, at // 2] = grads[at * size : (at + 1) * size]
    down_side = wires.send(r.down_grad.at[1 - side], r.down_side, beside)
    flat_normed = r.normed[...].reshape(4 * own, model)
    flat_grad = r.grad_hid[...].reshape(4 * own, ff)
    size = model // 4
    for at in range(shards):
        grads = rounded(
            contract_rows(flat_normed, flat_grad[:, at * ff // shards : (at + 1) * ff // shards])
        )
        for row in range(4):
            index = at * 4 + row
            r.up_grad[index % 2, index // 2] = grads[row * size : (row + 1) * size]
    up_side = wires.send(r.up_grad.at[1 - side], r.up_side, beside)
    feed_out(0)
    vec_rows = 4 + ff // model
    d_bias_up = jnp.sum(flat_grad.astype(f32), axis=0, keepdims=True)
    for at in range(ff // model):
        r.vec[4 + at : 5 + at, :] = d_bias_up[:, at * model : (at + 1) * model]

    part_core.wait_recv()
    part_far.wait_recv()
    grad_normed = r.part[0].astype(f32) + r.part_got[0].astype(f32) + r.part_got[2].astype(f32)
    xhat = r.hat_two[...]
    r.vec[2:3, :] = jnp.sum(grad_normed * xhat, axis=0, keepdims=True)
    r.vec[3:4, :] = jnp.sum(grad_normed, axis=0, keepdims=True)
    r.grad_mid[...] = r.cot[...].astype(f32) + norm_back(xhat, inverse_two, grad_normed, gain)
    branch = rounded(r.grad_mid[...])
    for group in range(groups):
        grad = rounded(contract_cols(branch, r.w_out[pl.ds(group * width, width), :]))
        for micro in range(mbs):
            r.att_out[micro * groups + group] = grad[micro * tokens : (micro + 1) * tokens]
    att_in = []
    for step in range(1, ctx_size):
        peer = lax.rem(ctx + step, ctx_size)
        att_in.append(wires.send(r.att_out.at[peer], r.grad_att.at[ctx], {"ctx": peer}))
    r.grad_att[ctx] = r.att_out[ctx]
    for group in range(groups):
        total = None
        for micro in range(mbs):
            some = contract_rows(
                branch[micro * tokens : (micro + 1) * tokens], r.att_got[micro * groups + group]
            )
            total = some if total is None else total + some
        r.out_grad[group] = rounded(total)
    out_grad_core = wires.send(r.out_grad.at[swap(dp)], r.out_grad_got.at[0], core)
    out_grad_far_core = wires.send(
        r.out_grad.at[lax.rem(swap(dp) + 2, 4)], r.out_grad_got.at[1], core
    )
    out_core.wait_recv()
    out_far.wait_recv()
    r.layer[...] = rounded(
        r.mid[...]
        + (r.out_part[0].astype(f32) + r.out_got[0].astype(f32) + r.out_got[2].astype(f32))
    )
    out_grad_far_core.wait_recv()
    mine = lax.rem(dp + 2, 4)
    r.out_grad[mine] = rounded(r.out_grad[mine].astype(f32) + r.out_grad_got[1].astype(f32))
    out_grad_far = wires.send(r.out_grad.at[mine], r.out_grad_got.at[2], far)
    for copy in att_in:
        copy.wait_recv()

    def spread(side_copy, grad, side_got, line_got):
        side_copy.wait_recv()
        for step in range(lines):
            place = lax.rem(line + step, lines)
            grad[side, place] = rounded(grad[side, place].astype(f32) + side_got[place].astype(f32))
        return [
            wires.send(
                grad.at[side, lax.rem(line + step, lines)],
                line_got.at[line],
                {"ctx": lax.rem(line + step, lines) * 2 + side},
            )
            for step in range(1, lines)
        ]

    def gather_up(copies, grad, line_got):
        line_got[line] = grad[side, line]
        for copy in copies:
            copy.wait_recv()
        total = line_got[0].astype(f32)
        for place in range(1, lines):
            total += line_got[place].astype(f32)
        return total

    r.suffix[...] = jnp.zeros_like(r.suffix)
    r.acc[...] = jnp.zeros_like(r.acc)

    def back_block(start):
        reach = start + block
        rows = pl.ds(start, block)
        probs_ref, slope_ref = getattr(r, f"probs_{start}"), getattr(r, f"slope_{start}")
        total = None
        first = start // tokens
        grad_block = r.grad_att[first : first + per_block].reshape(block, width)
        for head in range(hpg):
            at = head * HD
            query_t = rounded((r.proj[rows, at : at + HD].astype(f32) * scale).T)
            key = r.proj[:reach, width + at : width + at + HD]
            value = r.proj[:reach, 2 * width + at : 2 * width + at + HD]
            grad = grad_block[:, at : at + HD].astype(f32) * r.inverse[rows, head : head + 1]
            delta = jnp.sum(grad * r.out[rows, at : at + HD], axis=1, keepdims=True)
            probs = probs_ref[head]
            grad_probs = contract_cols(rounded(grad), value)
            grad_logits = probs.astype(f32) * (grad_probs - delta)
            total = grad_logits if total is None else total + grad_logits
            grad_scores = rounded(grad_logits)
            r.grad_proj[rows, at : at + HD] = rounded(matmul(grad_scores, key) * scale)
            r.acc[at : at + HD, :reach] += matmul(query_t, grad_scores)
            r.acc[width + at : width + at + HD, :reach] += matmul(rounded(grad.T), probs)
        query_t = rounded((r.proj[rows, 3 * width : 3 * width + HD].astype(f32) * scale).T)
        key = r.proj[:reach, 3 * width + HD : 3 * width + 2 * HD]
        flow = r.suffix[:, :reach] + matmul(later, rounded(total))
        grad_scores = rounded(-flow * slope_ref[...].astype(f32))
        r.grad_proj[rows, 3 * width : 3 * width + HD] = rounded(matmul(grad_scores, key) * scale)
        r.acc[2 * width : 2 * width + HD, :reach] += matmul(query_t, grad_scores)
        r.suffix[:, :reach] += jnp.sum(total, axis=0, keepdims=True)

    def one_grad(place):
        rows = pl.ds(pl.multiple_of(place * tokens, tokens), tokens)
        grad = contract_cols(r.grad_proj[rows, :], w_pick)
        r.vec[0:1, :] += jnp.sum(grad * r.hat_one[rows, :].astype(f32), axis=0, keepdims=True)
        r.vec[1:2, :] += jnp.sum(grad, axis=0, keepdims=True)
        return grad

    r.vec[0:2, :] = jnp.zeros((2, model), f32)
    one_side = {}

    def line_copy(at):
        return pltpu.make_async_remote_copy(
            src_ref=r.one_ready.at[at],
            dst_ref=r.one_line.at[line],
            send_sem=r.one_send.at[at],
            recv_sem=r.one_recv.at[line],
            device_id={"ctx": at * 2 + side},
            device_id_type=MESH,
        )

    def finish_block(at):
        start = at * block
        reach = start + block
        r.grad_proj[start:reach, width : 3 * width] = rounded(r.acc[: 2 * width, start:reach].T)
        r.grad_proj[start:reach, 3 * width + HD :] = rounded(r.acc[2 * width :, start:reach].T)
        r.one_piece[at] = rounded(one_grad(at * 2 + 1 - side))
        one_side[at] = wires.send(r.one_piece.at[at], r.one_side.at[at], beside)
        r.one_own[at] = one_grad(at * 2 + side)

    def pass_on(at):
        one_side[at].wait_recv()
        r.one_ready[at] = rounded(r.one_own[at] + r.one_side[at].astype(f32))
        copy = line_copy(at)

        @pl.when(line != at)
        def _():
            copy.start()

        @pl.when(line == at)
        def _():
            r.one_line[at] = r.one_ready[at]

    last = lines - 1
    back_block(last * block)
    finish_block(last)
    down_line = spread(down_side, r.down_grad, r.down_side, r.down_line)
    for at in reversed(range(last)):
        back_block(at * block)
        finish_block(at)
        pass_on(at + 1)
        if at == 1:
            up_line = spread(up_side, r.up_grad, r.up_side, r.up_line)
        if at == last - 1:
            out_grad_core.wait_recv()
            out_grad_far.wait_recv()
            grads = rounded(
                r.out_grad[dp].astype(f32)
                + r.out_grad_got[0].astype(f32)
                + r.out_grad_got[2].astype(f32)
            )
            size = model // ctx_size
            for row in range(ctx_size):
                r.out_piece[row % 2, row // 2] = grads[row * size : (row + 1) * size]
            out_side = wires.send(r.out_piece.at[1 - side], r.out_side, beside)
    r.grad_kv[...] = rounded(r.acc[...])
    vec_in = []
    for step in range(1, ctx_size):
        peer = lax.rem(ctx + step, ctx_size)
        vec_in.append(wires.send(r.vec, r.vec_got.at[ctx], {"ctx": peer}))
    r.vec_got[ctx] = r.vec[...]

    size = model // 4
    grads_q = rounded(
        contract_rows(
            jnp.concatenate(
                [r.grad_proj[:, :width], r.grad_proj[:, 3 * width : 3 * width + HD]], axis=1
            ),
            r.normed_one[...],
        )
    )
    for at in range(4):
        cols = slice(at * size, (at + 1) * size)
        r.qkv_grad[at, :width, :] = grads_q[:width, cols]
        r.qkv_grad[at, 3 * width : 3 * width + HD, :] = grads_q[width:, cols]
    grads_kv = rounded(matmul(r.grad_kv[...], r.normed_one[...]))
    for at in range(4):
        cols = slice(at * size, (at + 1) * size)
        r.qkv_grad[at, width : 3 * width, :] = grads_kv[: 2 * width, cols]
        r.qkv_grad[at, 3 * width + HD :, :] = grads_kv[2 * width :, cols]
    qkv_far_core = wires.send(r.qkv_grad.at[lax.rem(swap(dp) + 2, 4)], r.qkv_got.at[1], core)
    qkv_core = wires.send(r.qkv_grad.at[swap(dp)], r.qkv_got.at[0], core)
    pass_on(0)

    r.d_down[...] = gather_up(down_line, r.down_grad, r.down_line)
    r.up_sum[...] = rounded(gather_up(up_line, r.up_grad, r.up_line))
    stays = (lax.rem(ctx, 4) == dp) & (shards * dp + ctx // 4 == ctx)
    up_copy = pltpu.make_async_remote_copy(
        src_ref=r.up_sum,
        dst_ref=r.up_final,
        send_sem=r.up_send.at[0],
        recv_sem=r.up_recv.at[0],
        device_id=up_to,
        device_id_type=MESH,
    )

    @pl.when(jnp.logical_not(stays))
    def _():
        up_copy.start()

    @pl.when(stays)
    def _():
        r.up_final[...] = r.up_sum[...]

    qkv_far_core.wait_recv()
    r.qkv_grad[mine] = rounded(r.qkv_grad[mine].astype(f32) + r.qkv_got[1].astype(f32))
    qkv_far = wires.send(r.qkv_grad.at[mine], r.qkv_got.at[2], far)
    out_line = spread(out_side, r.out_piece, r.out_side, r.out_line)
    for copy in vec_in:
        copy.wait_recv()
    total = r.vec_got[0]
    for at in range(1, ctx_size):
        total += r.vec_got[at]
    r.vec_sum[...] = total
    vec_out = [
        wires.send(r.vec_sum, r.vecs.at[dp], where) for where in (core, far, far_core)
    ]
    r.vecs[dp] = total
    qkv_core.wait_recv()
    qkv_far.wait_recv()
    r.qkv_sum[...] = rounded(
        r.qkv_grad[dp].astype(f32) + r.qkv_got[0].astype(f32) + r.qkv_got[2].astype(f32)
    )
    part = r.deal_got.shape[2]
    per = width // part
    slots = r.deal_got.shape[0]

    def outgoing(kind, half):
        section = (kind * groups + my_group) * per + half
        target, slot = section // slots, lax.rem(section, slots)
        index = kind * per + half
        return target, slot, index, pltpu.make_async_remote_copy(
            src_ref=r.qkv_sum.at[pl.ds(index * part, part)],
            dst_ref=r.deal_got.at[slot, my_mb],
            send_sem=r.deal_send.at[index],
            recv_sem=r.deal_recv.at[slot, my_mb],
            device_id={"ctx": target},
            device_id_type=MESH,
        )

    def extra_copy(kind):
        return pltpu.make_async_remote_copy(
            src_ref=r.qkv_sum.at[pl.ds(3 * width + kind * HD, HD)],
            dst_ref=r.extra_got.at[ctx],
            send_sem=r.extra_send.at[kind],
            recv_sem=r.extra_recv.at[ctx],
            device_id={"ctx": kind * groups * per // slots},
            device_id_type=MESH,
        )

    for kind in range(3):
        for half in range(per):
            target, slot, index, copy = outgoing(kind, half)

            @pl.when(target != ctx)
            def _():
                copy.start()

            @pl.when(target == ctx)
            def _():
                r.deal_got[slot, my_mb] = r.qkv_sum[index * part : (index + 1) * part, :]

    for kind in range(2):
        target = kind * groups * per // slots
        copy = extra_copy(kind)

        @pl.when(ctx != target)
        def _():
            copy.start()

        @pl.when(ctx == target)
        def _():
            r.extra_got[ctx] = r.qkv_sum[3 * width + kind * HD : 3 * width + (kind + 1) * HD, :]

    xhat, inverse_one = norm_parts(r.x[...].astype(f32))
    for step in range(1, lines):
        place = lax.rem(line + step, lines)
        pltpu.make_async_copy(
            r.one_ready.at[0], r.one_line.at[place], r.one_recv.at[place]
        ).wait()
    half_lines = lines // mbs
    for micro in range(mbs):
        grad = r.one_line[micro * half_lines].astype(f32)
        for at in range(1, half_lines):
            grad += r.one_line[micro * half_lines + at].astype(f32)
        rows = slice(micro * tokens, (micro + 1) * tokens)
        r.d_x[rows, :] = rounded(
            r.grad_mid[rows, :] + norm_back(xhat[rows], inverse_one[rows], grad, gain_one)
        )
    r.d_out[...] = gather_up(out_line, r.out_piece, r.out_line).T

    @pl.when(jnp.logical_not(stays))
    def _():
        up_copy.wait_send()
        up_copy.wait_recv()

    r.d_up[...] = r.up_final[...].astype(f32)

    for kind in range(3):
        for half in range(per):
            target, slot, index, copy = outgoing(kind, half)

            @pl.when(target != ctx)
            def _():
                copy.wait_send()

    for slot in range(slots):
        section = ctx * slots + slot
        source_group = lax.rem(section // per, groups)
        for place in range(mbs):

            @pl.when(place * groups + source_group != ctx)
            def _():
                pltpu.make_async_copy(
                    r.qkv_sum.at[pl.ds(0, part)],
                    r.deal_got.at[slot, place],
                    r.deal_recv.at[slot, place],
                ).wait()

        total = r.deal_got[slot, 0].astype(f32)
        for place in range(1, mbs):
            total += r.deal_got[slot, place].astype(f32)
        r.deal_sum[slot * part : (slot + 1) * part, :] = total
    for kind in range(2):
        section = kind * groups * per
        target, slot = section // slots, section % slots
        copy = extra_copy(kind)

        @pl.when(ctx != target)
        def _():
            copy.wait_send()

        @pl.when(ctx == target)
        def _():
            total = jnp.zeros((HD, size), f32)
            for place in range(ctx_size):
                if place != target:
                    pltpu.make_async_copy(
                        r.qkv_sum.at[pl.ds(0, HD)], r.extra_got.at[place], r.extra_recv.at[place]
                    ).wait()
                total += r.extra_got[place].astype(f32)
            r.deal_sum[slot * part : slot * part + HD, :] += total

    r.d_qkv[...] = r.deal_sum[...].T
    for copy in vec_out:
        copy.wait_recv()
    for row in range(4):
        r.d_vec[row : row + 1, :] = (
            r.vecs[0, row : row + 1, :] + r.vecs[1, row : row + 1, :]
        ) + (r.vecs[2, row : row + 1, :] + r.vecs[3, row : row + 1, :])
    for at in range(4):
        r.d_bias[at] = r.vecs[at, 4:vec_rows, :]
    wires.drain()
    for place in range(ctx_size):
        copy = att_copy(place)

        @pl.when(ctx != place)
        def _():
            copy.wait_send()

    for at in range(lines):
        copy = line_copy(at)

        @pl.when(line != at)
        def _():
            copy.wait_send()


LAYER_COPIES = 72


def layer(collective_id, groups, shards, lengths, large):
    bf16, f32 = jnp.bfloat16, jnp.float32
    own, model = large["x"].shape
    ctx_size = lax.axis_size("ctx")
    tokens = own * groups // ctx_size
    hpg = model // HD // groups
    width = hpg * HD
    row_length = ctx_size * tokens
    lines = ctx_size // 2
    ff = large["w_down"].shape[0]
    size, shard = model // 4, 3 * model // ctx_size
    part = math.gcd(width, shard)
    slots, mbs = shard // part, ctx_size // groups
    picked = 3 * width + 2 * HD
    vec_rows = 4 + ff // model
    narrow = model // ctx_size
    vmem = pl.BlockSpec(memory_space=pltpu.VMEM)
    anywhere = pl.BlockSpec(memory_space=pl.ANY)
    outs = {
        "layer": ((own, model), bf16),
        "d_x": ((own, model), bf16),
        "d_vec": ((4, model), f32),
        "d_bias": ((4, ff // model, model), f32),
        "d_qkv": ((size, shard), f32),
        "d_out": ((size, narrow), f32),
        "d_up": ((size, ff // shards), f32),
        "d_down": ((narrow, ff), f32),
    }
    scratch = {name: (array.shape, array.dtype) for name, array in large.items()}
    scratch |= {
        "x_row": ((ctx_size, tokens, model), bf16),
        "hat_one": ((row_length, model), bf16),
        "normed_one": ((row_length, model), bf16),
        "w_pick": ((4, size, picked), bf16),
        "proj": ((row_length, picked), bf16),
        "w_out": ((model, model), bf16),
        "w_up": ((model, ff), bf16),
        "out": ((row_length, width), f32),
        "inverse": ((row_length, hpg), f32),
        "att": ((ctx_size, tokens, width), bf16),
        "att_got": ((ctx_size, tokens, width), bf16),
        "cots": ((4, own, model), bf16),
        "mid": ((own, model), f32),
        "hat_two": ((own, model), f32),
        "grad_mid": ((own, model), f32),
        "normed": ((4, own, model), bf16),
        "act": ((4, own, ff), bf16),
        "grad_hid": ((4, own, ff), bf16),
        "part": ((4, own, model), bf16),
        "out_part": ((4, own, model), bf16),
        "part_got": ((3, own, model), bf16),
        "out_got": ((3, own, model), bf16),
        "att_out": ((ctx_size, tokens, width), bf16),
        "grad_att": ((ctx_size, tokens, width), bf16),
        "down_grad": ((2, lines, narrow, ff), bf16),
        "down_side": ((lines, narrow, ff), bf16),
        "down_line": ((lines, narrow, ff), bf16),
        "up_grad": ((2, lines, size, ff // shards), bf16),
        "up_side": ((lines, size, ff // shards), bf16),
        "up_line": ((lines, size, ff // shards), bf16),
        "up_sum": ((size, ff // shards), bf16),
        "up_final": ((size, ff // shards), bf16),
        "out_grad": ((4, model, size), bf16),
        "out_grad_got": ((3, model, size), bf16),
        "out_piece": ((2, lines, narrow, size), bf16),
        "out_side": ((lines, narrow, size), bf16),
        "out_line": ((lines, narrow, size), bf16),
        "suffix": ((1, row_length), f32),
        "acc": ((2 * width + HD, row_length), f32),
        "grad_kv": ((2 * width + HD, row_length), bf16),
        "grad_proj": ((row_length, picked), bf16),
        "one_piece": ((lines, tokens, model), bf16),
        "one_own": ((lines, tokens, model), f32),
        "one_side": ((lines, tokens, model), bf16),
        "one_ready": ((lines, tokens, model), bf16),
        "one_line": ((lines, tokens, model), bf16),
        "qkv_grad": ((4, picked, size), bf16),
        "qkv_got": ((3, picked, size), bf16),
        "qkv_sum": ((picked, size), bf16),
        "deal_got": ((slots, mbs, part, size), bf16),
        "deal_sum": ((shard, size), f32),
        "extra_got": ((ctx_size, HD, size), bf16),
        "vec": ((vec_rows, model), f32),
        "vec_got": ((ctx_size, vec_rows, model), f32),
        "vec_sum": ((vec_rows, model), f32),
        "vecs": ((4, vec_rows, model), f32),
    }
    for start in range(0, row_length, QUERY_BLOCK):
        reach = start + QUERY_BLOCK
        scratch[f"probs_{start}"] = ((hpg, QUERY_BLOCK, reach), bf16)
        scratch[f"slope_{start}"] = ((QUERY_BLOCK, reach), bf16)
    dma = pltpu.SemaphoreType.DMA
    sems = {
        "send_sem": dma((LAYER_COPIES,)),
        "recv_sem": dma((LAYER_COPIES,)),
        "load_sem": dma((len(large),)),
        "att_send": dma((ctx_size,)),
        "att_recv": dma((ctx_size,)),
        "one_send": dma((lines,)),
        "one_recv": dma((lines,)),
        "up_send": dma((1,)),
        "up_recv": dma((1,)),
        "deal_send": dma((3 * (width // part),)),
        "deal_recv": dma((slots, mbs)),
        "extra_send": dma((2,)),
        "extra_recv": dma((ctx_size,)),
    }
    names = (
        ["lengths"]
        + [name + "_hbm" for name in large]
        + list(outs)
        + list(scratch)
        + list(sems)
    )
    return pl.pallas_call(
        partial(layer_body, (groups, shards), names),
        out_shape=[jax.ShapeDtypeStruct(*spec) for spec in outs.values()],
        in_specs=[pl.BlockSpec(memory_space=pltpu.SMEM)] + [anywhere] * len(large),
        out_specs=[vmem] * len(outs),
        scratch_shapes=[pltpu.VMEM(*spec) for spec in scratch.values()] + list(sems.values()),
        compiler_params=pltpu.CompilerParams(
            collective_id=collective_id, has_side_effects=True, vmem_limit_bytes=63 * 1024 * 1024
        ),
        name="layer",
    )(lengths, *large.values())


def per_head_device(
    layer_input,
    doc_lengths,
    ln1_gain,
    ln1_bias,
    w_qkv,
    w_out,
    ln2_gain,
    ln2_bias,
    w_up,
    b_up,
    w_down,
    cotangent,
):
    mbs, _, tokens, model = layer_input.shape
    ctx_size, dp_size = lax.axis_size("ctx"), lax.axis_size("dp")
    ff_own = b_up.shape[0] // dp_size
    large = {
        "x": layer_input.reshape(mbs * tokens, model),
        "w_qkv": w_qkv,
        "gain_one": ln1_gain,
        "bias_one": ln1_bias,
        "cot": cotangent.reshape(mbs * tokens, model),
        "w_out_own": w_out,
        "w_up_own": w_up,
        "gain_two": ln2_gain,
        "bias_two": ln2_bias,
        "w_down": w_down,
        "b_up": lax.dynamic_slice_in_dim(b_up, lax.axis_index("dp") * ff_own, ff_own, 0),
    }
    layer_out, d_x, d_vec, d_bias, d_qkv, d_out, d_up, d_down = layer(
        0, ctx_size // mbs, ctx_size // dp_size, doc_lengths, large
    )
    return (
        layer_out.reshape(mbs, 1, tokens, model),
        d_x.reshape(mbs, 1, tokens, model),
        d_vec[0],
        d_vec[1],
        d_qkv,
        d_out,
        d_vec[2],
        d_vec[3],
        d_up,
        d_bias.reshape(-1),
        d_down.T,
    )


def on_device(*arguments):
    layer_input = arguments[0]
    mbs, model = layer_input.shape[0], layer_input.shape[3]
    heads, ctx_size, dp_size = model // HD, lax.axis_size("ctx"), lax.axis_size("dp")
    groups = ctx_size // mbs
    fits = (
        ctx_size % mbs == 0
        and heads % groups == 0
        and dp_size == 4
        and ctx_size % dp_size == 0
        and ctx_size == 8
        and mbs == 2
        and (layer_input.shape[2] * ctx_size) % QUERY_BLOCK == 0
    )
    return (per_head_device if fits else per_token_device)(*arguments)


def solution(mesh):
    return jax.shard_map(
        on_device,
        mesh=mesh,
        in_specs=(
            P(None, "dp", "ctx", None),
            P(None, "dp", None),
            P(),
            P(),
            P("dp", None),
            P("dp", None),
            P(),
            P(),
            P("dp", None),
            P(),
            P("dp", None),
            P(None, "dp", "ctx", None),
        ),
        out_specs=(
            P(None, "dp", "ctx", None),
            P(None, "dp", "ctx", None),
            P(),
            P(),
            P("dp", "ctx"),
            P("dp", "ctx"),
            P(),
            P(),
            P("dp", "ctx"),
            P(),
            P("dp", "ctx"),
        ),
        check_vma=False,
    )
```

```python
import math
from functools import partial
from types import SimpleNamespace

import jax
import jax.numpy as jnp
from jax import lax
from jax.experimental import pallas as pl
from jax.experimental.pallas import tpu as pltpu
from jax.sharding import PartitionSpec as P

HD = 64


NORM_EPSILON = 1e-05
MASKED = -1e30
START_TOP = -1e20


def prefix_2(array, axis, combine, identity, reverse):
    peers, index = (lax.axis_size(axis), lax.axis_index(axis))
    everything = lax.all_gather(array, axis)
    start = jnp.broadcast_to(jnp.asarray(identity, array.dtype), array.shape)

    def turn(k, before):
        at = peers - 1 - k if reverse else k
        reached = at > index if reverse else at < index
        new = combine(before, everything[at])
        return jnp.where(reached, new, before)

    return lax.fori_loop(0, peers, turn, start)


def layer_norm(value, gain, bias):
    row_mean = jnp.mean(value, axis=-1, keepdims=True)
    centered = value - row_mean
    spread = jnp.mean(centered * centered, axis=-1, keepdims=True)
    return centered * lax.rsqrt(spread + NORM_EPSILON) * gain + bias


def matmul(left, right):
    return jnp.dot(left, right, preferred_element_type=jnp.float32)


def contract_rows(left, right):
    return lax.dot_general(
        left, right, (((0,), (0,)), ((), ())), preferred_element_type=jnp.float32
    )


def contract_cols(left, right):
    return lax.dot_general(
        left, right, (((1,), (1,)), ((), ())), preferred_element_type=jnp.float32
    )


def segment_table(lengths, row_length):
    doc_ends = jnp.cumsum(lengths)
    places = jnp.arange(row_length, dtype=jnp.int32)
    segment = jnp.sum((places[:, None] >= doc_ends[None, :]).astype(jnp.int32), axis=1)
    opening = jnp.concatenate([jnp.ones((1,), jnp.bool_), segment[1:] != segment[:-1]])
    return (segment, opening)


def add_up(earlier, later):
    return earlier + later


def per_token_device(
    layer_input,
    doc_lengths,
    ln1_gain,
    ln1_bias,
    w_qkv,
    w_out,
    ln2_gain,
    ln2_bias,
    w_up,
    b_up,
    w_down,
    cotangent,
):
    micro_count = layer_input.shape[0]
    query_rows = layer_input.shape[2]
    model_width = layer_input.shape[3]
    head_count = model_width // HD
    row_length = query_rows * lax.axis_size("ctx")
    key_block = min(512, row_length)
    score_scale = HD ** (-0.5)
    strength = 8.0 / row_length
    ctx_place = lax.axis_index("ctx")
    query_pos = ctx_place * query_rows + jnp.arange(query_rows, dtype=jnp.int32)
    block_total = ((ctx_place + 1) * query_rows + key_block - 1) // key_block
    later_heads = (jnp.arange(head_count) > 0).astype(jnp.float32)[:, None, None]
    zeros_row = jnp.zeros((row_length,), jnp.float32)
    gelu_exact = partial(jax.nn.gelu, approximate=False)
    output_list = []
    input_grads = []
    matrix_total = None
    vector_total = None
    for micro_step in range(micro_count):
        w_qkv_all, w_out_all, w_up_all, w_down_all = (
            lax.all_gather(w_qkv, "dp", axis=0, tiled=True),
            lax.all_gather(w_out, "dp", axis=0, tiled=True),
            lax.all_gather(w_up, "dp", axis=0, tiled=True),
            lax.all_gather(w_down, "dp", axis=0, tiled=True),
        )
        inputs = layer_input[micro_step, 0].astype(jnp.float32)
        segment, opening = segment_table(doc_lengths[micro_step, 0], row_length)
        query_seg = lax.dynamic_slice_in_dim(segment, ctx_place * query_rows, query_rows, 0)
        normed_one = layer_norm(inputs, ln1_gain, ln1_bias).astype(jnp.bfloat16)
        projected = matmul(normed_one, w_qkv_all).astype(jnp.bfloat16)
        queries = projected[:, :model_width]
        queries3 = queries.reshape(query_rows, head_count, HD)
        query_zero = queries[:, :HD]
        keys_all, values_all = (
            lax.all_gather(projected[:, model_width : 2 * model_width], "ctx", axis=0, tiled=True),
            lax.all_gather(projected[:, 2 * model_width :], "ctx", axis=0, tiled=True),
        )

        def masks(key_start):
            key_seg = lax.dynamic_slice_in_dim(segment, key_start, key_block, 0)
            key_open = lax.dynamic_slice_in_dim(opening, key_start, key_block, 0)
            key_pos = key_start + jnp.arange(key_block, dtype=jnp.int32)
            same_doc = query_seg[:, None] == key_seg[None, :]
            allowed = same_doc & (key_pos[None, :] <= query_pos[:, None])
            chosen = (
                same_doc
                & (key_pos[None, :] < query_pos[:, None])
                & jnp.logical_not(key_open)[None, :]
            )
            return (allowed, chosen.astype(jnp.float32))

        def head_scores(key_start):
            key_zero = lax.dynamic_slice_in_dim(keys_all, key_start, key_block, 0)[:, :HD]
            return (key_zero, contract_cols(query_zero, key_zero) * score_scale)

        def block_keys(key_start):
            keys3 = lax.dynamic_slice_in_dim(keys_all, key_start, key_block, 0).reshape(
                key_block, head_count, HD
            )
            values3 = lax.dynamic_slice_in_dim(values_all, key_start, key_block, 0).reshape(
                key_block, head_count, HD
            )
            return (keys3, values3)

        def logits_of(key_start, keys3):
            allowed, chosen = masks(key_start)
            raw_scores = (
                jnp.einsum("qhd,khd->hqk", queries3, keys3, preferred_element_type=jnp.float32)
                * score_scale
            )
            picked = strength * jax.nn.softplus(raw_scores[0]) * chosen
            before = lax.dynamic_slice_in_dim(prefix, key_start, key_block, 0)
            penalty = before[None, :] + jnp.cumsum(picked, axis=0) - picked
            return jnp.where(allowed[None], raw_scores - penalty[None], MASKED)

        def total_block(block_index, totals):
            key_start = block_index * key_block
            _, chosen = masks(key_start)
            _, first_scores = head_scores(key_start)
            picked = strength * jax.nn.softplus(first_scores) * chosen
            return lax.dynamic_update_slice_in_dim(totals, jnp.sum(picked, axis=0), key_start, 0)

        totals = lax.fori_loop(0, block_total, total_block, zeros_row)
        prefix = prefix_2(totals, "ctx", add_up, zeros_row, False)

        def stat_block(block_index, running):
            row_top, row_total = running
            key_start = block_index * key_block
            keys3, _ = block_keys(key_start)
            logits = logits_of(key_start, keys3)
            new_top = jnp.maximum(row_top, jnp.max(logits, axis=-1))
            row_total = row_total * jnp.exp(row_top - new_top) + jnp.sum(
                jnp.exp(logits - new_top[..., None]), axis=-1
            )
            return (new_top, row_total)

        row_top, row_total = lax.fori_loop(
            0,
            block_total,
            stat_block,
            (
                jnp.full((head_count, query_rows), START_TOP, jnp.float32),
                jnp.zeros((head_count, query_rows), jnp.float32),
            ),
        )
        log_total = row_top + jnp.log(row_total)

        def out_block(block_index, gathered_out):
            key_start = block_index * key_block
            keys3, values3 = block_keys(key_start)
            attn_probs = jnp.exp(logits_of(key_start, keys3) - log_total[..., None]).astype(
                jnp.bfloat16
            )
            return gathered_out + jnp.einsum(
                "hqk,khd->qhd", attn_probs, values3, preferred_element_type=jnp.float32
            )

        gathered_out = lax.fori_loop(
            0, block_total, out_block, jnp.zeros((query_rows, head_count, HD), jnp.float32)
        )
        attended = gathered_out.reshape(query_rows, model_width).astype(jnp.bfloat16)
        mid_stream = inputs + matmul(attended, w_out_all)
        normed_two = layer_norm(mid_stream, ln2_gain, ln2_bias).astype(jnp.bfloat16)
        hidden = matmul(normed_two, w_up_all) + b_up
        activated = gelu_exact(hidden).astype(jnp.bfloat16)
        output_list.append((mid_stream + matmul(activated, w_down_all)).astype(jnp.bfloat16))
        cot_rows = cotangent[micro_step, 0]
        grad_down = contract_rows(activated, cot_rows)
        grad_act = contract_cols(cot_rows, w_down_all)
        _, gelu_back = jax.vjp(gelu_exact, hidden)
        grad_hidden = gelu_back(grad_act)[0].astype(jnp.bfloat16)
        grad_up = contract_rows(normed_two, grad_hidden)
        grad_bias_up = jnp.sum(grad_hidden.astype(jnp.float32), axis=0)
        grad_normed_two = contract_cols(grad_hidden, w_up_all)
        _, norm_two_back = jax.vjp(layer_norm, mid_stream, ln2_gain, ln2_bias)
        grad_mid_part, grad_gain_two, grad_bias_two = norm_two_back(grad_normed_two)
        grad_mid = cot_rows.astype(jnp.float32) + grad_mid_part
        grad_branch = grad_mid.astype(jnp.bfloat16)
        grad_outproj = contract_rows(attended, grad_branch)
        grad_attended = contract_cols(grad_branch, w_out_all).astype(jnp.bfloat16)
        grad_att3 = grad_attended.reshape(query_rows, head_count, HD)
        row_delta = jnp.einsum("qhd,qhd->hq", grad_att3.astype(jnp.float32), gathered_out)

        def grad_block(block_index, running):
            grad_query, grad_key_all, grad_value_all, penalty_grad, first_grad = running
            key_start = block_index * key_block
            keys3, values3 = block_keys(key_start)
            probs_f32 = jnp.exp(logits_of(key_start, keys3) - log_total[..., None])
            grad_probs = jnp.einsum(
                "qhd,khd->hqk", grad_att3, values3, preferred_element_type=jnp.float32
            )
            grad_logits = probs_f32 * (grad_probs - row_delta[..., None])
            penalty_grad = lax.dynamic_update_slice_in_dim(
                penalty_grad, -jnp.sum(grad_logits, axis=0), key_start, 1
            )
            first_grad = lax.dynamic_update_slice_in_dim(first_grad, grad_logits[0], key_start, 1)
            grad_scores = (grad_logits * later_heads).astype(jnp.bfloat16)
            grad_query = (
                grad_query
                + jnp.einsum("hqk,khd->qhd", grad_scores, keys3, preferred_element_type=jnp.float32)
                * score_scale
            )
            key_part = (
                jnp.einsum(
                    "hqk,qhd->khd", grad_scores, queries3, preferred_element_type=jnp.float32
                )
                * score_scale
            )
            value_part = jnp.einsum(
                "hqk,qhd->khd",
                probs_f32.astype(jnp.bfloat16),
                grad_att3,
                preferred_element_type=jnp.float32,
            )
            grad_key_all = lax.dynamic_update_slice_in_dim(
                grad_key_all, key_part.reshape(key_block, model_width), key_start, 0
            )
            grad_value_all = lax.dynamic_update_slice_in_dim(
                grad_value_all, value_part.reshape(key_block, model_width), key_start, 0
            )
            return (grad_query, grad_key_all, grad_value_all, penalty_grad, first_grad)

        grad_query, grad_key_all, grad_value_all, penalty_grad, first_grad = lax.fori_loop(
            0,
            block_total,
            grad_block,
            (
                jnp.zeros((query_rows, head_count, HD), jnp.float32),
                jnp.zeros((row_length, model_width), jnp.float32),
                jnp.zeros((row_length, model_width), jnp.float32),
                jnp.zeros((query_rows, row_length), jnp.float32),
                jnp.zeros((query_rows, row_length), jnp.float32),
            ),
        )
        column_sums = jnp.sum(penalty_grad, axis=0)
        after = prefix_2(column_sums, "ctx", add_up, zeros_row, True)
        reach_sums = after + column_sums

        def head_block(block_index, running):
            grad_query_zero, grad_key_all = running
            key_start = block_index * key_block
            _, chosen = masks(key_start)
            key_zero, first_scores = head_scores(key_start)
            flow_block = lax.dynamic_slice_in_dim(penalty_grad, key_start, key_block, 1)
            reach_block = lax.dynamic_slice_in_dim(reach_sums, key_start, key_block, 0)
            grad_picked = reach_block[None, :] - jnp.cumsum(flow_block, axis=0)
            grad_select = grad_picked * strength * jax.nn.sigmoid(first_scores) * chosen
            grad_head = (
                lax.dynamic_slice_in_dim(first_grad, key_start, key_block, 1) + grad_select
            ).astype(jnp.bfloat16)
            grad_query_zero = grad_query_zero + matmul(grad_head, key_zero) * score_scale
            key_zero_grad = contract_rows(grad_head, query_zero) * score_scale
            grad_key_all = lax.dynamic_update_slice(
                grad_key_all, key_zero_grad, (key_start, jnp.zeros((), jnp.int32))
            )
            return (grad_query_zero, grad_key_all)

        grad_query_zero, grad_key_all = lax.fori_loop(
            0, block_total, head_block, (jnp.zeros((query_rows, HD), jnp.float32), grad_key_all)
        )
        grad_query = grad_query.at[:, 0, :].add(grad_query_zero).reshape(query_rows, model_width)
        grad_key_own, grad_value_own = (
            lax.psum_scatter(grad_key_all, "ctx", scatter_dimension=0, tiled=True),
            lax.psum_scatter(grad_value_all, "ctx", scatter_dimension=0, tiled=True),
        )
        grad_project = jnp.concatenate([grad_query, grad_key_own, grad_value_own], axis=1).astype(
            jnp.bfloat16
        )
        grad_qkv = contract_rows(normed_one, grad_project)
        grad_normed_one = contract_cols(grad_project, w_qkv_all)
        _, norm_one_back = jax.vjp(layer_norm, inputs, ln1_gain, ln1_bias)
        grad_in_part, grad_gain_one, grad_bias_one = norm_one_back(grad_normed_one)
        input_grads.append((grad_mid + grad_in_part).astype(jnp.bfloat16))
        matrix_grads = (grad_qkv, grad_outproj, grad_up, grad_down)
        vector_grads = (grad_gain_one, grad_bias_one, grad_gain_two, grad_bias_two, grad_bias_up)
        matrix_grads = (
            lax.psum_scatter(matrix_grads[0], "ctx", scatter_dimension=1, tiled=True),
            lax.psum_scatter(matrix_grads[1], "ctx", scatter_dimension=1, tiled=True),
            lax.psum_scatter(matrix_grads[2], "ctx", scatter_dimension=1, tiled=True),
            lax.psum_scatter(matrix_grads[3], "ctx", scatter_dimension=1, tiled=True),
        )
        matrix_grads = (
            lax.psum_scatter(
                matrix_grads[0].astype(jnp.bfloat16), "dp", scatter_dimension=0, tiled=True
            ).astype(jnp.float32),
            lax.psum_scatter(
                matrix_grads[1].astype(jnp.bfloat16), "dp", scatter_dimension=0, tiled=True
            ).astype(jnp.float32),
            lax.psum_scatter(
                matrix_grads[2].astype(jnp.bfloat16), "dp", scatter_dimension=0, tiled=True
            ).astype(jnp.float32),
            lax.psum_scatter(
                matrix_grads[3].astype(jnp.bfloat16), "dp", scatter_dimension=0, tiled=True
            ).astype(jnp.float32),
        )
        vector_grads = lax.psum(
            (vector_grads[0], vector_grads[1], vector_grads[2], vector_grads[3], vector_grads[4]),
            ("dp", "ctx"),
        )
        if matrix_total is None:
            matrix_total = matrix_grads
            vector_total = vector_grads
        else:
            matrix_total = tuple((old + new for old, new in zip(matrix_total, matrix_grads)))
            vector_total = tuple((old + new for old, new in zip(vector_total, vector_grads)))
    layer_out = jnp.stack(output_list)[:, None]
    input_out = jnp.stack(input_grads)[:, None]
    return (
        layer_out,
        input_out,
        vector_total[0],
        vector_total[1],
        matrix_total[0],
        matrix_total[1],
        vector_total[2],
        vector_total[3],
        matrix_total[2],
        vector_total[4],
        matrix_total[3],
    )


MESH = pl.DeviceIdType.MESH
EXCLUDED = 1e30
QUERY_BLOCK = 256


def norm_parts(value):
    row_mean = jnp.mean(value, axis=-1, keepdims=True)
    centered = value - row_mean
    spread = jnp.mean(centered * centered, axis=-1, keepdims=True)
    inverse = lax.rsqrt(spread + NORM_EPSILON)
    return centered * inverse, inverse


def norm_back(xhat, inverse, grad, gain):
    scaled = grad * gain
    return (
        scaled
        - jnp.mean(scaled, axis=-1, keepdims=True)
        - xhat * jnp.mean(scaled * xhat, axis=-1, keepdims=True)
    ) * inverse


class Wires:
    def __init__(self, send_sem, recv_sem):
        self.send_sem, self.recv_sem, self.used, self.made = send_sem, recv_sem, 0, []

    def send(self, source, target, where):
        copy = pltpu.make_async_remote_copy(
            src_ref=source,
            dst_ref=target,
            send_sem=self.send_sem.at[self.used],
            recv_sem=self.recv_sem.at[self.used],
            device_id=where,
            device_id_type=MESH,
        )
        copy.start()
        self.used += 1
        self.made.append(copy)
        return copy

    def drain(self):
        for copy in self.made:
            copy.wait_send()


def rounded(value):
    return value.astype(jnp.bfloat16)


def folded(array):
    half = array.shape[0] // 2
    return jnp.concatenate([array[:half], array[half:]], axis=1)


def unfolded(array):
    half = array.shape[1] // 2
    return jnp.concatenate([array[:, :half], array[:, half:]], axis=0)


def arrived(like, target, sem):
    pltpu.make_async_copy(like, target, sem).wait()


def swap(index):
    return index + 1 - 2 * lax.rem(index, 2)


def layer_body(plan, loaded, names, lengths, *refs):
    given, refs = refs[: len(loaded)], refs[len(loaded) :]
    r = SimpleNamespace(**dict(zip(names, refs)))
    groups, shards = plan
    f32 = jnp.float32
    ctx, dp = lax.axis_index("ctx"), lax.axis_index("dp")
    ctx_size, tokens, model = r.x_row.shape
    width = r.out.shape[1]
    lines = ctx_size // 2
    mbs = ctx_size // groups
    hpg = width // HD
    own = r.x.shape[0]
    ff = r.w_down.shape[0]
    row_length = tokens * ctx_size
    side, line = lax.rem(ctx, 2), ctx // 2
    my_mb, my_group = ctx // groups, lax.rem(ctx, groups)
    wires = Wires(r.send_sem, r.recv_sem)
    core, far, far_core = {"dp": swap(dp)}, {"dp": lax.rem(dp + 2, 4)}, {"dp": lax.rem(swap(dp) + 2, 4)}
    beside = {"ctx": swap(ctx)}
    up_to = {"dp": lax.rem(ctx, 4), "ctx": shards * dp + ctx // 4}
    up_from = {"dp": ctx // shards, "ctx": lax.rem(ctx, shards) * 4 + dp}
    around = [{"ctx": lax.rem(ctx + step, ctx_size)} for step in range(1, ctx_size)]

    mirror = {"ctx": lax.rem(line + lines // 2, lines) * 2 + side}
    ahead = {"ctx": swap(line) * 2 + side}
    beside_at, mirror_at, ahead_at = beside["ctx"], mirror["ctx"], ahead["ctx"]
    half = tokens // 2

    loads = SimpleNamespace()
    for at, name in enumerate(loaded):
        copy = pltpu.make_async_copy(given[at], getattr(r, name), r.load_sem.at[at])
        copy.start()
        setattr(loads, name, copy)
    barrier = pltpu.get_barrier_semaphore()
    for where in around + [core, far, far_core, up_from]:
        pl.semaphore_signal(barrier, inc=1, device_id=where, device_id_type=MESH)
    loads.x.wait()
    loads.w_qkv.wait()
    pl.semaphore_wait(barrier, ctx_size + 3)

    def x_of(micro):
        return r.x.at[pl.ds(pl.multiple_of(micro * tokens, tokens), tokens)]

    x_mirror = wires.send(x_of(1 - my_mb), r.x_row.at[ctx], mirror)
    x_beside = wires.send(x_of(my_mb), r.x_row.at[ctx], beside)
    x_ahead = wires.send(x_of(my_mb), r.x_row.at[ctx], ahead)
    for group in range(groups):

        @pl.when(my_group == group)
        def _():
            for kind in range(3):
                first = kind * model + group * width
                r.w_pick[dp, :, kind * width : (kind + 1) * width] = r.w_qkv[:, first : first + width]

    for kind in range(2):
        r.w_pick[dp, :, 3 * width + kind * HD : 3 * width + (kind + 1) * HD] = r.w_qkv[
            :, kind * model : kind * model + HD
        ]
    pick_far = wires.send(r.w_pick.at[dp], r.w_pick.at[dp], far)
    pick_core = wires.send(r.w_pick.at[dp], r.w_pick.at[dp], core)
    r.x_row[ctx] = x_of(my_mb)[...]

    loads.gain_one.wait()
    loads.bias_one.wait()
    gain_one = r.gain_one[...].reshape(1, model)
    bias_one = r.bias_one[...].reshape(1, model)

    def normalise(place):
        xhat, _ = norm_parts(r.x_row[place].astype(f32))
        rows = pl.ds(pl.multiple_of(place * tokens, tokens), tokens)
        r.hat_one[rows, :] = rounded(xhat)
        r.normed_one[rows, :] = rounded(xhat * gain_one + bias_one)

    x_beside.wait_recv()
    top, bottom = pl.ds(0, half), pl.ds(half, half)
    x_fwd_a = wires.send(r.x_row.at[beside_at, top], r.x_row.at[beside_at, top], ahead)
    x_ahead.wait_recv()
    x_fwd_b = wires.send(r.x_row.at[ahead_at, bottom], r.x_row.at[ahead_at, bottom], beside)
    normalise(ctx)
    x_mirror.wait_recv()
    x_mirror_beside = wires.send(r.x_row.at[mirror_at], r.x_row.at[mirror_at], beside)
    x_mirror_ahead = wires.send(r.x_row.at[mirror_at], r.x_row.at[mirror_at], ahead)
    pick_far.wait_recv()
    pick_at = far["dp"]
    pick_fwd = wires.send(r.w_pick.at[pick_at], r.w_pick.at[pick_at], core)

    for copy in (loads.cot, loads.w_out_own, loads.w_up_own):
        copy.wait()

    def rows_of(place):
        return pl.ds(pl.multiple_of(place * size_dp, size_dp), size_dp)

    size_dp = model // 4
    wout_far = wires.send(r.w_out_own, r.w_out.at[rows_of(dp)], far)
    wout_core = wires.send(r.w_out_own, r.w_out.at[rows_of(dp)], core)

    def up_part(peer):
        return r.w_up_own.at[:, pl.ds(pl.multiple_of(peer * ff, 128), ff)]

    up_in = [
        wires.send(up_part(where["dp"]), r.w_up.at[rows_of(dp)], where)
        for where in (far, far_core, core)
    ]
    cot_far = wires.send(r.cot, r.cots.at[2], far)
    cot_core = wires.send(r.cot, r.cots.at[1], core)
    r.w_out[rows_of(dp), :] = r.w_out_own[...]
    r.w_up[rows_of(dp), :] = up_part(dp)[...]
    r.cots[0] = r.cot[...]

    normalise(beside_at)
    normalise(ahead_at)
    normalise(mirror_at)
    x_mirror_beside.wait_recv()
    place = swap(mirror_at)
    x_fwd_c = wires.send(r.x_row.at[place, top], r.x_row.at[place, top], ahead)
    x_mirror_ahead.wait_recv()
    place = lax.rem(ahead_at + ctx_size // 2, ctx_size)
    x_fwd_d = wires.send(r.x_row.at[place, bottom], r.x_row.at[place, bottom], beside)
    normalise(swap(mirror_at))
    normalise(place)
    x_fwd_a.wait_recv()
    x_fwd_b.wait_recv()
    normalise(swap(ahead_at))
    pick_core.wait_recv()
    pick_fwd.wait_recv()
    x_fwd_c.wait_recv()
    x_fwd_d.wait_recv()
    normalise(swap(place))
    w_pick = r.w_pick[...].reshape(model, 3 * width + 2 * HD)
    r.proj[...] = rounded(matmul(r.normed_one[...], w_pick))

    def att_copy(place):
        return pltpu.make_async_remote_copy(
            src_ref=r.att.at[place],
            dst_ref=r.att_in.at[ctx],
            send_sem=r.att_send.at[place],
            recv_sem=r.att_recv.at[ctx],
            device_id={"ctx": place},
            device_id_type=MESH,
        )

    block = QUERY_BLOCK
    per_block = block // tokens
    scale = HD ** (-0.5)
    strength = 8.0 / row_length
    row_at = lax.broadcasted_iota(jnp.int32, (block, block), 0)
    col_at = lax.broadcasted_iota(jnp.int32, (block, block), 1)
    earlier = (col_at < row_at).astype(jnp.bfloat16)
    later = (col_at > row_at).astype(jnp.bfloat16)
    doc_ends, doc_end = [], 0
    for at in range(lengths.shape[2]):
        doc_end = doc_end + lengths[my_mb, 0, at]
        doc_ends.append(doc_end)

    def segment_of(places):
        total = jnp.zeros(places.shape, jnp.int32)
        for end in doc_ends:
            total += jnp.where(places >= end, 1, 0)
        return total

    r.suffix[...] = jnp.zeros_like(r.suffix)
    for start in range(0, row_length, block):
        reach = start + block
        rows = pl.ds(start, block)
        probs_ref, slope_ref = getattr(r, "probs%d" % start), getattr(r, "slope%d" % start)
        row_pos = start + lax.broadcasted_iota(jnp.int32, (block, 1), 0)
        col_pos = lax.broadcasted_iota(jnp.int32, (1, reach), 1)
        row_seg, col_seg = segment_of(row_pos), segment_of(col_pos)
        opening = (col_seg != segment_of(col_pos - 1)) | (col_pos == 0)
        pick_seg = jnp.where(opening, -1, col_seg)
        query = rounded(r.proj[rows, 3 * width : 3 * width + HD] * scale)
        key = r.proj[:reach, 3 * width + HD : 3 * width + 2 * HD]
        scores = contract_cols(query, key)
        small = jnp.exp(-jnp.abs(scores))
        soft = jnp.maximum(scores, 0.0) + jnp.log(1.0 + small)
        recip = 1.0 / (1.0 + small)
        sigmoid = jnp.where(scores >= 0.0, recip, small * recip)
        chosen = (row_seg == pick_seg) & (col_pos < row_pos)
        picked = jnp.where(chosen, strength * soft, 0.0)
        slope_ref[...] = rounded(jnp.where(chosen, strength * sigmoid, 0.0))
        high = rounded(picked)
        low = rounded(picked - high.astype(f32))
        penalty = r.suffix[:, :reach] + (matmul(earlier, high) + matmul(earlier, low))
        allowed = (row_seg == col_seg) & (col_pos <= row_pos)
        penalty = jnp.where(allowed, penalty, EXCLUDED)
        r.suffix[:, :reach] += jnp.sum(picked, axis=0, keepdims=True)
        for head in range(hpg):
            at = head * HD
            query = rounded(r.proj[rows, at : at + HD] * scale)
            key = r.proj[:reach, width + at : width + at + HD]
            value = r.proj[:reach, 2 * width + at : 2 * width + at + HD]
            logits = contract_cols(query, key) - penalty
            top_logit = jnp.max(logits, axis=1, keepdims=True)
            probs = jnp.exp(logits - top_logit)
            inverse = 1.0 / jnp.sum(probs, axis=1, keepdims=True)
            probs = rounded(probs)
            probs_ref[head] = probs
            r.out[rows, at : at + HD] = matmul(probs, value) * inverse
            r.inverse[rows, head : head + 1] = inverse
        for step in range(per_block):
            place = start // tokens + step
            r.att[place] = folded(rounded(r.out[place * tokens : (place + 1) * tokens, :]))
            copy = att_copy(place)

            @pl.when(ctx != place)
            def _():
                copy.start()

    r.att_in[ctx] = r.att[ctx]
    cot_far.wait_recv()
    cot_fwd = wires.send(r.cots.at[2], r.cots.at[3], core)
    wout_far.wait_recv()
    out_at = rows_of(far["dp"])
    wout_fwd = wires.send(r.w_out.at[out_at], r.w_out.at[out_at], core)
    for copy in up_in:
        copy.wait_recv()
    wout_core.wait_recv()
    wout_fwd.wait_recv()
    for copy in (loads.gain_two, loads.bias_two, loads.w_down, loads.b_up):
        copy.wait()
    for step in range(1, ctx_size):
        place = lax.rem(ctx + step, ctx_size)
        arrived(r.att.at[0], r.att_in.at[place], r.att_recv.at[place])
    for place in range(ctx_size):
        r.att_got[place] = unfolded(r.att_in[place])

    gain = r.gain_two[...].reshape(1, model)
    bias = r.bias_two[...].reshape(1, model)
    for at in range(4):

        @pl.when(dp == at)
        def _():
            r.b_own[...] = r.b_up[at * ff : (at + 1) * ff].reshape(1, ff)

    for micro in range(mbs):
        rows = pl.ds(micro * tokens, tokens)
        stream = r.x[rows, :].astype(f32)
        for group in range(groups):
            stream += matmul(
                r.att_got[micro * groups + group], r.w_out[pl.ds(group * width, width), :]
            )
        r.mid[rows, :] = stream
    xhat, inverse_two = norm_parts(r.mid[...])
    r.hat_two[...] = xhat
    r.normed[0] = rounded(xhat * gain + bias)
    to_core = wires.send(r.normed.at[0], r.normed.at[1], core)
    to_far = wires.send(r.normed.at[0], r.normed.at[2], far)

    def feed(slot):
        hidden = matmul(r.normed[slot], r.w_up[...]) + r.b_own[...]
        cdf = 0.5 * (1.0 + lax.erf(hidden * (2.0**-0.5)))
        density = jnp.exp(-0.5 * hidden * hidden) * ((2.0 * math.pi) ** -0.5)
        r.act[slot] = rounded(hidden * cdf)
        grad = contract_cols(r.cots[slot], r.w_down[...])
        r.grad_hid[slot] = rounded(grad * (cdf + hidden * density))
        r.part[slot] = rounded(contract_cols(r.grad_hid[slot], r.w_up[...]))

    def feed_out(slot):
        r.out_part[slot] = rounded(matmul(r.act[slot], r.w_down[...]))

    feed(0)
    cot_core.wait_recv()
    to_core.wait_recv()
    feed(1)
    part_core = wires.send(r.part.at[1], r.part_got.at[0], core)
    to_far.wait_recv()
    forward = wires.send(r.normed.at[2], r.normed.at[3], core)
    feed(2)
    forward.wait_recv()
    cot_fwd.wait_recv()
    feed(3)
    part_far_core = wires.send(r.part.at[3], r.part_got.at[1], core)
    feed_out(3)
    out_far_core = wires.send(r.out_part.at[3], r.out_got.at[1], core)
    part_far_core.wait_recv()
    r.part[2] = rounded(r.part[2].astype(f32) + r.part_got[1].astype(f32))
    part_far = wires.send(r.part.at[2], r.part_got.at[2], far)
    def side_pieces(grad, side_got):
        return [
            wires.send(
                grad.at[1 - side, lax.rem(line + step, lines)],
                side_got.at[lax.rem(line + step, lines)],
                beside,
            )
            for step in list(range(1, lines)) + [0]
        ]

    def line_piece(copies, at, grad, side_got, line_got):
        place = lax.rem(line + 1 + at, lines)
        copies[at].wait_recv()
        total = rounded(grad[side, place].astype(f32) + side_got[place].astype(f32))
        if at == lines - 1:
            line_got[line] = total
            return None
        grad[side, place] = total
        return wires.send(grad.at[side, place], line_got.at[line], {"ctx": place * 2 + side})

    def line_sum(copies, line_got):
        for copy in copies:
            copy.wait_recv()
        total = line_got[0].astype(f32)
        for place in range(1, lines):
            total += line_got[place].astype(f32)
        return total

    flat_cot = r.cots[...].reshape(4 * own, model)
    flat_act = r.act[...].reshape(4 * own, ff)
    grads = rounded(contract_rows(flat_cot, flat_act))
    size = model // ctx_size
    for at in range(ctx_size):
        r.down_grad[at % 2, at // 2] = grads[at * size : (at + 1) * size]
    down_side = side_pieces(r.down_grad, r.down_side)
    feed_out(1)
    out_core = wires.send(r.out_part.at[1], r.out_got.at[0], core)
    feed_out(2)
    out_far_core.wait_recv()
    r.out_part[2] = rounded(r.out_part[2].astype(f32) + r.out_got[1].astype(f32))
    out_far = wires.send(r.out_part.at[2], r.out_got.at[2], far)
    feed_out(0)
    flat_grad = r.grad_hid[...].reshape(4 * own, ff)
    vec_rows = 4 + ff // model
    d_bias_up = jnp.sum(flat_grad.astype(f32), axis=0, keepdims=True)
    for at in range(ff // model):
        r.vec[4 + at : 5 + at, :] = d_bias_up[:, at * model : (at + 1) * model]
    down_line = []

    def pump_down(at):
        down_line.append(line_piece(down_side, at, r.down_grad, r.down_side, r.down_line))

    part_core.wait_recv()
    part_far.wait_recv()
    grad_normed = r.part[0].astype(f32) + r.part_got[0].astype(f32) + r.part_got[2].astype(f32)
    xhat = r.hat_two[...]
    r.vec[2:3, :] = jnp.sum(grad_normed * xhat, axis=0, keepdims=True)
    r.vec[3:4, :] = jnp.sum(grad_normed, axis=0, keepdims=True)
    r.grad_mid[...] = r.cot[...].astype(f32) + norm_back(xhat, inverse_two, grad_normed, gain)
    branch = rounded(r.grad_mid[...])
    for group in range(groups):
        grad = rounded(contract_cols(branch, r.w_out[pl.ds(group * width, width), :]))
        for micro in range(mbs):
            r.att_out[micro * groups + group] = folded(
                grad[micro * tokens : (micro + 1) * tokens]
            )
    att_in = []
    for step in range(1, ctx_size):
        peer = lax.rem(ctx + step, ctx_size)
        att_in.append(wires.send(r.att_out.at[peer], r.grad_in.at[ctx], {"ctx": peer}))
    r.grad_in[ctx] = r.att_out[ctx]
    pump_down(0)
    pump_down(1)
    pump_down(2)
    pump_down(3)
    flat_normed = r.normed[...].reshape(4 * own, model)
    size = model // 4
    for at in range(shards):
        grads = rounded(
            contract_rows(flat_normed, flat_grad[:, at * ff // shards : (at + 1) * ff // shards])
        )
        for row in range(4):
            index = at * 4 + row
            r.up_grad[index % 2, index // 2] = grads[row * size : (row + 1) * size]
    up_side = side_pieces(r.up_grad, r.up_side)
    up_line = []

    def pump_up(at):
        up_line.append(line_piece(up_side, at, r.up_grad, r.up_side, r.up_line))

    for group in range(groups):
        total = None
        for micro in range(mbs):
            some = contract_rows(
                branch[micro * tokens : (micro + 1) * tokens], r.att_got[micro * groups + group]
            )
            total = some if total is None else total + some
        total = rounded(total)
        narrow = model // ctx_size
        for at in range(ctx_size):
            r.out_grad[group, at % 2, at // 2] = folded(total[at * narrow : (at + 1) * narrow])
    out_grad_core = wires.send(r.out_grad.at[swap(dp)], r.out_grad_got.at[0], core)
    out_grad_far_core = wires.send(
        r.out_grad.at[lax.rem(swap(dp) + 2, 4)], r.out_grad_got.at[1], core
    )
    out_core.wait_recv()
    out_far.wait_recv()
    r.layer[...] = rounded(
        r.mid[...]
        + (r.out_part[0].astype(f32) + r.out_got[0].astype(f32) + r.out_got[2].astype(f32))
    )
    out_grad_far_core.wait_recv()
    mine = lax.rem(dp + 2, 4)
    r.out_grad[mine] = rounded(r.out_grad[mine].astype(f32) + r.out_grad_got[1].astype(f32))
    out_grad_far = wires.send(r.out_grad.at[mine], r.out_grad_got.at[2], far)
    for copy in att_in:
        copy.wait_recv()

    for place in range(ctx_size):
        r.grad_att[place] = unfolded(r.grad_in[place])

    r.suffix[...] = jnp.zeros_like(r.suffix)
    r.acc[...] = jnp.zeros_like(r.acc)

    def back_block(start):
        reach = start + block
        rows = pl.ds(start, block)
        probs_ref, slope_ref = getattr(r, "probs%d" % start), getattr(r, "slope%d" % start)
        total = None
        first = start // tokens
        grad_block = r.grad_att[first : first + per_block].reshape(block, width)
        for head in range(hpg):
            at = head * HD
            query_t = rounded((r.proj[rows, at : at + HD].astype(f32) * scale).T)
            key = r.proj[:reach, width + at : width + at + HD]
            value = r.proj[:reach, 2 * width + at : 2 * width + at + HD]
            grad = grad_block[:, at : at + HD].astype(f32) * r.inverse[rows, head : head + 1]
            delta = jnp.sum(grad * r.out[rows, at : at + HD], axis=1, keepdims=True)
            probs = probs_ref[head]
            grad_probs = contract_cols(rounded(grad), value)
            grad_logits = probs.astype(f32) * (grad_probs - delta)
            total = grad_logits if total is None else total + grad_logits
            grad_scores = rounded(grad_logits)
            r.grad_proj[rows, at : at + HD] = rounded(matmul(grad_scores, key) * scale)
            r.acc[at : at + HD, :reach] += matmul(query_t, grad_scores)
            r.acc[width + at : width + at + HD, :reach] += matmul(rounded(grad.T), probs)
        query_t = rounded((r.proj[rows, 3 * width : 3 * width + HD].astype(f32) * scale).T)
        key = r.proj[:reach, 3 * width + HD : 3 * width + 2 * HD]
        flow = r.suffix[:, :reach] + matmul(later, rounded(total))
        grad_scores = rounded(-flow * slope_ref[...].astype(f32))
        r.grad_proj[rows, 3 * width : 3 * width + HD] = rounded(matmul(grad_scores, key) * scale)
        r.acc[2 * width : 2 * width + HD, :reach] += matmul(query_t, grad_scores)
        r.suffix[:, :reach] += jnp.sum(total, axis=0, keepdims=True)

    def one_grad(place):
        rows = pl.ds(pl.multiple_of(place * tokens, tokens), tokens)
        grad = contract_cols(r.grad_proj[rows, :], w_pick)
        r.vec[0:1, :] += jnp.sum(grad * r.hat_one[rows, :].astype(f32), axis=0, keepdims=True)
        r.vec[1:2, :] += jnp.sum(grad, axis=0, keepdims=True)
        return grad

    r.vec[0:2, :] = jnp.zeros((2, model), f32)
    one_side = {}

    def line_copy(at):
        return pltpu.make_async_remote_copy(
            src_ref=r.one_ready.at[at],
            dst_ref=r.one_line.at[line],
            send_sem=r.one_send.at[at],
            recv_sem=r.one_recv.at[line],
            device_id={"ctx": at * 2 + side},
            device_id_type=MESH,
        )

    def finish_block(at):
        start = at * block
        reach = start + block
        r.grad_proj[start:reach, width : 3 * width] = rounded(r.acc[: 2 * width, start:reach].T)
        r.grad_proj[start:reach, 3 * width + HD :] = rounded(r.acc[2 * width :, start:reach].T)
        r.one_piece[at] = rounded(one_grad(at * 2 + 1 - side))
        one_side[at] = wires.send(r.one_piece.at[at], r.one_side.at[at], beside)
        r.one_own[at] = one_grad(at * 2 + side)

    def pass_on(at):
        one_side[at].wait_recv()
        r.one_ready[at] = rounded(r.one_own[at] + r.one_side[at].astype(f32))
        copy = line_copy(at)

        @pl.when(line != at)
        def _():
            copy.start()

        @pl.when(line == at)
        def _():
            r.one_line[at] = r.one_ready[at]

    last = lines - 1
    back_block(last * block)
    finish_block(last)
    pump_up(0)
    pump_up(1)
    for at in reversed(range(last)):
        back_block(at * block)
        finish_block(at)
        pass_on(at + 1)
        if at == last - 1:
            pump_up(2)
            pump_up(3)
        if at == last - 1:
            out_grad_core.wait_recv()
            out_grad_far.wait_recv()
            r.out_piece[...] = rounded(
                r.out_grad[dp].astype(f32)
                + r.out_grad_got[0].astype(f32)
                + r.out_grad_got[2].astype(f32)
            )
            out_side = side_pieces(r.out_piece, r.out_side)
    r.grad_kv[...] = rounded(r.acc[...])
    vec_in = []
    for step in range(1, ctx_size):
        peer = lax.rem(ctx + step, ctx_size)
        vec_in.append(wires.send(r.vec, r.vec_got.at[ctx], {"ctx": peer}))
    r.vec_got[ctx] = r.vec[...]

    size = model // 4
    part = math.gcd(width, 3 * model // ctx_size)
    per = width // part
    folded_part, folded_head = part // 2, HD // 2

    def store_qkv(grads, parts):
        for at in range(4):
            cols = slice(at * size, (at + 1) * size)
            for source, target, count in parts:
                r.qkv_grad[at, target : target + count // 2, :] = folded(
                    grads[source : source + count, cols]
                )

    tail = 3 * width // 2
    grads_q = rounded(
        contract_rows(
            jnp.concatenate(
                [r.grad_proj[:, :width], r.grad_proj[:, 3 * width : 3 * width + HD]], axis=1
            ),
            r.normed_one[...],
        )
    )
    store_qkv(
        grads_q,
        [(at * part, at * folded_part, part) for at in range(per)] + [(width, tail, HD)],
    )
    grads_kv = rounded(matmul(r.grad_kv[...], r.normed_one[...]))
    store_qkv(
        grads_kv,
        [(at * part, (per + at) * folded_part, part) for at in range(2 * per)]
        + [(2 * width, tail + folded_head, HD)],
    )
    qkv_far_core = wires.send(r.qkv_grad.at[lax.rem(swap(dp) + 2, 4)], r.qkv_got.at[1], core)
    qkv_core = wires.send(r.qkv_grad.at[swap(dp)], r.qkv_got.at[0], core)
    pass_on(0)

    r.d_down[...] = line_sum(down_line[:-1], r.down_line)
    r.up_sum[...] = rounded(line_sum(up_line[:-1], r.up_line))
    stays = (lax.rem(ctx, 4) == dp) & (shards * dp + ctx // 4 == ctx)
    up_copy = pltpu.make_async_remote_copy(
        src_ref=r.up_sum,
        dst_ref=r.up_final,
        send_sem=r.up_send.at[0],
        recv_sem=r.up_recv.at[0],
        device_id=up_to,
        device_id_type=MESH,
    )

    @pl.when(jnp.logical_not(stays))
    def _():
        up_copy.start()

    @pl.when(stays)
    def _():
        r.up_final[...] = r.up_sum[...]

    qkv_far_core.wait_recv()
    r.qkv_grad[mine] = rounded(r.qkv_grad[mine].astype(f32) + r.qkv_got[1].astype(f32))
    qkv_far = wires.send(r.qkv_grad.at[mine], r.qkv_got.at[2], far)
    out_line = [
        line_piece(out_side, at, r.out_piece, r.out_side, r.out_line) for at in range(lines)
    ]
    for copy in vec_in:
        copy.wait_recv()
    total = r.vec_got[0]
    for at in range(1, ctx_size):
        total += r.vec_got[at]
    r.vec_sum[...] = total
    vec_out = [
        wires.send(r.vec_sum, r.vecs.at[dp], where) for where in (core, far, far_core)
    ]
    r.vecs[dp] = total
    qkv_core.wait_recv()
    qkv_far.wait_recv()
    r.qkv_sum[...] = rounded(
        r.qkv_grad[dp].astype(f32) + r.qkv_got[0].astype(f32) + r.qkv_got[2].astype(f32)
    )
    slots = r.deal_got.shape[0]

    def outgoing(kind, half):
        section = (kind * groups + my_group) * per + half
        target, slot = section // slots, lax.rem(section, slots)
        index = kind * per + half
        return target, slot, index, pltpu.make_async_remote_copy(
            src_ref=r.qkv_sum.at[pl.ds(index * folded_part, folded_part)],
            dst_ref=r.deal_got.at[slot, my_mb],
            send_sem=r.deal_send.at[index],
            recv_sem=r.deal_recv.at[slot, my_mb],
            device_id={"ctx": target},
            device_id_type=MESH,
        )

    def extra_copy(kind):
        return pltpu.make_async_remote_copy(
            src_ref=r.qkv_sum.at[pl.ds(tail + kind * folded_head, folded_head)],
            dst_ref=r.extra_got.at[ctx],
            send_sem=r.extra_send.at[kind],
            recv_sem=r.extra_recv.at[ctx],
            device_id={"ctx": kind * groups * per // slots},
            device_id_type=MESH,
        )

    for kind in range(3):
        for half in range(per):
            target, slot, index, copy = outgoing(kind, half)

            @pl.when(target != ctx)
            def _():
                copy.start()

            @pl.when(target == ctx)
            def _():
                r.deal_got[slot, my_mb] = r.qkv_sum[
                    index * folded_part : (index + 1) * folded_part, :
                ]

    for kind in range(2):
        target = kind * groups * per // slots
        copy = extra_copy(kind)

        @pl.when(ctx != target)
        def _():
            copy.start()

        @pl.when(ctx == target)
        def _():
            r.extra_got[ctx] = r.qkv_sum[
                tail + kind * folded_head : tail + (kind + 1) * folded_head, :
            ]

    xhat, inverse_one = norm_parts(r.x[...].astype(f32))
    for step in range(1, lines):
        place = lax.rem(line + step, lines)
        arrived(r.one_ready.at[0], r.one_line.at[place], r.one_recv.at[place])
    half_lines = lines // mbs
    for micro in range(mbs):
        grad = r.one_line[micro * half_lines].astype(f32)
        for at in range(1, half_lines):
            grad += r.one_line[micro * half_lines + at].astype(f32)
        rows = slice(micro * tokens, (micro + 1) * tokens)
        r.d_x[rows, :] = rounded(
            r.grad_mid[rows, :] + norm_back(xhat[rows], inverse_one[rows], grad, gain_one)
        )
    r.d_out[...] = unfolded(line_sum(out_line[:-1], r.out_line)).T

    @pl.when(jnp.logical_not(stays))
    def _():
        up_copy.wait_send()
        up_copy.wait_recv()

    r.d_up[...] = r.up_final[...].astype(f32)

    for kind in range(3):
        for half in range(per):
            target, slot, index, copy = outgoing(kind, half)

            @pl.when(target != ctx)
            def _():
                copy.wait_send()

    for slot in range(slots):
        section = ctx * slots + slot
        source_group = lax.rem(section // per, groups)
        for place in range(mbs):

            @pl.when(place * groups + source_group != ctx)
            def _():
                arrived(
                    r.qkv_sum.at[pl.ds(0, folded_part)],
                    r.deal_got.at[slot, place],
                    r.deal_recv.at[slot, place],
                )

        total = r.deal_got[slot, 0].astype(f32)
        for place in range(1, mbs):
            total += r.deal_got[slot, place].astype(f32)
        r.deal_sum[slot * part : (slot + 1) * part, :] = unfolded(total)
    for kind in range(2):
        section = kind * groups * per
        target, slot = section // slots, section % slots
        copy = extra_copy(kind)

        @pl.when(ctx != target)
        def _():
            copy.wait_send()

        @pl.when(ctx == target)
        def _():
            total = jnp.zeros((folded_head, 2 * size), f32)
            for place in range(ctx_size):
                if place != target:
                    arrived(
                        r.qkv_sum.at[pl.ds(0, folded_head)], r.extra_got.at[place], r.extra_recv.at[place]
                    )
                total += r.extra_got[place].astype(f32)
            r.deal_sum[slot * part : slot * part + HD, :] += unfolded(total)

    r.d_qkv[...] = r.deal_sum[...].T
    for copy in vec_out:
        copy.wait_recv()
    for row in range(4):
        r.d_vec[row : row + 1, :] = (
            r.vecs[0, row : row + 1, :] + r.vecs[1, row : row + 1, :]
        ) + (r.vecs[2, row : row + 1, :] + r.vecs[3, row : row + 1, :])
    for at in range(4):
        r.d_bias[at] = r.vecs[at, 4:vec_rows, :]
    wires.drain()
    for place in range(ctx_size):
        copy = att_copy(place)

        @pl.when(ctx != place)
        def _():
            copy.wait_send()

    for at in range(lines):
        copy = line_copy(at)

        @pl.when(line != at)
        def _():
            copy.wait_send()


LAYER_COPIES = 96


def layer(collective_id, groups, shards, lengths, large):
    bf16, f32 = jnp.bfloat16, jnp.float32
    own, model = large["x"].shape
    ctx_size = lax.axis_size("ctx")
    tokens = own * groups // ctx_size
    hpg = model // HD // groups
    width = hpg * HD
    row_length = ctx_size * tokens
    lines = ctx_size // 2
    ff = large["w_down"].shape[0]
    size, shard = model // 4, 3 * model // ctx_size
    part = math.gcd(width, shard)
    slots, mbs = shard // part, ctx_size // groups
    picked = 3 * width + 2 * HD
    vec_rows = 4 + ff // model
    narrow = model // ctx_size
    vmem = pl.BlockSpec(memory_space=pltpu.VMEM)
    anywhere = pl.BlockSpec(memory_space=pl.ANY)
    outs = dict(
        layer=((own, model), bf16),
        d_x=((own, model), bf16),
        d_vec=((4, model), f32),
        d_bias=((4, ff // model, model), f32),
        d_qkv=((size, shard), f32),
        d_out=((size, narrow), f32),
        d_up=((size, ff // shards), f32),
        d_down=((narrow, ff), f32),
    )
    scratch = {name: (array.shape, array.dtype) for name, array in large.items()}
    scratch |= dict(
        x_row=((ctx_size, tokens, model), bf16),
        hat_one=((row_length, model), bf16),
        normed_one=((row_length, model), bf16),
        w_pick=((4, size, picked), bf16),
        proj=((row_length, picked), bf16),
        w_out=((model, model), bf16),
        w_up=((model, ff), bf16),
        out=((row_length, width), f32),
        inverse=((row_length, hpg), f32),
        att=((ctx_size, tokens // 2, 2 * width), bf16),
        att_in=((ctx_size, tokens // 2, 2 * width), bf16),
        b_own=((1, ff), f32),
        att_got=((ctx_size, tokens, width), bf16),
        cots=((4, own, model), bf16),
        mid=((own, model), f32),
        hat_two=((own, model), f32),
        grad_mid=((own, model), f32),
        normed=((4, own, model), bf16),
        act=((4, own, ff), bf16),
        grad_hid=((4, own, ff), bf16),
        part=((4, own, model), bf16),
        out_part=((4, own, model), bf16),
        part_got=((3, own, model), bf16),
        out_got=((3, own, model), bf16),
        att_out=((ctx_size, tokens // 2, 2 * width), bf16),
        grad_in=((ctx_size, tokens // 2, 2 * width), bf16),
        grad_att=((ctx_size, tokens, width), bf16),
        down_grad=((2, lines, narrow, ff), bf16),
        down_side=((lines, narrow, ff), bf16),
        down_line=((lines, narrow, ff), bf16),
        up_grad=((2, lines, size, ff // shards), bf16),
        up_side=((lines, size, ff // shards), bf16),
        up_line=((lines, size, ff // shards), bf16),
        up_sum=((size, ff // shards), bf16),
        up_final=((size, ff // shards), bf16),
        out_grad=((4, 2, lines, narrow // 2, 2 * size), bf16),
        out_grad_got=((3, 2, lines, narrow // 2, 2 * size), bf16),
        out_piece=((2, lines, narrow // 2, 2 * size), bf16),
        out_side=((lines, narrow // 2, 2 * size), bf16),
        out_line=((lines, narrow // 2, 2 * size), bf16),
        suffix=((1, row_length), f32),
        acc=((2 * width + HD, row_length), f32),
        grad_kv=((2 * width + HD, row_length), bf16),
        grad_proj=((row_length, picked), bf16),
        one_piece=((lines, tokens, model), bf16),
        one_own=((lines, tokens, model), f32),
        one_side=((lines, tokens, model), bf16),
        one_ready=((lines, tokens, model), bf16),
        one_line=((lines, tokens, model), bf16),
        qkv_grad=((4, picked // 2, 2 * size), bf16),
        qkv_got=((3, picked // 2, 2 * size), bf16),
        qkv_sum=((picked // 2, 2 * size), bf16),
        deal_got=((slots, mbs, part // 2, 2 * size), bf16),
        deal_sum=((shard, size), f32),
        extra_got=((ctx_size, HD // 2, 2 * size), bf16),
        vec=((vec_rows, model), f32),
        vec_got=((ctx_size, vec_rows, model), f32),
        vec_sum=((vec_rows, model), f32),
        vecs=((4, vec_rows, model), f32),
    )
    for start in range(0, row_length, QUERY_BLOCK):
        reach = start + QUERY_BLOCK
        scratch["probs%d" % start] = ((hpg, QUERY_BLOCK, reach), bf16)
        scratch["slope%d" % start] = ((QUERY_BLOCK, reach), bf16)
    dma = pltpu.SemaphoreType.DMA
    sems = dict(
        send_sem=dma((LAYER_COPIES,)),
        recv_sem=dma((LAYER_COPIES,)),
        load_sem=dma((len(large),)),
        att_send=dma((ctx_size,)),
        att_recv=dma((ctx_size,)),
        one_send=dma((lines,)),
        one_recv=dma((lines,)),
        up_send=dma((1,)),
        up_recv=dma((1,)),
        deal_send=dma((3 * (width // part),)),
        deal_recv=dma((slots, mbs)),
        extra_send=dma((2,)),
        extra_recv=dma((ctx_size,)),
    )
    names = list(outs) + list(scratch) + list(sems)
    return pl.pallas_call(
        partial(layer_body, (groups, shards), list(large), names),
        out_shape=[jax.ShapeDtypeStruct(*spec) for spec in outs.values()],
        in_specs=[pl.BlockSpec(memory_space=pltpu.SMEM)] + [anywhere] * len(large),
        out_specs=[vmem] * len(outs),
        scratch_shapes=[pltpu.VMEM(*spec) for spec in scratch.values()] + list(sems.values()),
        compiler_params=pltpu.CompilerParams(
            collective_id=collective_id, has_side_effects=True, vmem_limit_bytes=63 * 1024 * 1024
        ),
        name="layer",
    )(lengths, *large.values())


def finish_body(*refs):
    sources, targets = refs[:8], refs[8:]
    for source, target in zip(sources[:6], targets[:6]):
        target[...] = source[...]
    for row in range(4):
        targets[6 + row][...] = sources[6][row]
    columns = sources[7].shape[2]
    rows = sources[7].shape[1]
    for at in range(4 * rows):
        targets[10][at * columns : (at + 1) * columns] = sources[7][at // rows, at % rows]


def finish(*arrays):
    vmem = pl.BlockSpec(memory_space=pltpu.VMEM)
    shape = jax.ShapeDtypeStruct
    model = arrays[6].shape[1]
    return pl.pallas_call(
        finish_body,
        out_shape=[shape(array.shape, array.dtype) for array in arrays[:6]]
        + [shape((model,), jnp.float32)] * 4
        + [shape((arrays[7].size,), jnp.float32)],
        in_specs=[vmem] * len(arrays),
        out_specs=[vmem] * 11,
        name="finish",
    )(*arrays)


def per_head_device(
    layer_input,
    doc_lengths,
    ln1_gain,
    ln1_bias,
    w_qkv,
    w_out,
    ln2_gain,
    ln2_bias,
    w_up,
    b_up,
    w_down,
    cotangent,
):
    mbs, _, tokens, model = layer_input.shape
    ctx_size, dp_size = lax.axis_size("ctx"), lax.axis_size("dp")
    large = dict(
        x=layer_input.reshape(mbs * tokens, model),
        w_qkv=w_qkv,
        gain_one=ln1_gain,
        bias_one=ln1_bias,
        cot=cotangent.reshape(mbs * tokens, model),
        w_out_own=w_out,
        w_up_own=w_up,
        gain_two=ln2_gain,
        bias_two=ln2_bias,
        w_down=w_down,
        b_up=b_up,
    )
    layer_out, d_x, d_vec, d_bias, d_qkv, d_out, d_up, d_down = layer(
        0, ctx_size // mbs, ctx_size // dp_size, doc_lengths, large
    )
    layer_out, d_x, d_qkv, d_out, d_up, d_down, gain_one, bias_one, gain_two, bias_two, d_bias = finish(
        layer_out, d_x, d_qkv, d_out, d_up, d_down, d_vec, d_bias
    )
    return (
        layer_out.reshape(mbs, 1, tokens, model),
        d_x.reshape(mbs, 1, tokens, model),
        gain_one,
        bias_one,
        d_qkv,
        d_out,
        gain_two,
        bias_two,
        d_up,
        d_bias,
        d_down.T,
    )


def on_device(*arguments):
    layer_input = arguments[0]
    mbs, model = layer_input.shape[0], layer_input.shape[3]
    heads, ctx_size, dp_size = model // HD, lax.axis_size("ctx"), lax.axis_size("dp")
    groups = ctx_size // mbs
    fits = (
        ctx_size % mbs == 0
        and heads % groups == 0
        and dp_size == 4
        and ctx_size % dp_size == 0
        and ctx_size == 8
        and mbs == 2
        and (layer_input.shape[2] * ctx_size) % QUERY_BLOCK == 0
    )
    return (per_head_device if fits else per_token_device)(*arguments)


def solution(mesh):
    return jax.shard_map(
        on_device,
        mesh=mesh,
        in_specs=(
            P(None, "dp", "ctx", None),
            P(None, "dp", None),
            P(),
            P(),
            P("dp", None),
            P("dp", None),
            P(),
            P(),
            P("dp", None),
            P(),
            P("dp", None),
            P(None, "dp", "ctx", None),
        ),
        out_specs=(
            P(None, "dp", "ctx", None),
            P(None, "dp", "ctx", None),
            P(),
            P(),
            P("dp", "ctx"),
            P("dp", "ctx"),
            P(),
            P(),
            P("dp", "ctx"),
            P(),
            P("dp", "ctx"),
        ),
        check_vma=False,
    )
```

```python
import math
from functools import partial
from types import SimpleNamespace

import jax
import jax.numpy as jnp
from jax import lax
from jax.experimental import pallas as pl
from jax.experimental.pallas import tpu as pltpu
from jax.sharding import PartitionSpec as P

HD = 64


NORM_EPSILON = 1e-05
MASKED = -1e30
START_TOP = -1e20


def prefix_2(array, axis, combine, identity, reverse):
    peers, index = (lax.axis_size(axis), lax.axis_index(axis))
    everything = lax.all_gather(array, axis)
    start = jnp.broadcast_to(jnp.asarray(identity, array.dtype), array.shape)

    def turn(k, before):
        at = peers - 1 - k if reverse else k
        reached = at > index if reverse else at < index
        new = combine(before, everything[at])
        return jnp.where(reached, new, before)

    return lax.fori_loop(0, peers, turn, start)


def layer_norm(value, gain, bias):
    row_mean = jnp.mean(value, axis=-1, keepdims=True)
    centered = value - row_mean
    spread = jnp.mean(centered * centered, axis=-1, keepdims=True)
    return centered * lax.rsqrt(spread + NORM_EPSILON) * gain + bias


def matmul(left, right):
    return jnp.dot(left, right, preferred_element_type=jnp.float32)


def contract_rows(left, right):
    return lax.dot_general(
        left, right, (((0,), (0,)), ((), ())), preferred_element_type=jnp.float32
    )


def contract_cols(left, right):
    return lax.dot_general(
        left, right, (((1,), (1,)), ((), ())), preferred_element_type=jnp.float32
    )


def segment_table(lengths, row_length):
    doc_ends = jnp.cumsum(lengths)
    places = jnp.arange(row_length, dtype=jnp.int32)
    segment = jnp.sum((places[:, None] >= doc_ends[None, :]).astype(jnp.int32), axis=1)
    opening = jnp.concatenate([jnp.ones((1,), jnp.bool_), segment[1:] != segment[:-1]])
    return (segment, opening)


def add_up(earlier, later):
    return earlier + later


def per_token_device(
    layer_input,
    doc_lengths,
    ln1_gain,
    ln1_bias,
    w_qkv,
    w_out,
    ln2_gain,
    ln2_bias,
    w_up,
    b_up,
    w_down,
    cotangent,
):
    micro_count = layer_input.shape[0]
    query_rows = layer_input.shape[2]
    model_width = layer_input.shape[3]
    head_count = model_width // HD
    row_length = query_rows * lax.axis_size("ctx")
    key_block = min(512, row_length)
    score_scale = HD ** (-0.5)
    strength = 8.0 / row_length
    ctx_place = lax.axis_index("ctx")
    query_pos = ctx_place * query_rows + jnp.arange(query_rows, dtype=jnp.int32)
    block_total = ((ctx_place + 1) * query_rows + key_block - 1) // key_block
    later_heads = (jnp.arange(head_count) > 0).astype(jnp.float32)[:, None, None]
    zeros_row = jnp.zeros((row_length,), jnp.float32)
    gelu_exact = partial(jax.nn.gelu, approximate=False)
    output_list = []
    input_grads = []
    matrix_total = None
    vector_total = None
    for micro_step in range(micro_count):
        w_qkv_all, w_out_all, w_up_all, w_down_all = (
            lax.all_gather(w_qkv, "dp", axis=0, tiled=True),
            lax.all_gather(w_out, "dp", axis=0, tiled=True),
            lax.all_gather(w_up, "dp", axis=0, tiled=True),
            lax.all_gather(w_down, "dp", axis=0, tiled=True),
        )
        inputs = layer_input[micro_step, 0].astype(jnp.float32)
        segment, opening = segment_table(doc_lengths[micro_step, 0], row_length)
        query_seg = lax.dynamic_slice_in_dim(segment, ctx_place * query_rows, query_rows, 0)
        normed_one = layer_norm(inputs, ln1_gain, ln1_bias).astype(jnp.bfloat16)
        projected = matmul(normed_one, w_qkv_all).astype(jnp.bfloat16)
        queries = projected[:, :model_width]
        queries3 = queries.reshape(query_rows, head_count, HD)
        query_zero = queries[:, :HD]
        keys_all, values_all = (
            lax.all_gather(projected[:, model_width : 2 * model_width], "ctx", axis=0, tiled=True),
            lax.all_gather(projected[:, 2 * model_width :], "ctx", axis=0, tiled=True),
        )

        def masks(key_start):
            key_seg = lax.dynamic_slice_in_dim(segment, key_start, key_block, 0)
            key_open = lax.dynamic_slice_in_dim(opening, key_start, key_block, 0)
            key_pos = key_start + jnp.arange(key_block, dtype=jnp.int32)
            same_doc = query_seg[:, None] == key_seg[None, :]
            allowed = same_doc & (key_pos[None, :] <= query_pos[:, None])
            chosen = (
                same_doc
                & (key_pos[None, :] < query_pos[:, None])
                & jnp.logical_not(key_open)[None, :]
            )
            return (allowed, chosen.astype(jnp.float32))

        def head_scores(key_start):
            key_zero = lax.dynamic_slice_in_dim(keys_all, key_start, key_block, 0)[:, :HD]
            return (key_zero, contract_cols(query_zero, key_zero) * score_scale)

        def block_keys(key_start):
            keys3 = lax.dynamic_slice_in_dim(keys_all, key_start, key_block, 0).reshape(
                key_block, head_count, HD
            )
            values3 = lax.dynamic_slice_in_dim(values_all, key_start, key_block, 0).reshape(
                key_block, head_count, HD
            )
            return (keys3, values3)

        def logits_of(key_start, keys3):
            allowed, chosen = masks(key_start)
            raw_scores = (
                jnp.einsum("qhd,khd->hqk", queries3, keys3, preferred_element_type=jnp.float32)
                * score_scale
            )
            picked = strength * jax.nn.softplus(raw_scores[0]) * chosen
            before = lax.dynamic_slice_in_dim(prefix, key_start, key_block, 0)
            penalty = before[None, :] + jnp.cumsum(picked, axis=0) - picked
            return jnp.where(allowed[None], raw_scores - penalty[None], MASKED)

        def total_block(block_index, totals):
            key_start = block_index * key_block
            _, chosen = masks(key_start)
            _, first_scores = head_scores(key_start)
            picked = strength * jax.nn.softplus(first_scores) * chosen
            return lax.dynamic_update_slice_in_dim(totals, jnp.sum(picked, axis=0), key_start, 0)

        totals = lax.fori_loop(0, block_total, total_block, zeros_row)
        prefix = prefix_2(totals, "ctx", add_up, zeros_row, False)

        def stat_block(block_index, running):
            row_top, row_total = running
            key_start = block_index * key_block
            keys3, _ = block_keys(key_start)
            logits = logits_of(key_start, keys3)
            new_top = jnp.maximum(row_top, jnp.max(logits, axis=-1))
            row_total = row_total * jnp.exp(row_top - new_top) + jnp.sum(
                jnp.exp(logits - new_top[..., None]), axis=-1
            )
            return (new_top, row_total)

        row_top, row_total = lax.fori_loop(
            0,
            block_total,
            stat_block,
            (
                jnp.full((head_count, query_rows), START_TOP, jnp.float32),
                jnp.zeros((head_count, query_rows), jnp.float32),
            ),
        )
        log_total = row_top + jnp.log(row_total)

        def out_block(block_index, gathered_out):
            key_start = block_index * key_block
            keys3, values3 = block_keys(key_start)
            attn_probs = jnp.exp(logits_of(key_start, keys3) - log_total[..., None]).astype(
                jnp.bfloat16
            )
            return gathered_out + jnp.einsum(
                "hqk,khd->qhd", attn_probs, values3, preferred_element_type=jnp.float32
            )

        gathered_out = lax.fori_loop(
            0, block_total, out_block, jnp.zeros((query_rows, head_count, HD), jnp.float32)
        )
        attended = gathered_out.reshape(query_rows, model_width).astype(jnp.bfloat16)
        mid_stream = inputs + matmul(attended, w_out_all)
        normed_two = layer_norm(mid_stream, ln2_gain, ln2_bias).astype(jnp.bfloat16)
        hidden = matmul(normed_two, w_up_all) + b_up
        activated = gelu_exact(hidden).astype(jnp.bfloat16)
        output_list.append((mid_stream + matmul(activated, w_down_all)).astype(jnp.bfloat16))
        cot_rows = cotangent[micro_step, 0]
        grad_down = contract_rows(activated, cot_rows)
        grad_act = contract_cols(cot_rows, w_down_all)
        _, gelu_back = jax.vjp(gelu_exact, hidden)
        grad_hidden = gelu_back(grad_act)[0].astype(jnp.bfloat16)
        grad_up = contract_rows(normed_two, grad_hidden)
        grad_bias_up = jnp.sum(grad_hidden.astype(jnp.float32), axis=0)
        grad_normed_two = contract_cols(grad_hidden, w_up_all)
        _, norm_two_back = jax.vjp(layer_norm, mid_stream, ln2_gain, ln2_bias)
        grad_mid_part, grad_gain_two, grad_bias_two = norm_two_back(grad_normed_two)
        grad_mid = cot_rows.astype(jnp.float32) + grad_mid_part
        grad_branch = grad_mid.astype(jnp.bfloat16)
        grad_outproj = contract_rows(attended, grad_branch)
        grad_attended = contract_cols(grad_branch, w_out_all).astype(jnp.bfloat16)
        grad_att3 = grad_attended.reshape(query_rows, head_count, HD)
        row_delta = jnp.einsum("qhd,qhd->hq", grad_att3.astype(jnp.float32), gathered_out)

        def grad_block(block_index, running):
            grad_query, grad_key_all, grad_value_all, penalty_grad, first_grad = running
            key_start = block_index * key_block
            keys3, values3 = block_keys(key_start)
            probs_f32 = jnp.exp(logits_of(key_start, keys3) - log_total[..., None])
            grad_probs = jnp.einsum(
                "qhd,khd->hqk", grad_att3, values3, preferred_element_type=jnp.float32
            )
            grad_logits = probs_f32 * (grad_probs - row_delta[..., None])
            penalty_grad = lax.dynamic_update_slice_in_dim(
                penalty_grad, -jnp.sum(grad_logits, axis=0), key_start, 1
            )
            first_grad = lax.dynamic_update_slice_in_dim(first_grad, grad_logits[0], key_start, 1)
            grad_scores = (grad_logits * later_heads).astype(jnp.bfloat16)
            grad_query = (
                grad_query
                + jnp.einsum("hqk,khd->qhd", grad_scores, keys3, preferred_element_type=jnp.float32)
                * score_scale
            )
            key_part = (
                jnp.einsum(
                    "hqk,qhd->khd", grad_scores, queries3, preferred_element_type=jnp.float32
                )
                * score_scale
            )
            value_part = jnp.einsum(
                "hqk,qhd->khd",
                probs_f32.astype(jnp.bfloat16),
                grad_att3,
                preferred_element_type=jnp.float32,
            )
            grad_key_all = lax.dynamic_update_slice_in_dim(
                grad_key_all, key_part.reshape(key_block, model_width), key_start, 0
            )
            grad_value_all = lax.dynamic_update_slice_in_dim(
                grad_value_all, value_part.reshape(key_block, model_width), key_start, 0
            )
            return (grad_query, grad_key_all, grad_value_all, penalty_grad, first_grad)

        grad_query, grad_key_all, grad_value_all, penalty_grad, first_grad = lax.fori_loop(
            0,
            block_total,
            grad_block,
            (
                jnp.zeros((query_rows, head_count, HD), jnp.float32),
                jnp.zeros((row_length, model_width), jnp.float32),
                jnp.zeros((row_length, model_width), jnp.float32),
                jnp.zeros((query_rows, row_length), jnp.float32),
                jnp.zeros((query_rows, row_length), jnp.float32),
            ),
        )
        column_sums = jnp.sum(penalty_grad, axis=0)
        after = prefix_2(column_sums, "ctx", add_up, zeros_row, True)
        reach_sums = after + column_sums

        def head_block(block_index, running):
            grad_query_zero, grad_key_all = running
            key_start = block_index * key_block
            _, chosen = masks(key_start)
            key_zero, first_scores = head_scores(key_start)
            flow_block = lax.dynamic_slice_in_dim(penalty_grad, key_start, key_block, 1)
            reach_block = lax.dynamic_slice_in_dim(reach_sums, key_start, key_block, 0)
            grad_picked = reach_block[None, :] - jnp.cumsum(flow_block, axis=0)
            grad_select = grad_picked * strength * jax.nn.sigmoid(first_scores) * chosen
            grad_head = (
                lax.dynamic_slice_in_dim(first_grad, key_start, key_block, 1) + grad_select
            ).astype(jnp.bfloat16)
            grad_query_zero = grad_query_zero + matmul(grad_head, key_zero) * score_scale
            key_zero_grad = contract_rows(grad_head, query_zero) * score_scale
            grad_key_all = lax.dynamic_update_slice(
                grad_key_all, key_zero_grad, (key_start, jnp.zeros((), jnp.int32))
            )
            return (grad_query_zero, grad_key_all)

        grad_query_zero, grad_key_all = lax.fori_loop(
            0, block_total, head_block, (jnp.zeros((query_rows, HD), jnp.float32), grad_key_all)
        )
        grad_query = grad_query.at[:, 0, :].add(grad_query_zero).reshape(query_rows, model_width)
        grad_key_own, grad_value_own = (
            lax.psum_scatter(grad_key_all, "ctx", scatter_dimension=0, tiled=True),
            lax.psum_scatter(grad_value_all, "ctx", scatter_dimension=0, tiled=True),
        )
        grad_project = jnp.concatenate([grad_query, grad_key_own, grad_value_own], axis=1).astype(
            jnp.bfloat16
        )
        grad_qkv = contract_rows(normed_one, grad_project)
        grad_normed_one = contract_cols(grad_project, w_qkv_all)
        _, norm_one_back = jax.vjp(layer_norm, inputs, ln1_gain, ln1_bias)
        grad_in_part, grad_gain_one, grad_bias_one = norm_one_back(grad_normed_one)
        input_grads.append((grad_mid + grad_in_part).astype(jnp.bfloat16))
        matrix_grads = (grad_qkv, grad_outproj, grad_up, grad_down)
        vector_grads = (grad_gain_one, grad_bias_one, grad_gain_two, grad_bias_two, grad_bias_up)
        matrix_grads = (
            lax.psum_scatter(matrix_grads[0], "ctx", scatter_dimension=1, tiled=True),
            lax.psum_scatter(matrix_grads[1], "ctx", scatter_dimension=1, tiled=True),
            lax.psum_scatter(matrix_grads[2], "ctx", scatter_dimension=1, tiled=True),
            lax.psum_scatter(matrix_grads[3], "ctx", scatter_dimension=1, tiled=True),
        )
        matrix_grads = (
            lax.psum_scatter(
                matrix_grads[0].astype(jnp.bfloat16), "dp", scatter_dimension=0, tiled=True
            ).astype(jnp.float32),
            lax.psum_scatter(
                matrix_grads[1].astype(jnp.bfloat16), "dp", scatter_dimension=0, tiled=True
            ).astype(jnp.float32),
            lax.psum_scatter(
                matrix_grads[2].astype(jnp.bfloat16), "dp", scatter_dimension=0, tiled=True
            ).astype(jnp.float32),
            lax.psum_scatter(
                matrix_grads[3].astype(jnp.bfloat16), "dp", scatter_dimension=0, tiled=True
            ).astype(jnp.float32),
        )
        vector_grads = lax.psum(
            (vector_grads[0], vector_grads[1], vector_grads[2], vector_grads[3], vector_grads[4]),
            ("dp", "ctx"),
        )
        if matrix_total is None:
            matrix_total = matrix_grads
            vector_total = vector_grads
        else:
            matrix_total = tuple((old + new for old, new in zip(matrix_total, matrix_grads)))
            vector_total = tuple((old + new for old, new in zip(vector_total, vector_grads)))
    layer_out = jnp.stack(output_list)[:, None]
    input_out = jnp.stack(input_grads)[:, None]
    return (
        layer_out,
        input_out,
        vector_total[0],
        vector_total[1],
        matrix_total[0],
        matrix_total[1],
        vector_total[2],
        vector_total[3],
        matrix_total[2],
        vector_total[4],
        matrix_total[3],
    )


MESH = pl.DeviceIdType.MESH
EXCLUDED = 1e30
QUERY_BLOCK = 256


def norm_parts(value):
    row_mean = jnp.mean(value, axis=-1, keepdims=True)
    centered = value - row_mean
    spread = jnp.mean(centered * centered, axis=-1, keepdims=True)
    inverse = lax.rsqrt(spread + NORM_EPSILON)
    return centered * inverse, inverse


def norm_back(xhat, inverse, grad, gain):
    scaled = grad * gain
    return (
        scaled
        - jnp.mean(scaled, axis=-1, keepdims=True)
        - xhat * jnp.mean(scaled * xhat, axis=-1, keepdims=True)
    ) * inverse


class Wires:
    def __init__(self, send_sem, recv_sem):
        self.send_sem, self.recv_sem, self.used, self.made = send_sem, recv_sem, 0, []

    def send(self, source, target, where):
        copy = pltpu.make_async_remote_copy(
            src_ref=source,
            dst_ref=target,
            send_sem=self.send_sem.at[self.used],
            recv_sem=self.recv_sem.at[self.used],
            device_id=where,
            device_id_type=MESH,
        )
        copy.start()
        self.used += 1
        self.made.append(copy)
        return copy

    def later(self, source, target, where):
        copy = pltpu.make_async_remote_copy(
            src_ref=source,
            dst_ref=target,
            send_sem=self.send_sem.at[self.used],
            recv_sem=self.recv_sem.at[self.used],
            device_id=where,
            device_id_type=MESH,
        )
        self.used += 1
        self.made.append(copy)
        return copy

    def drain(self):
        for copy in self.made:
            copy.wait_send()


def rounded(value):
    return value.astype(jnp.bfloat16)


def folded(array):
    half = array.shape[0] // 2
    return jnp.concatenate([array[:half], array[half:]], axis=1)


def unfolded(array):
    half = array.shape[1] // 2
    return jnp.concatenate([array[:, :half], array[:, half:]], axis=0)


def arrived(like, target, sem):
    pltpu.make_async_copy(like, target, sem).wait()


def swap(index):
    return index + 1 - 2 * lax.rem(index, 2)


def layer_body(plan, loaded, names, lengths, *refs):
    given, refs = refs[: len(loaded)], refs[len(loaded) :]
    r = SimpleNamespace(**dict(zip(names, refs)))
    groups, shards = plan
    f32 = jnp.float32
    ctx, dp = lax.axis_index("ctx"), lax.axis_index("dp")
    ctx_size, tokens, model = r.x_row.shape
    width = r.out.shape[1]
    lines = ctx_size // 2
    mbs = ctx_size // groups
    hpg = width // HD
    own = r.x.shape[0]
    ff = r.w_down.shape[0]
    row_length = tokens * ctx_size
    side, line = lax.rem(ctx, 2), ctx // 2
    my_mb, my_group = ctx // groups, lax.rem(ctx, groups)
    wires = Wires(r.send_sem, r.recv_sem)
    core, far, far_core = {"dp": swap(dp)}, {"dp": lax.rem(dp + 2, 4)}, {"dp": lax.rem(swap(dp) + 2, 4)}
    beside = {"ctx": swap(ctx)}
    up_to = {"dp": lax.rem(ctx, 4), "ctx": shards * dp + ctx // 4}
    up_from = {"dp": ctx // shards, "ctx": lax.rem(ctx, shards) * 4 + dp}
    around = [{"ctx": lax.rem(ctx + step, ctx_size)} for step in range(1, ctx_size)]

    mirror = {"ctx": lax.rem(line + lines // 2, lines) * 2 + side}
    ahead = {"ctx": swap(line) * 2 + side}
    beside_at, mirror_at, ahead_at = beside["ctx"], mirror["ctx"], ahead["ctx"]
    half = tokens // 4

    loads = SimpleNamespace()
    for at, name in enumerate(loaded):
        copy = pltpu.make_async_copy(given[at], getattr(r, name), r.load_sem.at[at])
        copy.start()
        setattr(loads, name, copy)
    barrier = pltpu.get_barrier_semaphore()
    for where in around + [core, far, far_core, up_from]:
        pl.semaphore_signal(barrier, inc=1, device_id=where, device_id_type=MESH)
    loads.x.wait()
    loads.w_qkv.wait()
    pl.semaphore_wait(barrier, ctx_size + 3)

    def x_of(micro):
        return r.x.at[pl.ds(pl.multiple_of(micro * tokens, tokens), tokens)]

    x_mirror = wires.send(x_of(1 - my_mb), r.x_row.at[ctx], mirror)
    x_beside = wires.send(x_of(my_mb), r.x_row.at[ctx], beside)
    x_ahead = wires.send(x_of(my_mb), r.x_row.at[ctx], ahead)
    for group in range(groups):

        @pl.when(my_group == group)
        def _():
            for kind in range(3):
                first = kind * model + group * width
                r.w_pick[dp, :, kind * width : (kind + 1) * width] = r.w_qkv[:, first : first + width]

    for kind in range(2):
        r.w_pick[dp, :, 3 * width + kind * HD : 3 * width + (kind + 1) * HD] = r.w_qkv[
            :, kind * model : kind * model + HD
        ]
    pick_far = wires.send(r.w_pick.at[dp], r.w_pick.at[dp], far)
    pick_core = wires.send(r.w_pick.at[dp], r.w_pick.at[dp], core)
    r.x_row[ctx] = x_of(my_mb)[...]

    for copy in (loads.cot, loads.w_out_own, loads.w_up_own):
        copy.wait()

    def rows_of(place):
        return pl.ds(pl.multiple_of(place * size_dp, size_dp), size_dp)

    size_dp = model // 4
    wout_far = wires.send(r.w_out_own, r.w_out.at[rows_of(dp)], far)
    wout_core = wires.send(r.w_out_own, r.w_out.at[rows_of(dp)], core)

    def up_part(peer):
        return r.w_up_own.at[:, pl.ds(pl.multiple_of(peer * ff, 128), ff)]

    up_in = [
        wires.send(up_part(where["dp"]), r.w_up.at[rows_of(dp)], where)
        for where in (far, far_core, core)
    ]
    cot_far = wires.send(r.cot, r.cots.at[2], far)
    cot_core = wires.send(r.cot, r.cots.at[1], core)
    r.w_out[rows_of(dp), :] = r.w_out_own[...]
    r.w_up[rows_of(dp), :] = up_part(dp)[...]
    r.cots[0] = r.cot[...]

    loads.gain_one.wait()
    loads.bias_one.wait()
    gain_one = r.gain_one[...].reshape(1, model)
    bias_one = r.bias_one[...].reshape(1, model)

    def normalise(place):
        xhat, _ = norm_parts(r.x_row[place].astype(f32))
        rows = pl.ds(pl.multiple_of(place * tokens, tokens), tokens)
        r.hat_one[rows, :] = rounded(xhat)
        r.normed_one[rows, :] = rounded(xhat * gain_one + bias_one)

    x_beside.wait_recv()
    top, bottom = pl.ds(0, half), pl.ds(half, tokens - half)
    x_fwd_a = wires.send(r.x_row.at[beside_at, top], r.x_row.at[beside_at, top], ahead)
    x_ahead.wait_recv()
    x_fwd_b = wires.send(r.x_row.at[ahead_at, bottom], r.x_row.at[ahead_at, bottom], beside)
    normalise(ctx)
    x_mirror.wait_recv()
    x_mirror_beside = wires.send(r.x_row.at[mirror_at], r.x_row.at[mirror_at], beside)
    x_mirror_ahead = wires.send(r.x_row.at[mirror_at], r.x_row.at[mirror_at], ahead)
    pick_far.wait_recv()
    pick_at = far["dp"]
    pick_fwd = wires.send(r.w_pick.at[pick_at], r.w_pick.at[pick_at], core)

    normalise(beside_at)
    normalise(ahead_at)
    normalise(mirror_at)
    x_mirror_beside.wait_recv()
    place = swap(mirror_at)
    x_fwd_c = wires.send(r.x_row.at[place, top], r.x_row.at[place, top], ahead)
    x_mirror_ahead.wait_recv()
    place = lax.rem(ahead_at + ctx_size // 2, ctx_size)
    x_fwd_d = wires.send(r.x_row.at[place, bottom], r.x_row.at[place, bottom], beside)
    normalise(swap(mirror_at))
    normalise(place)
    x_fwd_a.wait_recv()
    x_fwd_b.wait_recv()
    normalise(swap(ahead_at))
    pick_core.wait_recv()
    pick_fwd.wait_recv()
    x_fwd_c.wait_recv()
    x_fwd_d.wait_recv()
    normalise(swap(place))
    w_pick = r.w_pick[...].reshape(model, 3 * width + 2 * HD)
    r.proj[...] = rounded(matmul(r.normed_one[...], w_pick))

    def att_copy(place):
        return pltpu.make_async_remote_copy(
            src_ref=r.att.at[place],
            dst_ref=r.att_in.at[ctx],
            send_sem=r.att_send.at[place],
            recv_sem=r.att_recv.at[ctx],
            device_id={"ctx": place},
            device_id_type=MESH,
        )

    block = QUERY_BLOCK
    per_block = block // tokens
    scale = HD ** (-0.5)
    strength = 8.0 / row_length
    row_at = lax.broadcasted_iota(jnp.int32, (block, block), 0)
    col_at = lax.broadcasted_iota(jnp.int32, (block, block), 1)
    earlier = (col_at < row_at).astype(jnp.bfloat16)
    later = (col_at > row_at).astype(jnp.bfloat16)
    doc_ends, doc_end = [], 0
    for at in range(lengths.shape[2]):
        doc_end = doc_end + lengths[my_mb, 0, at]
        doc_ends.append(doc_end)

    def segment_of(places):
        total = jnp.zeros(places.shape, jnp.int32)
        for end in doc_ends:
            total += jnp.where(places >= end, 1, 0)
        return total

    r.suffix[...] = jnp.zeros_like(r.suffix)
    for start in range(0, row_length, block):
        reach = start + block
        rows = pl.ds(start, block)
        probs_ref, slope_ref = getattr(r, "probs%d" % start), getattr(r, "slope%d" % start)
        row_pos = start + lax.broadcasted_iota(jnp.int32, (block, 1), 0)
        col_pos = lax.broadcasted_iota(jnp.int32, (1, reach), 1)
        row_seg, col_seg = segment_of(row_pos), segment_of(col_pos)
        opening = (col_seg != segment_of(col_pos - 1)) | (col_pos == 0)
        pick_seg = jnp.where(opening, -1, col_seg)
        query = rounded(r.proj[rows, 3 * width : 3 * width + HD] * scale)
        key = r.proj[:reach, 3 * width + HD : 3 * width + 2 * HD]
        scores = contract_cols(query, key)
        small = jnp.exp(-jnp.abs(scores))
        soft = jnp.maximum(scores, 0.0) + jnp.log(1.0 + small)
        recip = 1.0 / (1.0 + small)
        sigmoid = jnp.where(scores >= 0.0, recip, small * recip)
        chosen = (row_seg == pick_seg) & (col_pos < row_pos)
        picked = jnp.where(chosen, strength * soft, 0.0)
        slope_ref[...] = rounded(jnp.where(chosen, strength * sigmoid, 0.0))
        high = rounded(picked)
        low = rounded(picked - high.astype(f32))
        penalty = r.suffix[:, :reach] + (matmul(earlier, high) + matmul(earlier, low))
        allowed = (row_seg == col_seg) & (col_pos <= row_pos)
        penalty = jnp.where(allowed, penalty, EXCLUDED)
        r.suffix[:, :reach] += jnp.sum(picked, axis=0, keepdims=True)
        for head in range(hpg):
            at = head * HD
            query = rounded(r.proj[rows, at : at + HD] * scale)
            key = r.proj[:reach, width + at : width + at + HD]
            value = r.proj[:reach, 2 * width + at : 2 * width + at + HD]
            logits = contract_cols(query, key) - penalty
            top_logit = jnp.max(logits, axis=1, keepdims=True)
            probs = jnp.exp(logits - top_logit)
            inverse = 1.0 / jnp.sum(probs, axis=1, keepdims=True)
            probs = rounded(probs)
            probs_ref[head] = probs
            r.out[rows, at : at + HD] = matmul(probs, value) * inverse
            r.inverse[rows, head : head + 1] = inverse
        for step in range(per_block):
            place = start // tokens + step
            r.att[place] = folded(rounded(r.out[place * tokens : (place + 1) * tokens, :]))
            copy = att_copy(place)

            @pl.when(ctx != place)
            def _():
                copy.start()

    r.att_in[ctx] = r.att[ctx]
    cot_far.wait_recv()
    cot_fwd = wires.send(r.cots.at[2], r.cots.at[3], core)
    wout_far.wait_recv()
    out_at = rows_of(far["dp"])
    wout_fwd = wires.send(r.w_out.at[out_at], r.w_out.at[out_at], core)
    for copy in up_in:
        copy.wait_recv()
    wout_core.wait_recv()
    wout_fwd.wait_recv()
    for copy in (loads.gain_two, loads.bias_two, loads.w_down, loads.b_up):
        copy.wait()
    for step in range(1, ctx_size):
        place = lax.rem(ctx + step, ctx_size)
        arrived(r.att.at[0], r.att_in.at[place], r.att_recv.at[place])
    for place in range(ctx_size):
        r.att_got[place] = unfolded(r.att_in[place])

    gain = r.gain_two[...].reshape(1, model)
    bias = r.bias_two[...].reshape(1, model)
    for at in range(4):

        @pl.when(dp == at)
        def _():
            r.b_own[...] = r.b_up[at * ff : (at + 1) * ff].reshape(1, ff)

    for micro in range(mbs):
        rows = pl.ds(micro * tokens, tokens)
        stream = r.x[rows, :].astype(f32)
        for group in range(groups):
            stream += matmul(
                r.att_got[micro * groups + group], r.w_out[pl.ds(group * width, width), :]
            )
        r.mid[rows, :] = stream
    xhat, inverse_two = norm_parts(r.mid[...])
    r.hat_two[...] = xhat
    r.normed[0] = rounded(xhat * gain + bias)
    to_core = wires.send(r.normed.at[0], r.normed.at[1], core)
    to_far = wires.send(r.normed.at[0], r.normed.at[2], far)

    def feed(slot):
        hidden = matmul(r.normed[slot], r.w_up[...]) + r.b_own[...]
        cdf = 0.5 * (1.0 + lax.erf(hidden * (2.0**-0.5)))
        density = jnp.exp(-0.5 * hidden * hidden) * ((2.0 * math.pi) ** -0.5)
        r.act[slot] = rounded(hidden * cdf)
        grad = contract_cols(r.cots[slot], r.w_down[...])
        r.grad_hid[slot] = rounded(grad * (cdf + hidden * density))
        r.part[slot] = rounded(contract_cols(r.grad_hid[slot], r.w_up[...]))

    def feed_out(slot):
        r.out_part[slot] = rounded(matmul(r.act[slot], r.w_down[...]))

    part_core, part_far_core, forward = (
        wires.later(r.part.at[1], r.part_got.at[0], core),
        wires.later(r.part.at[3], r.part_got.at[1], core),
        wires.later(r.normed.at[2], r.normed.at[3], core),
    )

    def feed_step(slot, carry):
        @pl.when(slot == 1)
        def _():
            cot_core.wait_recv()
            to_core.wait_recv()

        @pl.when(slot == 2)
        def _():
            part_core.start()
            to_far.wait_recv()
            forward.start()

        @pl.when(slot == 3)
        def _():
            forward.wait_recv()
            cot_fwd.wait_recv()

        feed(slot)
        return carry

    lax.fori_loop(0, 4, feed_step, 0)
    part_far_core.start()
    part_far_core.wait_recv()
    r.part[2] = rounded(r.part[2].astype(f32) + r.part_got[1].astype(f32))
    part_far = wires.send(r.part.at[2], r.part_got.at[2], far)
    pair = line // 2
    collects = lax.rem(line, 2) == 1 - pair
    other = pl.ds((1 - pair) * 2, 2)

    def line_copies(at, grad, near, distant, shared):
        def copy(source, target, kind, index, to_line):
            return pltpu.make_async_remote_copy(
                src_ref=source,
                dst_ref=target,
                send_sem=r.line_send.at[at, index],
                recv_sem=r.line_recv.at[at, kind],
                device_id={"ctx": to_line * 2 + side},
                device_id_type=MESH,
            )

        to_near = copy(grad.at[side, swap(line)], near, 0, 0, swap(line))
        to_shared = copy(grad.at[side, other], shared, 1, 1, swap(line))
        to_distant = [
            copy(grad.at[side, (1 - pair) * 2 + step], distant, 2, 1 + step, (1 - pair) * 2 + step)
            for step in range(2)
        ]
        return to_near, to_shared, to_distant

    def line_start(at, side_copy, side_got, grad, *targets):
        side_copy.wait_recv()
        grad[side] = rounded(grad[side].astype(f32) + side_got[...].astype(f32))
        to_near, to_shared, _ = line_copies(at, grad, *targets)
        to_near.start()

        @pl.when(jnp.logical_not(collects))
        def _():
            to_shared.start()

    def line_collect(at, grad, near, distant, shared):
        _, _, to_distant = line_copies(at, grad, near, distant, shared)

        @pl.when(collects)
        def _():
            arrived(grad.at[side, other], shared, r.line_recv.at[at, 1])
            grad[side, other] = rounded(grad[side, other].astype(f32) + shared[...].astype(f32))
            for copy in to_distant:
                copy.start()

    def line_finish(at, grad, near, distant, shared):
        arrived(near, near, r.line_recv.at[at, 0])
        arrived(distant, distant, r.line_recv.at[at, 2])
        return grad[side, line].astype(f32) + near[...].astype(f32) + distant[...].astype(f32)

    def line_drain(at, grad, near, distant, shared):
        to_near, to_shared, to_distant = line_copies(at, grad, near, distant, shared)
        to_near.wait_send()

        @pl.when(jnp.logical_not(collects))
        def _():
            to_shared.wait_send()

        @pl.when(collects)
        def _():
            for copy in to_distant:
                copy.wait_send()

    down_refs = (0, r.down_grad, r.down_near, r.down_distant, r.down_shared)
    up_refs = (1, r.up_grad, r.up_near, r.up_distant, r.up_shared)
    out_refs = (2, r.out_piece, r.out_near, r.out_distant, r.out_shared)

    def start_line(refs, side_copy, side_got):
        line_start(refs[0], side_copy, side_got, *refs[1:])

    flat_cot = r.cots[...].reshape(4 * own, model)
    flat_act = r.act[...].reshape(4 * own, ff)
    grads = rounded(contract_rows(flat_cot, flat_act))
    narrow = model // ctx_size
    for at in range(ctx_size):
        r.down_grad[at % 2, at // 2] = grads[at * narrow : (at + 1) * narrow]
    down_side = wires.send(r.down_grad.at[1 - side], r.down_side, beside)
    out_core, out_far_core = (
        wires.later(r.out_part.at[1], r.out_got.at[0], core),
        wires.later(r.out_part.at[3], r.out_got.at[1], core),
    )

    def out_step(step, carry):
        slot = 3 - step
        feed_out(slot)

        @pl.when(slot == 3)
        def _():
            out_far_core.start()

        @pl.when(slot == 1)
        def _():
            out_core.start()

        return carry

    lax.fori_loop(0, 4, out_step, 0)
    flat_grad = r.grad_hid[...].reshape(4 * own, ff)
    vec_rows = 4 + ff // model
    d_bias_up = jnp.sum(flat_grad.astype(f32), axis=0, keepdims=True)
    for at in range(ff // model):
        r.vec[4 + at : 5 + at, :] = d_bias_up[:, at * model : (at + 1) * model]
    flat_normed = r.normed[...].reshape(4 * own, model)
    size = model // 4
    for at in range(shards):
        grads = rounded(
            contract_rows(flat_normed, flat_grad[:, at * ff // shards : (at + 1) * ff // shards])
        )
        for row in range(4):
            index = at * 4 + row
            r.up_grad[index % 2, index // 2] = grads[row * size : (row + 1) * size]
    out_far_core.wait_recv()
    r.out_part[2] = rounded(r.out_part[2].astype(f32) + r.out_got[1].astype(f32))

    part_core.wait_recv()
    part_far.wait_recv()
    out_far = wires.send(r.out_part.at[2], r.out_got.at[2], far)
    grad_normed = r.part[0].astype(f32) + r.part_got[0].astype(f32) + r.part_got[2].astype(f32)
    xhat = r.hat_two[...]
    r.vec[2:3, :] = jnp.sum(grad_normed * xhat, axis=0, keepdims=True)
    r.vec[3:4, :] = jnp.sum(grad_normed, axis=0, keepdims=True)
    r.grad_mid[...] = r.cot[...].astype(f32) + norm_back(xhat, inverse_two, grad_normed, gain)
    branch = rounded(r.grad_mid[...])
    for group in range(groups):
        grad = rounded(contract_cols(branch, r.w_out[pl.ds(group * width, width), :]))
        for micro in range(mbs):
            r.att_out[micro * groups + group] = folded(
                grad[micro * tokens : (micro + 1) * tokens]
            )
    att_in = []
    for step in range(1, ctx_size):
        peer = lax.rem(ctx + step, ctx_size)
        att_in.append(wires.send(r.att_out.at[peer], r.grad_in.at[ctx], {"ctx": peer}))
    r.grad_in[ctx] = r.att_out[ctx]
    for group in range(groups):
        total = None
        for micro in range(mbs):
            some = contract_rows(
                branch[micro * tokens : (micro + 1) * tokens], r.att_got[micro * groups + group]
            )
            total = some if total is None else total + some
        total = rounded(total)
        for at in range(ctx_size):
            r.out_grad[group, at % 2, at // 2] = folded(total[at * narrow : (at + 1) * narrow])
    out_grad_core = wires.send(r.out_grad.at[swap(dp)], r.out_grad_got.at[0], core)
    out_grad_far_core = wires.send(
        r.out_grad.at[lax.rem(swap(dp) + 2, 4)], r.out_grad_got.at[1], core
    )
    out_grad_far_core.wait_recv()
    mine = lax.rem(dp + 2, 4)
    r.out_grad[mine] = rounded(r.out_grad[mine].astype(f32) + r.out_grad_got[1].astype(f32))
    out_grad_far = wires.send(r.out_grad.at[mine], r.out_grad_got.at[2], far)
    up_side = wires.send(r.up_grad.at[1 - side], r.up_side, beside)
    start_line(down_refs, down_side, r.down_side)
    for copy in att_in:
        copy.wait_recv()
    for place in range(ctx_size):
        r.grad_att[place] = unfolded(r.grad_in[place])

    r.suffix[...] = jnp.zeros_like(r.suffix)
    r.acc[...] = jnp.zeros_like(r.acc)

    def back_block(start):
        reach = start + block
        rows = pl.ds(start, block)
        probs_ref, slope_ref = getattr(r, "probs%d" % start), getattr(r, "slope%d" % start)
        total = None
        first = start // tokens
        grad_block = r.grad_att[first : first + per_block].reshape(block, width)
        for head in range(hpg):
            at = head * HD
            query_t = rounded((r.proj[rows, at : at + HD].astype(f32) * scale).T)
            key = r.proj[:reach, width + at : width + at + HD]
            value = r.proj[:reach, 2 * width + at : 2 * width + at + HD]
            grad = grad_block[:, at : at + HD].astype(f32) * r.inverse[rows, head : head + 1]
            delta = jnp.sum(grad * r.out[rows, at : at + HD], axis=1, keepdims=True)
            probs = probs_ref[head]
            grad_probs = contract_cols(rounded(grad), value)
            grad_logits = probs.astype(f32) * (grad_probs - delta)
            total = grad_logits if total is None else total + grad_logits
            grad_scores = rounded(grad_logits)
            r.grad_proj[rows, at : at + HD] = rounded(matmul(grad_scores, key) * scale)
            r.acc[at : at + HD, :reach] += matmul(query_t, grad_scores)
            r.acc[width + at : width + at + HD, :reach] += matmul(rounded(grad.T), probs)
        query_t = rounded((r.proj[rows, 3 * width : 3 * width + HD].astype(f32) * scale).T)
        key = r.proj[:reach, 3 * width + HD : 3 * width + 2 * HD]
        flow = r.suffix[:, :reach] + matmul(later, rounded(total))
        grad_scores = rounded(-flow * slope_ref[...].astype(f32))
        r.grad_proj[rows, 3 * width : 3 * width + HD] = rounded(matmul(grad_scores, key) * scale)
        r.acc[2 * width : 2 * width + HD, :reach] += matmul(query_t, grad_scores)
        r.suffix[:, :reach] += jnp.sum(total, axis=0, keepdims=True)

    def one_grad(place):
        rows = pl.ds(pl.multiple_of(place * tokens, tokens), tokens)
        grad = contract_cols(r.grad_proj[rows, :], r.w_pick[...].reshape(model, 3 * width + 2 * HD))
        r.vec[0:1, :] += jnp.sum(grad * r.hat_one[rows, :].astype(f32), axis=0, keepdims=True)
        r.vec[1:2, :] += jnp.sum(grad, axis=0, keepdims=True)
        return grad

    r.vec[0:2, :] = jnp.zeros((2, model), f32)
    one_side = {}

    def one_copy(source, target, kind, at, to_line):
        return pltpu.make_async_remote_copy(
            src_ref=source,
            dst_ref=target,
            send_sem=r.one_send.at[at],
            recv_sem=r.one_recv.at[kind],
            device_id={"ctx": to_line * 2 + side},
            device_id_type=MESH,
        )

    def to_near(at):
        return one_copy(r.one_ready.at[at], r.one_near, 0, at, at)

    def to_far(at):
        return one_copy(r.one_ready.at[at], r.one_far, 1, at, at)

    def to_collect(at):
        return one_copy(r.one_ready.at[at], r.one_pair.at[at % 2], 2 + at % 2, at, swap(line))

    def finish_block(at):
        start = at * block
        reach = start + block
        r.grad_proj[start:reach, width : 3 * width] = rounded(r.acc[: 2 * width, start:reach].T)
        r.grad_proj[start:reach, 3 * width + HD :] = rounded(r.acc[2 * width :, start:reach].T)
        one_side[at] = wires.later(r.one_piece.at[at], r.one_side.at[at], beside)

        def one_step(step, carry):
            r.one_own[at] = one_grad(at * 2 + lax.rem(1 - side + step, 2))

            @pl.when(step == 0)
            def _():
                r.one_piece[at] = rounded(r.one_own[at])
                one_side[at].start()

            return carry

        lax.fori_loop(0, 2, one_step, 0)

    def pass_on(at):
        one_side[at].wait_recv()
        r.one_ready[at] = rounded(r.one_own[at] + r.one_side[at].astype(f32))
        near, shared = to_near(at), to_collect(at)

        @pl.when((pair == at // 2) & (line != at))
        def _():
            near.start()

        @pl.when((pair != at // 2) & jnp.logical_not(collects))
        def _():
            shared.start()

    def collect(at):
        distant = to_far(at)

        @pl.when((pair != at // 2) & collects)
        def _():
            arrived(r.one_ready.at[at], r.one_pair.at[at % 2], r.one_recv.at[2 + at % 2])
            r.one_ready[at] = rounded(
                r.one_own[at] + r.one_side[at].astype(f32) + r.one_pair[at % 2].astype(f32)
            )
            distant.start()

    back_block(3 * block)
    finish_block(3)
    back_block(2 * block)
    finish_block(2)
    line_collect(*down_refs)
    start_line(up_refs, up_side, r.up_side)
    back_block(block)
    finish_block(1)
    pass_on(3)
    back_block(0)
    finish_block(0)
    vec_in = []
    for step in range(1, ctx_size):
        peer = lax.rem(ctx + step, ctx_size)
        vec_in.append(wires.send(r.vec, r.vec_got.at[ctx], {"ctx": peer}))
    r.vec_got[ctx] = r.vec[...]
    out_grad_core.wait_recv()
    out_grad_far.wait_recv()
    r.out_piece[...] = rounded(
        r.out_grad[dp].astype(f32)
        + r.out_grad_got[0].astype(f32)
        + r.out_grad_got[2].astype(f32)
    )
    out_side = wires.send(r.out_piece.at[1 - side], r.out_side, beside)

    size = model // 4
    part = math.gcd(width, 3 * model // ctx_size)
    per = width // part
    folded_part, folded_head = part // 2, HD // 2

    def store_qkv(grads, parts):
        for at in range(4):
            cols = slice(at * size, (at + 1) * size)
            for source, target, count in parts:
                r.qkv_grad[at, target : target + count // 2, :] = folded(
                    grads[source : source + count, cols]
                )

    tail = 3 * width // 2
    grads_q = rounded(
        contract_rows(
            jnp.concatenate(
                [r.grad_proj[:, :width], r.grad_proj[:, 3 * width : 3 * width + HD]], axis=1
            ),
            r.normed_one[...],
        )
    )
    store_qkv(
        grads_q,
        [(at * part, at * folded_part, part) for at in range(per)] + [(width, tail, HD)],
    )
    pass_on(2)
    grads_kv = rounded(matmul(rounded(r.acc[...]), r.normed_one[...]))
    store_qkv(
        grads_kv,
        [(at * part, (per + at) * folded_part, part) for at in range(2 * per)]
        + [(2 * width, tail + folded_head, HD)],
    )
    qkv_far_core = wires.send(r.qkv_grad.at[lax.rem(swap(dp) + 2, 4)], r.qkv_got.at[1], core)
    qkv_core = wires.send(r.qkv_grad.at[swap(dp)], r.qkv_got.at[0], core)
    collect(3)
    line_collect(*up_refs)
    pass_on(1)
    qkv_far_core.wait_recv()
    r.qkv_grad[mine] = rounded(r.qkv_grad[mine].astype(f32) + r.qkv_got[1].astype(f32))
    qkv_far = wires.send(r.qkv_grad.at[mine], r.qkv_got.at[2], far)
    collect(2)
    pass_on(0)
    collect(1)
    start_line(out_refs, out_side, r.out_side)
    collect(0)
    line_collect(*out_refs)
    r.d_down[...] = line_finish(*down_refs)
    out_core.wait_recv()
    out_far.wait_recv()
    r.layer[...] = rounded(
        r.mid[...]
        + (r.out_part[0].astype(f32) + r.out_got[0].astype(f32) + r.out_got[2].astype(f32))
    )
    r.up_sum[...] = rounded(line_finish(*up_refs))
    stays = (lax.rem(ctx, 4) == dp) & (shards * dp + ctx // 4 == ctx)
    up_copy = pltpu.make_async_remote_copy(
        src_ref=r.up_sum,
        dst_ref=r.up_final,
        send_sem=r.up_send.at[0],
        recv_sem=r.up_recv.at[0],
        device_id=up_to,
        device_id_type=MESH,
    )

    @pl.when(jnp.logical_not(stays))
    def _():
        up_copy.start()

    @pl.when(stays)
    def _():
        r.up_final[...] = r.up_sum[...]

    for copy in vec_in:
        copy.wait_recv()
    total = r.vec_got[0]
    for at in range(1, ctx_size):
        total += r.vec_got[at]
    r.vec_sum[...] = total
    vec_out = [
        wires.send(r.vec_sum, r.vecs.at[dp], where) for where in (core, far, far_core)
    ]
    r.vecs[dp] = total
    qkv_core.wait_recv()
    qkv_far.wait_recv()
    r.qkv_sum[...] = rounded(
        r.qkv_grad[dp].astype(f32) + r.qkv_got[0].astype(f32) + r.qkv_got[2].astype(f32)
    )
    slots = r.deal_got.shape[0]

    def outgoing(kind, half):
        section = (kind * groups + my_group) * per + half
        target, slot = section // slots, lax.rem(section, slots)
        index = kind * per + half
        return target, slot, index, pltpu.make_async_remote_copy(
            src_ref=r.qkv_sum.at[pl.ds(index * folded_part, folded_part)],
            dst_ref=r.deal_got.at[slot, my_mb],
            send_sem=r.deal_send.at[index],
            recv_sem=r.deal_recv.at[slot, my_mb],
            device_id={"ctx": target},
            device_id_type=MESH,
        )

    def extra_copy(kind):
        return pltpu.make_async_remote_copy(
            src_ref=r.qkv_sum.at[pl.ds(tail + kind * folded_head, folded_head)],
            dst_ref=r.extra_got.at[ctx],
            send_sem=r.extra_send.at[kind],
            recv_sem=r.extra_recv.at[ctx],
            device_id={"ctx": kind * groups * per // slots},
            device_id_type=MESH,
        )

    for kind in range(3):
        for half in range(per):
            target, slot, index, copy = outgoing(kind, half)

            @pl.when(target != ctx)
            def _():
                copy.start()

            @pl.when(target == ctx)
            def _():
                r.deal_got[slot, my_mb] = r.qkv_sum[
                    index * folded_part : (index + 1) * folded_part, :
                ]

    for kind in range(2):
        target = kind * groups * per // slots
        copy = extra_copy(kind)

        @pl.when(ctx != target)
        def _():
            copy.start()

        @pl.when(ctx == target)
        def _():
            r.extra_got[ctx] = r.qkv_sum[
                tail + kind * folded_head : tail + (kind + 1) * folded_head, :
            ]

    xhat, inverse_one = norm_parts(r.x[...].astype(f32))
    arrived(r.one_ready.at[0], r.one_near, r.one_recv.at[0])
    arrived(r.one_ready.at[0], r.one_far, r.one_recv.at[1])
    near = r.one_ready[line].astype(f32) + r.one_near[...].astype(f32)
    distant = r.one_far[...].astype(f32)
    for micro in range(mbs):
        grad = jnp.where(pair == micro, near, distant)
        rows = slice(micro * tokens, (micro + 1) * tokens)
        r.d_x[rows, :] = rounded(
            r.grad_mid[rows, :] + norm_back(xhat[rows], inverse_one[rows], grad, gain_one)
        )
    r.d_out[...] = unfolded(line_finish(*out_refs)).T

    @pl.when(jnp.logical_not(stays))
    def _():
        up_copy.wait_send()
        up_copy.wait_recv()

    r.d_up[...] = r.up_final[...].astype(f32)

    for kind in range(3):
        for half in range(per):
            target, slot, index, copy = outgoing(kind, half)

            @pl.when(target != ctx)
            def _():
                copy.wait_send()

    for slot in range(slots):
        section = ctx * slots + slot
        source_group = lax.rem(section // per, groups)
        for place in range(mbs):

            @pl.when(place * groups + source_group != ctx)
            def _():
                arrived(
                    r.qkv_sum.at[pl.ds(0, folded_part)],
                    r.deal_got.at[slot, place],
                    r.deal_recv.at[slot, place],
                )

        total = r.deal_got[slot, 0].astype(f32)
        for place in range(1, mbs):
            total += r.deal_got[slot, place].astype(f32)
        r.deal_sum[slot * part : (slot + 1) * part, :] = unfolded(total)
    for kind in range(2):
        section = kind * groups * per
        target, slot = section // slots, section % slots
        copy = extra_copy(kind)

        @pl.when(ctx != target)
        def _():
            copy.wait_send()

        @pl.when(ctx == target)
        def _():
            total = jnp.zeros((folded_head, 2 * size), f32)
            for place in range(ctx_size):
                if place != target:
                    arrived(
                        r.qkv_sum.at[pl.ds(0, folded_head)], r.extra_got.at[place], r.extra_recv.at[place]
                    )
                total += r.extra_got[place].astype(f32)
            r.deal_sum[slot * part : slot * part + HD, :] += unfolded(total)

    r.d_qkv[...] = r.deal_sum[...].T
    for copy in vec_out:
        copy.wait_recv()
    for row in range(4):
        r.d_vec[row : row + 1, :] = (
            r.vecs[0, row : row + 1, :] + r.vecs[1, row : row + 1, :]
        ) + (r.vecs[2, row : row + 1, :] + r.vecs[3, row : row + 1, :])
    for at in range(4):
        r.d_bias[at] = r.vecs[at, 4:vec_rows, :]
    wires.drain()
    for refs in (down_refs, up_refs, out_refs):
        line_drain(*refs)
    for place in range(ctx_size):
        copy = att_copy(place)

        @pl.when(ctx != place)
        def _():
            copy.wait_send()

    for at in range(lines):
        copy = to_near(at)

        @pl.when(line != at)
        def _():
            copy.wait_send()


LAYER_COPIES = 96


def layer(collective_id, groups, shards, lengths, large):
    bf16, f32 = jnp.bfloat16, jnp.float32
    own, model = large["x"].shape
    ctx_size = lax.axis_size("ctx")
    tokens = own * groups // ctx_size
    hpg = model // HD // groups
    width = hpg * HD
    row_length = ctx_size * tokens
    lines = ctx_size // 2
    ff = large["w_down"].shape[0]
    size, shard = model // 4, 3 * model // ctx_size
    part = math.gcd(width, shard)
    slots, mbs = shard // part, ctx_size // groups
    picked = 3 * width + 2 * HD
    vec_rows = 4 + ff // model
    narrow = model // ctx_size
    vmem = pl.BlockSpec(memory_space=pltpu.VMEM)
    anywhere = pl.BlockSpec(memory_space=pl.ANY)
    outs = dict(
        layer=((own, model), bf16),
        d_x=((own, model), bf16),
        d_vec=((4, model), f32),
        d_bias=((4, ff // model, model), f32),
        d_qkv=((size, shard), f32),
        d_out=((size, narrow), f32),
        d_up=((size, ff // shards), f32),
        d_down=((narrow, ff), f32),
    )
    scratch = {name: (array.shape, array.dtype) for name, array in large.items()}
    scratch |= dict(
        x_row=((ctx_size, tokens, model), bf16),
        hat_one=((row_length, model), bf16),
        normed_one=((row_length, model), bf16),
        w_pick=((4, size, picked), bf16),
        proj=((row_length, picked), bf16),
        w_out=((model, model), bf16),
        w_up=((model, ff), bf16),
        out=((row_length, width), f32),
        inverse=((row_length, hpg), f32),
        att=((ctx_size, tokens // 2, 2 * width), bf16),
        att_in=((ctx_size, tokens // 2, 2 * width), bf16),
        b_own=((1, ff), f32),
        att_got=((ctx_size, tokens, width), bf16),
        cots=((4, own, model), bf16),
        mid=((own, model), f32),
        hat_two=((own, model), f32),
        grad_mid=((own, model), f32),
        normed=((4, own, model), bf16),
        act=((4, own, ff), bf16),
        grad_hid=((4, own, ff), bf16),
        part=((4, own, model), bf16),
        out_part=((4, own, model), bf16),
        part_got=((3, own, model), bf16),
        out_got=((3, own, model), bf16),
        att_out=((ctx_size, tokens // 2, 2 * width), bf16),
        grad_in=((ctx_size, tokens // 2, 2 * width), bf16),
        grad_att=((ctx_size, tokens, width), bf16),
        down_grad=((2, lines, narrow, ff), bf16),
        down_side=((lines, narrow, ff), bf16),
        down_near=((narrow, ff), bf16),
        down_distant=((narrow, ff), bf16),
        down_shared=((2, narrow, ff), bf16),
        up_grad=((2, lines, size, ff // shards), bf16),
        up_side=((lines, size, ff // shards), bf16),
        up_near=((size, ff // shards), bf16),
        up_distant=((size, ff // shards), bf16),
        up_shared=((2, size, ff // shards), bf16),
        up_sum=((size, ff // shards), bf16),
        up_final=((size, ff // shards), bf16),
        out_grad=((4, 2, lines, narrow // 2, 2 * size), bf16),
        out_grad_got=((3, 2, lines, narrow // 2, 2 * size), bf16),
        out_piece=((2, lines, narrow // 2, 2 * size), bf16),
        out_side=((lines, narrow // 2, 2 * size), bf16),
        out_near=((narrow // 2, 2 * size), bf16),
        out_distant=((narrow // 2, 2 * size), bf16),
        out_shared=((2, narrow // 2, 2 * size), bf16),
        suffix=((1, row_length), f32),
        acc=((2 * width + HD, row_length), f32),
        grad_proj=((row_length, picked), bf16),
        one_piece=((lines, tokens, model), bf16),
        one_own=((lines, tokens, model), f32),
        one_side=((lines, tokens, model), bf16),
        one_ready=((lines, tokens, model), bf16),
        one_near=((tokens, model), bf16),
        one_far=((tokens, model), bf16),
        one_pair=((2, tokens, model), bf16),
        qkv_grad=((4, picked // 2, 2 * size), bf16),
        qkv_got=((3, picked // 2, 2 * size), bf16),
        qkv_sum=((picked // 2, 2 * size), bf16),
        deal_got=((slots, mbs, part // 2, 2 * size), bf16),
        deal_sum=((shard, size), f32),
        extra_got=((ctx_size, HD // 2, 2 * size), bf16),
        vec=((vec_rows, model), f32),
        vec_got=((ctx_size, vec_rows, model), f32),
        vec_sum=((vec_rows, model), f32),
        vecs=((4, vec_rows, model), f32),
    )
    for start in range(0, row_length, QUERY_BLOCK):
        reach = start + QUERY_BLOCK
        scratch["probs%d" % start] = ((hpg, QUERY_BLOCK, reach), bf16)
        scratch["slope%d" % start] = ((QUERY_BLOCK, reach), bf16)
    dma = pltpu.SemaphoreType.DMA
    sems = dict(
        send_sem=dma((LAYER_COPIES,)),
        recv_sem=dma((LAYER_COPIES,)),
        load_sem=dma((len(large),)),
        att_send=dma((ctx_size,)),
        att_recv=dma((ctx_size,)),
        one_send=dma((lines,)),
        one_recv=dma((4,)),
        line_send=dma((3, 3)),
        line_recv=dma((3, 3)),
        up_send=dma((1,)),
        up_recv=dma((1,)),
        deal_send=dma((3 * (width // part),)),
        deal_recv=dma((slots, mbs)),
        extra_send=dma((2,)),
        extra_recv=dma((ctx_size,)),
    )
    names = list(outs) + list(scratch) + list(sems)
    return pl.pallas_call(
        partial(layer_body, (groups, shards), list(large), names),
        out_shape=[jax.ShapeDtypeStruct(*spec) for spec in outs.values()],
        in_specs=[pl.BlockSpec(memory_space=pltpu.SMEM)] + [anywhere] * len(large),
        out_specs=[vmem] * len(outs),
        scratch_shapes=[pltpu.VMEM(*spec) for spec in scratch.values()] + list(sems.values()),
        compiler_params=pltpu.CompilerParams(
            collective_id=collective_id, has_side_effects=True, vmem_limit_bytes=63 * 1024 * 1024
        ),
        name="layer",
    )(lengths, *large.values())


def finish_body(*refs):
    sources, targets = refs[:8], refs[8:]
    for source, target in zip(sources[:6], targets[:6]):
        target[...] = source[...]
    for row in range(4):
        targets[6 + row][...] = sources[6][row]
    columns = sources[7].shape[2]
    rows = sources[7].shape[1]
    for at in range(4 * rows):
        targets[10][at * columns : (at + 1) * columns] = sources[7][at // rows, at % rows]


def finish(*arrays):
    vmem = pl.BlockSpec(memory_space=pltpu.VMEM)
    shape = jax.ShapeDtypeStruct
    model = arrays[6].shape[1]
    return pl.pallas_call(
        finish_body,
        out_shape=[shape(array.shape, array.dtype) for array in arrays[:6]]
        + [shape((model,), jnp.float32)] * 4
        + [shape((arrays[7].size,), jnp.float32)],
        in_specs=[vmem] * len(arrays),
        out_specs=[vmem] * 11,
        name="finish",
    )(*arrays)


def per_head_device(
    layer_input,
    doc_lengths,
    ln1_gain,
    ln1_bias,
    w_qkv,
    w_out,
    ln2_gain,
    ln2_bias,
    w_up,
    b_up,
    w_down,
    cotangent,
):
    mbs, _, tokens, model = layer_input.shape
    ctx_size, dp_size = lax.axis_size("ctx"), lax.axis_size("dp")
    large = dict(
        x=layer_input.reshape(mbs * tokens, model),
        w_qkv=w_qkv,
        gain_one=ln1_gain,
        bias_one=ln1_bias,
        cot=cotangent.reshape(mbs * tokens, model),
        w_out_own=w_out,
        w_up_own=w_up,
        gain_two=ln2_gain,
        bias_two=ln2_bias,
        w_down=w_down,
        b_up=b_up,
    )
    layer_out, d_x, d_vec, d_bias, d_qkv, d_out, d_up, d_down = layer(
        0, ctx_size // mbs, ctx_size // dp_size, doc_lengths, large
    )
    layer_out, d_x, d_qkv, d_out, d_up, d_down, gain_one, bias_one, gain_two, bias_two, d_bias = finish(
        layer_out, d_x, d_qkv, d_out, d_up, d_down, d_vec, d_bias
    )
    return (
        layer_out.reshape(mbs, 1, tokens, model),
        d_x.reshape(mbs, 1, tokens, model),
        gain_one,
        bias_one,
        d_qkv,
        d_out,
        gain_two,
        bias_two,
        d_up,
        d_bias,
        d_down.T,
    )


def on_device(*arguments):
    layer_input = arguments[0]
    mbs, model = layer_input.shape[0], layer_input.shape[3]
    heads, ctx_size, dp_size = model // HD, lax.axis_size("ctx"), lax.axis_size("dp")
    groups = ctx_size // mbs
    fits = (
        ctx_size % mbs == 0
        and heads % groups == 0
        and dp_size == 4
        and ctx_size % dp_size == 0
        and ctx_size == 8
        and mbs == 2
        and (layer_input.shape[2] * ctx_size) % QUERY_BLOCK == 0
    )
    return (per_head_device if fits else per_token_device)(*arguments)


def solution(mesh):
    return jax.shard_map(
        on_device,
        mesh=mesh,
        in_specs=(
            P(None, "dp", "ctx", None),
            P(None, "dp", None),
            P(),
            P(),
            P("dp", None),
            P("dp", None),
            P(),
            P(),
            P("dp", None),
            P(),
            P("dp", None),
            P(None, "dp", "ctx", None),
        ),
        out_specs=(
            P(None, "dp", "ctx", None),
            P(None, "dp", "ctx", None),
            P(),
            P(),
            P("dp", "ctx"),
            P("dp", "ctx"),
            P(),
            P(),
            P("dp", "ctx"),
            P(),
            P("dp", "ctx"),
        ),
        check_vma=False,
    )
```

```python
import math
from functools import partial
from types import SimpleNamespace

import jax
import jax.numpy as jnp
from jax import lax
from jax.experimental import pallas as pl
from jax.experimental.pallas import tpu as pltpu
from jax.sharding import PartitionSpec as P

HD = 64


NORM_EPSILON = 1e-05
MASKED = -1e30
START_TOP = -1e20


def prefix_2(array, axis, combine, identity, reverse):
    peers, index = (lax.axis_size(axis), lax.axis_index(axis))
    everything = lax.all_gather(array, axis)
    start = jnp.broadcast_to(jnp.asarray(identity, array.dtype), array.shape)

    def turn(k, before):
        at = peers - 1 - k if reverse else k
        reached = at > index if reverse else at < index
        new = combine(before, everything[at])
        return jnp.where(reached, new, before)

    return lax.fori_loop(0, peers, turn, start)


def layer_norm(value, gain, bias):
    row_mean = jnp.mean(value, axis=-1, keepdims=True)
    centered = value - row_mean
    spread = jnp.mean(centered * centered, axis=-1, keepdims=True)
    return centered * lax.rsqrt(spread + NORM_EPSILON) * gain + bias


def matmul(left, right):
    return jnp.dot(left, right, preferred_element_type=jnp.float32)


def contract_rows(left, right):
    return lax.dot_general(
        left, right, (((0,), (0,)), ((), ())), preferred_element_type=jnp.float32
    )


def contract_cols(left, right):
    return lax.dot_general(
        left, right, (((1,), (1,)), ((), ())), preferred_element_type=jnp.float32
    )


def segment_table(lengths, row_length):
    doc_ends = jnp.cumsum(lengths)
    places = jnp.arange(row_length, dtype=jnp.int32)
    segment = jnp.sum((places[:, None] >= doc_ends[None, :]).astype(jnp.int32), axis=1)
    opening = jnp.concatenate([jnp.ones((1,), jnp.bool_), segment[1:] != segment[:-1]])
    return (segment, opening)


def add_up(earlier, later):
    return earlier + later


def per_token_device(
    layer_input,
    doc_lengths,
    ln1_gain,
    ln1_bias,
    w_qkv,
    w_out,
    ln2_gain,
    ln2_bias,
    w_up,
    b_up,
    w_down,
    cotangent,
):
    micro_count = layer_input.shape[0]
    query_rows = layer_input.shape[2]
    model_width = layer_input.shape[3]
    head_count = model_width // HD
    row_length = query_rows * lax.axis_size("ctx")
    key_block = min(512, row_length)
    score_scale = HD ** (-0.5)
    strength = 8.0 / row_length
    ctx_place = lax.axis_index("ctx")
    query_pos = ctx_place * query_rows + jnp.arange(query_rows, dtype=jnp.int32)
    block_total = ((ctx_place + 1) * query_rows + key_block - 1) // key_block
    later_heads = (jnp.arange(head_count) > 0).astype(jnp.float32)[:, None, None]
    zeros_row = jnp.zeros((row_length,), jnp.float32)
    gelu_exact = partial(jax.nn.gelu, approximate=False)
    output_list = []
    input_grads = []
    matrix_total = None
    vector_total = None
    for micro_step in range(micro_count):
        w_qkv_all, w_out_all, w_up_all, w_down_all = (
            lax.all_gather(w_qkv, "dp", axis=0, tiled=True),
            lax.all_gather(w_out, "dp", axis=0, tiled=True),
            lax.all_gather(w_up, "dp", axis=0, tiled=True),
            lax.all_gather(w_down, "dp", axis=0, tiled=True),
        )
        inputs = layer_input[micro_step, 0].astype(jnp.float32)
        segment, opening = segment_table(doc_lengths[micro_step, 0], row_length)
        query_seg = lax.dynamic_slice_in_dim(segment, ctx_place * query_rows, query_rows, 0)
        normed_one = layer_norm(inputs, ln1_gain, ln1_bias).astype(jnp.bfloat16)
        projected = matmul(normed_one, w_qkv_all).astype(jnp.bfloat16)
        queries = projected[:, :model_width]
        queries3 = queries.reshape(query_rows, head_count, HD)
        query_zero = queries[:, :HD]
        keys_all, values_all = (
            lax.all_gather(projected[:, model_width : 2 * model_width], "ctx", axis=0, tiled=True),
            lax.all_gather(projected[:, 2 * model_width :], "ctx", axis=0, tiled=True),
        )

        def masks(key_start):
            key_seg = lax.dynamic_slice_in_dim(segment, key_start, key_block, 0)
            key_open = lax.dynamic_slice_in_dim(opening, key_start, key_block, 0)
            key_pos = key_start + jnp.arange(key_block, dtype=jnp.int32)
            same_doc = query_seg[:, None] == key_seg[None, :]
            allowed = same_doc & (key_pos[None, :] <= query_pos[:, None])
            chosen = (
                same_doc
                & (key_pos[None, :] < query_pos[:, None])
                & jnp.logical_not(key_open)[None, :]
            )
            return (allowed, chosen.astype(jnp.float32))

        def head_scores(key_start):
            key_zero = lax.dynamic_slice_in_dim(keys_all, key_start, key_block, 0)[:, :HD]
            return (key_zero, contract_cols(query_zero, key_zero) * score_scale)

        def block_keys(key_start):
            keys3 = lax.dynamic_slice_in_dim(keys_all, key_start, key_block, 0).reshape(
                key_block, head_count, HD
            )
            values3 = lax.dynamic_slice_in_dim(values_all, key_start, key_block, 0).reshape(
                key_block, head_count, HD
            )
            return (keys3, values3)

        def logits_of(key_start, keys3):
            allowed, chosen = masks(key_start)
            raw_scores = (
                jnp.einsum("qhd,khd->hqk", queries3, keys3, preferred_element_type=jnp.float32)
                * score_scale
            )
            picked = strength * jax.nn.softplus(raw_scores[0]) * chosen
            before = lax.dynamic_slice_in_dim(prefix, key_start, key_block, 0)
            penalty = before[None, :] + jnp.cumsum(picked, axis=0) - picked
            return jnp.where(allowed[None], raw_scores - penalty[None], MASKED)

        def total_block(block_index, totals):
            key_start = block_index * key_block
            _, chosen = masks(key_start)
            _, first_scores = head_scores(key_start)
            picked = strength * jax.nn.softplus(first_scores) * chosen
            return lax.dynamic_update_slice_in_dim(totals, jnp.sum(picked, axis=0), key_start, 0)

        totals = lax.fori_loop(0, block_total, total_block, zeros_row)
        prefix = prefix_2(totals, "ctx", add_up, zeros_row, False)

        def stat_block(block_index, running):
            row_top, row_total = running
            key_start = block_index * key_block
            keys3, _ = block_keys(key_start)
            logits = logits_of(key_start, keys3)
            new_top = jnp.maximum(row_top, jnp.max(logits, axis=-1))
            row_total = row_total * jnp.exp(row_top - new_top) + jnp.sum(
                jnp.exp(logits - new_top[..., None]), axis=-1
            )
            return (new_top, row_total)

        row_top, row_total = lax.fori_loop(
            0,
            block_total,
            stat_block,
            (
                jnp.full((head_count, query_rows), START_TOP, jnp.float32),
                jnp.zeros((head_count, query_rows), jnp.float32),
            ),
        )
        log_total = row_top + jnp.log(row_total)

        def out_block(block_index, gathered_out):
            key_start = block_index * key_block
            keys3, values3 = block_keys(key_start)
            attn_probs = jnp.exp(logits_of(key_start, keys3) - log_total[..., None]).astype(
                jnp.bfloat16
            )
            return gathered_out + jnp.einsum(
                "hqk,khd->qhd", attn_probs, values3, preferred_element_type=jnp.float32
            )

        gathered_out = lax.fori_loop(
            0, block_total, out_block, jnp.zeros((query_rows, head_count, HD), jnp.float32)
        )
        attended = gathered_out.reshape(query_rows, model_width).astype(jnp.bfloat16)
        mid_stream = inputs + matmul(attended, w_out_all)
        normed_two = layer_norm(mid_stream, ln2_gain, ln2_bias).astype(jnp.bfloat16)
        hidden = matmul(normed_two, w_up_all) + b_up
        activated = gelu_exact(hidden).astype(jnp.bfloat16)
        output_list.append((mid_stream + matmul(activated, w_down_all)).astype(jnp.bfloat16))
        cot_rows = cotangent[micro_step, 0]
        grad_down = contract_rows(activated, cot_rows)
        grad_act = contract_cols(cot_rows, w_down_all)
        _, gelu_back = jax.vjp(gelu_exact, hidden)
        grad_hidden = gelu_back(grad_act)[0].astype(jnp.bfloat16)
        grad_up = contract_rows(normed_two, grad_hidden)
        grad_bias_up = jnp.sum(grad_hidden.astype(jnp.float32), axis=0)
        grad_normed_two = contract_cols(grad_hidden, w_up_all)
        _, norm_two_back = jax.vjp(layer_norm, mid_stream, ln2_gain, ln2_bias)
        grad_mid_part, grad_gain_two, grad_bias_two = norm_two_back(grad_normed_two)
        grad_mid = cot_rows.astype(jnp.float32) + grad_mid_part
        grad_branch = grad_mid.astype(jnp.bfloat16)
        grad_outproj = contract_rows(attended, grad_branch)
        grad_attended = contract_cols(grad_branch, w_out_all).astype(jnp.bfloat16)
        grad_att3 = grad_attended.reshape(query_rows, head_count, HD)
        row_delta = jnp.einsum("qhd,qhd->hq", grad_att3.astype(jnp.float32), gathered_out)

        def grad_block(block_index, running):
            grad_query, grad_key_all, grad_value_all, penalty_grad, first_grad = running
            key_start = block_index * key_block
            keys3, values3 = block_keys(key_start)
            probs_f32 = jnp.exp(logits_of(key_start, keys3) - log_total[..., None])
            grad_probs = jnp.einsum(
                "qhd,khd->hqk", grad_att3, values3, preferred_element_type=jnp.float32
            )
            grad_logits = probs_f32 * (grad_probs - row_delta[..., None])
            penalty_grad = lax.dynamic_update_slice_in_dim(
                penalty_grad, -jnp.sum(grad_logits, axis=0), key_start, 1
            )
            first_grad = lax.dynamic_update_slice_in_dim(first_grad, grad_logits[0], key_start, 1)
            grad_scores = (grad_logits * later_heads).astype(jnp.bfloat16)
            grad_query = (
                grad_query
                + jnp.einsum("hqk,khd->qhd", grad_scores, keys3, preferred_element_type=jnp.float32)
                * score_scale
            )
            key_part = (
                jnp.einsum(
                    "hqk,qhd->khd", grad_scores, queries3, preferred_element_type=jnp.float32
                )
                * score_scale
            )
            value_part = jnp.einsum(
                "hqk,qhd->khd",
                probs_f32.astype(jnp.bfloat16),
                grad_att3,
                preferred_element_type=jnp.float32,
            )
            grad_key_all = lax.dynamic_update_slice_in_dim(
                grad_key_all, key_part.reshape(key_block, model_width), key_start, 0
            )
            grad_value_all = lax.dynamic_update_slice_in_dim(
                grad_value_all, value_part.reshape(key_block, model_width), key_start, 0
            )
            return (grad_query, grad_key_all, grad_value_all, penalty_grad, first_grad)

        grad_query, grad_key_all, grad_value_all, penalty_grad, first_grad = lax.fori_loop(
            0,
            block_total,
            grad_block,
            (
                jnp.zeros((query_rows, head_count, HD), jnp.float32),
                jnp.zeros((row_length, model_width), jnp.float32),
                jnp.zeros((row_length, model_width), jnp.float32),
                jnp.zeros((query_rows, row_length), jnp.float32),
                jnp.zeros((query_rows, row_length), jnp.float32),
            ),
        )
        column_sums = jnp.sum(penalty_grad, axis=0)
        after = prefix_2(column_sums, "ctx", add_up, zeros_row, True)
        reach_sums = after + column_sums

        def head_block(block_index, running):
            grad_query_zero, grad_key_all = running
            key_start = block_index * key_block
            _, chosen = masks(key_start)
            key_zero, first_scores = head_scores(key_start)
            flow_block = lax.dynamic_slice_in_dim(penalty_grad, key_start, key_block, 1)
            reach_block = lax.dynamic_slice_in_dim(reach_sums, key_start, key_block, 0)
            grad_picked = reach_block[None, :] - jnp.cumsum(flow_block, axis=0)
            grad_select = grad_picked * strength * jax.nn.sigmoid(first_scores) * chosen
            grad_head = (
                lax.dynamic_slice_in_dim(first_grad, key_start, key_block, 1) + grad_select
            ).astype(jnp.bfloat16)
            grad_query_zero = grad_query_zero + matmul(grad_head, key_zero) * score_scale
            key_zero_grad = contract_rows(grad_head, query_zero) * score_scale
            grad_key_all = lax.dynamic_update_slice(
                grad_key_all, key_zero_grad, (key_start, jnp.zeros((), jnp.int32))
            )
            return (grad_query_zero, grad_key_all)

        grad_query_zero, grad_key_all = lax.fori_loop(
            0, block_total, head_block, (jnp.zeros((query_rows, HD), jnp.float32), grad_key_all)
        )
        grad_query = grad_query.at[:, 0, :].add(grad_query_zero).reshape(query_rows, model_width)
        grad_key_own, grad_value_own = (
            lax.psum_scatter(grad_key_all, "ctx", scatter_dimension=0, tiled=True),
            lax.psum_scatter(grad_value_all, "ctx", scatter_dimension=0, tiled=True),
        )
        grad_project = jnp.concatenate([grad_query, grad_key_own, grad_value_own], axis=1).astype(
            jnp.bfloat16
        )
        grad_qkv = contract_rows(normed_one, grad_project)
        grad_normed_one = contract_cols(grad_project, w_qkv_all)
        _, norm_one_back = jax.vjp(layer_norm, inputs, ln1_gain, ln1_bias)
        grad_in_part, grad_gain_one, grad_bias_one = norm_one_back(grad_normed_one)
        input_grads.append((grad_mid + grad_in_part).astype(jnp.bfloat16))
        matrix_grads = (grad_qkv, grad_outproj, grad_up, grad_down)
        vector_grads = (grad_gain_one, grad_bias_one, grad_gain_two, grad_bias_two, grad_bias_up)
        matrix_grads = (
            lax.psum_scatter(matrix_grads[0], "ctx", scatter_dimension=1, tiled=True),
            lax.psum_scatter(matrix_grads[1], "ctx", scatter_dimension=1, tiled=True),
            lax.psum_scatter(matrix_grads[2], "ctx", scatter_dimension=1, tiled=True),
            lax.psum_scatter(matrix_grads[3], "ctx", scatter_dimension=1, tiled=True),
        )
        matrix_grads = (
            lax.psum_scatter(
                matrix_grads[0].astype(jnp.bfloat16), "dp", scatter_dimension=0, tiled=True
            ).astype(jnp.float32),
            lax.psum_scatter(
                matrix_grads[1].astype(jnp.bfloat16), "dp", scatter_dimension=0, tiled=True
            ).astype(jnp.float32),
            lax.psum_scatter(
                matrix_grads[2].astype(jnp.bfloat16), "dp", scatter_dimension=0, tiled=True
            ).astype(jnp.float32),
            lax.psum_scatter(
                matrix_grads[3].astype(jnp.bfloat16), "dp", scatter_dimension=0, tiled=True
            ).astype(jnp.float32),
        )
        vector_grads = lax.psum(
            (vector_grads[0], vector_grads[1], vector_grads[2], vector_grads[3], vector_grads[4]),
            ("dp", "ctx"),
        )
        if matrix_total is None:
            matrix_total = matrix_grads
            vector_total = vector_grads
        else:
            matrix_total = tuple((old + new for old, new in zip(matrix_total, matrix_grads)))
            vector_total = tuple((old + new for old, new in zip(vector_total, vector_grads)))
    layer_out = jnp.stack(output_list)[:, None]
    input_out = jnp.stack(input_grads)[:, None]
    return (
        layer_out,
        input_out,
        vector_total[0],
        vector_total[1],
        matrix_total[0],
        matrix_total[1],
        vector_total[2],
        vector_total[3],
        matrix_total[2],
        vector_total[4],
        matrix_total[3],
    )


MESH = pl.DeviceIdType.MESH
EXCLUDED = 1e30
QUERY_BLOCK = 256


def norm_parts(value):
    row_mean = jnp.mean(value, axis=-1, keepdims=True)
    centered = value - row_mean
    spread = jnp.mean(centered * centered, axis=-1, keepdims=True)
    inverse = lax.rsqrt(spread + NORM_EPSILON)
    return centered * inverse, inverse


def norm_back(xhat, inverse, grad, gain):
    scaled = grad * gain
    return (
        scaled
        - jnp.mean(scaled, axis=-1, keepdims=True)
        - xhat * jnp.mean(scaled * xhat, axis=-1, keepdims=True)
    ) * inverse


class Wires:
    def __init__(self, send_sem, recv_sem):
        self.send_sem, self.recv_sem, self.used, self.made = send_sem, recv_sem, 0, []

    def send(self, source, target, where):
        copy = pltpu.make_async_remote_copy(
            src_ref=source,
            dst_ref=target,
            send_sem=self.send_sem.at[self.used],
            recv_sem=self.recv_sem.at[self.used],
            device_id=where,
            device_id_type=MESH,
        )
        copy.start()
        self.used += 1
        self.made.append(copy)
        return copy

    def later(self, source, target, where):
        copy = pltpu.make_async_remote_copy(
            src_ref=source,
            dst_ref=target,
            send_sem=self.send_sem.at[self.used],
            recv_sem=self.recv_sem.at[self.used],
            device_id=where,
            device_id_type=MESH,
        )
        self.used += 1
        self.made.append(copy)
        return copy

    def sent(self, copy):
        copy.wait_send()
        self.made.remove(copy)

    def drain(self):
        for copy in self.made:
            copy.wait_send()


def rounded(value):
    return value.astype(jnp.bfloat16)


def folded(array):
    half = array.shape[0] // 2
    return jnp.concatenate([array[:half], array[half:]], axis=1)


def unfolded(array):
    half = array.shape[1] // 2
    return jnp.concatenate([array[:, :half], array[:, half:]], axis=0)


def arrived(like, target, sem):
    pltpu.make_async_copy(like, target, sem).wait()


def swap(index):
    return index + 1 - 2 * lax.rem(index, 2)


def layer_body(plan, loaded, names, lengths, w_down, *refs):
    given, refs = refs[: len(loaded)], refs[len(loaded) :]
    r = SimpleNamespace(**dict(zip(names, refs)))
    groups, shards = plan
    f32 = jnp.float32
    ctx, dp = lax.axis_index("ctx"), lax.axis_index("dp")
    ctx_size, tokens, model = r.x_row.shape
    width = r.out.shape[1]
    lines = ctx_size // 2
    mbs = ctx_size // groups
    hpg = width // HD
    own = r.x.shape[0]
    ff = r.w_ff.shape[0]
    row_length = tokens * ctx_size
    side, line = lax.rem(ctx, 2), ctx // 2
    my_mb, my_group = ctx // groups, lax.rem(ctx, groups)
    wires = Wires(r.send_sem, r.recv_sem)
    core, far, far_core = {"dp": swap(dp)}, {"dp": lax.rem(dp + 2, 4)}, {"dp": lax.rem(swap(dp) + 2, 4)}
    beside = {"ctx": swap(ctx)}
    upper, which = dp // 2, lax.rem(dp, 2)
    odd, distant_half = lax.rem(line, 2), line // 2
    ff_block = 2 * odd + which
    owns_block = ff_block == dp
    up_to = {"dp": 2 * upper + distant_half, "ctx": 2 * ff_block + side}
    up_from = {"dp": 2 * upper + lax.rem(line, 2), "ctx": 2 * (2 * which + line // 2) + side}
    across = {"dp": ff_block, "ctx": 2 * (2 * distant_half + upper) + side}
    around = [{"ctx": lax.rem(ctx + step, ctx_size)} for step in range(1, ctx_size)]

    mirror = {"ctx": lax.rem(line + lines // 2, lines) * 2 + side}
    ahead = {"ctx": swap(line) * 2 + side}
    beside_at, mirror_at, ahead_at = beside["ctx"], mirror["ctx"], ahead["ctx"]
    half = tokens // 4

    loads = SimpleNamespace()
    for at, name in enumerate(loaded):
        copy = pltpu.make_async_copy(given[at], getattr(r, name), r.load_sem.at[at])
        copy.start()
        setattr(loads, name, copy)
    down_load = pltpu.make_async_copy(w_down, r.w_ff, r.ff_sem.at[0])
    down_copy = pltpu.make_async_remote_copy(
        src_ref=w_down,
        dst_ref=r.w_ff,
        send_sem=r.ff_sem.at[1],
        recv_sem=r.ff_sem.at[2],
        device_id=far,
        device_id_type=MESH,
    )
    pl.when(owns_block)(down_load.start)
    barrier = pltpu.get_barrier_semaphore()
    for where in around + [core, far, far_core, up_from, across]:
        pl.semaphore_signal(barrier, inc=1, device_id=where, device_id_type=MESH)
    loads.x.wait()
    loads.w_qkv.wait()
    pl.semaphore_wait(barrier, ctx_size + 4)

    def x_of(micro):
        return r.x.at[pl.ds(pl.multiple_of(micro * tokens, tokens), tokens)]

    first, second = pl.ds(0, tokens // 2), pl.ds(tokens // 2, tokens // 2)

    def x_half(micro, at):
        rows = pl.ds(pl.multiple_of(micro * tokens + at * (tokens // 2), tokens // 2), tokens // 2)
        return r.x.at[rows]

    x_mirror_a = wires.send(x_half(1 - my_mb, 0), r.x_row.at[ctx, first], mirror)
    x_beside = wires.send(x_of(my_mb), r.x_row.at[ctx], beside)
    for group in range(groups):

        @pl.when(my_group == group)
        def _():
            for kind in range(3):
                first = kind * model + group * width
                r.w_pick[dp, :, kind * width : (kind + 1) * width] = r.w_qkv[:, first : first + width]

    for kind in range(2):
        r.w_pick[dp, :, 3 * width + kind * HD : 3 * width + (kind + 1) * HD] = r.w_qkv[
            :, kind * model : kind * model + HD
        ]
    pick_far = wires.send(r.w_pick.at[dp], r.w_pick.at[dp], far)
    pick_core = wires.send(r.w_pick.at[dp], r.w_pick.at[dp], core)
    r.x_row[ctx] = x_of(my_mb)[...]

    for copy in (loads.cot, loads.w_out_own, loads.w_up_own):
        copy.wait()

    def rows_of(place):
        return pl.ds(pl.multiple_of(place * size_dp, size_dp), size_dp)

    size_dp = model // 4
    wout_far = wires.send(r.w_out_own, r.w_out.at[rows_of(dp)], far)
    wout_core = wires.send(r.w_out_own, r.w_out.at[rows_of(dp)], core)

    def up_part(peer):
        block = 2 * odd + lax.rem(peer, 2)
        return r.w_up_own.at[:, pl.ds(pl.multiple_of(block * ff, 128), ff)]

    up_in = [
        wires.send(up_part(where["dp"]), r.w_up.at[rows_of(dp)], where)
        for where in (far, far_core, core)
    ]
    r.w_out[rows_of(dp), :] = r.w_out_own[...]
    r.w_up[rows_of(dp), :] = up_part(dp)[...]
    r.cots[0] = r.cot[...]

    loads.gain_one.wait()
    loads.bias_one.wait()
    gain_one = r.gain_one[...].reshape(1, model)
    bias_one = r.bias_one[...].reshape(1, model)

    def normalise(place):
        xhat, _ = norm_parts(r.x_row[place].astype(f32))
        rows = pl.ds(pl.multiple_of(place * tokens, tokens), tokens)
        r.hat_one[rows, :] = rounded(xhat)
        r.normed_one[rows, :] = rounded(xhat * gain_one + bias_one)

    wires.sent(x_mirror_a)
    x_mirror_b = wires.send(x_half(1 - my_mb, 1), r.x_row.at[ctx, second], mirror)
    x_ahead = wires.send(x_of(my_mb), r.x_row.at[ctx], ahead)
    normalise(ctx)
    mirror_beside, mirror_ahead = swap(mirror_at), lax.rem(ahead_at + ctx_size // 2, ctx_size)

    def relay(place, part, where):
        return wires.send(r.x_row.at[place, part], r.x_row.at[place, part], where)

    x_mirror_a.wait_recv()
    a_beside = relay(mirror_at, first, beside)
    a_ahead = relay(mirror_at, first, ahead)
    x_beside.wait_recv()
    top, bottom = pl.ds(0, half), pl.ds(half, tokens - half)
    x_fwd_a = relay(beside_at, top, ahead)
    normalise(beside_at)
    x_mirror_b.wait_recv()
    b_beside = relay(mirror_at, second, beside)
    b_ahead = relay(mirror_at, second, ahead)
    x_ahead.wait_recv()
    x_fwd_b = relay(ahead_at, bottom, beside)
    a_beside.wait_recv()
    a_over = relay(mirror_beside, first, ahead)
    pl.when(owns_block)(down_copy.start)
    pick_far.wait_recv()
    pick_at = far["dp"]
    pick_fwd = wires.send(r.w_pick.at[pick_at], r.w_pick.at[pick_at], core)
    normalise(ahead_at)
    normalise(mirror_at)
    b_ahead.wait_recv()
    b_over = relay(mirror_ahead, second, beside)
    a_ahead.wait_recv()
    b_beside.wait_recv()
    normalise(mirror_beside)
    normalise(mirror_ahead)
    x_fwd_a.wait_recv()
    x_fwd_b.wait_recv()
    normalise(swap(ahead_at))
    pick_core.wait_recv()
    pick_fwd.wait_recv()
    a_over.wait_recv()
    b_over.wait_recv()
    normalise(swap(mirror_ahead))
    cot_far = wires.send(r.cot, r.cots.at[2], ahead)
    cot_core = wires.send(r.cot, r.cots.at[1], core)
    w_pick = r.w_pick[...].reshape(model, 3 * width + 2 * HD)
    r.proj[...] = rounded(matmul(r.normed_one[...], w_pick))

    def att_copy(place):
        return pltpu.make_async_remote_copy(
            src_ref=r.att.at[place],
            dst_ref=r.att_in.at[ctx],
            send_sem=r.att_send.at[place],
            recv_sem=r.att_recv.at[ctx],
            device_id={"ctx": place},
            device_id_type=MESH,
        )

    block = QUERY_BLOCK
    per_block = block // tokens
    scale = HD ** (-0.5)
    strength = 8.0 / row_length
    row_at = lax.broadcasted_iota(jnp.int32, (block, block), 0)
    col_at = lax.broadcasted_iota(jnp.int32, (block, block), 1)
    earlier = (col_at < row_at).astype(jnp.bfloat16)
    later = (col_at > row_at).astype(jnp.bfloat16)
    doc_ends, doc_end = [], 0
    for at in range(lengths.shape[2]):
        doc_end = doc_end + lengths[my_mb, 0, at]
        doc_ends.append(doc_end)

    def segment_of(places):
        total = jnp.zeros(places.shape, jnp.int32)
        for end in doc_ends:
            total += jnp.where(places >= end, 1, 0)
        return total

    r.suffix[...] = jnp.zeros_like(r.suffix)
    for start in range(0, row_length, block):
        reach = start + block
        rows = pl.ds(start, block)
        probs_ref, slope_ref = getattr(r, "probs%d" % start), getattr(r, "slope%d" % start)
        row_pos = start + lax.broadcasted_iota(jnp.int32, (block, 1), 0)
        col_pos = lax.broadcasted_iota(jnp.int32, (1, reach), 1)
        row_seg, col_seg = segment_of(row_pos), segment_of(col_pos)
        opening = (col_seg != segment_of(col_pos - 1)) | (col_pos == 0)
        pick_seg = jnp.where(opening, -1, col_seg)
        query = rounded(r.proj[rows, 3 * width : 3 * width + HD] * scale)
        key = r.proj[:reach, 3 * width + HD : 3 * width + 2 * HD]
        scores = contract_cols(query, key)
        small = jnp.exp(-jnp.abs(scores))
        soft = jnp.maximum(scores, 0.0) + jnp.log(1.0 + small)
        recip = pl.reciprocal(1.0 + small, approx=True)
        sigmoid = jnp.where(scores >= 0.0, recip, small * recip)
        chosen = (row_seg == pick_seg) & (col_pos < row_pos)
        picked = jnp.where(chosen, strength * soft, 0.0)
        slope_ref[...] = rounded(jnp.where(chosen, strength * sigmoid, 0.0))
        high = rounded(picked)
        low = rounded(picked - high.astype(f32))
        penalty = r.suffix[:, :reach] + (matmul(earlier, high) + matmul(earlier, low))
        allowed = (row_seg == col_seg) & (col_pos <= row_pos)
        penalty = jnp.where(allowed, penalty, EXCLUDED)
        r.suffix[:, :reach] += jnp.sum(picked, axis=0, keepdims=True)
        for head in range(hpg):
            at = head * HD
            query = rounded(r.proj[rows, at : at + HD] * scale)
            key = r.proj[:reach, width + at : width + at + HD]
            value = r.proj[:reach, 2 * width + at : 2 * width + at + HD]
            logits = contract_cols(query, key) - penalty
            top_logit = jnp.max(logits, axis=1, keepdims=True)
            probs = jnp.exp(logits - top_logit)
            inverse = 1.0 / jnp.sum(probs, axis=1, keepdims=True)
            probs = rounded(probs)
            probs_ref[head] = probs
            r.out[rows, at : at + HD] = matmul(probs, value) * inverse
            r.inverse[rows, head : head + 1] = inverse
        for step in range(per_block):
            place = start // tokens + step
            r.att[place] = folded(rounded(r.out[place * tokens : (place + 1) * tokens, :]))
            copy = att_copy(place)

            @pl.when(ctx != place)
            def _():
                copy.start()

    r.att_in[ctx] = r.att[ctx]
    cot_far.wait_recv()
    cot_fwd = wires.send(r.cots.at[2], r.cots.at[3], core)
    wout_far.wait_recv()
    out_at = rows_of(far["dp"])
    wout_fwd = wires.send(r.w_out.at[out_at], r.w_out.at[out_at], core)
    for copy in up_in:
        copy.wait_recv()
    wout_core.wait_recv()
    wout_fwd.wait_recv()
    for copy in (loads.gain_two, loads.bias_two, loads.b_up):
        copy.wait()
    for step in range(1, ctx_size):
        place = lax.rem(ctx + step, ctx_size)
        arrived(r.att.at[0], r.att_in.at[place], r.att_recv.at[place])
    for place in range(ctx_size):
        r.att_got[place] = unfolded(r.att_in[place])

    gain = r.gain_two[...].reshape(1, model)
    bias = r.bias_two[...].reshape(1, model)
    for at in range(4):

        @pl.when(ff_block == at)
        def _():
            r.b_own[...] = r.b_up[at * ff : (at + 1) * ff].reshape(1, ff)

    for micro in range(mbs):
        rows = pl.ds(micro * tokens, tokens)
        stream = r.x[rows, :].astype(f32)
        for group in range(groups):
            stream += matmul(
                r.att_got[micro * groups + group], r.w_out[pl.ds(group * width, width), :]
            )
        r.mid[rows, :] = stream
    xhat, inverse_two = norm_parts(r.mid[...])
    r.hat_two[...] = xhat
    r.normed[0] = rounded(xhat * gain + bias)
    to_core = wires.send(r.normed.at[0], r.normed.at[1], core)
    to_far = wires.send(r.normed.at[0], r.normed.at[2], ahead)

    def feed(slot):
        hidden = matmul(r.normed[slot], r.w_up[...]) + r.b_own[...]
        cdf = 0.5 * (1.0 + lax.erf(hidden * (2.0**-0.5)))
        density = jnp.exp(-0.5 * hidden * hidden) * ((2.0 * math.pi) ** -0.5)
        r.act[slot] = rounded(hidden * cdf)
        r.part[slot] = rounded(cdf + hidden * density)

    def feed_back(slot):
        grad = contract_cols(r.cots[slot], r.w_ff[...])
        r.grad_hid[slot] = rounded(grad * r.part[slot].astype(f32))
        r.part[slot] = rounded(contract_cols(r.grad_hid[slot], r.w_up[...]))

    def feed_out(slot):
        r.out_part[slot] = rounded(matmul(r.act[slot], r.w_ff[...]))

    part_core, part_far_core, part_far, forward = (
        wires.later(r.part.at[1], r.part_got.at[0], core),
        wires.later(r.part.at[3], r.part_got.at[1], core),
        wires.later(r.part.at[2], r.part_got.at[2], ahead),
        wires.later(r.normed.at[2], r.normed.at[3], core),
    )

    def feed_step(slot, carry):
        @pl.when(slot == 1)
        def _():
            to_core.wait_recv()

        @pl.when(slot == 2)
        def _():
            to_far.wait_recv()
            forward.start()

        @pl.when(slot == 3)
        def _():
            forward.wait_recv()

        feed(slot)
        return carry

    lax.fori_loop(0, 4, feed_step, 0)
    cot_core.wait_recv()
    cot_fwd.wait_recv()
    pl.when(owns_block)(down_load.wait)
    pl.when(jnp.logical_not(owns_block))(down_copy.wait_recv)

    def feed_back_step(step, carry):
        slot = 3 - step
        feed_back(slot)

        @pl.when(slot == 3)
        def _():
            part_far_core.start()

        @pl.when(slot == 2)
        def _():
            part_far_core.wait_recv()
            r.part[2] = rounded(r.part[2].astype(f32) + r.part_got[1].astype(f32))
            part_far.start()

        @pl.when(slot == 1)
        def _():
            part_core.start()

        return carry

    lax.fori_loop(0, 4, feed_back_step, 0)
    pair = line // 2
    collects = lax.rem(line, 2) == 1 - pair
    mirrored = {"ctx": mirror_at}
    down_steps = (r.down_grad, (upper, side, distant_half), (far, beside, mirrored), (r.down_y, r.down_x, r.down_z))
    up_steps = (r.up_grad, (upper, distant_half, side), (far, mirrored, beside), (r.up_y, r.up_z, r.up_x))
    out_steps = (r.out_piece, (odd, distant_half, side), (ahead, mirrored, beside), (r.out_a, r.out_z, r.out_x))

    def give(steps, at):
        grad, mine, where, got = steps
        index = mine[:at] + (1 - mine[at],)
        if at == 0:
            source = grad.at[index[0]]
        elif at == 1:
            source = grad.at[index[0], index[1]]
        else:
            source = grad.at[index[0], index[1], index[2]]
        return wires.send(source, got[at], where[at])

    def take(steps, at, copy):
        grad, mine, _, got = steps
        copy.wait_recv()
        if at == 0:
            grad[mine[0]] = rounded(grad[mine[0]].astype(f32) + got[0][...].astype(f32))
        elif at == 1:
            grad[mine[0], mine[1]] = rounded(
                grad[mine[0], mine[1]].astype(f32) + got[1][...].astype(f32)
            )
        else:
            return grad[mine[0], mine[1], mine[2]].astype(f32) + got[2][...].astype(f32)

    flat_cot = r.cots[...].reshape(4 * own, model)
    flat_act = r.act[...].reshape(4 * own, ff)
    grads = rounded(contract_rows(flat_cot, flat_act))
    narrow = model // ctx_size
    for at in range(ctx_size):
        r.down_grad[at // 2 % 2, at % 2, at // 4] = grads[at * narrow : (at + 1) * narrow]
    down_y = give(down_steps, 0)
    out_core, out_far_core = (
        wires.later(r.out_part.at[1], r.out_got.at[0], core),
        wires.later(r.out_part.at[3], r.out_got.at[1], core),
    )

    def out_step(step, carry):
        slot = 3 - step
        feed_out(slot)

        @pl.when(slot == 3)
        def _():
            out_far_core.start()

        @pl.when(slot == 1)
        def _():
            out_core.start()

        return carry

    lax.fori_loop(0, 4, out_step, 0)
    flat_grad = r.grad_hid[...].reshape(4 * own, ff)
    d_bias_up = jnp.sum(flat_grad.astype(f32), axis=0, keepdims=True)
    for at in range(4):
        r.vec[4 + at : 5 + at, :] = jnp.where(ff_block == at, d_bias_up, 0.0)
    flat_normed = r.normed[...].reshape(4 * own, model)
    size = model // 4
    for at in range(shards):
        grads = rounded(
            contract_rows(flat_normed, flat_grad[:, at * ff // shards : (at + 1) * ff // shards])
        )
        for row in range(4):
            r.up_grad[row // 2, row % 2, at] = grads[row * size : (row + 1) * size]
    out_far_core.wait_recv()
    r.out_part[2] = rounded(r.out_part[2].astype(f32) + r.out_got[1].astype(f32))

    part_core.wait_recv()
    part_far.wait_recv()
    grad_normed = r.part[0].astype(f32) + r.part_got[0].astype(f32) + r.part_got[2].astype(f32)
    xhat = r.hat_two[...]
    r.vec[2:3, :] = jnp.sum(grad_normed * xhat, axis=0, keepdims=True)
    r.vec[3:4, :] = jnp.sum(grad_normed, axis=0, keepdims=True)
    r.grad_mid[...] = r.cot[...].astype(f32) + norm_back(xhat, inverse_two, grad_normed, gain)
    branch = rounded(r.grad_mid[...])
    for group in range(groups):
        grad = rounded(contract_cols(branch, r.w_out[pl.ds(group * width, width), :]))
        for micro in range(mbs):
            r.att_out[micro * groups + group] = folded(
                grad[micro * tokens : (micro + 1) * tokens]
            )
    att_in = []
    for step in range(1, ctx_size):
        peer = lax.rem(ctx + step, ctx_size)
        att_in.append(wires.send(r.att_out.at[peer], r.grad_in.at[ctx], {"ctx": peer}))
    r.grad_in[ctx] = r.att_out[ctx]
    up_y = give(up_steps, 0)
    for group in range(groups):
        total = None
        for micro in range(mbs):
            some = contract_rows(
                branch[micro * tokens : (micro + 1) * tokens], r.att_got[micro * groups + group]
            )
            total = some if total is None else total + some
        total = rounded(total)
        for at in range(ctx_size):
            r.out_grad[group, at // 2 % 2, at // 4, at % 2] = folded(
                total[at * narrow : (at + 1) * narrow]
            )
    out_grad_core = wires.send(r.out_grad.at[swap(dp)], r.out_grad_got.at[0], core)
    out_grad_far_core = wires.send(
        r.out_grad.at[lax.rem(swap(dp) + 2, 4)], r.out_grad_got.at[1], core
    )
    take(down_steps, 0, down_y)
    down_x = give(down_steps, 1)
    for copy in att_in:
        copy.wait_recv()
    out_far = wires.send(r.out_part.at[2], r.out_got.at[2], ahead)
    out_grad_far_core.wait_recv()
    mine = lax.rem(dp + 2, 4)
    r.out_grad[mine] = rounded(r.out_grad[mine].astype(f32) + r.out_grad_got[1].astype(f32))
    out_grad_far = wires.send(r.out_grad.at[mine], r.out_grad_got.at[2], far)
    for place in range(ctx_size):
        r.grad_att[place] = unfolded(r.grad_in[place])

    r.suffix[...] = jnp.zeros_like(r.suffix)
    r.acc[...] = jnp.zeros_like(r.acc)

    def back_block(start):
        reach = start + block
        rows = pl.ds(start, block)
        probs_ref, slope_ref = getattr(r, "probs%d" % start), getattr(r, "slope%d" % start)
        total = None
        first = start // tokens
        grad_block = r.grad_att[first : first + per_block].reshape(block, width)
        for head in range(hpg):
            at = head * HD
            query_t = rounded((r.proj[rows, at : at + HD].astype(f32) * scale).T)
            key = r.proj[:reach, width + at : width + at + HD]
            value = r.proj[:reach, 2 * width + at : 2 * width + at + HD]
            grad = grad_block[:, at : at + HD].astype(f32) * r.inverse[rows, head : head + 1]
            delta = jnp.sum(grad * r.out[rows, at : at + HD], axis=1, keepdims=True)
            probs = probs_ref[head]
            grad_probs = contract_cols(rounded(grad), value)
            grad_logits = probs.astype(f32) * (grad_probs - delta)
            total = grad_logits if total is None else total + grad_logits
            grad_scores = rounded(grad_logits)
            r.grad_proj[rows, at : at + HD] = rounded(matmul(grad_scores, key) * scale)
            r.acc[at : at + HD, :reach] += matmul(query_t, grad_scores)
            r.acc[width + at : width + at + HD, :reach] += matmul(rounded(grad.T), probs)
        query_t = rounded((r.proj[rows, 3 * width : 3 * width + HD].astype(f32) * scale).T)
        key = r.proj[:reach, 3 * width + HD : 3 * width + 2 * HD]
        flow = r.suffix[:, :reach] + matmul(later, rounded(total))
        grad_scores = rounded(-flow * slope_ref[...].astype(f32))
        r.grad_proj[rows, 3 * width : 3 * width + HD] = rounded(matmul(grad_scores, key) * scale)
        r.acc[2 * width : 2 * width + HD, :reach] += matmul(query_t, grad_scores)
        r.suffix[:, :reach] += jnp.sum(total, axis=0, keepdims=True)

    def one_grad(place):
        rows = pl.ds(pl.multiple_of(place * tokens, tokens), tokens)
        grad = contract_cols(r.grad_proj[rows, :], r.w_pick[...].reshape(model, 3 * width + 2 * HD))
        r.vec[0:1, :] += jnp.sum(grad * r.hat_one[rows, :].astype(f32), axis=0, keepdims=True)
        r.vec[1:2, :] += jnp.sum(grad, axis=0, keepdims=True)
        return grad

    r.vec[0:2, :] = jnp.zeros((2, model), f32)
    one_side = {}

    def one_copy(source, target, kind, at, to_line):
        return pltpu.make_async_remote_copy(
            src_ref=source,
            dst_ref=target,
            send_sem=r.one_send.at[at],
            recv_sem=r.one_recv.at[kind],
            device_id={"ctx": to_line * 2 + side},
            device_id_type=MESH,
        )

    def to_near(at):
        return one_copy(r.one_ready.at[at], r.one_near, 0, at, at)

    def to_far(at):
        return one_copy(r.one_ready.at[at], r.one_far, 1, at, at)

    def to_collect(at):
        return one_copy(r.one_ready.at[at], r.one_pair.at[at % 2], 2 + at % 2, at, swap(line))

    def finish_block(at):
        start = at * block
        reach = start + block
        r.grad_proj[start:reach, width : 3 * width] = rounded(r.acc[: 2 * width, start:reach].T)
        r.grad_proj[start:reach, 3 * width + HD :] = rounded(r.acc[2 * width :, start:reach].T)
        one_side[at] = wires.later(r.one_piece.at[at], r.one_side.at[at], beside)

        def one_step(step, carry):
            r.one_own[at] = one_grad(at * 2 + lax.rem(1 - side + step, 2))

            @pl.when(step == 0)
            def _():
                r.one_piece[at] = rounded(r.one_own[at])
                one_side[at].start()

            return carry

        lax.fori_loop(0, 2, one_step, 0)

    def pass_on(at):
        one_side[at].wait_recv()
        r.one_ready[at] = rounded(r.one_own[at] + r.one_side[at].astype(f32))
        near, shared = to_near(at), to_collect(at)

        if at != 2:

            @pl.when((pair == at // 2) & (line != at))
            def _():
                near.start()

        @pl.when((pair != at // 2) & jnp.logical_not(collects))
        def _():
            shared.start()

    def collect(at):
        distant = to_far(at)

        @pl.when((pair != at // 2) & collects)
        def _():
            arrived(r.one_ready.at[at], r.one_pair.at[at % 2], r.one_recv.at[2 + at % 2])
            r.one_ready[at] = rounded(
                r.one_own[at] + r.one_side[at].astype(f32) + r.one_pair[at % 2].astype(f32)
            )
            distant.start()

    back_block(3 * block)
    finish_block(3)
    back_block(2 * block)
    finish_block(2)
    take(down_steps, 1, down_x)
    down_z = give(down_steps, 2)
    take(up_steps, 0, up_y)
    up_z = give(up_steps, 1)
    back_block(block)
    finish_block(1)
    pass_on(3)
    back_block(0)
    finish_block(0)

    size = model // 4
    part = math.gcd(width, 3 * model // ctx_size)
    per = width // part
    folded_part, folded_head = part // 2, HD // 2

    def store_qkv(grads, parts):
        for at in range(4):
            cols = slice(at * size, (at + 1) * size)
            for source, target, count in parts:
                r.qkv_grad[at, target : target + count // 2, :] = folded(
                    grads[source : source + count, cols]
                )

    tail = 3 * width // 2
    grads_q = rounded(
        contract_rows(
            jnp.concatenate(
                [r.grad_proj[:, :width], r.grad_proj[:, 3 * width : 3 * width + HD]], axis=1
            ),
            r.normed_one[...],
        )
    )
    store_qkv(
        grads_q,
        [(at * part, at * folded_part, part) for at in range(per)] + [(width, tail, HD)],
    )
    grads_kv = rounded(matmul(rounded(r.acc[...]), r.normed_one[...]))
    store_qkv(
        grads_kv,
        [(at * part, (per + at) * folded_part, part) for at in range(2 * per)]
        + [(2 * width, tail + folded_head, HD)],
    )
    qkv_far_core = wires.send(r.qkv_grad.at[lax.rem(swap(dp) + 2, 4)], r.qkv_got.at[1], core)
    qkv_core = wires.send(r.qkv_grad.at[swap(dp)], r.qkv_got.at[0], core)
    out_grad_core.wait_recv()
    out_grad_far.wait_recv()
    r.out_piece[...] = rounded(
        r.out_grad[dp].astype(f32)
        + r.out_grad_got[0].astype(f32)
        + r.out_grad_got[2].astype(f32)
    )
    out_a = give(out_steps, 0)
    for row in range(8):
        r.vec_rows[row] = r.vec[row : row + 1, :]
    vec_in = []
    for step in range(1, ctx_size):
        peer = lax.rem(ctx + step, ctx_size)
        vec_in.append(wires.send(r.vec_rows.at[peer], r.vec_got.at[ctx], {"ctx": peer}))
    r.vec_got[ctx] = r.vec_rows[ctx]
    pass_on(2)
    qkv_far_core.wait_recv()
    r.qkv_grad[mine] = rounded(r.qkv_grad[mine].astype(f32) + r.qkv_got[1].astype(f32))
    qkv_far = wires.send(r.qkv_grad.at[mine], r.qkv_got.at[2], far)
    collect(3)
    pass_on(1)
    pass_on(0)
    near_two = to_near(2)

    @pl.when(line == 3)
    def _():
        near_two.start()

    take(up_steps, 1, up_z)
    up_x = give(up_steps, 2)
    collect(2)
    qkv_core.wait_recv()
    qkv_far.wait_recv()
    r.qkv_sum[...] = rounded(
        r.qkv_grad[dp].astype(f32) + r.qkv_got[0].astype(f32) + r.qkv_got[2].astype(f32)
    )
    slots = r.deal_got.shape[0]

    def outgoing(kind, half):
        section = (kind * groups + my_group) * per + half
        target, slot = section // slots, lax.rem(section, slots)
        index = kind * per + half
        return target, slot, index, pltpu.make_async_remote_copy(
            src_ref=r.qkv_sum.at[pl.ds(index * folded_part, folded_part)],
            dst_ref=r.deal_got.at[slot, my_mb],
            send_sem=r.deal_send.at[index],
            recv_sem=r.deal_recv.at[slot, my_mb],
            device_id={"ctx": target},
            device_id_type=MESH,
        )

    def extra_copy(kind):
        return pltpu.make_async_remote_copy(
            src_ref=r.qkv_sum.at[pl.ds(tail + kind * folded_head, folded_head)],
            dst_ref=r.extra_got.at[ctx],
            send_sem=r.extra_send.at[kind],
            recv_sem=r.extra_recv.at[ctx],
            device_id={"ctx": kind * groups * per // slots},
            device_id_type=MESH,
        )

    for kind in range(3):
        for half in range(per):
            target, slot, index, copy = outgoing(kind, half)

            @pl.when(target != ctx)
            def _():
                copy.start()

            @pl.when(target == ctx)
            def _():
                r.deal_got[slot, my_mb] = r.qkv_sum[
                    index * folded_part : (index + 1) * folded_part, :
                ]

    for kind in range(2):
        target = kind * groups * per // slots
        copy = extra_copy(kind)

        @pl.when(ctx != target)
        def _():
            copy.start()

        @pl.when(ctx == target)
        def _():
            r.extra_got[ctx] = r.qkv_sum[
                tail + kind * folded_head : tail + (kind + 1) * folded_head, :
            ]

    collect(1)
    collect(0)
    take(out_steps, 0, out_a)
    out_z = give(out_steps, 1)
    for copy in vec_in:
        copy.wait_recv()
    total = r.vec_got[0]
    for at in range(1, ctx_size):
        total += r.vec_got[at]
    r.vec_sum[...] = total
    vec_out = [
        wires.send(r.vec_sum, r.vecs.at[dp], where) for where in (core, far, far_core)
    ]
    r.vecs[dp] = total
    for copy in vec_out:
        copy.wait_recv()
    r.vec_total[...] = (r.vecs[0] + r.vecs[1]) + (r.vecs[2] + r.vecs[3])
    vec_all = [wires.send(r.vec_total, r.vec_last.at[ctx], where) for where in around]
    r.vec_last[ctx] = r.vec_total[...]
    r.down_sum[...] = rounded(take(down_steps, 2, down_z))
    down_final = pltpu.make_async_remote_copy(
        src_ref=r.down_sum,
        dst_ref=r.down_final,
        send_sem=r.up_send.at[1],
        recv_sem=r.up_recv.at[1],
        device_id=across,
        device_id_type=MESH,
    )

    @pl.when(jnp.logical_not(owns_block))
    def _():
        down_final.start()

    @pl.when(owns_block)
    def _():
        r.down_final[...] = r.down_sum[...]

    out_core.wait_recv()
    out_far.wait_recv()
    r.layer[...] = rounded(
        r.mid[...]
        + (r.out_part[0].astype(f32) + r.out_got[0].astype(f32) + r.out_got[2].astype(f32))
    )
    r.up_sum[...] = rounded(take(up_steps, 2, up_x))
    stays = (2 * upper + distant_half == dp) & (2 * ff_block + side == ctx)
    up_copy = pltpu.make_async_remote_copy(
        src_ref=r.up_sum,
        dst_ref=r.up_final,
        send_sem=r.up_send.at[0],
        recv_sem=r.up_recv.at[0],
        device_id=up_to,
        device_id_type=MESH,
    )

    @pl.when(jnp.logical_not(stays))
    def _():
        up_copy.start()

    @pl.when(stays)
    def _():
        r.up_final[...] = r.up_sum[...]

    take(out_steps, 1, out_z)
    out_x = give(out_steps, 2)
    xhat, inverse_one = norm_parts(r.x[...].astype(f32))
    arrived(r.one_ready.at[0], r.one_near, r.one_recv.at[0])
    arrived(r.one_ready.at[0], r.one_far, r.one_recv.at[1])
    near = r.one_ready[line].astype(f32) + r.one_near[...].astype(f32)
    distant = r.one_far[...].astype(f32)
    for micro in range(mbs):
        grad = jnp.where(pair == micro, near, distant)
        rows = slice(micro * tokens, (micro + 1) * tokens)
        r.d_x[rows, :] = rounded(
            r.grad_mid[rows, :] + norm_back(xhat[rows], inverse_one[rows], grad, gain_one)
        )
    r.d_out[...] = unfolded(take(out_steps, 2, out_x)).T

    @pl.when(jnp.logical_not(stays))
    def _():
        up_copy.wait_send()
        up_copy.wait_recv()

    r.d_up[...] = r.up_final[...].astype(f32)

    @pl.when(jnp.logical_not(owns_block))
    def _():
        down_final.wait_send()
        down_final.wait_recv()

    @pl.when(owns_block)
    def _():
        down_copy.wait_send()

    r.d_down[...] = r.down_final[...].astype(f32)

    for kind in range(3):
        for half in range(per):
            target, slot, index, copy = outgoing(kind, half)

            @pl.when(target != ctx)
            def _():
                copy.wait_send()

    for slot in range(slots):
        section = ctx * slots + slot
        source_group = lax.rem(section // per, groups)
        for place in range(mbs):

            @pl.when(place * groups + source_group != ctx)
            def _():
                arrived(
                    r.qkv_sum.at[pl.ds(0, folded_part)],
                    r.deal_got.at[slot, place],
                    r.deal_recv.at[slot, place],
                )

        total = r.deal_got[slot, 0].astype(f32)
        for place in range(1, mbs):
            total += r.deal_got[slot, place].astype(f32)
        r.deal_sum[slot * part : (slot + 1) * part, :] = unfolded(total)
    for kind in range(2):
        section = kind * groups * per
        target, slot = section // slots, section % slots
        copy = extra_copy(kind)

        @pl.when(ctx != target)
        def _():
            copy.wait_send()

        @pl.when(ctx == target)
        def _():
            total = jnp.zeros((folded_head, 2 * size), f32)
            for place in range(ctx_size):
                if place != target:
                    arrived(
                        r.qkv_sum.at[pl.ds(0, folded_head)], r.extra_got.at[place], r.extra_recv.at[place]
                    )
                total += r.extra_got[place].astype(f32)
            r.deal_sum[slot * part : slot * part + HD, :] += unfolded(total)

    r.d_qkv[...] = r.deal_sum[...].T
    for copy in vec_all:
        copy.wait_recv()
    for row in range(4):
        r.d_vec[row : row + 1, :] = r.vec_last[row]
        r.d_bias[row] = r.vec_last[4 + row]
    wires.drain()
    for place in range(ctx_size):
        copy = att_copy(place)

        @pl.when(ctx != place)
        def _():
            copy.wait_send()

    for at in range(lines):
        copy = to_near(at)

        @pl.when(line != at)
        def _():
            copy.wait_send()


LAYER_COPIES = 112


def layer(collective_id, groups, shards, lengths, w_down, large):
    bf16, f32 = jnp.bfloat16, jnp.float32
    own, model = large["x"].shape
    ctx_size = lax.axis_size("ctx")
    tokens = own * groups // ctx_size
    hpg = model // HD // groups
    width = hpg * HD
    row_length = ctx_size * tokens
    lines = ctx_size // 2
    ff = w_down.shape[0]
    size, shard = model // 4, 3 * model // ctx_size
    part = math.gcd(width, shard)
    slots, mbs = shard // part, ctx_size // groups
    picked = 3 * width + 2 * HD
    vec_rows = 8
    narrow = model // ctx_size
    vmem = pl.BlockSpec(memory_space=pltpu.VMEM)
    anywhere = pl.BlockSpec(memory_space=pl.ANY)
    outs = dict(
        layer=((own, model), bf16),
        d_x=((own, model), bf16),
        d_vec=((4, model), f32),
        d_bias=((4, ff // model, model), f32),
        d_qkv=((size, shard), f32),
        d_out=((size, narrow), f32),
        d_up=((size, ff // shards), f32),
        d_down=((narrow, ff), f32),
    )
    scratch = {name: (array.shape, array.dtype) for name, array in large.items()}
    scratch |= dict(
        x_row=((ctx_size, tokens, model), bf16),
        hat_one=((row_length, model), bf16),
        normed_one=((row_length, model), bf16),
        w_pick=((4, size, picked), bf16),
        proj=((row_length, picked), bf16),
        w_out=((model, model), bf16),
        w_up=((model, ff), bf16),
        out=((row_length, width), f32),
        inverse=((row_length, hpg), f32),
        att=((ctx_size, tokens // 2, 2 * width), bf16),
        att_in=((ctx_size, tokens // 2, 2 * width), bf16),
        b_own=((1, ff), f32),
        att_got=((ctx_size, tokens, width), bf16),
        cots=((4, own, model), bf16),
        mid=((own, model), f32),
        hat_two=((own, model), f32),
        grad_mid=((own, model), f32),
        normed=((4, own, model), bf16),
        act=((4, own, ff), bf16),
        grad_hid=((4, own, ff), bf16),
        part=((4, own, model), bf16),
        out_part=((4, own, model), bf16),
        part_got=((3, own, model), bf16),
        out_got=((3, own, model), bf16),
        att_out=((ctx_size, tokens // 2, 2 * width), bf16),
        grad_in=((ctx_size, tokens // 2, 2 * width), bf16),
        grad_att=((ctx_size, tokens, width), bf16),
        down_grad=((2, 2, 2, narrow, ff), bf16),
        down_y=((2, 2, narrow, ff), bf16),
        down_x=((2, narrow, ff), bf16),
        down_z=((narrow, ff), bf16),
        up_grad=((2, 2, 2, size, ff // shards), bf16),
        up_y=((2, 2, size, ff // shards), bf16),
        up_z=((2, size, ff // shards), bf16),
        up_x=((size, ff // shards), bf16),
        up_sum=((size, ff // shards), bf16),
        up_final=((size, ff // shards), bf16),
        down_sum=((narrow, ff), bf16),
        down_final=((narrow, ff), bf16),
        w_ff=(w_down.shape, bf16),
        out_grad=((4, 2, 2, 2, narrow // 2, 2 * size), bf16),
        out_grad_got=((3, 2, 2, 2, narrow // 2, 2 * size), bf16),
        out_piece=((2, 2, 2, narrow // 2, 2 * size), bf16),
        out_a=((2, 2, narrow // 2, 2 * size), bf16),
        out_z=((2, narrow // 2, 2 * size), bf16),
        out_x=((narrow // 2, 2 * size), bf16),
        suffix=((1, row_length), f32),
        acc=((2 * width + HD, row_length), f32),
        grad_proj=((row_length, picked), bf16),
        one_piece=((lines, tokens, model), bf16),
        one_own=((lines, tokens, model), f32),
        one_side=((lines, tokens, model), bf16),
        one_ready=((lines, tokens, model), bf16),
        one_near=((tokens, model), bf16),
        one_far=((tokens, model), bf16),
        one_pair=((2, tokens, model), bf16),
        qkv_grad=((4, picked // 2, 2 * size), bf16),
        qkv_got=((3, picked // 2, 2 * size), bf16),
        qkv_sum=((picked // 2, 2 * size), bf16),
        deal_got=((slots, mbs, part // 2, 2 * size), bf16),
        deal_sum=((shard, size), f32),
        extra_got=((ctx_size, HD // 2, 2 * size), bf16),
        vec=((vec_rows, model), f32),
        vec_rows=((vec_rows, 1, model), f32),
        vec_got=((ctx_size, 1, model), f32),
        vec_sum=((1, model), f32),
        vecs=((4, 1, model), f32),
        vec_total=((1, model), f32),
        vec_last=((ctx_size, 1, model), f32),
    )
    for start in range(0, row_length, QUERY_BLOCK):
        reach = start + QUERY_BLOCK
        scratch["probs%d" % start] = ((hpg, QUERY_BLOCK, reach), bf16)
        scratch["slope%d" % start] = ((QUERY_BLOCK, reach), bf16)
    dma = pltpu.SemaphoreType.DMA
    sems = dict(
        send_sem=dma((LAYER_COPIES,)),
        recv_sem=dma((LAYER_COPIES,)),
        load_sem=dma((len(large),)),
        att_send=dma((ctx_size,)),
        att_recv=dma((ctx_size,)),
        one_send=dma((lines,)),
        one_recv=dma((4,)),
        ff_sem=dma((3,)),
        up_send=dma((2,)),
        up_recv=dma((2,)),
        deal_send=dma((3 * (width // part),)),
        deal_recv=dma((slots, mbs)),
        extra_send=dma((2,)),
        extra_recv=dma((ctx_size,)),
    )
    names = list(outs) + list(scratch) + list(sems)
    return pl.pallas_call(
        partial(layer_body, (groups, shards), list(large), names),
        out_shape=[jax.ShapeDtypeStruct(*spec) for spec in outs.values()],
        in_specs=[pl.BlockSpec(memory_space=pltpu.SMEM)] + [anywhere] * (1 + len(large)),
        out_specs=[vmem] * len(outs),
        scratch_shapes=[pltpu.VMEM(*spec) for spec in scratch.values()] + list(sems.values()),
        compiler_params=pltpu.CompilerParams(
            collective_id=collective_id, has_side_effects=True, vmem_limit_bytes=63 * 1024 * 1024
        ),
        name="layer",
    )(lengths, w_down, *large.values())


def finish_body(*refs):
    sources, targets = refs[:8], refs[8:]
    for source, target in zip(sources[:6], targets[:6]):
        target[...] = source[...]
    for row in range(4):
        targets[6 + row][...] = sources[6][row]
    columns = sources[7].shape[2]
    rows = sources[7].shape[1]
    for at in range(4 * rows):
        targets[10][at * columns : (at + 1) * columns] = sources[7][at // rows, at % rows]


def finish(*arrays):
    vmem = pl.BlockSpec(memory_space=pltpu.VMEM)
    shape = jax.ShapeDtypeStruct
    model = arrays[6].shape[1]
    return pl.pallas_call(
        finish_body,
        out_shape=[shape(array.shape, array.dtype) for array in arrays[:6]]
        + [shape((model,), jnp.float32)] * 4
        + [shape((arrays[7].size,), jnp.float32)],
        in_specs=[vmem] * len(arrays),
        out_specs=[vmem] * 11,
        name="finish",
    )(*arrays)


def per_head_device(
    layer_input,
    doc_lengths,
    ln1_gain,
    ln1_bias,
    w_qkv,
    w_out,
    ln2_gain,
    ln2_bias,
    w_up,
    b_up,
    w_down,
    cotangent,
):
    mbs, _, tokens, model = layer_input.shape
    ctx_size, dp_size = lax.axis_size("ctx"), lax.axis_size("dp")
    large = dict(
        x=layer_input.reshape(mbs * tokens, model),
        w_qkv=w_qkv,
        gain_one=ln1_gain,
        bias_one=ln1_bias,
        cot=cotangent.reshape(mbs * tokens, model),
        w_out_own=w_out,
        w_up_own=w_up,
        gain_two=ln2_gain,
        bias_two=ln2_bias,
        b_up=b_up,
    )
    layer_out, d_x, d_vec, d_bias, d_qkv, d_out, d_up, d_down = layer(
        0, ctx_size // mbs, ctx_size // dp_size, doc_lengths, w_down, large
    )
    layer_out, d_x, d_qkv, d_out, d_up, d_down, gain_one, bias_one, gain_two, bias_two, d_bias = finish(
        layer_out, d_x, d_qkv, d_out, d_up, d_down, d_vec, d_bias
    )
    return (
        layer_out.reshape(mbs, 1, tokens, model),
        d_x.reshape(mbs, 1, tokens, model),
        gain_one,
        bias_one,
        d_qkv,
        d_out,
        gain_two,
        bias_two,
        d_up,
        d_bias,
        d_down.T,
    )


def on_device(*arguments):
    layer_input = arguments[0]
    mbs, model = layer_input.shape[0], layer_input.shape[3]
    heads, ctx_size, dp_size = model // HD, lax.axis_size("ctx"), lax.axis_size("dp")
    groups = ctx_size // mbs
    fits = (
        ctx_size % mbs == 0
        and heads % groups == 0
        and dp_size == 4
        and ctx_size % dp_size == 0
        and ctx_size == 8
        and mbs == 2
        and arguments[9].shape[0] == 4 * model
        and (layer_input.shape[2] * ctx_size) % QUERY_BLOCK == 0
    )
    return (per_head_device if fits else per_token_device)(*arguments)


def solution(mesh):
    return jax.shard_map(
        on_device,
        mesh=mesh,
        in_specs=(
            P(None, "dp", "ctx", None),
            P(None, "dp", None),
            P(),
            P(),
            P("dp", None),
            P("dp", None),
            P(),
            P(),
            P("dp", None),
            P(),
            P("dp", None),
            P(None, "dp", "ctx", None),
        ),
        out_specs=(
            P(None, "dp", "ctx", None),
            P(None, "dp", "ctx", None),
            P(),
            P(),
            P("dp", "ctx"),
            P("dp", "ctx"),
            P(),
            P(),
            P("dp", "ctx"),
            P(),
            P("dp", "ctx"),
        ),
        check_vma=False,
    )
```

```python
import math
from functools import partial
from types import SimpleNamespace

import jax
import jax.numpy as jnp
from jax import lax
from jax.experimental import pallas as pl
from jax.experimental.pallas import tpu as pltpu
from jax.sharding import PartitionSpec as P

HD = 64


NORM_EPSILON = 1e-05
MASKED = -1e30
START_TOP = -1e20


def prefix_2(array, axis, combine, identity, reverse):
    peers, index = (lax.axis_size(axis), lax.axis_index(axis))
    everything = lax.all_gather(array, axis)
    start = jnp.broadcast_to(jnp.asarray(identity, array.dtype), array.shape)

    def turn(k, before):
        at = peers - 1 - k if reverse else k
        reached = at > index if reverse else at < index
        new = combine(before, everything[at])
        return jnp.where(reached, new, before)

    return lax.fori_loop(0, peers, turn, start)


def layer_norm(value, gain, bias):
    row_mean = jnp.mean(value, axis=-1, keepdims=True)
    centered = value - row_mean
    spread = jnp.mean(centered * centered, axis=-1, keepdims=True)
    return centered * lax.rsqrt(spread + NORM_EPSILON) * gain + bias


def matmul(left, right):
    return jnp.dot(left, right, preferred_element_type=jnp.float32)


def contract_rows(left, right):
    return lax.dot_general(
        left, right, (((0,), (0,)), ((), ())), preferred_element_type=jnp.float32
    )


def contract_cols(left, right):
    return lax.dot_general(
        left, right, (((1,), (1,)), ((), ())), preferred_element_type=jnp.float32
    )


def segment_table(lengths, row_length):
    doc_ends = jnp.cumsum(lengths)
    places = jnp.arange(row_length, dtype=jnp.int32)
    segment = jnp.sum((places[:, None] >= doc_ends[None, :]).astype(jnp.int32), axis=1)
    opening = jnp.concatenate([jnp.ones((1,), jnp.bool_), segment[1:] != segment[:-1]])
    return (segment, opening)


def add_up(earlier, later):
    return earlier + later


def per_token_device(
    layer_input,
    doc_lengths,
    ln1_gain,
    ln1_bias,
    w_qkv,
    w_out,
    ln2_gain,
    ln2_bias,
    w_up,
    b_up,
    w_down,
    cotangent,
):
    micro_count = layer_input.shape[0]
    query_rows = layer_input.shape[2]
    model_width = layer_input.shape[3]
    head_count = model_width // HD
    row_length = query_rows * lax.axis_size("ctx")
    key_block = min(512, row_length)
    score_scale = HD ** (-0.5)
    strength = 8.0 / row_length
    ctx_place = lax.axis_index("ctx")
    query_pos = ctx_place * query_rows + jnp.arange(query_rows, dtype=jnp.int32)
    block_total = ((ctx_place + 1) * query_rows + key_block - 1) // key_block
    later_heads = (jnp.arange(head_count) > 0).astype(jnp.float32)[:, None, None]
    zeros_row = jnp.zeros((row_length,), jnp.float32)
    gelu_exact = partial(jax.nn.gelu, approximate=False)
    output_list = []
    input_grads = []
    matrix_total = None
    vector_total = None
    for micro_step in range(micro_count):
        w_qkv_all, w_out_all, w_up_all, w_down_all = (
            lax.all_gather(w_qkv, "dp", axis=0, tiled=True),
            lax.all_gather(w_out, "dp", axis=0, tiled=True),
            lax.all_gather(w_up, "dp", axis=0, tiled=True),
            lax.all_gather(w_down, "dp", axis=0, tiled=True),
        )
        inputs = layer_input[micro_step, 0].astype(jnp.float32)
        segment, opening = segment_table(doc_lengths[micro_step, 0], row_length)
        query_seg = lax.dynamic_slice_in_dim(segment, ctx_place * query_rows, query_rows, 0)
        normed_one = layer_norm(inputs, ln1_gain, ln1_bias).astype(jnp.bfloat16)
        projected = matmul(normed_one, w_qkv_all).astype(jnp.bfloat16)
        queries = projected[:, :model_width]
        queries3 = queries.reshape(query_rows, head_count, HD)
        query_zero = queries[:, :HD]
        keys_all, values_all = (
            lax.all_gather(projected[:, model_width : 2 * model_width], "ctx", axis=0, tiled=True),
            lax.all_gather(projected[:, 2 * model_width :], "ctx", axis=0, tiled=True),
        )

        def masks(key_start):
            key_seg = lax.dynamic_slice_in_dim(segment, key_start, key_block, 0)
            key_open = lax.dynamic_slice_in_dim(opening, key_start, key_block, 0)
            key_pos = key_start + jnp.arange(key_block, dtype=jnp.int32)
            same_doc = query_seg[:, None] == key_seg[None, :]
            allowed = same_doc & (key_pos[None, :] <= query_pos[:, None])
            chosen = (
                same_doc
                & (key_pos[None, :] < query_pos[:, None])
                & jnp.logical_not(key_open)[None, :]
            )
            return (allowed, chosen.astype(jnp.float32))

        def head_scores(key_start):
            key_zero = lax.dynamic_slice_in_dim(keys_all, key_start, key_block, 0)[:, :HD]
            return (key_zero, contract_cols(query_zero, key_zero) * score_scale)

        def block_keys(key_start):
            keys3 = lax.dynamic_slice_in_dim(keys_all, key_start, key_block, 0).reshape(
                key_block, head_count, HD
            )
            values3 = lax.dynamic_slice_in_dim(values_all, key_start, key_block, 0).reshape(
                key_block, head_count, HD
            )
            return (keys3, values3)

        def logits_of(key_start, keys3):
            allowed, chosen = masks(key_start)
            raw_scores = (
                jnp.einsum("qhd,khd->hqk", queries3, keys3, preferred_element_type=jnp.float32)
                * score_scale
            )
            picked = strength * jax.nn.softplus(raw_scores[0]) * chosen
            before = lax.dynamic_slice_in_dim(prefix, key_start, key_block, 0)
            penalty = before[None, :] + jnp.cumsum(picked, axis=0) - picked
            return jnp.where(allowed[None], raw_scores - penalty[None], MASKED)

        def total_block(block_index, totals):
            key_start = block_index * key_block
            _, chosen = masks(key_start)
            _, first_scores = head_scores(key_start)
            picked = strength * jax.nn.softplus(first_scores) * chosen
            return lax.dynamic_update_slice_in_dim(totals, jnp.sum(picked, axis=0), key_start, 0)

        totals = lax.fori_loop(0, block_total, total_block, zeros_row)
        prefix = prefix_2(totals, "ctx", add_up, zeros_row, False)

        def stat_block(block_index, running):
            row_top, row_total = running
            key_start = block_index * key_block
            keys3, _ = block_keys(key_start)
            logits = logits_of(key_start, keys3)
            new_top = jnp.maximum(row_top, jnp.max(logits, axis=-1))
            row_total = row_total * jnp.exp(row_top - new_top) + jnp.sum(
                jnp.exp(logits - new_top[..., None]), axis=-1
            )
            return (new_top, row_total)

        row_top, row_total = lax.fori_loop(
            0,
            block_total,
            stat_block,
            (
                jnp.full((head_count, query_rows), START_TOP, jnp.float32),
                jnp.zeros((head_count, query_rows), jnp.float32),
            ),
        )
        log_total = row_top + jnp.log(row_total)

        def out_block(block_index, gathered_out):
            key_start = block_index * key_block
            keys3, values3 = block_keys(key_start)
            attn_probs = jnp.exp(logits_of(key_start, keys3) - log_total[..., None]).astype(
                jnp.bfloat16
            )
            return gathered_out + jnp.einsum(
                "hqk,khd->qhd", attn_probs, values3, preferred_element_type=jnp.float32
            )

        gathered_out = lax.fori_loop(
            0, block_total, out_block, jnp.zeros((query_rows, head_count, HD), jnp.float32)
        )
        attended = gathered_out.reshape(query_rows, model_width).astype(jnp.bfloat16)
        mid_stream = inputs + matmul(attended, w_out_all)
        normed_two = layer_norm(mid_stream, ln2_gain, ln2_bias).astype(jnp.bfloat16)
        hidden = matmul(normed_two, w_up_all) + b_up
        activated = gelu_exact(hidden).astype(jnp.bfloat16)
        output_list.append((mid_stream + matmul(activated, w_down_all)).astype(jnp.bfloat16))
        cot_rows = cotangent[micro_step, 0]
        grad_down = contract_rows(activated, cot_rows)
        grad_act = contract_cols(cot_rows, w_down_all)
        _, gelu_back = jax.vjp(gelu_exact, hidden)
        grad_hidden = gelu_back(grad_act)[0].astype(jnp.bfloat16)
        grad_up = contract_rows(normed_two, grad_hidden)
        grad_bias_up = jnp.sum(grad_hidden.astype(jnp.float32), axis=0)
        grad_normed_two = contract_cols(grad_hidden, w_up_all)
        _, norm_two_back = jax.vjp(layer_norm, mid_stream, ln2_gain, ln2_bias)
        grad_mid_part, grad_gain_two, grad_bias_two = norm_two_back(grad_normed_two)
        grad_mid = cot_rows.astype(jnp.float32) + grad_mid_part
        grad_branch = grad_mid.astype(jnp.bfloat16)
        grad_outproj = contract_rows(attended, grad_branch)
        grad_attended = contract_cols(grad_branch, w_out_all).astype(jnp.bfloat16)
        grad_att3 = grad_attended.reshape(query_rows, head_count, HD)
        row_delta = jnp.einsum("qhd,qhd->hq", grad_att3.astype(jnp.float32), gathered_out)

        def grad_block(block_index, running):
            grad_query, grad_key_all, grad_value_all, penalty_grad, first_grad = running
            key_start = block_index * key_block
            keys3, values3 = block_keys(key_start)
            probs_f32 = jnp.exp(logits_of(key_start, keys3) - log_total[..., None])
            grad_probs = jnp.einsum(
                "qhd,khd->hqk", grad_att3, values3, preferred_element_type=jnp.float32
            )
            grad_logits = probs_f32 * (grad_probs - row_delta[..., None])
            penalty_grad = lax.dynamic_update_slice_in_dim(
                penalty_grad, -jnp.sum(grad_logits, axis=0), key_start, 1
            )
            first_grad = lax.dynamic_update_slice_in_dim(first_grad, grad_logits[0], key_start, 1)
            grad_scores = (grad_logits * later_heads).astype(jnp.bfloat16)
            grad_query = (
                grad_query
                + jnp.einsum("hqk,khd->qhd", grad_scores, keys3, preferred_element_type=jnp.float32)
                * score_scale
            )
            key_part = (
                jnp.einsum(
                    "hqk,qhd->khd", grad_scores, queries3, preferred_element_type=jnp.float32
                )
                * score_scale
            )
            value_part = jnp.einsum(
                "hqk,qhd->khd",
                probs_f32.astype(jnp.bfloat16),
                grad_att3,
                preferred_element_type=jnp.float32,
            )
            grad_key_all = lax.dynamic_update_slice_in_dim(
                grad_key_all, key_part.reshape(key_block, model_width), key_start, 0
            )
            grad_value_all = lax.dynamic_update_slice_in_dim(
                grad_value_all, value_part.reshape(key_block, model_width), key_start, 0
            )
            return (grad_query, grad_key_all, grad_value_all, penalty_grad, first_grad)

        grad_query, grad_key_all, grad_value_all, penalty_grad, first_grad = lax.fori_loop(
            0,
            block_total,
            grad_block,
            (
                jnp.zeros((query_rows, head_count, HD), jnp.float32),
                jnp.zeros((row_length, model_width), jnp.float32),
                jnp.zeros((row_length, model_width), jnp.float32),
                jnp.zeros((query_rows, row_length), jnp.float32),
                jnp.zeros((query_rows, row_length), jnp.float32),
            ),
        )
        column_sums = jnp.sum(penalty_grad, axis=0)
        after = prefix_2(column_sums, "ctx", add_up, zeros_row, True)
        reach_sums = after + column_sums

        def head_block(block_index, running):
            grad_query_zero, grad_key_all = running
            key_start = block_index * key_block
            _, chosen = masks(key_start)
            key_zero, first_scores = head_scores(key_start)
            flow_block = lax.dynamic_slice_in_dim(penalty_grad, key_start, key_block, 1)
            reach_block = lax.dynamic_slice_in_dim(reach_sums, key_start, key_block, 0)
            grad_picked = reach_block[None, :] - jnp.cumsum(flow_block, axis=0)
            grad_select = grad_picked * strength * jax.nn.sigmoid(first_scores) * chosen
            grad_head = (
                lax.dynamic_slice_in_dim(first_grad, key_start, key_block, 1) + grad_select
            ).astype(jnp.bfloat16)
            grad_query_zero = grad_query_zero + matmul(grad_head, key_zero) * score_scale
            key_zero_grad = contract_rows(grad_head, query_zero) * score_scale
            grad_key_all = lax.dynamic_update_slice(
                grad_key_all, key_zero_grad, (key_start, jnp.zeros((), jnp.int32))
            )
            return (grad_query_zero, grad_key_all)

        grad_query_zero, grad_key_all = lax.fori_loop(
            0, block_total, head_block, (jnp.zeros((query_rows, HD), jnp.float32), grad_key_all)
        )
        grad_query = grad_query.at[:, 0, :].add(grad_query_zero).reshape(query_rows, model_width)
        grad_key_own, grad_value_own = (
            lax.psum_scatter(grad_key_all, "ctx", scatter_dimension=0, tiled=True),
            lax.psum_scatter(grad_value_all, "ctx", scatter_dimension=0, tiled=True),
        )
        grad_project = jnp.concatenate([grad_query, grad_key_own, grad_value_own], axis=1).astype(
            jnp.bfloat16
        )
        grad_qkv = contract_rows(normed_one, grad_project)
        grad_normed_one = contract_cols(grad_project, w_qkv_all)
        _, norm_one_back = jax.vjp(layer_norm, inputs, ln1_gain, ln1_bias)
        grad_in_part, grad_gain_one, grad_bias_one = norm_one_back(grad_normed_one)
        input_grads.append((grad_mid + grad_in_part).astype(jnp.bfloat16))
        matrix_grads = (grad_qkv, grad_outproj, grad_up, grad_down)
        vector_grads = (grad_gain_one, grad_bias_one, grad_gain_two, grad_bias_two, grad_bias_up)
        matrix_grads = (
            lax.psum_scatter(matrix_grads[0], "ctx", scatter_dimension=1, tiled=True),
            lax.psum_scatter(matrix_grads[1], "ctx", scatter_dimension=1, tiled=True),
            lax.psum_scatter(matrix_grads[2], "ctx", scatter_dimension=1, tiled=True),
            lax.psum_scatter(matrix_grads[3], "ctx", scatter_dimension=1, tiled=True),
        )
        matrix_grads = (
            lax.psum_scatter(
                matrix_grads[0].astype(jnp.bfloat16), "dp", scatter_dimension=0, tiled=True
            ).astype(jnp.float32),
            lax.psum_scatter(
                matrix_grads[1].astype(jnp.bfloat16), "dp", scatter_dimension=0, tiled=True
            ).astype(jnp.float32),
            lax.psum_scatter(
                matrix_grads[2].astype(jnp.bfloat16), "dp", scatter_dimension=0, tiled=True
            ).astype(jnp.float32),
            lax.psum_scatter(
                matrix_grads[3].astype(jnp.bfloat16), "dp", scatter_dimension=0, tiled=True
            ).astype(jnp.float32),
        )
        vector_grads = lax.psum(
            (vector_grads[0], vector_grads[1], vector_grads[2], vector_grads[3], vector_grads[4]),
            ("dp", "ctx"),
        )
        if matrix_total is None:
            matrix_total = matrix_grads
            vector_total = vector_grads
        else:
            matrix_total = tuple((old + new for old, new in zip(matrix_total, matrix_grads)))
            vector_total = tuple((old + new for old, new in zip(vector_total, vector_grads)))
    layer_out = jnp.stack(output_list)[:, None]
    input_out = jnp.stack(input_grads)[:, None]
    return (
        layer_out,
        input_out,
        vector_total[0],
        vector_total[1],
        matrix_total[0],
        matrix_total[1],
        vector_total[2],
        vector_total[3],
        matrix_total[2],
        vector_total[4],
        matrix_total[3],
    )


MESH = pl.DeviceIdType.MESH
EXCLUDED = 1e30
QUERY_BLOCK = 256


def norm_parts(value):
    row_mean = jnp.mean(value, axis=-1, keepdims=True)
    centered = value - row_mean
    spread = jnp.mean(centered * centered, axis=-1, keepdims=True)
    inverse = lax.rsqrt(spread + NORM_EPSILON)
    return centered * inverse, inverse


def norm_back(xhat, inverse, grad, gain):
    scaled = grad * gain
    return (
        scaled
        - jnp.mean(scaled, axis=-1, keepdims=True)
        - xhat * jnp.mean(scaled * xhat, axis=-1, keepdims=True)
    ) * inverse


class Wires:
    def __init__(self, send_sem, recv_sem):
        self.send_sem, self.recv_sem, self.used, self.made = send_sem, recv_sem, 0, []

    def send(self, source, target, where):
        copy = pltpu.make_async_remote_copy(
            src_ref=source,
            dst_ref=target,
            send_sem=self.send_sem.at[self.used],
            recv_sem=self.recv_sem.at[self.used],
            device_id=where,
            device_id_type=MESH,
        )
        copy.start()
        self.used += 1
        self.made.append(copy)
        return copy

    def later(self, source, target, where):
        copy = pltpu.make_async_remote_copy(
            src_ref=source,
            dst_ref=target,
            send_sem=self.send_sem.at[self.used],
            recv_sem=self.recv_sem.at[self.used],
            device_id=where,
            device_id_type=MESH,
        )
        self.used += 1
        self.made.append(copy)
        return copy

    def sent(self, copy):
        copy.wait_send()
        self.made.remove(copy)

    def drain(self):
        for copy in self.made:
            copy.wait_send()


def rounded(value):
    return value.astype(jnp.bfloat16)


def folded(array):
    half = array.shape[0] // 2
    return jnp.concatenate([array[:half], array[half:]], axis=1)


def unfolded(array):
    half = array.shape[1] // 2
    return jnp.concatenate([array[:, :half], array[:, half:]], axis=0)


def arrived(like, target, sem):
    pltpu.make_async_copy(like, target, sem).wait()


def swap(index):
    return index + 1 - 2 * lax.rem(index, 2)


def layer_body(plan, loaded, names, lengths, w_down, *refs):
    given, refs = refs[: len(loaded)], refs[len(loaded) :]
    r = SimpleNamespace(**dict(zip(names, refs)))
    groups, shards = plan
    f32 = jnp.float32
    ctx, dp = lax.axis_index("ctx"), lax.axis_index("dp")
    ctx_size, tokens, model = r.x_row.shape
    width = r.out.shape[1]
    lines = ctx_size // 2
    mbs = ctx_size // groups
    hpg = width // HD
    own = r.x.shape[0]
    ff = r.w_ff.shape[0]
    row_length = tokens * ctx_size
    side, line = lax.rem(ctx, 2), ctx // 2
    my_mb, my_group = ctx // groups, lax.rem(ctx, groups)
    wires = Wires(r.send_sem, r.recv_sem)
    core, far, far_core = {"dp": swap(dp)}, {"dp": lax.rem(dp + 2, 4)}, {"dp": lax.rem(swap(dp) + 2, 4)}
    beside = {"ctx": swap(ctx)}
    upper, which = dp // 2, lax.rem(dp, 2)
    odd, distant_half = lax.rem(line, 2), line // 2
    ff_block = 2 * odd + which
    owns_block = ff_block == dp
    up_to = {"dp": 2 * upper + distant_half, "ctx": 2 * ff_block + side}
    up_from = {"dp": 2 * upper + lax.rem(line, 2), "ctx": 2 * (2 * which + line // 2) + side}
    across = {"dp": ff_block, "ctx": 2 * (2 * distant_half + upper) + side}
    around = [{"ctx": lax.rem(ctx + step, ctx_size)} for step in range(1, ctx_size)]

    mirror = {"ctx": lax.rem(line + lines // 2, lines) * 2 + side}
    ahead = {"ctx": swap(line) * 2 + side}
    beside_at, mirror_at, ahead_at = beside["ctx"], mirror["ctx"], ahead["ctx"]
    half = tokens // 4

    loads = SimpleNamespace()
    for at, name in enumerate(loaded):
        copy = pltpu.make_async_copy(given[at], getattr(r, name), r.load_sem.at[at])
        copy.start()
        setattr(loads, name, copy)
    down_load = pltpu.make_async_copy(w_down, r.w_ff, r.ff_sem.at[0])
    down_copy = pltpu.make_async_remote_copy(
        src_ref=w_down,
        dst_ref=r.w_ff,
        send_sem=r.ff_sem.at[1],
        recv_sem=r.ff_sem.at[2],
        device_id=far,
        device_id_type=MESH,
    )
    pl.when(owns_block)(down_load.start)
    barrier = pltpu.get_barrier_semaphore()
    for where in around + [core, far, far_core, up_from, across]:
        pl.semaphore_signal(barrier, inc=1, device_id=where, device_id_type=MESH)
    loads.x.wait()
    loads.w_qkv.wait()
    pl.semaphore_wait(barrier, ctx_size + 4)

    flushed = []

    def flush(name):
        at = len(flushed)
        copy = pltpu.make_async_copy(
            getattr(r, name), getattr(r, name + "_hbm"), r.out_sem.at[at]
        )
        copy.start()
        flushed.append(copy)

    def x_of(micro):
        return r.x.at[pl.ds(pl.multiple_of(micro * tokens, tokens), tokens)]

    first, second = pl.ds(0, tokens // 2), pl.ds(tokens // 2, tokens // 2)

    def x_half(micro, at):
        rows = pl.ds(pl.multiple_of(micro * tokens + at * (tokens // 2), tokens // 2), tokens // 2)
        return r.x.at[rows]

    x_mirror_a = wires.send(x_half(1 - my_mb, 0), r.x_row.at[ctx, first], mirror)
    x_beside = wires.send(x_of(my_mb), r.x_row.at[ctx], beside)
    for group in range(groups):

        @pl.when(my_group == group)
        def _():
            for kind in range(3):
                first = kind * model + group * width
                r.w_pick[dp, :, kind * width : (kind + 1) * width] = r.w_qkv[:, first : first + width]

    for kind in range(2):
        r.w_pick[dp, :, 3 * width + kind * HD : 3 * width + (kind + 1) * HD] = r.w_qkv[
            :, kind * model : kind * model + HD
        ]
    pick_far = wires.send(r.w_pick.at[dp], r.w_pick.at[dp], far)
    pick_core = wires.send(r.w_pick.at[dp], r.w_pick.at[dp], core)
    r.x_row[ctx] = x_of(my_mb)[...]

    for copy in (loads.cot, loads.w_out_own, loads.w_up_own):
        copy.wait()

    def rows_of(place):
        return pl.ds(pl.multiple_of(place * size_dp, size_dp), size_dp)

    size_dp = model // 4
    wout_far = wires.send(r.w_out_own, r.w_out.at[rows_of(dp)], far)
    wout_core = wires.send(r.w_out_own, r.w_out.at[rows_of(dp)], core)

    def up_part(peer):
        block = 2 * odd + lax.rem(peer, 2)
        return r.w_up_own.at[:, pl.ds(pl.multiple_of(block * ff, 128), ff)]

    up_in = [
        wires.send(up_part(where["dp"]), r.w_up.at[rows_of(dp)], where)
        for where in (far, far_core, core)
    ]
    r.w_out[rows_of(dp), :] = r.w_out_own[...]
    r.w_up[rows_of(dp), :] = up_part(dp)[...]
    r.cots[0] = r.cot[...]

    loads.gain_one.wait()
    loads.bias_one.wait()
    gain_one = r.gain_one[...].reshape(1, model)
    bias_one = r.bias_one[...].reshape(1, model)

    def normalise(place):
        xhat, _ = norm_parts(r.x_row[place].astype(f32))
        rows = pl.ds(pl.multiple_of(place * tokens, tokens), tokens)
        r.hat_one[rows, :] = rounded(xhat)
        r.normed_one[rows, :] = rounded(xhat * gain_one + bias_one)

    wires.sent(x_mirror_a)
    x_mirror_b = wires.send(x_half(1 - my_mb, 1), r.x_row.at[ctx, second], mirror)
    x_ahead = wires.send(x_of(my_mb), r.x_row.at[ctx], ahead)
    normalise(ctx)
    mirror_beside, mirror_ahead = swap(mirror_at), lax.rem(ahead_at + ctx_size // 2, ctx_size)

    def relay(place, part, where):
        return wires.send(r.x_row.at[place, part], r.x_row.at[place, part], where)

    x_mirror_a.wait_recv()
    a_beside = relay(mirror_at, first, beside)
    a_ahead = relay(mirror_at, first, ahead)
    x_beside.wait_recv()
    top, bottom = pl.ds(0, half), pl.ds(half, tokens - half)
    x_fwd_a = relay(beside_at, top, ahead)
    normalise(beside_at)
    x_mirror_b.wait_recv()
    b_beside = relay(mirror_at, second, beside)
    b_ahead = relay(mirror_at, second, ahead)
    x_ahead.wait_recv()
    x_fwd_b = relay(ahead_at, bottom, beside)
    a_beside.wait_recv()
    a_over = relay(mirror_beside, first, ahead)
    pl.when(owns_block)(down_copy.start)
    pick_far.wait_recv()
    pick_at = far["dp"]
    pick_fwd = wires.send(r.w_pick.at[pick_at], r.w_pick.at[pick_at], core)
    normalise(ahead_at)
    normalise(mirror_at)
    b_ahead.wait_recv()
    b_over = relay(mirror_ahead, second, beside)
    a_ahead.wait_recv()
    b_beside.wait_recv()
    normalise(mirror_beside)
    normalise(mirror_ahead)
    x_fwd_a.wait_recv()
    x_fwd_b.wait_recv()
    normalise(swap(ahead_at))
    pick_core.wait_recv()
    pick_fwd.wait_recv()
    a_over.wait_recv()
    b_over.wait_recv()
    normalise(swap(mirror_ahead))
    cot_far = wires.send(r.cot, r.cots.at[2], ahead)
    cot_core = wires.send(r.cot, r.cots.at[1], core)
    w_pick = r.w_pick[...].reshape(model, 3 * width + 2 * HD)
    r.proj[...] = rounded(matmul(r.normed_one[...], w_pick))

    def att_copy(place):
        return pltpu.make_async_remote_copy(
            src_ref=r.att.at[place],
            dst_ref=r.att_in.at[ctx],
            send_sem=r.att_send.at[place],
            recv_sem=r.att_recv.at[ctx],
            device_id={"ctx": place},
            device_id_type=MESH,
        )

    block = QUERY_BLOCK
    per_block = block // tokens
    scale = HD ** (-0.5)
    strength = 8.0 / row_length
    row_at = lax.broadcasted_iota(jnp.int32, (block, block), 0)
    col_at = lax.broadcasted_iota(jnp.int32, (block, block), 1)
    earlier = (col_at < row_at).astype(jnp.bfloat16)
    later = (col_at > row_at).astype(jnp.bfloat16)
    doc_ends, doc_end = [], 0
    for at in range(lengths.shape[2]):
        doc_end = doc_end + lengths[my_mb, 0, at]
        doc_ends.append(doc_end)

    def segment_of(places):
        total = jnp.zeros(places.shape, jnp.int32)
        for end in doc_ends:
            total += jnp.where(places >= end, 1, 0)
        return total

    r.suffix[...] = jnp.zeros_like(r.suffix)
    for start in range(0, row_length, block):
        reach = start + block
        rows = pl.ds(start, block)
        probs_ref, slope_ref = getattr(r, "probs%d" % start), getattr(r, "slope%d" % start)
        row_pos = start + lax.broadcasted_iota(jnp.int32, (block, 1), 0)
        col_pos = lax.broadcasted_iota(jnp.int32, (1, reach), 1)
        row_seg, col_seg = segment_of(row_pos), segment_of(col_pos)
        opening = (col_seg != segment_of(col_pos - 1)) | (col_pos == 0)
        pick_seg = jnp.where(opening, -1, col_seg)
        query = rounded(r.proj[rows, 3 * width : 3 * width + HD] * scale)
        key = r.proj[:reach, 3 * width + HD : 3 * width + 2 * HD]
        scores = contract_cols(query, key)
        small = jnp.exp(-jnp.abs(scores))
        soft = jnp.maximum(scores, 0.0) + jnp.log(1.0 + small)
        recip = pl.reciprocal(1.0 + small, approx=True)
        sigmoid = jnp.where(scores >= 0.0, recip, small * recip)
        chosen = (row_seg == pick_seg) & (col_pos < row_pos)
        picked = jnp.where(chosen, strength * soft, 0.0)
        slope_ref[...] = rounded(jnp.where(chosen, strength * sigmoid, 0.0))
        high = rounded(picked)
        low = rounded(picked - high.astype(f32))
        penalty = r.suffix[:, :reach] + (matmul(earlier, high) + matmul(earlier, low))
        allowed = (row_seg == col_seg) & (col_pos <= row_pos)
        penalty = jnp.where(allowed, penalty, EXCLUDED)
        r.suffix[:, :reach] += jnp.sum(picked, axis=0, keepdims=True)
        for head in range(hpg):
            at = head * HD
            query = rounded(r.proj[rows, at : at + HD] * scale)
            key = r.proj[:reach, width + at : width + at + HD]
            value = r.proj[:reach, 2 * width + at : 2 * width + at + HD]
            logits = contract_cols(query, key) - penalty
            top_logit = jnp.max(logits, axis=1, keepdims=True)
            probs = jnp.exp(logits - top_logit)
            inverse = 1.0 / jnp.sum(probs, axis=1, keepdims=True)
            probs = rounded(probs)
            probs_ref[head] = probs
            r.out[rows, at : at + HD] = matmul(probs, value) * inverse
            r.inverse[rows, head : head + 1] = inverse
        for step in range(per_block):
            place = start // tokens + step
            r.att[place] = folded(rounded(r.out[place * tokens : (place + 1) * tokens, :]))
            copy = att_copy(place)

            @pl.when(ctx != place)
            def _():
                copy.start()

    r.att_in[ctx] = r.att[ctx]
    cot_far.wait_recv()
    cot_fwd = wires.send(r.cots.at[2], r.cots.at[3], core)
    wout_far.wait_recv()
    out_at = rows_of(far["dp"])
    wout_fwd = wires.send(r.w_out.at[out_at], r.w_out.at[out_at], core)
    for copy in up_in:
        copy.wait_recv()
    wout_core.wait_recv()
    wout_fwd.wait_recv()
    for copy in (loads.gain_two, loads.bias_two, loads.b_up):
        copy.wait()
    for step in range(1, ctx_size):
        place = lax.rem(ctx + step, ctx_size)
        arrived(r.att.at[0], r.att_in.at[place], r.att_recv.at[place])
    for place in range(ctx_size):
        r.att_got[place] = unfolded(r.att_in[place])

    gain = r.gain_two[...].reshape(1, model)
    bias = r.bias_two[...].reshape(1, model)
    for at in range(4):

        @pl.when(ff_block == at)
        def _():
            r.b_own[...] = r.b_up[at * ff : (at + 1) * ff].reshape(1, ff)

    for micro in range(mbs):
        rows = pl.ds(micro * tokens, tokens)
        stream = r.x[rows, :].astype(f32)
        for group in range(groups):
            stream += matmul(
                r.att_got[micro * groups + group], r.w_out[pl.ds(group * width, width), :]
            )
        r.mid[rows, :] = stream
    xhat, inverse_two = norm_parts(r.mid[...])
    r.hat_two[...] = xhat
    r.normed[0] = rounded(xhat * gain + bias)
    to_core = wires.send(r.normed.at[0], r.normed.at[1], core)
    to_far = wires.send(r.normed.at[0], r.normed.at[2], ahead)

    def feed(slot):
        hidden = matmul(r.normed[slot], r.w_up[...]) + r.b_own[...]
        cdf = 0.5 * (1.0 + lax.erf(hidden * (2.0**-0.5)))
        density = jnp.exp(-0.5 * hidden * hidden) * ((2.0 * math.pi) ** -0.5)
        r.act[slot] = rounded(hidden * cdf)
        r.part[slot] = rounded(cdf + hidden * density)

    def feed_back(slot):
        grad = contract_cols(r.cots[slot], r.w_ff[...])
        r.grad_hid[slot] = rounded(grad * r.part[slot].astype(f32))
        r.part[slot] = rounded(contract_cols(r.grad_hid[slot], r.w_up[...]))

    def feed_out(slot):
        r.out_part[slot] = rounded(matmul(r.act[slot], r.w_ff[...]))

    part_core, part_far_core, part_far, forward = (
        wires.later(r.part.at[1], r.part_got.at[0], core),
        wires.later(r.part.at[3], r.part_got.at[1], core),
        wires.later(r.part.at[2], r.part_got.at[2], ahead),
        wires.later(r.normed.at[2], r.normed.at[3], core),
    )

    def feed_step(slot, carry):
        @pl.when(slot == 1)
        def _():
            to_core.wait_recv()

        @pl.when(slot == 2)
        def _():
            to_far.wait_recv()
            forward.start()

        @pl.when(slot == 3)
        def _():
            forward.wait_recv()

        feed(slot)
        return carry

    lax.fori_loop(0, 4, feed_step, 0)
    cot_core.wait_recv()
    cot_fwd.wait_recv()
    pl.when(owns_block)(down_load.wait)
    pl.when(jnp.logical_not(owns_block))(down_copy.wait_recv)

    def feed_back_step(step, carry):
        slot = 3 - step
        feed_back(slot)

        @pl.when(slot == 3)
        def _():
            part_far_core.start()

        @pl.when(slot == 2)
        def _():
            part_far_core.wait_recv()
            r.part[2] = rounded(r.part[2].astype(f32) + r.part_got[1].astype(f32))
            part_far.start()

        @pl.when(slot == 1)
        def _():
            part_core.start()

        return carry

    lax.fori_loop(0, 4, feed_back_step, 0)
    pair = line // 2
    collects = lax.rem(line, 2) == 1 - pair
    mirrored = {"ctx": mirror_at}
    down_steps = (r.down_grad, (upper, side, distant_half), (far, beside, mirrored), (r.down_y, r.down_x, r.down_z))
    up_steps = (r.up_grad, (upper, distant_half, side), (far, mirrored, beside), (r.up_y, r.up_z, r.up_x))
    out_steps = (r.out_piece, (odd, distant_half, side), (ahead, mirrored, beside), (r.out_a, r.out_z, r.out_x))

    def give(steps, at):
        grad, mine, where, got = steps
        index = mine[:at] + (1 - mine[at],)
        if at == 0:
            source = grad.at[index[0]]
        elif at == 1:
            source = grad.at[index[0], index[1]]
        else:
            source = grad.at[index[0], index[1], index[2]]
        return wires.send(source, got[at], where[at])

    def take(steps, at, copy):
        grad, mine, _, got = steps
        copy.wait_recv()
        if at == 0:
            grad[mine[0]] = rounded(grad[mine[0]].astype(f32) + got[0][...].astype(f32))
        elif at == 1:
            grad[mine[0], mine[1]] = rounded(
                grad[mine[0], mine[1]].astype(f32) + got[1][...].astype(f32)
            )
        else:
            return grad[mine[0], mine[1], mine[2]].astype(f32) + got[2][...].astype(f32)

    flat_cot = r.cots[...].reshape(4 * own, model)
    flat_act = r.act[...].reshape(4 * own, ff)
    grads = rounded(contract_rows(flat_cot, flat_act))
    narrow = model // ctx_size
    for at in range(ctx_size):
        r.down_grad[at // 2 % 2, at % 2, at // 4] = grads[at * narrow : (at + 1) * narrow]
    down_y = give(down_steps, 0)
    out_core, out_far_core = (
        wires.later(r.out_part.at[1], r.out_got.at[0], core),
        wires.later(r.out_part.at[3], r.out_got.at[1], core),
    )

    def out_step(step, carry):
        slot = 3 - step
        feed_out(slot)

        @pl.when(slot == 3)
        def _():
            out_far_core.start()

        @pl.when(slot == 1)
        def _():
            out_core.start()

        return carry

    lax.fori_loop(0, 4, out_step, 0)
    flat_grad = r.grad_hid[...].reshape(4 * own, ff)
    d_bias_up = jnp.sum(flat_grad.astype(f32), axis=0, keepdims=True)
    for at in range(4):
        r.vec[4 + at : 5 + at, :] = jnp.where(ff_block == at, d_bias_up, 0.0)
    flat_normed = r.normed[...].reshape(4 * own, model)
    size = model // 4
    for at in range(shards):
        grads = rounded(
            contract_rows(flat_normed, flat_grad[:, at * ff // shards : (at + 1) * ff // shards])
        )
        for row in range(4):
            r.up_grad[row // 2, row % 2, at] = grads[row * size : (row + 1) * size]
    out_far_core.wait_recv()
    r.out_part[2] = rounded(r.out_part[2].astype(f32) + r.out_got[1].astype(f32))

    part_core.wait_recv()
    part_far.wait_recv()
    grad_normed = r.part[0].astype(f32) + r.part_got[0].astype(f32) + r.part_got[2].astype(f32)
    xhat = r.hat_two[...]
    r.vec[2:3, :] = jnp.sum(grad_normed * xhat, axis=0, keepdims=True)
    r.vec[3:4, :] = jnp.sum(grad_normed, axis=0, keepdims=True)
    r.grad_mid[...] = r.cot[...].astype(f32) + norm_back(xhat, inverse_two, grad_normed, gain)
    branch = rounded(r.grad_mid[...])
    for group in range(groups):
        grad = rounded(contract_cols(branch, r.w_out[pl.ds(group * width, width), :]))
        for micro in range(mbs):
            r.att_out[micro * groups + group] = folded(
                grad[micro * tokens : (micro + 1) * tokens]
            )
    att_in = []
    for step in range(1, ctx_size):
        peer = lax.rem(ctx + step, ctx_size)
        att_in.append(wires.send(r.att_out.at[peer], r.grad_in.at[ctx], {"ctx": peer}))
    r.grad_in[ctx] = r.att_out[ctx]
    up_y = give(up_steps, 0)
    for group in range(groups):
        total = None
        for micro in range(mbs):
            some = contract_rows(
                branch[micro * tokens : (micro + 1) * tokens], r.att_got[micro * groups + group]
            )
            total = some if total is None else total + some
        total = rounded(total)
        for at in range(ctx_size):
            r.out_grad[group, at // 2 % 2, at // 4, at % 2] = folded(
                total[at * narrow : (at + 1) * narrow]
            )
    out_grad_core = wires.send(r.out_grad.at[swap(dp)], r.out_grad_got.at[0], core)
    out_grad_far_core = wires.send(
        r.out_grad.at[lax.rem(swap(dp) + 2, 4)], r.out_grad_got.at[1], core
    )
    take(down_steps, 0, down_y)
    down_x = give(down_steps, 1)
    for copy in att_in:
        copy.wait_recv()
    out_far = wires.send(r.out_part.at[2], r.out_got.at[2], ahead)
    out_grad_far_core.wait_recv()
    mine = lax.rem(dp + 2, 4)
    r.out_grad[mine] = rounded(r.out_grad[mine].astype(f32) + r.out_grad_got[1].astype(f32))
    out_grad_far = wires.send(r.out_grad.at[mine], r.out_grad_got.at[2], far)
    for place in range(ctx_size):
        r.grad_att[place] = unfolded(r.grad_in[place])

    r.suffix[...] = jnp.zeros_like(r.suffix)
    r.acc[...] = jnp.zeros_like(r.acc)

    def back_block(start):
        reach = start + block
        rows = pl.ds(start, block)
        probs_ref, slope_ref = getattr(r, "probs%d" % start), getattr(r, "slope%d" % start)
        total = None
        first = start // tokens
        grad_block = r.grad_att[first : first + per_block].reshape(block, width)
        for head in range(hpg):
            at = head * HD
            query_t = rounded((r.proj[rows, at : at + HD].astype(f32) * scale).T)
            key = r.proj[:reach, width + at : width + at + HD]
            value = r.proj[:reach, 2 * width + at : 2 * width + at + HD]
            grad = grad_block[:, at : at + HD].astype(f32) * r.inverse[rows, head : head + 1]
            delta = jnp.sum(grad * r.out[rows, at : at + HD], axis=1, keepdims=True)
            probs = probs_ref[head]
            grad_probs = contract_cols(rounded(grad), value)
            grad_logits = probs.astype(f32) * (grad_probs - delta)
            total = grad_logits if total is None else total + grad_logits
            grad_scores = rounded(grad_logits)
            r.grad_proj[rows, at : at + HD] = rounded(matmul(grad_scores, key) * scale)
            r.acc[at : at + HD, :reach] += matmul(query_t, grad_scores)
            r.acc[width + at : width + at + HD, :reach] += matmul(rounded(grad.T), probs)
        query_t = rounded((r.proj[rows, 3 * width : 3 * width + HD].astype(f32) * scale).T)
        key = r.proj[:reach, 3 * width + HD : 3 * width + 2 * HD]
        flow = r.suffix[:, :reach] + matmul(later, rounded(total))
        grad_scores = rounded(-flow * slope_ref[...].astype(f32))
        r.grad_proj[rows, 3 * width : 3 * width + HD] = rounded(matmul(grad_scores, key) * scale)
        r.acc[2 * width : 2 * width + HD, :reach] += matmul(query_t, grad_scores)
        r.suffix[:, :reach] += jnp.sum(total, axis=0, keepdims=True)

    def one_grad(place):
        rows = pl.ds(pl.multiple_of(place * tokens, tokens), tokens)
        grad = contract_cols(r.grad_proj[rows, :], r.w_pick[...].reshape(model, 3 * width + 2 * HD))
        r.vec[0:1, :] += jnp.sum(grad * r.hat_one[rows, :].astype(f32), axis=0, keepdims=True)
        r.vec[1:2, :] += jnp.sum(grad, axis=0, keepdims=True)
        return grad

    r.vec[0:2, :] = jnp.zeros((2, model), f32)
    one_side = {}

    def one_copy(source, target, kind, at, to_line):
        return pltpu.make_async_remote_copy(
            src_ref=source,
            dst_ref=target,
            send_sem=r.one_send.at[at],
            recv_sem=r.one_recv.at[kind],
            device_id={"ctx": to_line * 2 + side},
            device_id_type=MESH,
        )

    def to_near(at):
        return one_copy(r.one_ready.at[at], r.one_near, 0, at, at)

    def to_far(at):
        return one_copy(r.one_ready.at[at], r.one_far, 1, at, at)

    def to_collect(at):
        return one_copy(r.one_ready.at[at], r.one_pair.at[at % 2], 2 + at % 2, at, swap(line))

    def finish_block(at):
        start = at * block
        reach = start + block
        r.grad_proj[start:reach, width : 3 * width] = rounded(r.acc[: 2 * width, start:reach].T)
        r.grad_proj[start:reach, 3 * width + HD :] = rounded(r.acc[2 * width :, start:reach].T)
        one_side[at] = wires.later(r.one_piece.at[at], r.one_side.at[at], beside)

        def one_step(step, carry):
            r.one_own[at] = one_grad(at * 2 + lax.rem(1 - side + step, 2))

            @pl.when(step == 0)
            def _():
                r.one_piece[at] = rounded(r.one_own[at])
                one_side[at].start()

            return carry

        lax.fori_loop(0, 2, one_step, 0)

    def pass_on(at):
        one_side[at].wait_recv()
        r.one_ready[at] = rounded(r.one_own[at] + r.one_side[at].astype(f32))
        near, shared = to_near(at), to_collect(at)

        if at != 2:

            @pl.when((pair == at // 2) & (line != at))
            def _():
                near.start()

        @pl.when((pair != at // 2) & jnp.logical_not(collects))
        def _():
            shared.start()

    def collect(at):
        distant = to_far(at)

        @pl.when((pair != at // 2) & collects)
        def _():
            arrived(r.one_ready.at[at], r.one_pair.at[at % 2], r.one_recv.at[2 + at % 2])
            r.one_ready[at] = rounded(
                r.one_own[at] + r.one_side[at].astype(f32) + r.one_pair[at % 2].astype(f32)
            )
            distant.start()

    back_block(3 * block)
    finish_block(3)
    back_block(2 * block)
    finish_block(2)
    take(down_steps, 1, down_x)
    down_z = give(down_steps, 2)
    take(up_steps, 0, up_y)
    up_z = give(up_steps, 1)
    back_block(block)
    finish_block(1)
    pass_on(3)
    back_block(0)
    finish_block(0)

    size = model // 4
    part = math.gcd(width, 3 * model // ctx_size)
    per = width // part
    folded_part, folded_head = part // 2, HD // 2

    def store_qkv(grads, parts):
        for at in range(4):
            cols = slice(at * size, (at + 1) * size)
            for source, target, count in parts:
                r.qkv_grad[at, target : target + count // 2, :] = folded(
                    grads[source : source + count, cols]
                )

    tail = 3 * width // 2
    grads_q = rounded(
        contract_rows(
            jnp.concatenate(
                [r.grad_proj[:, :width], r.grad_proj[:, 3 * width : 3 * width + HD]], axis=1
            ),
            r.normed_one[...],
        )
    )
    store_qkv(
        grads_q,
        [(at * part, at * folded_part, part) for at in range(per)] + [(width, tail, HD)],
    )
    grads_kv = rounded(matmul(rounded(r.acc[...]), r.normed_one[...]))
    store_qkv(
        grads_kv,
        [(at * part, (per + at) * folded_part, part) for at in range(2 * per)]
        + [(2 * width, tail + folded_head, HD)],
    )
    qkv_far_core = wires.send(r.qkv_grad.at[lax.rem(swap(dp) + 2, 4)], r.qkv_got.at[1], core)
    qkv_core = wires.send(r.qkv_grad.at[swap(dp)], r.qkv_got.at[0], core)
    out_grad_core.wait_recv()
    out_grad_far.wait_recv()
    r.out_piece[...] = rounded(
        r.out_grad[dp].astype(f32)
        + r.out_grad_got[0].astype(f32)
        + r.out_grad_got[2].astype(f32)
    )
    out_a = give(out_steps, 0)
    for row in range(8):
        r.vec_rows[row] = r.vec[row : row + 1, :]
    vec_in = []
    for step in range(1, ctx_size):
        peer = lax.rem(ctx + step, ctx_size)
        vec_in.append(wires.send(r.vec_rows.at[peer], r.vec_got.at[ctx], {"ctx": peer}))
    r.vec_got[ctx] = r.vec_rows[ctx]
    pass_on(2)
    qkv_far_core.wait_recv()
    r.qkv_grad[mine] = rounded(r.qkv_grad[mine].astype(f32) + r.qkv_got[1].astype(f32))
    qkv_far = wires.send(r.qkv_grad.at[mine], r.qkv_got.at[2], far)
    collect(3)
    pass_on(1)
    pass_on(0)
    near_two = to_near(2)

    @pl.when(line == 3)
    def _():
        near_two.start()

    take(up_steps, 1, up_z)
    up_x = give(up_steps, 2)
    collect(2)
    qkv_core.wait_recv()
    qkv_far.wait_recv()
    r.qkv_sum[...] = rounded(
        r.qkv_grad[dp].astype(f32) + r.qkv_got[0].astype(f32) + r.qkv_got[2].astype(f32)
    )
    slots = r.deal_got.shape[0]

    def outgoing(kind, half):
        section = (kind * groups + my_group) * per + half
        target, slot = section // slots, lax.rem(section, slots)
        index = kind * per + half
        return target, slot, index, pltpu.make_async_remote_copy(
            src_ref=r.qkv_sum.at[pl.ds(index * folded_part, folded_part)],
            dst_ref=r.deal_got.at[slot, my_mb],
            send_sem=r.deal_send.at[index],
            recv_sem=r.deal_recv.at[slot, my_mb],
            device_id={"ctx": target},
            device_id_type=MESH,
        )

    def extra_copy(kind):
        return pltpu.make_async_remote_copy(
            src_ref=r.qkv_sum.at[pl.ds(tail + kind * folded_head, folded_head)],
            dst_ref=r.extra_got.at[ctx],
            send_sem=r.extra_send.at[kind],
            recv_sem=r.extra_recv.at[ctx],
            device_id={"ctx": kind * groups * per // slots},
            device_id_type=MESH,
        )

    for kind in range(3):
        for half in range(per):
            target, slot, index, copy = outgoing(kind, half)

            @pl.when(target != ctx)
            def _():
                copy.start()

            @pl.when(target == ctx)
            def _():
                r.deal_got[slot, my_mb] = r.qkv_sum[
                    index * folded_part : (index + 1) * folded_part, :
                ]

    for kind in range(2):
        target = kind * groups * per // slots
        copy = extra_copy(kind)

        @pl.when(ctx != target)
        def _():
            copy.start()

        @pl.when(ctx == target)
        def _():
            r.extra_got[ctx] = r.qkv_sum[
                tail + kind * folded_head : tail + (kind + 1) * folded_head, :
            ]

    collect(1)
    collect(0)
    take(out_steps, 0, out_a)
    out_z = give(out_steps, 1)
    for copy in vec_in:
        copy.wait_recv()
    total = r.vec_got[0]
    for at in range(1, ctx_size):
        total += r.vec_got[at]
    r.vec_sum[...] = total
    vec_out = [
        wires.send(r.vec_sum, r.vecs.at[dp], where) for where in (core, far, far_core)
    ]
    r.vecs[dp] = total
    for copy in vec_out:
        copy.wait_recv()
    r.vec_total[...] = (r.vecs[0] + r.vecs[1]) + (r.vecs[2] + r.vecs[3])
    vec_all = [wires.send(r.vec_total, r.vec_last.at[ctx], where) for where in around]
    r.vec_last[ctx] = r.vec_total[...]
    r.down_sum[...] = rounded(take(down_steps, 2, down_z))
    down_final = pltpu.make_async_remote_copy(
        src_ref=r.down_sum,
        dst_ref=r.down_final,
        send_sem=r.up_send.at[1],
        recv_sem=r.up_recv.at[1],
        device_id=across,
        device_id_type=MESH,
    )

    @pl.when(jnp.logical_not(owns_block))
    def _():
        down_final.start()

    @pl.when(owns_block)
    def _():
        r.down_final[...] = r.down_sum[...]

    out_core.wait_recv()
    out_far.wait_recv()
    r.layer[...] = rounded(
        r.mid[...]
        + (r.out_part[0].astype(f32) + r.out_got[0].astype(f32) + r.out_got[2].astype(f32))
    )
    flush("layer")
    r.up_sum[...] = rounded(take(up_steps, 2, up_x))
    stays = (2 * upper + distant_half == dp) & (2 * ff_block + side == ctx)
    up_copy = pltpu.make_async_remote_copy(
        src_ref=r.up_sum,
        dst_ref=r.up_final,
        send_sem=r.up_send.at[0],
        recv_sem=r.up_recv.at[0],
        device_id=up_to,
        device_id_type=MESH,
    )

    @pl.when(jnp.logical_not(stays))
    def _():
        up_copy.start()

    @pl.when(stays)
    def _():
        r.up_final[...] = r.up_sum[...]

    take(out_steps, 1, out_z)
    out_x = give(out_steps, 2)
    xhat, inverse_one = norm_parts(r.x[...].astype(f32))
    arrived(r.one_ready.at[0], r.one_near, r.one_recv.at[0])
    arrived(r.one_ready.at[0], r.one_far, r.one_recv.at[1])
    near = r.one_ready[line].astype(f32) + r.one_near[...].astype(f32)
    distant = r.one_far[...].astype(f32)
    for micro in range(mbs):
        grad = jnp.where(pair == micro, near, distant)
        rows = slice(micro * tokens, (micro + 1) * tokens)
        r.d_x[rows, :] = rounded(
            r.grad_mid[rows, :] + norm_back(xhat[rows], inverse_one[rows], grad, gain_one)
        )
    flush("d_x")
    r.d_out[...] = unfolded(take(out_steps, 2, out_x)).T
    flush("d_out")

    @pl.when(jnp.logical_not(stays))
    def _():
        up_copy.wait_send()
        up_copy.wait_recv()

    r.d_up[...] = r.up_final[...].astype(f32)
    flush("d_up")

    @pl.when(jnp.logical_not(owns_block))
    def _():
        down_final.wait_send()
        down_final.wait_recv()

    @pl.when(owns_block)
    def _():
        down_copy.wait_send()

    r.d_down[...] = r.down_final[...].astype(f32)
    flush("d_down")

    for kind in range(3):
        for half in range(per):
            target, slot, index, copy = outgoing(kind, half)

            @pl.when(target != ctx)
            def _():
                copy.wait_send()

    for slot in range(slots):
        section = ctx * slots + slot
        source_group = lax.rem(section // per, groups)
        for place in range(mbs):

            @pl.when(place * groups + source_group != ctx)
            def _():
                arrived(
                    r.qkv_sum.at[pl.ds(0, folded_part)],
                    r.deal_got.at[slot, place],
                    r.deal_recv.at[slot, place],
                )

        total = r.deal_got[slot, 0].astype(f32)
        for place in range(1, mbs):
            total += r.deal_got[slot, place].astype(f32)
        r.deal_sum[slot * part : (slot + 1) * part, :] = unfolded(total)
    for kind in range(2):
        section = kind * groups * per
        target, slot = section // slots, section % slots
        copy = extra_copy(kind)

        @pl.when(ctx != target)
        def _():
            copy.wait_send()

        @pl.when(ctx == target)
        def _():
            total = jnp.zeros((folded_head, 2 * size), f32)
            for place in range(ctx_size):
                if place != target:
                    arrived(
                        r.qkv_sum.at[pl.ds(0, folded_head)], r.extra_got.at[place], r.extra_recv.at[place]
                    )
                total += r.extra_got[place].astype(f32)
            r.deal_sum[slot * part : slot * part + HD, :] += unfolded(total)

    r.d_qkv[...] = r.deal_sum[...].T
    flush("d_qkv")
    for copy in vec_all:
        copy.wait_recv()
    for row in range(4):
        r.d_vec[row : row + 1, :] = r.vec_last[row]
        r.d_bias[row] = r.vec_last[4 + row]
    flush("d_vec")
    flush("d_bias")
    wires.drain()
    for place in range(ctx_size):
        copy = att_copy(place)

        @pl.when(ctx != place)
        def _():
            copy.wait_send()

    for at in range(lines):
        copy = to_near(at)

        @pl.when(line != at)
        def _():
            copy.wait_send()

    for copy in flushed:
        copy.wait()


LAYER_COPIES = 76


def layer(collective_id, groups, shards, lengths, w_down, large):
    bf16, f32 = jnp.bfloat16, jnp.float32
    own, model = large["x"].shape
    ctx_size = lax.axis_size("ctx")
    tokens = own * groups // ctx_size
    hpg = model // HD // groups
    width = hpg * HD
    row_length = ctx_size * tokens
    lines = ctx_size // 2
    ff = w_down.shape[0]
    size, shard = model // 4, 3 * model // ctx_size
    part = math.gcd(width, shard)
    slots, mbs = shard // part, ctx_size // groups
    picked = 3 * width + 2 * HD
    vec_rows = 8
    narrow = model // ctx_size
    vmem = pl.BlockSpec(memory_space=pltpu.VMEM)
    anywhere = pl.BlockSpec(memory_space=pl.ANY)
    outs = dict(
        layer=((own, model), bf16),
        d_x=((own, model), bf16),
        d_vec=((4, model), f32),
        d_bias=((4, ff // model, model), f32),
        d_qkv=((size, shard), f32),
        d_out=((size, narrow), f32),
        d_up=((size, ff // shards), f32),
        d_down=((narrow, ff), f32),
    )
    scratch = {name: (array.shape, array.dtype) for name, array in large.items()}
    scratch |= dict(
        x_row=((ctx_size, tokens, model), bf16),
        hat_one=((row_length, model), bf16),
        normed_one=((row_length, model), bf16),
        w_pick=((4, size, picked), bf16),
        proj=((row_length, picked), bf16),
        w_out=((model, model), bf16),
        w_up=((model, ff), bf16),
        out=((row_length, width), f32),
        inverse=((row_length, hpg), f32),
        att=((ctx_size, tokens // 2, 2 * width), bf16),
        att_in=((ctx_size, tokens // 2, 2 * width), bf16),
        b_own=((1, ff), f32),
        att_got=((ctx_size, tokens, width), bf16),
        cots=((4, own, model), bf16),
        mid=((own, model), f32),
        hat_two=((own, model), f32),
        grad_mid=((own, model), f32),
        normed=((4, own, model), bf16),
        act=((4, own, ff), bf16),
        grad_hid=((4, own, ff), bf16),
        part=((4, own, model), bf16),
        out_part=((4, own, model), bf16),
        part_got=((3, own, model), bf16),
        out_got=((3, own, model), bf16),
        att_out=((ctx_size, tokens // 2, 2 * width), bf16),
        grad_in=((ctx_size, tokens // 2, 2 * width), bf16),
        grad_att=((ctx_size, tokens, width), bf16),
        down_grad=((2, 2, 2, narrow, ff), bf16),
        down_y=((2, 2, narrow, ff), bf16),
        down_x=((2, narrow, ff), bf16),
        down_z=((narrow, ff), bf16),
        up_grad=((2, 2, 2, size, ff // shards), bf16),
        up_y=((2, 2, size, ff // shards), bf16),
        up_z=((2, size, ff // shards), bf16),
        up_x=((size, ff // shards), bf16),
        up_sum=((size, ff // shards), bf16),
        up_final=((size, ff // shards), bf16),
        down_sum=((narrow, ff), bf16),
        down_final=((narrow, ff), bf16),
        w_ff=(w_down.shape, bf16),
        out_grad=((4, 2, 2, 2, narrow // 2, 2 * size), bf16),
        out_grad_got=((3, 2, 2, 2, narrow // 2, 2 * size), bf16),
        out_piece=((2, 2, 2, narrow // 2, 2 * size), bf16),
        out_a=((2, 2, narrow // 2, 2 * size), bf16),
        out_z=((2, narrow // 2, 2 * size), bf16),
        out_x=((narrow // 2, 2 * size), bf16),
        suffix=((1, row_length), f32),
        acc=((2 * width + HD, row_length), f32),
        grad_proj=((row_length, picked), bf16),
        one_piece=((lines, tokens, model), bf16),
        one_own=((lines, tokens, model), f32),
        one_side=((lines, tokens, model), bf16),
        one_ready=((lines, tokens, model), bf16),
        one_near=((tokens, model), bf16),
        one_far=((tokens, model), bf16),
        one_pair=((2, tokens, model), bf16),
        qkv_grad=((4, picked // 2, 2 * size), bf16),
        qkv_got=((3, picked // 2, 2 * size), bf16),
        qkv_sum=((picked // 2, 2 * size), bf16),
        deal_got=((slots, mbs, part // 2, 2 * size), bf16),
        deal_sum=((shard, size), f32),
        extra_got=((ctx_size, HD // 2, 2 * size), bf16),
        vec=((vec_rows, model), f32),
        vec_rows=((vec_rows, 1, model), f32),
        vec_got=((ctx_size, 1, model), f32),
        vec_sum=((1, model), f32),
        vecs=((4, 1, model), f32),
        vec_total=((1, model), f32),
        vec_last=((ctx_size, 1, model), f32),
    )
    for start in range(0, row_length, QUERY_BLOCK):
        reach = start + QUERY_BLOCK
        scratch["probs%d" % start] = ((hpg, QUERY_BLOCK, reach), bf16)
        scratch["slope%d" % start] = ((QUERY_BLOCK, reach), bf16)
    dma = pltpu.SemaphoreType.DMA
    sems = dict(
        send_sem=dma((LAYER_COPIES,)),
        recv_sem=dma((LAYER_COPIES,)),
        load_sem=dma((len(large),)),
        att_send=dma((ctx_size,)),
        att_recv=dma((ctx_size,)),
        one_send=dma((lines,)),
        one_recv=dma((4,)),
        out_sem=dma((len(outs),)),
        ff_sem=dma((3,)),
        up_send=dma((2,)),
        up_recv=dma((2,)),
        deal_send=dma((3 * (width // part),)),
        deal_recv=dma((slots, mbs)),
        extra_send=dma((2,)),
        extra_recv=dma((ctx_size,)),
    )
    names = [name + "_hbm" for name in outs] + list(outs) + list(scratch) + list(sems)
    scratch = outs | scratch
    return pl.pallas_call(
        partial(layer_body, (groups, shards), list(large), names),
        out_shape=[jax.ShapeDtypeStruct(*spec) for spec in outs.values()],
        in_specs=[pl.BlockSpec(memory_space=pltpu.SMEM)] + [anywhere] * (1 + len(large)),
        out_specs=[anywhere] * len(outs),
        scratch_shapes=[pltpu.VMEM(*spec) for spec in scratch.values()] + list(sems.values()),
        compiler_params=pltpu.CompilerParams(
            collective_id=collective_id, has_side_effects=True, vmem_limit_bytes=63 * 1024 * 1024
        ),
        name="layer",
    )(lengths, w_down, *large.values())


def finish_body(*refs):
    sources, targets = refs[:8], refs[8:]
    for source, target in zip(sources[:6], targets[:6]):
        target[...] = source[...]
    for row in range(4):
        targets[6 + row][...] = sources[6][row]
    columns = sources[7].shape[2]
    rows = sources[7].shape[1]
    for at in range(4 * rows):
        targets[10][at * columns : (at + 1) * columns] = sources[7][at // rows, at % rows]


def finish(*arrays):
    vmem = pl.BlockSpec(memory_space=pltpu.VMEM)
    shape = jax.ShapeDtypeStruct
    model = arrays[6].shape[1]
    return pl.pallas_call(
        finish_body,
        out_shape=[shape(array.shape, array.dtype) for array in arrays[:6]]
        + [shape((model,), jnp.float32)] * 4
        + [shape((arrays[7].size,), jnp.float32)],
        in_specs=[vmem] * len(arrays),
        out_specs=[vmem] * 11,
        name="finish",
    )(*arrays)


def per_head_device(
    layer_input,
    doc_lengths,
    ln1_gain,
    ln1_bias,
    w_qkv,
    w_out,
    ln2_gain,
    ln2_bias,
    w_up,
    b_up,
    w_down,
    cotangent,
):
    mbs, _, tokens, model = layer_input.shape
    ctx_size, dp_size = lax.axis_size("ctx"), lax.axis_size("dp")
    large = dict(
        x=layer_input.reshape(mbs * tokens, model),
        w_qkv=w_qkv,
        gain_one=ln1_gain,
        bias_one=ln1_bias,
        cot=cotangent.reshape(mbs * tokens, model),
        w_out_own=w_out,
        w_up_own=w_up,
        gain_two=ln2_gain,
        bias_two=ln2_bias,
        b_up=b_up,
    )
    layer_out, d_x, d_vec, d_bias, d_qkv, d_out, d_up, d_down = layer(
        0, ctx_size // mbs, ctx_size // dp_size, doc_lengths, w_down, large
    )
    layer_out, d_x, d_qkv, d_out, d_up, d_down, gain_one, bias_one, gain_two, bias_two, d_bias = finish(
        layer_out, d_x, d_qkv, d_out, d_up, d_down, d_vec, d_bias
    )
    return (
        layer_out.reshape(mbs, 1, tokens, model),
        d_x.reshape(mbs, 1, tokens, model),
        gain_one,
        bias_one,
        d_qkv,
        d_out,
        gain_two,
        bias_two,
        d_up,
        d_bias,
        d_down.T,
    )


def on_device(*arguments):
    layer_input = arguments[0]
    mbs, model = layer_input.shape[0], layer_input.shape[3]
    heads, ctx_size, dp_size = model // HD, lax.axis_size("ctx"), lax.axis_size("dp")
    groups = ctx_size // mbs
    fits = (
        ctx_size % mbs == 0
        and heads % groups == 0
        and dp_size == 4
        and ctx_size % dp_size == 0
        and ctx_size == 8
        and mbs == 2
        and arguments[9].shape[0] == 4 * model
        and (layer_input.shape[2] * ctx_size) % QUERY_BLOCK == 0
    )
    return (per_head_device if fits else per_token_device)(*arguments)


def solution(mesh):
    return jax.shard_map(
        on_device,
        mesh=mesh,
        in_specs=(
            P(None, "dp", "ctx", None),
            P(None, "dp", None),
            P(),
            P(),
            P("dp", None),
            P("dp", None),
            P(),
            P(),
            P("dp", None),
            P(),
            P("dp", None),
            P(None, "dp", "ctx", None),
        ),
        out_specs=(
            P(None, "dp", "ctx", None),
            P(None, "dp", "ctx", None),
            P(),
            P(),
            P("dp", "ctx"),
            P("dp", "ctx"),
            P(),
            P(),
            P("dp", "ctx"),
            P(),
            P("dp", "ctx"),
        ),
        check_vma=False,
    )
```
